32 devices in a mesh: grp: 2 (over y), head: 4 (over z), tm: 4 (over x, core).
Axes of the slice: x: 2, y: 2, z: 4, core: 2. Of those that a mesh axis runs over, the one named last changes fastest.
Arguments:
- query_rows: bfloat16 [32, 64, 3072], P(('grp', 'tm'), 'head'), parts along dimension 0, may hold values from -180 to 180
- key_rows: bfloat16 [32, 64, 3072], P(('grp', 'tm'), 'head'), parts along dimension 0, may hold values from -6 to 6
- value_rows: bfloat16 [32, 64, 3072], P(('grp', 'tm'), 'head'), parts along dimension 0, may hold values from -6 to 6
- pair_list: int32 [32, 32], P('grp'), parts along dimension 0, may hold values from 0 to 15, as said below
- block_tokens: int32 [32], P('grp'), parts along dimension 0, may hold values from 1 to 64, 768 in all
Outputs:
- attended: bfloat16 [32, 64, 3072], P(('grp', 'tm'), 'head'), parts along dimension 0
The draws below stay inside these ranges and needn't reach their ends.
There are 2 independent parts, one for each index of `grp`. The reference program is written for one: setup_inputs(seed, part) draws one part's arguments, and reference() takes and returns one part's arrays. A program takes and returns all parts, laid end to end along the dimension named above; each array names one. Nothing has to cross between parts.
Inputs may be any that keep to these rules, and one draw needn't show every extreme that they name: `pair_list`: row q names q in column 0 and q xor 1 in column 1; a block may be named twice in a row. The query blocks of one time shard name at most 2 different blocks of a time shard beside it and at most 1 of a time shard two or more away; both bounds are reached.
All inputs are finite; a program needn't handle non-finite values.
Results may differ from the reference program's by a relative error of at most 0.0012.
The reference program's roundings to bfloat16 on the way (of `query_rot`, `key_rot`, `value_rot` and `weights_half`) count: a program that leaves them out, or rounds other values in their place, can miss the bound.
Values may be sent and summed in bfloat16 or wider, within the bound.
No kernel may reach another device: no remote copies, remote signals or barrier semaphores. Data moves between devices by JAX's collectives and lax.ppermute only.
A program may use at most 128 MiB of HBM per device.

```python
import math
import jax
import jax.numpy as jnp
import numpy as np
from jax import lax

HEADS = 24
HD = 128
BLK = 64
KPB = 32
NB_DEV = 4
NBLK = 16


def attention_inputs(key):
    base_key = jax.random.fold_in(key, 31)
    query_seed, key_seed = jax.random.split(base_key)
    query_all = jnp.clip(jax.random.normal(query_seed, (NBLK, BLK, HEADS, HD), jnp.float32), -6.0, 6.0)
    key_all = jnp.clip(jax.random.normal(key_seed, (NBLK, BLK, HEADS, HD), jnp.float32), -6.0, 6.0)
    return (query_all.reshape(NBLK, BLK, HEADS * HD), key_all.reshape(NBLK, BLK, HEADS * HD))


def draw_query_rows(key, part):
    return attention_inputs(key)[0].astype(jnp.bfloat16)


def draw_key_rows(key, part):
    return attention_inputs(key)[1].astype(jnp.bfloat16)


def draw_pair_list(key, part):
    seeds = jax.random.split(jax.random.fold_in(key, 47), 8)
    shards = NBLK // NB_DEV
    blocks = jnp.arange(NBLK, dtype=jnp.int32)
    owner = blocks // NB_DEV
    inside = blocks % NB_DEV
    first_pick = jax.random.randint(seeds[0], (shards, shards), 0, NB_DEV)
    step_pick = jax.random.randint(seeds[1], (shards, shards), 1, NB_DEV)
    second_pick = (first_pick + step_pick) % NB_DEV
    far_pick = jax.random.randint(seeds[2], (shards, shards), 0, NB_DEV)
    offsets = jax.random.randint(seeds[3], (NBLK, KPB - 12), -3, 4)
    local_cols = owner[:, None] * NB_DEV + jnp.clip(inside[:, None] + offsets, 0, NB_DEV - 1)
    upper = jnp.where(owner + 1 < shards, owner + 1, owner - 1)
    lower = jnp.where(owner >= 1, owner - 1, owner + 1)
    up_col = upper * NB_DEV + jnp.where(inside % 2 == 0, first_pick[owner, upper], second_pick[owner, upper])
    coin_flip = jax.random.randint(seeds[4], (NBLK,), 0, 2)
    low_col = lower * NB_DEV + jnp.where(coin_flip == 0, first_pick[owner, lower], second_pick[owner, lower])
    span_top = max(shards - 2, 1)
    dist_first = jax.random.randint(seeds[5], (NBLK, 8), 0, span_top)
    dist_second = jax.random.randint(seeds[6], (NBLK, 8), 0, span_top)
    reach = 2 + jnp.minimum(dist_first, dist_second)
    side_sign = jax.random.randint(seeds[7], (NBLK, 8), 0, 2) * 2 - 1
    target = owner[:, None] + side_sign * reach
    target = jnp.where((target >= 0) & (target < shards), target, owner[:, None] - side_sign * reach)
    usable = (target >= 0) & (target < shards)
    safe_target = jnp.clip(target, 0, shards - 1)
    owner_wide = jnp.broadcast_to(owner[:, None], (NBLK, 8))
    far_cols = jnp.where(usable, safe_target * NB_DEV + far_pick[owner_wide, safe_target], blocks[:, None])
    columns = [blocks[:, None], (blocks ^ 1)[:, None], local_cols, up_col[:, None], low_col[:, None], far_cols]
    return jnp.concatenate(columns, axis=1).astype(jnp.int32)


def block_levels(rng, extent, cuts, least, high):
    factor_of, own = 1.0, jax.random.fold_in(rng, 6)
    for axis_at, blocks in cuts:
        draws = jnp.exp(jax.random.uniform(jax.random.fold_in(own, axis_at), (blocks,), jnp.float32, least / len(cuts), high / len(cuts)))
        factor_of = factor_of * jnp.repeat(draws, extent[axis_at] // blocks).reshape([-1 if axis == axis_at else 1 for axis in range(len(extent))])
    return factor_of


def length_profile(number_of, total, most, skew):
    weights = [(1 << 20) // math.isqrt(rank ** skew) + 1 for rank in range(2, number_of + 1)]
    rest, holding = total - most - (number_of - 1), [1] * (number_of - 1)
    while rest > 0:
        candidates = [i for i in range(number_of - 1) if holding[i] < most]
        pool, budget = sum([weights[i] for i in candidates]), rest
        for i in candidates:
            extra = min(most - holding[i], max(1, budget * weights[i] // pool), rest)
            holding[i] = holding[i] + extra
            rest = rest - extra
    return np.array([most] + holding)


def ragged(own_key, count, total, bound, slope):
    if count == 2:
        one = jax.random.randint(own_key, (), max(1, total - bound), min(bound, total - 1) + 1)
        return jnp.stack([one, total - one])
    sizes = jnp.asarray(length_profile(count, total, bound, slope), jnp.int32)
    couples = (count - 1) // 2
    donor, receiver = sizes[1:1 + 2 * couples:2], sizes[2:2 + 2 * couples:2]
    margin = jnp.minimum(donor - 1, bound - receiver)
    moved = jax.random.randint(jax.random.fold_in(own_key, 1), (couples,), 0, 1 << 20) % (margin + 1)
    sizes = sizes.at[1:1 + 2 * couples:2].set(donor - moved).at[2:2 + 2 * couples:2].set(receiver + moved)
    return sizes[jax.random.permutation(jax.random.fold_in(own_key, 2), count)]


def bell_draw(own_key, dims, deviation, most, cuts=(), held_as=jnp.bfloat16):
    drawn = jax.random.normal(own_key, dims, jnp.float32) * deviation
    if len(cuts) > 0:
        drawn = block_levels(own_key, dims, cuts, -0.22, 0.18) * drawn
    return jnp.clip(drawn, min=-most, max=most).astype(held_as)


def setup_inputs(seed: int = 0, part: int = 0) -> dict:
    key_list = jax.random.split(jax.random.key(seed), 6)
    part_keys = jax.random.split(jax.random.fold_in(key_list[5], part), 6)
    query_rows = draw_query_rows(jax.random.fold_in(jax.random.fold_in(key_list[5], part), 71), part)
    key_rows = draw_key_rows(jax.random.fold_in(jax.random.fold_in(key_list[5], part), 71), part)
    value_rows = bell_draw(part_keys[2], (NBLK, BLK, HEADS * HD), 1.0, 6.0, ((0, 4), (1, 4)))
    pair_list = draw_pair_list(jax.random.fold_in(jax.random.fold_in(key_list[5], part), 71), part)
    block_tokens = ragged(part_keys[4], NBLK, NBLK * BLK * 3 // 4, BLK, 2).astype(jnp.int32)
    return {"query_rows": query_rows, "key_rows": key_rows, "value_rows": value_rows, "pair_list": pair_list, "block_tokens": block_tokens}


def sign_table(dimension):
    indices = jnp.arange(dimension, dtype=jnp.int32)
    common = indices[:, None] & indices[None, :]
    parity = jnp.zeros((dimension, dimension), jnp.int32)
    for bit_level in range(dimension.bit_length() - 1):
        parity = parity + (common >> bit_level & 1)
    return jnp.where(parity % 2 == 0, 1.0, -1.0).astype(jnp.float32)

def reference(query_rows, key_rows, value_rows, pair_list, block_tokens):
    sign_rows = sign_table(HD)
    sign_half = sign_rows.astype(jnp.bfloat16)
    rotate_scale = 1.0 / math.sqrt(HD)
    score_scale = 1.0 / math.sqrt(HD)

    def rotate(source):
        flattened = source.reshape(-1, HD)
        turned = jnp.dot(flattened, sign_half, preferred_element_type=jnp.float32) * rotate_scale
        return turned.astype(jnp.bfloat16).reshape(NBLK, BLK, HEADS, HD)
    query_rot = rotate(query_rows)
    key_rot = rotate(key_rows)
    value_rot = rotate(value_rows)
    positions = jnp.arange(BLK, dtype=jnp.int32)
    live_keys = positions[None, :] < block_tokens[:, None]
    earlier = jnp.arange(KPB)[:, None] > jnp.arange(KPB)[None, :]

    def one_block(block_id):
        listed = pair_list[block_id]
        repeated = jnp.any((listed[:, None] == listed[None, :]) & earlier, axis=1)
        key_keep = (live_keys[listed] & ~repeated[:, None]).reshape(KPB * BLK)
        key_block = key_rot[listed].reshape(KPB * BLK, HEADS, HD).astype(jnp.float32)
        value_block = value_rot[listed].reshape(KPB * BLK, HEADS, HD).astype(jnp.float32)
        query_block = query_rot[block_id].astype(jnp.float32)
        scores = jnp.einsum('qhd,khd->hqk', query_block, key_block) * score_scale
        scores = jnp.where(key_keep[None, None, :], scores, -1e+30)
        row_peak = lax.optimization_barrier(jnp.max(scores, axis=-1, keepdims=True))
        weights = jnp.exp(scores - row_peak)
        denominator = lax.optimization_barrier(jnp.sum(weights, axis=-1))
        weights_half = lax.optimization_barrier(weights.astype(jnp.bfloat16)).astype(jnp.float32)
        mixed_rows = jnp.einsum('hqk,khd->qhd', weights_half, value_block)
        mixed_rows = mixed_rows / jnp.transpose(denominator)[:, :, None]
        turned = jnp.dot(mixed_rows.reshape(-1, HD), sign_rows, precision=lax.Precision.HIGHEST) * rotate_scale
        turned = turned.reshape(BLK, HEADS * HD)
        live_rows = positions[:, None] < block_tokens[block_id]
        return jnp.where(live_rows, turned, 0.0).astype(jnp.bfloat16)
    return lax.map(one_block, jnp.arange(NBLK, dtype=jnp.int32))
```

```python
import functools
import math

import jax
import jax.numpy as jnp
import numpy as np
from jax import lax
from jax.experimental import pallas as pl
from jax.experimental.pallas import tpu as pltpu
from jax.sharding import PartitionSpec as P

HD = 128
BLK = 64
NEG = -1e30
ROTATE_SCALE = 1.0 / math.sqrt(HD)
SCORE_SCALE = 1.0 / math.sqrt(HD)
VMEM = 48 * 1024 * 1024


def sign_matrix(width):
    ids = np.arange(HD)
    common = ids[:, None] & ids[None, :]
    parity = np.zeros((HD, HD), np.int64)
    for bit in range(HD.bit_length() - 1):
        parity += (common >> bit) & 1
    signs = np.where(parity % 2 == 0, 1.0, -1.0)
    return np.kron(np.eye(width // HD), signs).astype(np.float32)


def rotate_kernel(count, sign_ref, *refs):
    sources, out_ref = refs[:count], refs[count]
    sign = sign_ref[...]
    step = sign.shape[0]
    for place, source in enumerate(sources):
        for at in range(0, source.shape[1], step):
            turned = jnp.dot(
                source[:, at : at + step], sign, preferred_element_type=jnp.float32
            )
            out_ref[0, place, :, at : at + step] = (turned * ROTATE_SCALE).astype(jnp.bfloat16)


def rotate_pack(sources, parts, sign):
    rows, width = sources[0].shape
    part_width = width // parts
    count = len(sources)
    return pl.pallas_call(
        functools.partial(rotate_kernel, count),
        grid=(parts,),
        in_specs=[pl.BlockSpec(sign.shape, lambda d: (0, 0))]
        + [pl.BlockSpec((rows, part_width), lambda d: (0, d))] * count,
        out_specs=pl.BlockSpec((1, count, rows, part_width), lambda d: (d, 0, 0, 0)),
        out_shape=jax.ShapeDtypeStruct((parts, count, rows, part_width), jnp.bfloat16),
        compiler_params=pltpu.CompilerParams(vmem_limit_bytes=VMEM),
    )(sign, *sources)


def pick_kernel(picks_ref, source_ref, out_ref):
    out_ref[0] = source_ref[:, :, 0]


def pick_blocks(picks, key_value, slots):
    sources, kinds, blocks, tokens, width = key_value.shape
    return pl.pallas_call(
        pick_kernel,
        grid_spec=pltpu.PrefetchScalarGridSpec(
            num_scalar_prefetch=1,
            grid=(slots,),
            in_specs=[
                pl.BlockSpec(
                    (sources, kinds, 1, tokens, width), lambda i, picks: (0, 0, picks[i], 0, 0)
                )
            ],
            out_specs=pl.BlockSpec(
                (1, sources, kinds, tokens, width), lambda i, picks: (i, 0, 0, 0, 0)
            ),
        ),
        out_shape=jax.ShapeDtypeStruct((slots, sources, kinds, tokens, width), jnp.bfloat16),
        compiler_params=pltpu.CompilerParams(vmem_limit_bytes=VMEM),
    )(picks, key_value)


def joined_rows(block):
    rows = block.shape[0] * block.shape[1]
    if block.shape[1] % 16 == 0:
        return block.reshape(rows, HD)
    return block.astype(jnp.float32).reshape(rows, HD).astype(block.dtype)


def attend_kernel(tokens_ref, bias_ref, sign_ref, query_ref, own_ref, slot_ref, prev_ref, next_ref, out_ref):
    sources, blocks, tokens, _ = query_ref.shape
    slots = slot_ref.shape[0]
    query = jnp.concatenate([joined_rows(query_ref[:, i]) for i in range(blocks)], axis=0)

    def gathered(kind):
        pieces = [joined_rows(own_ref[:, kind, i]) for i in range(blocks)]
        pieces += [joined_rows(slot_ref[i, :, kind]) for i in range(slots)]
        pieces += [joined_rows(ref[:, kind]) for ref in (prev_ref, next_ref)]
        return jnp.concatenate(pieces, axis=0)

    keys, values = gathered(0), gathered(1)
    total = keys.shape[0]
    dots = lax.dot_general(
        query, keys, (((1,), (1,)), ((), ())), preferred_element_type=jnp.float32
    )
    dots = dots.reshape(blocks, BLK, total) + bias_ref[...][:, None, :]
    peak = jnp.max(dots, axis=-1, keepdims=True)
    weights = jnp.exp((dots - peak) * SCORE_SCALE)
    denominator = jnp.sum(weights, axis=-1, keepdims=True).reshape(blocks * BLK, 1)
    weights_half = weights.astype(jnp.bfloat16).reshape(blocks * BLK, total)
    mixed = jnp.dot(weights_half, values, preferred_element_type=jnp.float32) / denominator
    sign = sign_ref[...]
    turned = jnp.zeros_like(mixed)
    rest = mixed
    for _ in range(3):
        piece = rest.astype(jnp.bfloat16)
        turned = turned + jnp.dot(piece, sign, preferred_element_type=jnp.float32)
        rest = rest - piece.astype(jnp.float32)
    turned = (turned * ROTATE_SCALE).reshape(blocks, sources, tokens, HD)
    shape = (sources, tokens, HD)
    position = lax.broadcasted_iota(jnp.int32, shape, 0) * tokens
    position = position + lax.broadcasted_iota(jnp.int32, shape, 1)
    for i in range(blocks):
        live = position < tokens_ref[i]
        out_ref[:, i] = jnp.where(live, turned[i], 0.0).astype(jnp.bfloat16)


def attend(own_tokens, bias, sign, query, own, slot, before, after):
    sources, blocks, tokens, width = query.shape
    slots = slot.shape[0]
    heads = width // HD
    total = bias.shape[1]

    def spec(*shape):
        return pl.BlockSpec(
            shape + (HD,), lambda h, *_: (0,) * len(shape) + (h,)
        )

    flops = 4 * heads * blocks * BLK * total * HD
    return pl.pallas_call(
        attend_kernel,
        grid_spec=pltpu.PrefetchScalarGridSpec(
            num_scalar_prefetch=1,
            grid=(heads,),
            in_specs=[
                pl.BlockSpec(bias.shape, lambda h, *_: (0, 0)),
                pl.BlockSpec(sign.shape, lambda h, *_: (0, 0)),
                spec(sources, blocks, tokens),
                spec(sources, 2, blocks, tokens),
                spec(slots, sources, 2, tokens),
                spec(sources, 2, tokens),
                spec(sources, 2, tokens),
            ],
            out_specs=spec(sources, blocks, tokens),
        ),
        out_shape=jax.ShapeDtypeStruct(query.shape, jnp.bfloat16),
        cost_estimate=pl.CostEstimate(
            flops=flops, bytes_accessed=4 * 1024 * 1024, transcendentals=heads * blocks * BLK * total
        ),
        compiler_params=pltpu.CompilerParams(vmem_limit_bytes=VMEM),
    )(own_tokens, bias, sign, query, own, slot, before, after)


def routes(pair_list, block_tokens, shard, count_tm, blocks):
    total_blocks = count_tm * blocks
    ids = jnp.arange(total_blocks, dtype=jnp.int32)
    named = jnp.any(pair_list[:, :, None] == ids, axis=1)
    wanted = jnp.any(
        named.reshape(count_tm, blocks, count_tm, blocks), axis=1
    )
    place = jnp.arange(blocks, dtype=jnp.int32)
    rank = jnp.sum(
        (wanted[..., None, :] & (place[None, :] < place[:, None])).astype(jnp.int32), axis=-1
    )
    chosen = [wanted & (rank == k) for k in (0, 1)]
    index = [jnp.sum(jnp.where(c, place, 0), axis=-1) for c in chosen]
    found = [jnp.any(c, axis=-1) for c in chosen]
    shards = jnp.arange(count_tm, dtype=jnp.int32)
    upward = jnp.minimum(shard + 1, count_tm - 1)
    downward = jnp.maximum(shard - 1, 0)

    def at_row(table, row):
        return lax.dynamic_index_in_dim(table, row, 0, keepdims=False)

    sent_first = at_row(index[0].T, shard)
    sent_second = at_row(index[1].T, shard)
    picks = jnp.concatenate(
        [sent_first, at_row(sent_second, upward)[None], at_row(sent_second, downward)[None]]
    )
    got_first = at_row(index[0], shard) + shards * blocks
    ok_first = at_row(found[0], shard) & (shards != shard)
    got_second = at_row(index[1], shard) + shards * blocks
    ok_second = at_row(found[1], shard)
    row_block = jnp.concatenate(
        [
            shard * blocks + place,
            got_first,
            at_row(got_second, downward)[None],
            at_row(got_second, upward)[None],
        ]
    )
    row_ok = jnp.concatenate(
        [
            jnp.ones((blocks,), bool),
            ok_first,
            (at_row(ok_second, downward) & (shard > 0))[None],
            (at_row(ok_second, upward) & (shard < count_tm - 1))[None],
        ]
    )
    mine = lax.dynamic_slice_in_dim(named, shard * blocks, blocks, 0)
    match = row_block[:, None] == ids[None, :]
    row_tokens = jnp.sum(jnp.where(match, block_tokens, 0), axis=1)
    row_named = jnp.any(match[None] & mine[:, None, :], axis=2)
    kept = jnp.where(row_named & row_ok, row_tokens, 0)
    positions = jnp.arange(BLK, dtype=jnp.int32)
    bias = jnp.where(positions < kept[:, :, None], 0.0, NEG).astype(jnp.float32)
    own_tokens = lax.dynamic_slice_in_dim(block_tokens, shard * blocks, blocks, 0)
    return picks, bias.reshape(blocks, -1), own_tokens


def passed_along(block, axis, distance):
    devices = range(lax.axis_size(axis))
    route = [(i - distance, i) for i in devices if i - distance in devices]
    return lax.ppermute(block, axis, route)


def shards(query_rows, key_rows, value_rows, pair_list, block_tokens):
    count_head = lax.axis_size("head")
    count_tm = lax.axis_size("tm")
    shard = lax.axis_index("tm")
    blocks, tokens, width = query_rows.shape
    width_here = width // count_head
    flat = (blocks * tokens, width)
    wide = 2 * HD if width_here % (2 * HD) == 0 else HD
    wide_sign = jnp.asarray(sign_matrix(wide), jnp.bfloat16)
    sign = jnp.asarray(sign_matrix(HD), jnp.bfloat16)

    def exchange(packed):
        return lax.all_to_all(packed, "head", split_axis=0, concat_axis=0, tiled=True)

    key_value = rotate_pack(
        [key_rows.reshape(flat), value_rows.reshape(flat)], count_head, wide_sign
    )
    key_value = exchange(key_value).reshape(count_head, 2, blocks, tokens, width_here)
    query = rotate_pack([query_rows.reshape(flat)], count_head, wide_sign)
    query = exchange(query).reshape(count_head, blocks, tokens, width_here)
    picks, bias, own_tokens = routes(pair_list, block_tokens, shard, count_tm, blocks)
    picked = pick_blocks(picks, key_value, count_tm + 2)
    slot = lax.all_to_all(picked[:count_tm], "tm", split_axis=0, concat_axis=0, tiled=True)
    before = passed_along(picked[count_tm], "tm", 1)
    after = passed_along(picked[count_tm + 1], "tm", -1)
    attended = attend(own_tokens, bias, sign, query, key_value, slot, before, after)
    attended = exchange(attended.reshape(count_head, blocks * tokens, width_here))
    attended = jnp.transpose(attended, (1, 0, 2))
    return attended.reshape(blocks, tokens, width)


def solution(mesh):
    placed = (
        P(("grp", "tm"), "head", None),
        P(("grp", "tm"), "head", None),
        P(("grp", "tm"), "head", None),
        P("grp", None),
        P("grp"),
    )
    return jax.shard_map(
        shards,
        mesh=mesh,
        in_specs=placed,
        out_specs=P(("grp", "tm"), "head", None),
        check_vma=False,
    )
```

```python
import functools
import math

import jax
import jax.numpy as jnp
import numpy as np
from jax import lax
from jax.experimental import pallas as pl
from jax.experimental.pallas import tpu as pltpu
from jax.sharding import PartitionSpec as P

HD = 128
BLK = 64
NEG = -1e30
ROTATE_SCALE = 1.0 / math.sqrt(HD)
SCORE_SCALE = 1.0 / math.sqrt(HD)
VMEM = 24 * 1024 * 1024
LOG2E = math.log2(math.e)


def sign_matrix():
    ids = np.arange(HD)
    common = ids[:, None] & ids[None, :]
    parity = np.zeros((HD, HD), np.int64)
    for bit in range(HD.bit_length() - 1):
        parity += (common >> bit) & 1
    return np.where(parity % 2 == 0, 1.0, -1.0).astype(np.float32)


def rows_of(block):
    rows, width = math.prod(block.shape[:-1]), block.shape[-1]
    if block.shape[-2] % 16 == 0:
        return block.reshape(rows, width)
    return block.astype(jnp.float32).reshape(rows, width).astype(block.dtype)


def rotate_kernel(groups, count_head, sign_ref, *refs):
    count = 1 + max(max(ids) for ids, _, _ in groups)
    sources = refs[:count]
    outs = refs[count : count + len(groups) * count_head]
    scratch = refs[count + len(groups) * count_head :]
    buffers, sems = scratch[: len(groups)], scratch[len(groups)]
    blocks, tokens, width = sources[0].shape
    width_here = width // count_head
    me = lax.axis_index("head")
    order = list(range(1, count_head)) + [0]
    copies = {}
    for g, (ids, start, size) in enumerate(groups):
        for s in order:
            goal = lax.rem(me + s, count_head)
            column = pl.multiple_of(goal * width_here + start, HD)
            for k, source in enumerate(ids):
                copies[g, s, k] = pltpu.make_async_copy(
                    sources[source].at[:, :, pl.ds(column, size)],
                    buffers[g].at[s, k],
                    sems.at[g, s, k],
                )
                copies[g, s, k].start()
    sign = sign_ref[...]
    for g, (ids, start, size) in enumerate(groups):
        for s in order:
            for k in range(len(ids)):
                copies[g, s, k].wait()
                flat = rows_of(buffers[g][s, k])
                heads = [flat[:, at : at + HD] for at in range(0, size, HD)]
                turned = jnp.dot(
                    jnp.concatenate(heads, axis=0), sign, preferred_element_type=jnp.float32
                )
                turned = (turned * ROTATE_SCALE).reshape(size // HD, blocks, tokens, HD)
                for h in range(size // HD):
                    outs[g * count_head + s][k, :, :, h * HD : (h + 1) * HD] = turned[h].astype(
                        jnp.bfloat16
                    )


def rotate_pieces(sources, groups, count_head, sign):
    blocks, tokens, _ = sources[0].shape
    shapes = [
        jax.ShapeDtypeStruct((len(ids), blocks, tokens, size), jnp.bfloat16)
        for ids, _, size in groups
        for _ in range(count_head)
    ]
    kinds = max(len(ids) for ids, _, _ in groups)
    moved = 4 * sum(math.prod(shape.shape) for shape in shapes)
    outs = pl.pallas_call(
        functools.partial(rotate_kernel, groups, count_head),
        in_specs=[pl.BlockSpec(memory_space=pltpu.VMEM)]
        + [pl.BlockSpec(memory_space=pltpu.HBM)] * len(sources),
        out_specs=[pl.BlockSpec(memory_space=pltpu.VMEM)] * len(shapes),
        out_shape=shapes,
        scratch_shapes=[
            pltpu.VMEM((count_head, len(ids), blocks, tokens, size), jnp.bfloat16)
            for ids, _, size in groups
        ]
        + [pltpu.SemaphoreType.DMA((len(groups), count_head, kinds))],
        cost_estimate=pl.CostEstimate(flops=HD * moved, bytes_accessed=moved, transcendentals=0),
        compiler_params=pltpu.CompilerParams(vmem_limit_bytes=VMEM),
    )(sign, *sources)
    return [list(outs[g * count_head : (g + 1) * count_head]) for g in range(len(groups))]


def pick_kernel(count_head, count_tm, picks_ref, *refs):
    pieces = refs[:count_head]
    first_ref, next_ref, prev_ref = refs[count_head:]
    for s in range(count_head):
        for i in range(count_tm):
            first_ref[i, s] = pieces[s][:, picks_ref[i]]
        next_ref[s] = pieces[s][:, picks_ref[count_tm]]
        prev_ref[s] = pieces[s][:, picks_ref[count_tm + 1]]


def pick_blocks(picks, pieces, count_tm):
    count_head = len(pieces)
    kinds, _, tokens, width = pieces[0].shape
    one = (count_head, kinds, tokens, width)
    vmem = pl.BlockSpec(memory_space=pltpu.VMEM)
    moved = 4 * (count_tm + 2) * math.prod(one)
    return pl.pallas_call(
        functools.partial(pick_kernel, count_head, count_tm),
        in_specs=[pl.BlockSpec(memory_space=pltpu.SMEM)] + [vmem] * count_head,
        out_specs=[vmem] * 3,
        out_shape=[
            jax.ShapeDtypeStruct((count_tm,) + one, jnp.bfloat16),
            jax.ShapeDtypeStruct(one, jnp.bfloat16),
            jax.ShapeDtypeStruct(one, jnp.bfloat16),
        ],
        cost_estimate=pl.CostEstimate(flops=0, bytes_accessed=moved, transcendentals=0),
        compiler_params=pltpu.CompilerParams(vmem_limit_bytes=VMEM),
    )(picks, *pieces)


def attend_kernel(count_head, start, tokens_ref, bias_ref, sign_ref, *refs):
    queries, owns = refs[:count_head], refs[count_head : 2 * count_head]
    slot_ref, prev_ref, next_ref = refs[2 * count_head : 2 * count_head + 3]
    outs = refs[2 * count_head + 3 :]
    _, blocks, tokens, size = owns[0].shape
    slots = slot_ref.shape[0]
    me = lax.axis_index("head")
    sign = sign_ref[...]
    for h in range(size // HD):
        lanes = slice(h * HD, (h + 1) * HD)
        query_lanes = slice(start + h * HD, start + (h + 1) * HD)
        query = jnp.concatenate(
            [rows_of(queries[s][0, i, :, query_lanes]) for i in range(blocks) for s in range(count_head)],
            axis=0,
        )

        def gathered(kind):
            pieces = [rows_of(own[kind, :, :, lanes]) for own in owns]
            pieces += [rows_of(slot_ref[i, :, kind, :, lanes]) for i in range(slots)]
            pieces += [rows_of(ref[:, kind, :, lanes]) for ref in (prev_ref, next_ref)]
            return jnp.concatenate(pieces, axis=0)

        keys, values = gathered(0), gathered(1)
        total = keys.shape[0]
        dots = lax.dot_general(
            query, keys, (((1,), (1,)), ((), ())), preferred_element_type=jnp.float32
        )
        dots = dots.reshape(blocks, BLK, total) + bias_ref[...][:, None, :]
        peak = jnp.max(dots, axis=-1, keepdims=True)
        weights = jnp.exp2((dots - peak) * (SCORE_SCALE * LOG2E))
        denominator = jnp.sum(weights, axis=-1, keepdims=True).reshape(blocks * BLK, 1)
        weights_half = weights.astype(jnp.bfloat16).reshape(blocks * BLK, total)
        mixed = jnp.dot(weights_half, values, preferred_element_type=jnp.float32) / denominator
        turned = jnp.zeros_like(mixed)
        rest = mixed
        for _ in range(3):
            piece = rest.astype(jnp.bfloat16)
            turned = turned + jnp.dot(piece, sign, preferred_element_type=jnp.float32)
            rest = rest - piece.astype(jnp.float32)
        turned = (turned * ROTATE_SCALE).reshape(blocks, count_head, tokens, HD)
        token = lax.broadcasted_iota(jnp.int32, (tokens, HD), 0)
        for s in range(count_head):
            position = lax.rem(me - s + count_head, count_head) * tokens + token
            for i in range(blocks):
                outs[s][i, :, lanes] = jnp.where(
                    position < tokens_ref[i], turned[i, s], 0.0
                ).astype(jnp.bfloat16)


def attend(own_tokens, bias, sign, start, queries, owns, slot, before, after):
    count_head = len(owns)
    _, blocks, tokens, size = owns[0].shape
    total = bias.shape[1]
    scores = size // HD * blocks * BLK * total
    vmem = pl.BlockSpec(memory_space=pltpu.VMEM)
    return pl.pallas_call(
        functools.partial(attend_kernel, count_head, start),
        in_specs=[pl.BlockSpec(memory_space=pltpu.SMEM)] + [vmem] * (2 * count_head + 5),
        out_specs=[vmem] * count_head,
        out_shape=[jax.ShapeDtypeStruct((blocks, tokens, size), jnp.bfloat16)] * count_head,
        cost_estimate=pl.CostEstimate(
            flops=4 * HD * scores, bytes_accessed=8 * HD * total, transcendentals=scores
        ),
        compiler_params=pltpu.CompilerParams(vmem_limit_bytes=VMEM),
    )(own_tokens, bias, sign, *queries, *owns, slot, before, after)


def place_kernel(count_head, starts, width_here, *refs):
    pieces, out_ref, sems = refs[:-2], refs[-2], refs[-1]
    me = lax.axis_index("head")
    copies = []
    for at, piece in enumerate(pieces):
        part, s = at // count_head, at % count_head
        column = lax.rem(me + s, count_head) * width_here + starts[part]
        copies.append(
            pltpu.make_async_copy(
                piece,
                out_ref.at[:, :, pl.ds(pl.multiple_of(column, HD), piece.shape[-1])],
                sems.at[at],
            )
        )
        copies[-1].start()
    for copy in copies:
        copy.wait()


def place_pieces(parts, starts, width_here):
    count_head = len(parts[0])
    pieces = [piece for part in parts for piece in part]
    blocks, tokens, _ = pieces[0].shape
    return pl.pallas_call(
        functools.partial(place_kernel, count_head, starts, width_here),
        in_specs=[pl.BlockSpec(memory_space=pl.ANY)] * len(pieces),
        out_specs=pl.BlockSpec(memory_space=pltpu.HBM),
        out_shape=jax.ShapeDtypeStruct((blocks, tokens, count_head * width_here), jnp.bfloat16),
        scratch_shapes=[pltpu.SemaphoreType.DMA((len(pieces),))],
        compiler_params=pltpu.CompilerParams(vmem_limit_bytes=VMEM),
    )(*pieces)


def routes(pair_list, block_tokens, shard, count_tm, blocks, place_head, count_head, tokens):
    total_blocks = count_tm * blocks
    ids = jnp.arange(total_blocks, dtype=jnp.int32)
    named = jnp.any(pair_list[:, :, None] == ids, axis=1)
    wanted = jnp.any(
        named.reshape(count_tm, blocks, count_tm, blocks), axis=1
    )
    place = jnp.arange(blocks, dtype=jnp.int32)
    rank = jnp.sum(
        (wanted[..., None, :] & (place[None, :] < place[:, None])).astype(jnp.int32), axis=-1
    )
    chosen = [wanted & (rank == k) for k in (0, 1)]
    index = [jnp.sum(jnp.where(c, place, 0), axis=-1) for c in chosen]
    found = [jnp.any(c, axis=-1) for c in chosen]
    shards = jnp.arange(count_tm, dtype=jnp.int32)
    upward = jnp.minimum(shard + 1, count_tm - 1)
    downward = jnp.maximum(shard - 1, 0)

    def at_row(table, row):
        return lax.dynamic_index_in_dim(table, row, 0, keepdims=False)

    sent_first = at_row(index[0].T, shard)
    sent_second = at_row(index[1].T, shard)
    picks = jnp.concatenate(
        [sent_first, at_row(sent_second, upward)[None], at_row(sent_second, downward)[None]]
    )
    got_first = at_row(index[0], shard) + shards * blocks
    ok_first = at_row(found[0], shard) & (shards != shard)
    got_second = at_row(index[1], shard) + shards * blocks
    ok_second = at_row(found[1], shard)
    row_block = jnp.concatenate(
        [
            shard * blocks + place,
            got_first,
            at_row(got_second, downward)[None],
            at_row(got_second, upward)[None],
        ]
    )
    row_ok = jnp.concatenate(
        [
            jnp.ones((blocks,), bool),
            ok_first,
            (at_row(ok_second, downward) & (shard > 0))[None],
            (at_row(ok_second, upward) & (shard < count_tm - 1))[None],
        ]
    )
    mine = lax.dynamic_slice_in_dim(named, shard * blocks, blocks, 0)
    match = row_block[:, None] == ids[None, :]
    row_tokens = jnp.sum(jnp.where(match, block_tokens, 0), axis=1)
    row_named = jnp.any(match[None] & mine[:, None, :], axis=2)
    kept = jnp.where(row_named & row_ok, row_tokens, 0)
    piece = jnp.arange(count_head, dtype=jnp.int32)
    source = lax.rem(place_head - piece + count_head, count_head)
    positions = source[:, None] * tokens + jnp.arange(tokens, dtype=jnp.int32)
    own_keep = positions[:, None, :] < kept[:, None, :blocks, None]
    far_keep = positions < kept[:, blocks:, None, None]
    keep = jnp.concatenate([own_keep.reshape(blocks, -1), far_keep.reshape(blocks, -1)], axis=1)
    bias = jnp.where(keep, 0.0, NEG).astype(jnp.float32)
    own_tokens = lax.dynamic_slice_in_dim(block_tokens, shard * blocks, blocks, 0)
    return picks, bias, own_tokens


def passed_along(block, axis, distance):
    devices = range(lax.axis_size(axis))
    route = [(i - distance, i) for i in devices if i - distance in devices]
    return lax.ppermute(block, axis, route)


def ring_exchange(pieces, direction):
    count = lax.axis_size("head")
    received = [pieces[0]]
    for s in range(1, count):
        route = [(i, (i + direction * s) % count) for i in range(count)]
        received.append(lax.ppermute(pieces[s], "head", route))
    return received


def shards(query_rows, key_rows, value_rows, pair_list, block_tokens):
    count_head = lax.axis_size("head")
    count_tm = lax.axis_size("tm")
    shard = lax.axis_index("tm")
    place_head = lax.axis_index("head")
    blocks, tokens, width = query_rows.shape
    width_here = width // count_head
    heads = width_here // HD
    cut = (heads + 1) // 2 * HD
    parts = [(0, cut), (cut, width_here - cut)] if heads > 1 else [(0, width_here)]
    sign = jnp.asarray(sign_matrix(), jnp.bfloat16)
    (first,) = rotate_pieces([key_rows, value_rows], [((0, 1),) + parts[0]], count_head, sign)
    groups = [((0, 1),) + part for part in parts[1:]] + [((2,), 0, width_here)]
    later = rotate_pieces([key_rows, value_rows, query_rows], groups, count_head, sign)
    key_values = [ring_exchange(pieces, 1) for pieces in [first] + later[:-1]]
    queries = ring_exchange(later[-1], 1)
    picks, bias, own_tokens = routes(
        pair_list, block_tokens, shard, count_tm, blocks, place_head, count_head, tokens
    )
    returned = []
    for (start, _), owns in zip(parts, key_values):
        outgoing, to_next, to_prev = pick_blocks(picks, owns, count_tm)
        slot = lax.all_to_all(outgoing, "tm", split_axis=0, concat_axis=0, tiled=True)
        before = passed_along(to_next, "tm", 1)
        after = passed_along(to_prev, "tm", -1)
        attended = attend(
            own_tokens, bias, sign, start, queries, owns, slot, before, after
        )
        returned.append(ring_exchange(attended, -1))
    return place_pieces(returned, [start for start, _ in parts], width_here)


def solution(mesh):
    placed = (
        P(("grp", "tm"), "head", None),
        P(("grp", "tm"), "head", None),
        P(("grp", "tm"), "head", None),
        P("grp", None),
        P("grp"),
    )
    return jax.shard_map(
        shards,
        mesh=mesh,
        in_specs=placed,
        out_specs=P(("grp", "tm"), "head", None),
        check_vma=False,
    )
```

```python
import functools
import math

import jax
import jax.numpy as jnp
from jax import lax
from jax.experimental import pallas as pl
from jax.experimental.pallas import tpu as pltpu
from jax.sharding import PartitionSpec as P

HD = 128
BLK = 64
NEAR_CAP = 2
FAR_CAP = 1
NEG = -1e30
ROTATE_SCALE = 1.0 / math.sqrt(HD)
SCORE_SCALE = 1.0 / math.sqrt(HD)
VMEM = 24 * 1024 * 1024
LOG2E = math.log2(math.e)


def sign_matrix():
    common = lax.broadcasted_iota(jnp.int32, (HD, HD), 0) & lax.broadcasted_iota(
        jnp.int32, (HD, HD), 1
    )
    bits = HD.bit_length() - 1
    parity = common
    for bit in range(1, bits):
        parity = parity ^ (common >> bit)
    return jnp.where((parity & 1) == 0, 1.0, -1.0).astype(jnp.bfloat16)


def rows_of(block):
    rows, width = math.prod(block.shape[:-1]), block.shape[-1]
    if block.shape[-2] % 16 == 0:
        return block.reshape(rows, width)
    return block.astype(jnp.float32).reshape(rows, width).astype(block.dtype)


def rotate_kernel(groups, count_head, *refs):
    count = 1 + max(max(ids) for ids, _, _ in groups)
    sources = refs[:count]
    outs = refs[count : count + len(groups) * count_head]
    scratch = refs[count + len(groups) * count_head :]
    buffers, sems = scratch[: len(groups)], scratch[len(groups)]
    blocks, tokens, width = sources[0].shape
    width_here = width // count_head
    me = lax.axis_index("head")
    order = list(range(1, count_head)) + [0]
    copies = {}
    for g, (ids, start, size) in enumerate(groups):
        for s in order:
            goal = lax.rem(me + s, count_head)
            column = pl.multiple_of(goal * width_here + start, HD)
            for k, source in enumerate(ids):
                copies[g, s, k] = pltpu.make_async_copy(
                    sources[source].at[:, :, pl.ds(column, size)],
                    buffers[g].at[s, k],
                    sems.at[g, s, k],
                )
                copies[g, s, k].start()
    sign = sign_matrix()
    for g, (ids, start, size) in enumerate(groups):
        for s in order:
            for k in range(len(ids)):
                copies[g, s, k].wait()
                flat = rows_of(buffers[g][s, k])
                heads = [flat[:, at : at + HD] for at in range(0, size, HD)]
                turned = jnp.dot(
                    jnp.concatenate(heads, axis=0), sign, preferred_element_type=jnp.float32
                )
                turned = (turned * ROTATE_SCALE).reshape(size // HD, blocks, tokens, HD)
                for h in range(size // HD):
                    outs[g * count_head + s][k, :, :, h * HD : (h + 1) * HD] = turned[h].astype(
                        jnp.bfloat16
                    )


def rotate_pieces(sources, groups, count_head):
    blocks, tokens, _ = sources[0].shape
    shapes = [
        jax.ShapeDtypeStruct((len(ids), blocks, tokens, size), jnp.bfloat16)
        for ids, _, size in groups
        for _ in range(count_head)
    ]
    kinds = max(len(ids) for ids, _, _ in groups)
    moved = 4 * sum(math.prod(shape.shape) for shape in shapes)
    outs = pl.pallas_call(
        functools.partial(rotate_kernel, groups, count_head),
        in_specs=[pl.BlockSpec(memory_space=pltpu.HBM)] * len(sources),
        out_specs=[pl.BlockSpec(memory_space=pltpu.VMEM)] * len(shapes),
        out_shape=shapes,
        scratch_shapes=[
            pltpu.VMEM((count_head, len(ids), blocks, tokens, size), jnp.bfloat16)
            for ids, _, size in groups
        ]
        + [pltpu.SemaphoreType.DMA((len(groups), count_head, kinds))],
        cost_estimate=pl.CostEstimate(flops=HD * moved, bytes_accessed=moved, transcendentals=0),
        compiler_params=pltpu.CompilerParams(vmem_limit_bytes=VMEM),
    )(*sources)
    return [list(outs[g * count_head : (g + 1) * count_head]) for g in range(len(groups))]


def pick_kernel(count_head, count_tm, picks_ref, *refs):
    pieces, out_ref = refs[:count_head], refs[count_head]
    for s in range(count_head):
        for i in range(count_tm):
            for k in range(NEAR_CAP):
                out_ref[i, k, s] = pieces[s][:, picks_ref[NEAR_CAP * i + k]]


def pick_blocks(picks, pieces, count_tm):
    count_head = len(pieces)
    kinds, _, tokens, width = pieces[0].shape
    shape = (count_tm, NEAR_CAP, count_head, kinds, tokens, width)
    vmem = pl.BlockSpec(memory_space=pltpu.VMEM)
    return pl.pallas_call(
        functools.partial(pick_kernel, count_head, count_tm),
        in_specs=[pl.BlockSpec(memory_space=pltpu.SMEM)] + [vmem] * count_head,
        out_specs=vmem,
        out_shape=jax.ShapeDtypeStruct(shape, jnp.bfloat16),
        cost_estimate=pl.CostEstimate(
            flops=0, bytes_accessed=4 * math.prod(shape), transcendentals=0
        ),
        compiler_params=pltpu.CompilerParams(vmem_limit_bytes=VMEM),
    )(picks, *pieces)


def remote_rows(count_tm):
    return [
        (distance, k)
        for distance in range(1, count_tm)
        for k in range(NEAR_CAP if distance in (1, count_tm - 1) else FAR_CAP)
    ]


def plan_kernel(count_head, count_tm, blocks, pair_ref, tokens_ref, picks_ref, bias_ref, named_ref, table_ref, sem):
    total_blocks, columns = pair_ref.shape
    pairs = pair_ref[...]
    lane = lax.broadcasted_iota(jnp.int32, named_ref.shape, 1)
    named = jnp.zeros(named_ref.shape, jnp.int32)
    for c in range(columns):
        named = jnp.where(pairs[:, c : c + 1] == lane, 1, named)
    named_ref[...] = named
    copy = pltpu.make_async_copy(named_ref, table_ref, sem)
    copy.start()
    copy.wait()
    shard = lax.axis_index("tm")
    place = lax.axis_index("head")
    mine = shard * blocks

    def two_picks(wanted):
        picks = [jnp.int32(0)] * NEAR_CAP
        count = jnp.int32(0)
        for j in range(blocks):
            for k in range(NEAR_CAP):
                picks[k] = jnp.where((wanted[j] > 0) & (count == k), j, picks[k])
            count = count + wanted[j]
        return picks, count

    def named_by(rows, column):
        found = table_ref[rows, column]
        for i in range(1, blocks):
            found = found | table_ref[rows + i, column]
        return found

    for d in range(count_tm):
        picks, _ = two_picks([named_by(d * blocks, mine + j) for j in range(blocks)])
        for k in range(NEAR_CAP):
            picks_ref[NEAR_CAP * d + k] = picks[k]

    kept = [[table_ref[mine + i, mine + j] * tokens_ref[mine + j] for j in range(blocks)] for i in range(blocks)]
    arrivals = {}
    for distance, k in remote_rows(count_tm):
        first = lax.rem(shard + distance, count_tm) * blocks
        if k == 0:
            arrivals[distance] = two_picks([named_by(mine, first + j) for j in range(blocks)])
        picks, count = arrivals[distance]
        there = first + picks[k]
        live = jnp.where(count > k, tokens_ref[there], 0)
        for i in range(blocks):
            kept[i].append(table_ref[mine + i, there] * live)

    total = bias_ref.shape[1]
    piece_rows = BLK // count_head
    at = lax.broadcasted_iota(jnp.int32, (blocks, total), 1)
    query = lax.broadcasted_iota(jnp.int32, (blocks, total), 0)
    own = at < blocks * BLK
    row = jnp.where(own, lax.rem(lax.div(at, piece_rows), blocks), lax.div(at, BLK))
    piece = jnp.where(own, lax.div(at, blocks * piece_rows), lax.div(lax.rem(at, BLK), piece_rows))
    source = lax.rem(place - piece + count_head, count_head)
    position = source * piece_rows + lax.rem(at, piece_rows)
    limit = jnp.zeros((blocks, total), jnp.int32)
    for r in range(len(kept[0])):
        value = jnp.zeros((blocks, total), jnp.int32)
        for i in range(blocks):
            value = jnp.where(query == i, kept[i][r], value)
        limit = jnp.where(row == r, value, limit)
    bias_ref[...] = jnp.where(position < limit, 0.0, NEG)


def plan(pair_list, block_tokens, blocks, count_head, count_tm):
    total_blocks = pair_list.shape[0]
    lanes = -(-total_blocks // 128) * 128
    total = (blocks + len(remote_rows(count_tm))) * BLK
    return pl.pallas_call(
        functools.partial(plan_kernel, count_head, count_tm, blocks),
        in_specs=[pl.BlockSpec(memory_space=pltpu.VMEM), pl.BlockSpec(memory_space=pltpu.SMEM)],
        out_specs=[pl.BlockSpec(memory_space=pltpu.SMEM), pl.BlockSpec(memory_space=pltpu.VMEM)],
        out_shape=[
            jax.ShapeDtypeStruct((NEAR_CAP * count_tm,), jnp.int32),
            jax.ShapeDtypeStruct((blocks, total), jnp.float32),
        ],
        scratch_shapes=[
            pltpu.VMEM((total_blocks, lanes), jnp.int32),
            pltpu.SMEM((total_blocks, lanes), jnp.int32),
            pltpu.SemaphoreType.DMA,
        ],
        compiler_params=pltpu.CompilerParams(vmem_limit_bytes=VMEM),
    )(pair_list, block_tokens)


def attend_kernel(count_head, count_tm, start, tokens_ref, bias_ref, *refs):
    queries, owns = refs[:count_head], refs[count_head : 2 * count_head]
    slot_ref = refs[2 * count_head]
    outs = refs[2 * count_head + 1 :]
    _, blocks, tokens, size = owns[0].shape
    shard = lax.axis_index("tm")
    me = lax.axis_index("head")
    sign = sign_matrix()
    for h in range(size // HD):
        lanes = slice(h * HD, (h + 1) * HD)
        query_lanes = slice(start + h * HD, start + (h + 1) * HD)
        query = jnp.concatenate(
            [rows_of(queries[s][0, i, :, query_lanes]) for i in range(blocks) for s in range(count_head)],
            axis=0,
        )

        def gathered(kind):
            pieces = [rows_of(own[kind, :, :, lanes]) for own in owns]
            pieces += [
                rows_of(slot_ref[lax.rem(shard + distance, count_tm), k, :, kind, :, lanes])
                for distance, k in remote_rows(count_tm)
            ]
            return jnp.concatenate(pieces, axis=0)

        keys, values = gathered(0), gathered(1)
        total = keys.shape[0]
        dots = lax.dot_general(
            query, keys, (((1,), (1,)), ((), ())), preferred_element_type=jnp.float32
        )
        dots = dots.reshape(blocks, BLK, total) + bias_ref[...][:, None, :]
        peak = jnp.max(dots, axis=-1, keepdims=True)
        weights = jnp.exp2((dots - peak) * (SCORE_SCALE * LOG2E))
        denominator = jnp.sum(weights, axis=-1, keepdims=True).reshape(blocks * BLK, 1)
        weights_half = weights.astype(jnp.bfloat16).reshape(blocks * BLK, total)
        mixed = jnp.dot(weights_half, values, preferred_element_type=jnp.float32) / denominator
        turned = jnp.zeros_like(mixed)
        rest = mixed
        for _ in range(3):
            piece = rest.astype(jnp.bfloat16)
            turned = turned + jnp.dot(piece, sign, preferred_element_type=jnp.float32)
            rest = rest - piece.astype(jnp.float32)
        turned = (turned * ROTATE_SCALE).reshape(blocks, count_head, tokens, HD)
        token = lax.broadcasted_iota(jnp.int32, (tokens, HD), 0)
        for s in range(count_head):
            position = lax.rem(me - s + count_head, count_head) * tokens + token
            for i in range(blocks):
                outs[s][i, :, lanes] = jnp.where(
                    position < tokens_ref[shard * blocks + i], turned[i, s], 0.0
                ).astype(jnp.bfloat16)


def attend(block_tokens, bias, start, queries, owns, slot):
    count_head, count_tm = len(owns), slot.shape[0]
    _, blocks, tokens, size = owns[0].shape
    total = bias.shape[1]
    scores = size // HD * blocks * BLK * total
    vmem = pl.BlockSpec(memory_space=pltpu.VMEM)
    return pl.pallas_call(
        functools.partial(attend_kernel, count_head, count_tm, start),
        in_specs=[pl.BlockSpec(memory_space=pltpu.SMEM)] + [vmem] * (2 * count_head + 2),
        out_specs=[vmem] * count_head,
        out_shape=[jax.ShapeDtypeStruct((blocks, tokens, size), jnp.bfloat16)] * count_head,
        cost_estimate=pl.CostEstimate(
            flops=4 * HD * scores, bytes_accessed=8 * HD * total, transcendentals=scores
        ),
        compiler_params=pltpu.CompilerParams(vmem_limit_bytes=VMEM),
    )(block_tokens, bias, *queries, *owns, slot)


def place_kernel(count_head, starts, width_here, *refs):
    pieces, out_ref, sems = refs[:-2], refs[-2], refs[-1]
    me = lax.axis_index("head")
    copies = []
    for at, piece in enumerate(pieces):
        part, s = at // count_head, at % count_head
        column = lax.rem(me + s, count_head) * width_here + starts[part]
        copies.append(
            pltpu.make_async_copy(
                piece,
                out_ref.at[:, :, pl.ds(pl.multiple_of(column, HD), piece.shape[-1])],
                sems.at[at],
            )
        )
        copies[-1].start()
    for copy in copies:
        copy.wait()


def place_pieces(parts, starts, width_here):
    count_head = len(parts[0])
    pieces = [piece for part in parts for piece in part]
    blocks, tokens, _ = pieces[0].shape
    return pl.pallas_call(
        functools.partial(place_kernel, count_head, starts, width_here),
        in_specs=[pl.BlockSpec(memory_space=pl.ANY)] * len(pieces),
        out_specs=pl.BlockSpec(memory_space=pltpu.HBM),
        out_shape=jax.ShapeDtypeStruct((blocks, tokens, count_head * width_here), jnp.bfloat16),
        scratch_shapes=[pltpu.SemaphoreType.DMA((len(pieces),))],
        compiler_params=pltpu.CompilerParams(vmem_limit_bytes=VMEM),
    )(*pieces)


def ring_exchange(pieces, direction):
    count = lax.axis_size("head")
    received = [pieces[0]]
    for s in range(1, count):
        route = [(i, (i + direction * s) % count) for i in range(count)]
        received.append(lax.ppermute(pieces[s], "head", route))
    return received


def shards(query_rows, key_rows, value_rows, pair_list, block_tokens):
    count_head = lax.axis_size("head")
    count_tm = lax.axis_size("tm")
    blocks, tokens, width = query_rows.shape
    width_here = width // count_head
    heads = width_here // HD
    cut = (heads + 1) // 2 * HD
    parts = [(0, cut), (cut, width_here - cut)] if heads > 1 else [(0, width_here)]
    (first,) = rotate_pieces([key_rows, value_rows], [((0, 1),) + parts[0]], count_head)
    groups = [((0, 1),) + part for part in parts[1:]] + [((2,), 0, width_here)]
    later = rotate_pieces([key_rows, value_rows, query_rows], groups, count_head)
    key_values = [ring_exchange(pieces, 1) for pieces in [first] + later[:-1]]
    queries = ring_exchange(later[-1], 1)
    picks, bias = plan(pair_list, block_tokens, blocks, count_head, count_tm)
    returned = []
    for (start, _), owns in zip(parts, key_values):
        outgoing = pick_blocks(picks, owns, count_tm)
        slot = lax.all_to_all(outgoing, "tm", split_axis=0, concat_axis=0, tiled=True)
        attended = attend(block_tokens, bias, start, queries, owns, slot)
        returned.append(ring_exchange(attended, -1))
    return place_pieces(returned, [start for start, _ in parts], width_here)


def solution(mesh):
    placed = (
        P(("grp", "tm"), "head", None),
        P(("grp", "tm"), "head", None),
        P(("grp", "tm"), "head", None),
        P("grp", None),
        P("grp"),
    )
    return jax.shard_map(
        shards,
        mesh=mesh,
        in_specs=placed,
        out_specs=P(("grp", "tm"), "head", None),
        check_vma=False,
    )
```

```python
import functools
import math

import jax
import jax.numpy as jnp
from jax import lax
from jax.experimental import pallas as pl
from jax.experimental.pallas import tpu as pltpu
from jax.sharding import PartitionSpec as P

HD = 128
BLK = 64
NEAR_CAP = 2
FAR_CAP = 1
NEG = -1e30
ROTATE_SCALE = 1.0 / math.sqrt(HD)
SCORE_SCALE = 1.0 / math.sqrt(HD)
VMEM = 24 * 1024 * 1024
WIDE_VMEM = 60 * 1024 * 1024
NO_COST = pl.CostEstimate(flops=0, bytes_accessed=0, transcendentals=0)
LOG2E = math.log2(math.e)


def sign_matrix():
    common = lax.broadcasted_iota(jnp.int32, (HD, HD), 0) & lax.broadcasted_iota(
        jnp.int32, (HD, HD), 1
    )
    bits = HD.bit_length() - 1
    parity = common
    for bit in range(1, bits):
        parity = parity ^ (common >> bit)
    return jnp.where((parity & 1) == 0, 1.0, -1.0).astype(jnp.bfloat16)


def rows_of(block):
    rows, width = math.prod(block.shape[:-1]), block.shape[-1]
    if block.shape[-2] % 16 == 0:
        return block.reshape(rows, width)
    return block.astype(jnp.float32).reshape(rows, width).astype(block.dtype)


def rotate_kernel(groups, count_head, skipped, *refs):
    count = 1 + max(max(ids) for ids, _, _ in groups)
    sources = refs[:count]
    refs = refs[:count] + refs[count + skipped :]
    outs = refs[count : count + len(groups) * count_head]
    scratch = refs[count + len(groups) * count_head :]
    buffers, sems = scratch[: len(groups)], scratch[len(groups)]
    blocks, tokens, width = sources[0].shape
    width_here = width // count_head
    me = lax.axis_index("head")
    order = list(range(1, count_head)) + [0]
    copies = {}
    for g, (ids, start, size) in enumerate(groups):
        for s in order:
            goal = lax.rem(me + s, count_head)
            column = pl.multiple_of(goal * width_here + start, HD)
            for k, source in enumerate(ids):
                copies[g, s, k] = pltpu.make_async_copy(
                    sources[source].at[:, :, pl.ds(column, size)],
                    buffers[g].at[s, k],
                    sems.at[g, s, k],
                )
                copies[g, s, k].start()
    sign = sign_matrix()
    for g, (ids, start, size) in enumerate(groups):
        for s in order:
            for k in range(len(ids)):
                copies[g, s, k].wait()
                flat = rows_of(buffers[g][s, k])
                heads = [flat[:, at : at + HD] for at in range(0, size, HD)]
                turned = jnp.dot(
                    jnp.concatenate(heads, axis=0), sign, preferred_element_type=jnp.float32
                )
                turned = (turned * ROTATE_SCALE).reshape(size // HD, blocks, tokens, HD)
                for h in range(size // HD):
                    outs[g * count_head + s][k, :, :, h * HD : (h + 1) * HD] = turned[h].astype(
                        jnp.bfloat16
                    )


def rotate_pieces(sources, groups, count_head, after=(), limit=VMEM):
    blocks, tokens, _ = sources[0].shape
    shapes = [
        jax.ShapeDtypeStruct((len(ids), blocks, tokens, size), jnp.bfloat16)
        for ids, _, size in groups
        for _ in range(count_head)
    ]
    kinds = max(len(ids) for ids, _, _ in groups)
    outs = pl.pallas_call(
        functools.partial(rotate_kernel, groups, count_head, len(after)),
        in_specs=[pl.BlockSpec(memory_space=pltpu.HBM)] * len(sources)
        + [pl.BlockSpec(memory_space=pl.ANY)] * len(after),
        out_specs=[pl.BlockSpec(memory_space=pltpu.VMEM)] * len(shapes),
        out_shape=shapes,
        scratch_shapes=[
            pltpu.VMEM((count_head, len(ids), blocks, tokens, size), jnp.bfloat16)
            for ids, _, size in groups
        ]
        + [pltpu.SemaphoreType.DMA((len(groups), count_head, kinds))],
        cost_estimate=NO_COST,
        compiler_params=pltpu.CompilerParams(vmem_limit_bytes=limit),
    )(*sources, *after)
    return [list(outs[g * count_head : (g + 1) * count_head]) for g in range(len(groups))]


def pick_kernel(count_head, count_tm, picks_ref, *refs):
    pieces, out_ref = refs[:count_head], refs[count_head]
    for s in range(count_head):
        for i in range(count_tm):
            for k in range(NEAR_CAP):
                out_ref[i, k, s] = pieces[s][:, picks_ref[NEAR_CAP * i + k]]


def pick_blocks(picks, pieces, count_tm):
    count_head = len(pieces)
    kinds, _, tokens, width = pieces[0].shape
    shape = (count_tm, NEAR_CAP, count_head, kinds, tokens, width)
    vmem = pl.BlockSpec(memory_space=pltpu.VMEM)
    return pl.pallas_call(
        functools.partial(pick_kernel, count_head, count_tm),
        in_specs=[pl.BlockSpec(memory_space=pltpu.SMEM)] + [vmem] * count_head,
        out_specs=vmem,
        out_shape=jax.ShapeDtypeStruct(shape, jnp.bfloat16),
        cost_estimate=NO_COST,
        compiler_params=pltpu.CompilerParams(vmem_limit_bytes=VMEM),
    )(picks, *pieces)


def remote_rows(count_tm):
    return [
        (distance, k)
        for distance in range(1, count_tm)
        for k in range(NEAR_CAP if distance in (1, count_tm - 1) else FAR_CAP)
    ]


def plan_kernel(count_head, count_tm, blocks, pair_ref, tokens_ref, _, picks_ref, bias_ref, named_ref, table_ref, sem):
    total_blocks, columns = pair_ref.shape
    pairs = pair_ref[...]
    lane = lax.broadcasted_iota(jnp.int32, named_ref.shape, 1)
    named = jnp.zeros(named_ref.shape, jnp.int32)
    for c in range(columns):
        named = jnp.where(pairs[:, c : c + 1] == lane, 1, named)
    named_ref[...] = named
    copy = pltpu.make_async_copy(named_ref, table_ref, sem)
    copy.start()
    copy.wait()
    shard = lax.axis_index("tm")
    place = lax.axis_index("head")
    mine = shard * blocks

    def two_picks(wanted):
        picks = [jnp.int32(0)] * NEAR_CAP
        count = jnp.int32(0)
        for j in range(blocks):
            for k in range(NEAR_CAP):
                picks[k] = jnp.where((wanted[j] > 0) & (count == k), j, picks[k])
            count = count + wanted[j]
        return picks, count

    def named_by(rows, column):
        found = table_ref[rows, column]
        for i in range(1, blocks):
            found = found | table_ref[rows + i, column]
        return found

    for d in range(count_tm):
        picks, _ = two_picks([named_by(d * blocks, mine + j) for j in range(blocks)])
        for k in range(NEAR_CAP):
            picks_ref[NEAR_CAP * d + k] = picks[k]

    kept = [[table_ref[mine + i, mine + j] * tokens_ref[mine + j] for j in range(blocks)] for i in range(blocks)]
    arrivals = {}
    for distance, k in remote_rows(count_tm):
        first = lax.rem(shard + distance, count_tm) * blocks
        if k == 0:
            arrivals[distance] = two_picks([named_by(mine, first + j) for j in range(blocks)])
        picks, count = arrivals[distance]
        there = first + picks[k]
        live = jnp.where(count > k, tokens_ref[there], 0)
        for i in range(blocks):
            kept[i].append(table_ref[mine + i, there] * live)

    total = bias_ref.shape[1]
    piece_rows = BLK // count_head
    at = lax.broadcasted_iota(jnp.int32, (blocks, total), 1)
    query = lax.broadcasted_iota(jnp.int32, (blocks, total), 0)
    own = at < blocks * BLK
    row = jnp.where(own, lax.rem(lax.div(at, piece_rows), blocks), lax.div(at, BLK))
    piece = jnp.where(own, lax.div(at, blocks * piece_rows), lax.div(lax.rem(at, BLK), piece_rows))
    source = lax.rem(place - piece + count_head, count_head)
    position = source * piece_rows + lax.rem(at, piece_rows)
    limit = jnp.zeros((blocks, total), jnp.int32)
    for r in range(len(kept[0])):
        value = jnp.zeros((blocks, total), jnp.int32)
        for i in range(blocks):
            value = jnp.where(query == i, kept[i][r], value)
        limit = jnp.where(row == r, value, limit)
    bias_ref[...] = jnp.where(position < limit, 0.0, NEG)


def plan(pair_list, block_tokens, after, blocks, count_head, count_tm):
    total_blocks = pair_list.shape[0]
    lanes = -(-total_blocks // 128) * 128
    total = (blocks + len(remote_rows(count_tm))) * BLK
    return pl.pallas_call(
        functools.partial(plan_kernel, count_head, count_tm, blocks),
        in_specs=[
            pl.BlockSpec(memory_space=pltpu.VMEM),
            pl.BlockSpec(memory_space=pltpu.SMEM),
            pl.BlockSpec(memory_space=pl.ANY),
        ],
        out_specs=[pl.BlockSpec(memory_space=pltpu.SMEM), pl.BlockSpec(memory_space=pltpu.VMEM)],
        out_shape=[
            jax.ShapeDtypeStruct((NEAR_CAP * count_tm,), jnp.int32),
            jax.ShapeDtypeStruct((blocks, total), jnp.float32),
        ],
        scratch_shapes=[
            pltpu.VMEM((total_blocks, lanes), jnp.int32),
            pltpu.SMEM((total_blocks, lanes), jnp.int32),
            pltpu.SemaphoreType.DMA,
        ],
        cost_estimate=NO_COST,
        compiler_params=pltpu.CompilerParams(vmem_limit_bytes=VMEM),
    )(pair_list, block_tokens, after)


def attend_kernel(count_head, count_tm, start, tokens_ref, bias_ref, *refs):
    queries, owns = refs[:count_head], refs[count_head : 2 * count_head]
    slot_ref = refs[2 * count_head]
    outs = refs[2 * count_head + 1 :]
    _, blocks, tokens, size = owns[0].shape
    shard = lax.axis_index("tm")
    me = lax.axis_index("head")
    sign = sign_matrix()
    for h in range(size // HD):
        lanes = slice(h * HD, (h + 1) * HD)
        query_lanes = slice(start + h * HD, start + (h + 1) * HD)
        query = jnp.concatenate(
            [rows_of(queries[s][0, i, :, query_lanes]) for i in range(blocks) for s in range(count_head)],
            axis=0,
        )

        def gathered(kind):
            pieces = [rows_of(own[kind, :, :, lanes]) for own in owns]
            pieces += [
                rows_of(slot_ref[lax.rem(shard + distance, count_tm), k, :, kind, :, lanes])
                for distance, k in remote_rows(count_tm)
            ]
            return jnp.concatenate(pieces, axis=0)

        keys, values = gathered(0), gathered(1)
        total = keys.shape[0]
        dots = lax.dot_general(
            query, keys, (((1,), (1,)), ((), ())), preferred_element_type=jnp.float32
        )
        dots = dots.reshape(blocks, BLK, total) + bias_ref[...][:, None, :]
        peak = jnp.max(dots, axis=-1, keepdims=True)
        weights = jnp.exp2((dots - peak) * (SCORE_SCALE * LOG2E))
        denominator = jnp.sum(weights, axis=-1, keepdims=True).reshape(blocks * BLK, 1)
        weights_half = weights.astype(jnp.bfloat16).reshape(blocks * BLK, total)
        mixed = jnp.dot(weights_half, values, preferred_element_type=jnp.float32) / denominator
        turned = jnp.zeros_like(mixed)
        rest = mixed
        for _ in range(3):
            piece = rest.astype(jnp.bfloat16)
            turned = turned + jnp.dot(piece, sign, preferred_element_type=jnp.float32)
            rest = rest - piece.astype(jnp.float32)
        turned = (turned * ROTATE_SCALE).reshape(blocks, count_head, tokens, HD)
        token = lax.broadcasted_iota(jnp.int32, (tokens, HD), 0)
        for s in range(count_head):
            position = lax.rem(me - s + count_head, count_head) * tokens + token
            for i in range(blocks):
                outs[s][i, :, lanes] = jnp.where(
                    position < tokens_ref[shard * blocks + i], turned[i, s], 0.0
                ).astype(jnp.bfloat16)


def attend(block_tokens, bias, start, queries, owns, slot):
    count_head, count_tm = len(owns), slot.shape[0]
    _, blocks, tokens, size = owns[0].shape
    vmem = pl.BlockSpec(memory_space=pltpu.VMEM)
    return pl.pallas_call(
        functools.partial(attend_kernel, count_head, count_tm, start),
        in_specs=[pl.BlockSpec(memory_space=pltpu.SMEM)] + [vmem] * (2 * count_head + 2),
        out_specs=[vmem] * count_head,
        out_shape=[jax.ShapeDtypeStruct((blocks, tokens, size), jnp.bfloat16)] * count_head,
        cost_estimate=NO_COST,
        compiler_params=pltpu.CompilerParams(vmem_limit_bytes=VMEM),
    )(block_tokens, bias, *queries, *owns, slot)


def place_kernel(count_head, starts, width_here, *refs):
    pieces, out_ref, sems = refs[:-2], refs[-2], refs[-1]
    me = lax.axis_index("head")
    copies = []
    for at, piece in enumerate(pieces):
        part, s = at // count_head, at % count_head
        column = lax.rem(me + s, count_head) * width_here + starts[part]
        copies.append(
            pltpu.make_async_copy(
                piece,
                out_ref.at[:, :, pl.ds(pl.multiple_of(column, HD), piece.shape[-1])],
                sems.at[at],
            )
        )
        copies[-1].start()
    for copy in copies:
        copy.wait()


def place_pieces(parts, starts, width_here):
    count_head = len(parts[0])
    pieces = [piece for part in parts for piece in part]
    blocks, tokens, _ = pieces[0].shape
    return pl.pallas_call(
        functools.partial(place_kernel, count_head, starts, width_here),
        in_specs=[pl.BlockSpec(memory_space=pl.ANY)] * len(pieces),
        out_specs=pl.BlockSpec(memory_space=pltpu.HBM),
        out_shape=jax.ShapeDtypeStruct((blocks, tokens, count_head * width_here), jnp.bfloat16),
        scratch_shapes=[pltpu.SemaphoreType.DMA((len(pieces),))],
        compiler_params=pltpu.CompilerParams(vmem_limit_bytes=VMEM),
    )(*pieces)


def ring_exchange(pieces, direction):
    count = lax.axis_size("head")
    received = [pieces[0]]
    for s in range(1, count):
        route = [(i, (i + direction * s) % count) for i in range(count)]
        received.append(lax.ppermute(pieces[s], "head", route))
    return received


def shards(query_rows, key_rows, value_rows, pair_list, block_tokens):
    count_head = lax.axis_size("head")
    count_tm = lax.axis_size("tm")
    blocks, tokens, width = query_rows.shape
    width_here = width // count_head
    heads = width_here // HD
    cut = (heads + 1) // 2 * HD
    parts = [(0, cut), (cut, width_here - cut)] if heads > 1 else [(0, width_here)]
    (first,) = rotate_pieces(
        [key_rows, value_rows], [((0, 1),) + parts[0]], count_head, limit=WIDE_VMEM
    )
    packed = [first]
    for part in parts[1:]:
        packed += rotate_pieces([key_rows, value_rows], [((0, 1),) + part], count_head)
    key_values = [ring_exchange(pieces, 1) for pieces in packed]
    picks, bias = plan(pair_list, block_tokens, packed[-1][1], blocks, count_head, count_tm)
    outgoing = [pick_blocks(picks, owns, count_tm) for owns in key_values]
    (query,) = rotate_pieces(
        [query_rows], [((0,), 0, width_here)], count_head, after=(outgoing[0],)
    )
    queries = ring_exchange(query, 1)
    returned = []
    for (start, _), owns, sent in zip(parts, key_values, outgoing):
        slot = lax.all_to_all(sent, "tm", split_axis=0, concat_axis=0, tiled=True)
        attended = attend(block_tokens, bias, start, queries, owns, slot)
        returned.append(ring_exchange(attended, -1))
    return place_pieces(returned, [start for start, _ in parts], width_here)


def solution(mesh):
    placed = (
        P(("grp", "tm"), "head", None),
        P(("grp", "tm"), "head", None),
        P(("grp", "tm"), "head", None),
        P("grp", None),
        P("grp"),
    )
    return jax.shard_map(
        shards,
        mesh=mesh,
        in_specs=placed,
        out_specs=P(("grp", "tm"), "head", None),
        check_vma=False,
    )
```

```python
import functools
import math

import jax
import jax.numpy as jnp
from jax import lax
from jax.experimental import pallas as pl
from jax.experimental.pallas import tpu as pltpu
from jax.sharding import PartitionSpec as P

HD = 128
BLK = 64
NEAR_CAP = 2
FAR_CAP = 1
NEG = -1e30
ROTATE_SCALE = 1.0 / math.sqrt(HD)
SCORE_SCALE = 1.0 / math.sqrt(HD)
VMEM = 24 * 1024 * 1024
WIDE_VMEM = 60 * 1024 * 1024
NO_COST = pl.CostEstimate(flops=0, bytes_accessed=0, transcendentals=0)
LOG2E = math.log2(math.e)


def sign_matrix():
    common = lax.broadcasted_iota(jnp.int32, (HD, HD), 0) & lax.broadcasted_iota(
        jnp.int32, (HD, HD), 1
    )
    bits = HD.bit_length() - 1
    parity = common
    for bit in range(1, bits):
        parity = parity ^ (common >> bit)
    return jnp.where((parity & 1) == 0, 1.0, -1.0).astype(jnp.bfloat16)


def rows_of(block):
    rows, width = math.prod(block.shape[:-1]), block.shape[-1]
    if block.shape[-2] % 16 == 0:
        return block.reshape(rows, width)
    return block.astype(jnp.float32).reshape(rows, width).astype(block.dtype)


def by_distance(refs, count, direction):
    if len(refs) > 1:
        return list(refs)
    me = lax.axis_index("head")
    return [refs[0].at[lax.rem(me + direction * s + count, count)] for s in range(count)]


def rotate_kernel(group, count_head, skipped, *refs):
    ids, start, size = group
    count = len(ids)
    sources, outs = refs[:count], by_distance(refs[count + skipped : -2], count_head, 1)
    buffer, sems = refs[-2:]
    blocks, tokens, width = sources[0].shape
    width_here = width // count_head
    me = lax.axis_index("head")
    order = list(range(1, count_head)) + [0]
    copies = {}
    for s in order:
        goal = lax.rem(me + s, count_head)
        column = pl.multiple_of(goal * width_here + start, HD)
        for k, source in enumerate(sources):
            copies[s, k] = pltpu.make_async_copy(
                source.at[:, :, pl.ds(column, size)], buffer.at[s, k], sems.at[s, k]
            )
            copies[s, k].start()
    sign = sign_matrix()
    for s in order:
        for k in range(count):
            copies[s, k].wait()
            flat = rows_of(buffer[s, k])
            heads = [flat[:, at : at + HD] for at in range(0, size, HD)]
            turned = jnp.dot(
                jnp.concatenate(heads, axis=0), sign, preferred_element_type=jnp.float32
            )
            turned = (turned * ROTATE_SCALE).reshape(size // HD, blocks, tokens, HD)
            for h in range(size // HD):
                outs[s][k, :, :, h * HD : (h + 1) * HD] = turned[h].astype(jnp.bfloat16)


def rotate_pieces(sources, start, size, count_head, stacked, after=(), limit=VMEM):
    blocks, tokens, _ = sources[0].shape
    count = len(sources)
    one = (count, blocks, tokens, size)
    shapes = [(count_head,) + one] if stacked else [one] * count_head
    return pl.pallas_call(
        functools.partial(
            rotate_kernel, (tuple(range(count)), start, size), count_head, len(after)
        ),
        in_specs=[pl.BlockSpec(memory_space=pltpu.HBM)] * count
        + [pl.BlockSpec(memory_space=pl.ANY)] * len(after),
        out_specs=[pl.BlockSpec(memory_space=pltpu.VMEM)] * len(shapes),
        out_shape=[jax.ShapeDtypeStruct(shape, jnp.bfloat16) for shape in shapes],
        scratch_shapes=[
            pltpu.VMEM((count_head,) + one, jnp.bfloat16),
            pltpu.SemaphoreType.DMA((count_head, count)),
        ],
        cost_estimate=NO_COST,
        compiler_params=pltpu.CompilerParams(vmem_limit_bytes=limit),
    )(*sources, *after)


def slots_at(distance, count_tm):
    return NEAR_CAP if distance in (1, count_tm - 1) else FAR_CAP


def pick_kernel(count_head, count_tm, own_count, picks_ref, *refs):
    pieces, outs = by_distance(refs[:own_count], count_head, -1), refs[own_count:]
    shard = lax.axis_index("tm")
    for distance, out in enumerate(outs, 1):
        goal = lax.rem(shard + distance, count_tm)
        for k in range(out.shape[0]):
            pick = picks_ref[NEAR_CAP * goal + k]
            for s in range(count_head):
                out[k, s] = pieces[s][:, pick]


def pick_blocks(picks, owns, count_head, count_tm):
    kinds, _, tokens, width = owns[0].shape[-4:]
    vmem = pl.BlockSpec(memory_space=pltpu.VMEM)
    return pl.pallas_call(
        functools.partial(pick_kernel, count_head, count_tm, len(owns)),
        in_specs=[pl.BlockSpec(memory_space=pltpu.SMEM)] + [vmem] * len(owns),
        out_specs=[vmem] * (count_tm - 1),
        out_shape=[
            jax.ShapeDtypeStruct(
                (slots_at(distance, count_tm), count_head, kinds, tokens, width), jnp.bfloat16
            )
            for distance in range(1, count_tm)
        ],
        cost_estimate=NO_COST,
        compiler_params=pltpu.CompilerParams(vmem_limit_bytes=VMEM),
    )(picks, *owns)


def remote_rows(count_tm):
    return [
        (distance, k)
        for distance in range(1, count_tm)
        for k in range(slots_at(distance, count_tm))
    ]


def plan_kernel(count_head, count_tm, blocks, pair_ref, tokens_ref, _, picks_ref, bias_ref, named_ref, table_ref, sem):
    total_blocks, columns = pair_ref.shape
    pairs = pair_ref[...]
    lane = lax.broadcasted_iota(jnp.int32, named_ref.shape, 1)
    named = jnp.zeros(named_ref.shape, jnp.int32)
    for c in range(columns):
        named = jnp.where(pairs[:, c : c + 1] == lane, 1, named)
    named_ref[...] = named
    copy = pltpu.make_async_copy(named_ref, table_ref, sem)
    copy.start()
    copy.wait()
    shard = lax.axis_index("tm")
    place = lax.axis_index("head")
    mine = shard * blocks

    def two_picks(wanted):
        picks = [jnp.int32(0)] * NEAR_CAP
        count = jnp.int32(0)
        for j in range(blocks):
            for k in range(NEAR_CAP):
                picks[k] = jnp.where((wanted[j] > 0) & (count == k), j, picks[k])
            count = count + wanted[j]
        return picks, count

    def named_by(rows, column):
        found = table_ref[rows, column]
        for i in range(1, blocks):
            found = found | table_ref[rows + i, column]
        return found

    for d in range(count_tm):
        picks, _ = two_picks([named_by(d * blocks, mine + j) for j in range(blocks)])
        for k in range(NEAR_CAP):
            picks_ref[NEAR_CAP * d + k] = picks[k]

    kept = [[table_ref[mine + i, mine + j] * tokens_ref[mine + j] for j in range(blocks)] for i in range(blocks)]
    arrivals = {}
    for distance, k in remote_rows(count_tm):
        first = lax.rem(shard - distance + count_tm, count_tm) * blocks
        if k == 0:
            arrivals[distance] = two_picks([named_by(mine, first + j) for j in range(blocks)])
        picks, count = arrivals[distance]
        there = first + picks[k]
        live = jnp.where(count > k, tokens_ref[there], 0)
        for i in range(blocks):
            kept[i].append(table_ref[mine + i, there] * live)

    total = bias_ref.shape[1]
    piece_rows = BLK // count_head
    at = lax.broadcasted_iota(jnp.int32, (blocks, total), 1)
    query = lax.broadcasted_iota(jnp.int32, (blocks, total), 0)
    own = at < blocks * BLK
    row = jnp.where(own, lax.rem(lax.div(at, piece_rows), blocks), lax.div(at, BLK))
    piece = jnp.where(own, lax.div(at, blocks * piece_rows), lax.div(lax.rem(at, BLK), piece_rows))
    source = lax.rem(place - piece + count_head, count_head)
    position = source * piece_rows + lax.rem(at, piece_rows)
    limit = jnp.zeros((blocks, total), jnp.int32)
    for r in range(len(kept[0])):
        value = jnp.zeros((blocks, total), jnp.int32)
        for i in range(blocks):
            value = jnp.where(query == i, kept[i][r], value)
        limit = jnp.where(row == r, value, limit)
    bias_ref[...] = jnp.where(position < limit, 0.0, NEG)


def plan(pair_list, block_tokens, after, blocks, count_head, count_tm):
    total_blocks = pair_list.shape[0]
    lanes = -(-total_blocks // 128) * 128
    total = (blocks + len(remote_rows(count_tm))) * BLK
    return pl.pallas_call(
        functools.partial(plan_kernel, count_head, count_tm, blocks),
        in_specs=[
            pl.BlockSpec(memory_space=pltpu.VMEM),
            pl.BlockSpec(memory_space=pltpu.SMEM),
            pl.BlockSpec(memory_space=pl.ANY),
        ],
        out_specs=[pl.BlockSpec(memory_space=pltpu.SMEM), pl.BlockSpec(memory_space=pltpu.VMEM)],
        out_shape=[
            jax.ShapeDtypeStruct((NEAR_CAP * count_tm,), jnp.int32),
            jax.ShapeDtypeStruct((blocks, total), jnp.float32),
        ],
        scratch_shapes=[
            pltpu.VMEM((total_blocks, lanes), jnp.int32),
            pltpu.SMEM((total_blocks, lanes), jnp.int32),
            pltpu.SemaphoreType.DMA,
        ],
        cost_estimate=NO_COST,
        compiler_params=pltpu.CompilerParams(vmem_limit_bytes=VMEM),
    )(pair_list, block_tokens, after)


def attend_kernel(counts, start, tokens_ref, bias_ref, *refs):
    count_head, count_tm, query_count, own_count = counts
    at = [query_count, query_count + own_count, query_count + own_count + count_tm - 1]
    queries = by_distance(refs[: at[0]], count_head, -1)
    owns = by_distance(refs[at[0] : at[1]], count_head, -1)
    slots = refs[at[1] : at[2]]
    outs = by_distance(refs[at[2] :], count_head, -1)
    _, blocks, tokens, size = owns[0].shape
    shard = lax.axis_index("tm")
    me = lax.axis_index("head")
    sign = sign_matrix()
    for h in range(size // HD):
        lanes = slice(h * HD, (h + 1) * HD)
        query_lanes = slice(start + h * HD, start + (h + 1) * HD)
        query = jnp.concatenate(
            [rows_of(queries[s][0, i, :, query_lanes]) for i in range(blocks) for s in range(count_head)],
            axis=0,
        )

        def gathered(kind):
            pieces = [rows_of(own[kind, :, :, lanes]) for own in owns]
            pieces += [
                rows_of(slots[distance - 1][k, :, kind, :, lanes])
                for distance, k in remote_rows(count_tm)
            ]
            return jnp.concatenate(pieces, axis=0)

        keys, values = gathered(0), gathered(1)
        total = keys.shape[0]
        dots = lax.dot_general(
            query, keys, (((1,), (1,)), ((), ())), preferred_element_type=jnp.float32
        )
        dots = dots.reshape(blocks, BLK, total) + bias_ref[...][:, None, :]
        peak = jnp.max(dots, axis=-1, keepdims=True)
        weights = jnp.exp2((dots - peak) * (SCORE_SCALE * LOG2E))
        denominator = jnp.sum(weights, axis=-1, keepdims=True).reshape(blocks * BLK, 1)
        weights_half = weights.astype(jnp.bfloat16).reshape(blocks * BLK, total)
        mixed = jnp.dot(weights_half, values, preferred_element_type=jnp.float32) / denominator
        turned = jnp.zeros_like(mixed)
        rest = mixed
        for _ in range(3):
            piece = rest.astype(jnp.bfloat16)
            turned = turned + jnp.dot(piece, sign, preferred_element_type=jnp.float32)
            rest = rest - piece.astype(jnp.float32)
        turned = (turned * ROTATE_SCALE).reshape(blocks, count_head, tokens, HD)
        token = lax.broadcasted_iota(jnp.int32, (tokens, HD), 0)
        for s in range(count_head):
            position = lax.rem(me - s + count_head, count_head) * tokens + token
            for i in range(blocks):
                outs[s][i, :, lanes] = jnp.where(
                    position < tokens_ref[shard * blocks + i], turned[i, s], 0.0
                ).astype(jnp.bfloat16)


def attend(block_tokens, bias, start, queries, owns, slots, count_head, stacked):
    count_tm = len(slots) + 1
    _, blocks, tokens, size = owns[0].shape[-4:]
    one = (blocks, tokens, size)
    shapes = [(count_head,) + one] if stacked else [one] * count_head
    counts = (count_head, count_tm, len(queries), len(owns))
    vmem = pl.BlockSpec(memory_space=pltpu.VMEM)
    return pl.pallas_call(
        functools.partial(attend_kernel, counts, start),
        in_specs=[pl.BlockSpec(memory_space=pltpu.SMEM)]
        + [vmem] * (1 + len(queries) + len(owns) + len(slots)),
        out_specs=[vmem] * len(shapes),
        out_shape=[jax.ShapeDtypeStruct(shape, jnp.bfloat16) for shape in shapes],
        cost_estimate=NO_COST,
        compiler_params=pltpu.CompilerParams(vmem_limit_bytes=VMEM),
    )(block_tokens, bias, *queries, *owns, *slots)


def place_kernel(counts, starts, width_here, *refs):
    count_head = counts[0]
    out_ref, sems = refs[-2:]
    copies = []
    at = 0
    for count, start in zip(counts[1:], starts):
        pieces = by_distance(refs[at : at + count], count_head, 1)
        at += count
        for s, piece in enumerate(pieces):
            column = lax.rem(lax.axis_index("head") + s, count_head) * width_here + start
            copies.append(
                pltpu.make_async_copy(
                    piece,
                    out_ref.at[:, :, pl.ds(pl.multiple_of(column, HD), piece.shape[-1])],
                    sems.at[len(copies)],
                )
            )
            copies[-1].start()
    for copy in copies:
        copy.wait()


def place_pieces(parts, starts, count_head, width_here):
    pieces = [piece for part in parts for piece in part]
    blocks, tokens, _ = pieces[0].shape[-3:]
    counts = (count_head,) + tuple(len(part) for part in parts)
    return pl.pallas_call(
        functools.partial(place_kernel, counts, starts, width_here),
        in_specs=[pl.BlockSpec(memory_space=pl.ANY)] * len(pieces),
        out_specs=pl.BlockSpec(memory_space=pltpu.HBM),
        out_shape=jax.ShapeDtypeStruct((blocks, tokens, count_head * width_here), jnp.bfloat16),
        scratch_shapes=[pltpu.SemaphoreType.DMA((len(parts) * count_head,))],
        compiler_params=pltpu.CompilerParams(vmem_limit_bytes=VMEM),
    )(*pieces)


def shifted(array, axis, distance):
    count = lax.axis_size(axis)
    return lax.ppermute(array, axis, [(i, (i + distance) % count) for i in range(count)])


def exchange(pieces, direction):
    if len(pieces) == 1:
        return [lax.all_to_all(pieces[0], "head", split_axis=0, concat_axis=0, tiled=True)]
    return [pieces[0]] + [
        shifted(piece, "head", direction * s) for s, piece in enumerate(pieces[1:], 1)
    ]


def shards(query_rows, key_rows, value_rows, pair_list, block_tokens):
    count_head = lax.axis_size("head")
    count_tm = lax.axis_size("tm")
    blocks, tokens, width = query_rows.shape
    width_here = width // count_head
    heads = width_here // HD
    cut = (heads + 1) // 2 * HD
    parts = [(0, cut), (cut, width_here - cut)] if heads > 1 else [(0, width_here)]
    sources = [key_rows, value_rows]
    packed = [rotate_pieces(sources, *parts[0], count_head, False, limit=WIDE_VMEM)]
    packed += [rotate_pieces(sources, *part, count_head, True) for part in parts[1:]]
    key_values = [exchange(pieces, 1) for pieces in packed]
    picks, bias = plan(pair_list, block_tokens, packed[-1][0], blocks, count_head, count_tm)
    query = rotate_pieces([query_rows], 0, width_here, count_head, True, after=(bias,))
    queries = exchange(query, 1)
    outgoing = [pick_blocks(picks, owns, count_head, count_tm) for owns in key_values]
    returned = []
    for at, (owns, sent) in enumerate(zip(key_values, outgoing)):
        slots = [shifted(block, "tm", distance) for distance, block in enumerate(sent, 1)]
        attended = attend(
            block_tokens, bias, parts[at][0], queries, owns, slots, count_head, at > 0
        )
        returned.append(exchange(attended, -1))
    return place_pieces(returned, [start for start, _ in parts], count_head, width_here)


def solution(mesh):
    placed = (
        P(("grp", "tm"), "head", None),
        P(("grp", "tm"), "head", None),
        P(("grp", "tm"), "head", None),
        P("grp", None),
        P("grp"),
    )
    return jax.shard_map(
        shards,
        mesh=mesh,
        in_specs=placed,
        out_specs=P(("grp", "tm"), "head", None),
        check_vma=False,
    )
```

```python
import functools
import math

import jax
import jax.numpy as jnp
from jax import lax
from jax.experimental import pallas as pl
from jax.experimental.pallas import tpu as pltpu
from jax.sharding import PartitionSpec as P

HD = 128
BLK = 64
NEAR_CAP = 2
FAR_CAP = 1
NEG = -1e30
ROTATE_SCALE = 1.0 / math.sqrt(HD)
SCORE_SCALE = 1.0 / math.sqrt(HD)
VMEM = 24 * 1024 * 1024
WIDE_VMEM = 60 * 1024 * 1024
NO_COST = pl.CostEstimate(flops=0, bytes_accessed=0, transcendentals=0)
LOG2E = math.log2(math.e)


def sign_matrix():
    common = lax.broadcasted_iota(jnp.int32, (HD, HD), 0) & lax.broadcasted_iota(
        jnp.int32, (HD, HD), 1
    )
    bits = HD.bit_length() - 1
    parity = common
    for bit in range(1, bits):
        parity = parity ^ (common >> bit)
    return jnp.where((parity & 1) == 0, 1.0, -1.0).astype(jnp.bfloat16)


def rows_of(block):
    rows, width = math.prod(block.shape[:-1]), block.shape[-1]
    if block.shape[-2] % 16 == 0:
        return block.reshape(rows, width)
    return block.astype(jnp.float32).reshape(rows, width).astype(block.dtype)


def by_distance(refs, count, direction, axis="head"):
    if len(refs) > 1:
        return list(refs)
    me = lax.axis_index(axis)
    return [refs[0].at[lax.rem(me + direction * s + count, count)] for s in range(count)]


def rotate_kernel(group, count_head, skipped, *refs):
    ids, start, size = group
    count = len(ids)
    sources, outs = refs[:count], by_distance(refs[count + skipped : -2], count_head, 1)
    buffer, sems = refs[-2:]
    blocks, tokens, width = sources[0].shape
    width_here = width // count_head
    me = lax.axis_index("head")
    order = list(range(1, count_head)) + [0]
    copies = {}
    for s in order:
        goal = lax.rem(me + s, count_head)
        column = pl.multiple_of(goal * width_here + start, HD)
        for k, source in enumerate(sources):
            copies[s, k] = pltpu.make_async_copy(
                source.at[:, :, pl.ds(column, size)], buffer.at[s, k], sems.at[s, k]
            )
            copies[s, k].start()
    sign = sign_matrix()
    for s in order:
        for k in range(count):
            copies[s, k].wait()
            flat = rows_of(buffer[s, k])
            heads = [flat[:, at : at + HD] for at in range(0, size, HD)]
            turned = jnp.dot(
                jnp.concatenate(heads, axis=0), sign, preferred_element_type=jnp.float32
            )
            turned = (turned * ROTATE_SCALE).reshape(size // HD, blocks, tokens, HD)
            for h in range(size // HD):
                outs[s][k, :, :, h * HD : (h + 1) * HD] = turned[h].astype(jnp.bfloat16)


def rotate_pieces(sources, start, size, count_head, stacked, after=(), limit=VMEM):
    blocks, tokens, _ = sources[0].shape
    count = len(sources)
    one = (count, blocks, tokens, size)
    shapes = [(count_head,) + one] if stacked else [one] * count_head
    return pl.pallas_call(
        functools.partial(
            rotate_kernel, (tuple(range(count)), start, size), count_head, len(after)
        ),
        in_specs=[pl.BlockSpec(memory_space=pltpu.HBM)] * count
        + [pl.BlockSpec(memory_space=pl.ANY)] * len(after),
        out_specs=[pl.BlockSpec(memory_space=pltpu.VMEM)] * len(shapes),
        out_shape=[jax.ShapeDtypeStruct(shape, jnp.bfloat16) for shape in shapes],
        scratch_shapes=[
            pltpu.VMEM((count_head,) + one, jnp.bfloat16),
            pltpu.SemaphoreType.DMA((count_head, count)),
        ],
        cost_estimate=NO_COST,
        compiler_params=pltpu.CompilerParams(vmem_limit_bytes=limit),
    )(*sources, *after)


def slots_at(distance, count_tm):
    return NEAR_CAP if distance in (1, count_tm - 1) else FAR_CAP


def pick_kernel(count_head, count_tm, own_count, picks_ref, *refs):
    pieces = by_distance(refs[:own_count], count_head, -1)
    outs = by_distance(refs[own_count:], count_tm, 1, "tm")[-(count_tm - 1) :]
    shard = lax.axis_index("tm")
    for distance, out in enumerate(outs, 1):
        goal = lax.rem(shard + distance, count_tm)
        for k in range(slots_at(distance, count_tm)):
            pick = picks_ref[NEAR_CAP * goal + k]
            for s in range(count_head):
                out[k, s] = pieces[s][:, pick]


def pick_blocks(picks, owns, count_head, count_tm, stacked):
    kinds, _, tokens, width = owns[0].shape[-4:]
    one = (count_head, kinds, tokens, width)
    if stacked:
        shapes = [(count_tm, NEAR_CAP) + one]
    else:
        shapes = [(slots_at(distance, count_tm),) + one for distance in range(1, count_tm)]
    vmem = pl.BlockSpec(memory_space=pltpu.VMEM)
    return pl.pallas_call(
        functools.partial(pick_kernel, count_head, count_tm, len(owns)),
        in_specs=[pl.BlockSpec(memory_space=pltpu.SMEM)] + [vmem] * len(owns),
        out_specs=[vmem] * len(shapes),
        out_shape=[jax.ShapeDtypeStruct(shape, jnp.bfloat16) for shape in shapes],
        cost_estimate=NO_COST,
        compiler_params=pltpu.CompilerParams(vmem_limit_bytes=VMEM),
    )(picks, *owns)


def remote_rows(count_tm):
    return [
        (distance, k)
        for distance in range(1, count_tm)
        for k in range(slots_at(distance, count_tm))
    ]


def plan_kernel(count_head, count_tm, blocks, pair_ref, tokens_ref, _, picks_ref, bias_ref, named_ref, table_ref, sem):
    total_blocks, columns = pair_ref.shape
    pairs = pair_ref[...]
    lane = lax.broadcasted_iota(jnp.int32, named_ref.shape, 1)
    named = jnp.zeros(named_ref.shape, jnp.int32)
    for c in range(columns):
        named = jnp.where(pairs[:, c : c + 1] == lane, 1, named)
    named_ref[...] = named
    copy = pltpu.make_async_copy(named_ref, table_ref, sem)
    copy.start()
    copy.wait()
    shard = lax.axis_index("tm")
    place = lax.axis_index("head")
    mine = shard * blocks

    def two_picks(wanted):
        picks = [jnp.int32(0)] * NEAR_CAP
        count = jnp.int32(0)
        for j in range(blocks):
            for k in range(NEAR_CAP):
                picks[k] = jnp.where((wanted[j] > 0) & (count == k), j, picks[k])
            count = count + wanted[j]
        return picks, count

    def named_by(rows, column):
        found = table_ref[rows, column]
        for i in range(1, blocks):
            found = found | table_ref[rows + i, column]
        return found

    for d in range(count_tm):
        picks, _ = two_picks([named_by(d * blocks, mine + j) for j in range(blocks)])
        for k in range(NEAR_CAP):
            picks_ref[NEAR_CAP * d + k] = picks[k]

    kept = [[table_ref[mine + i, mine + j] * tokens_ref[mine + j] for j in range(blocks)] for i in range(blocks)]
    arrivals = {}
    for distance, k in remote_rows(count_tm):
        first = lax.rem(shard - distance + count_tm, count_tm) * blocks
        if k == 0:
            arrivals[distance] = two_picks([named_by(mine, first + j) for j in range(blocks)])
        picks, count = arrivals[distance]
        there = first + picks[k]
        live = jnp.where(count > k, tokens_ref[there], 0)
        for i in range(blocks):
            kept[i].append(table_ref[mine + i, there] * live)

    total = bias_ref.shape[1]
    piece_rows = BLK // count_head
    at = lax.broadcasted_iota(jnp.int32, (blocks, total), 1)
    query = lax.broadcasted_iota(jnp.int32, (blocks, total), 0)
    own = at < blocks * BLK
    row = jnp.where(own, lax.rem(lax.div(at, piece_rows), blocks), lax.div(at, BLK))
    piece = jnp.where(own, lax.div(at, blocks * piece_rows), lax.div(lax.rem(at, BLK), piece_rows))
    source = lax.rem(place - piece + count_head, count_head)
    position = source * piece_rows + lax.rem(at, piece_rows)
    limit = jnp.zeros((blocks, total), jnp.int32)
    for r in range(len(kept[0])):
        value = jnp.zeros((blocks, total), jnp.int32)
        for i in range(blocks):
            value = jnp.where(query == i, kept[i][r], value)
        limit = jnp.where(row == r, value, limit)
    bias_ref[...] = jnp.where(position < limit, 0.0, NEG)


def plan(pair_list, block_tokens, after, blocks, count_head, count_tm):
    total_blocks = pair_list.shape[0]
    lanes = -(-total_blocks // 128) * 128
    total = (blocks + len(remote_rows(count_tm))) * BLK
    return pl.pallas_call(
        functools.partial(plan_kernel, count_head, count_tm, blocks),
        in_specs=[
            pl.BlockSpec(memory_space=pltpu.VMEM),
            pl.BlockSpec(memory_space=pltpu.SMEM),
            pl.BlockSpec(memory_space=pl.ANY),
        ],
        out_specs=[pl.BlockSpec(memory_space=pltpu.SMEM), pl.BlockSpec(memory_space=pltpu.VMEM)],
        out_shape=[
            jax.ShapeDtypeStruct((NEAR_CAP * count_tm,), jnp.int32),
            jax.ShapeDtypeStruct((blocks, total), jnp.float32),
        ],
        scratch_shapes=[
            pltpu.VMEM((total_blocks, lanes), jnp.int32),
            pltpu.SMEM((total_blocks, lanes), jnp.int32),
            pltpu.SemaphoreType.DMA,
        ],
        cost_estimate=NO_COST,
        compiler_params=pltpu.CompilerParams(vmem_limit_bytes=VMEM),
    )(pair_list, block_tokens, after)


def attend_kernel(counts, start, tokens_ref, bias_ref, *refs):
    count_head, count_tm, query_count, own_count, slot_count = counts
    at = [query_count, query_count + own_count, query_count + own_count + slot_count]
    queries = by_distance(refs[: at[0]], count_head, -1)
    owns = by_distance(refs[at[0] : at[1]], count_head, -1)
    slots = by_distance(refs[at[1] : at[2]], count_tm, -1, "tm")[-(count_tm - 1) :]
    outs = by_distance(refs[at[2] :], count_head, -1)
    _, blocks, tokens, size = owns[0].shape
    shard = lax.axis_index("tm")
    me = lax.axis_index("head")
    sign = sign_matrix()
    for h in range(size // HD):
        lanes = slice(h * HD, (h + 1) * HD)
        query_lanes = slice(start + h * HD, start + (h + 1) * HD)
        query = jnp.concatenate(
            [rows_of(queries[s][0, i, :, query_lanes]) for i in range(blocks) for s in range(count_head)],
            axis=0,
        )

        def gathered(kind):
            pieces = [rows_of(own[kind, :, :, lanes]) for own in owns]
            pieces += [
                rows_of(slots[distance - 1][k, :, kind, :, lanes])
                for distance, k in remote_rows(count_tm)
            ]
            return jnp.concatenate(pieces, axis=0)

        keys, values = gathered(0), gathered(1)
        total = keys.shape[0]
        dots = lax.dot_general(
            query, keys, (((1,), (1,)), ((), ())), preferred_element_type=jnp.float32
        )
        dots = dots.reshape(blocks, BLK, total) + bias_ref[...][:, None, :]
        peak = jnp.max(dots, axis=-1, keepdims=True)
        weights = jnp.exp2((dots - peak) * (SCORE_SCALE * LOG2E))
        denominator = jnp.sum(weights, axis=-1, keepdims=True).reshape(blocks * BLK, 1)
        weights_half = weights.astype(jnp.bfloat16).reshape(blocks * BLK, total)
        mixed = jnp.dot(weights_half, values, preferred_element_type=jnp.float32) / denominator
        turned = jnp.zeros_like(mixed)
        rest = mixed
        for _ in range(3):
            piece = rest.astype(jnp.bfloat16)
            turned = turned + jnp.dot(piece, sign, preferred_element_type=jnp.float32)
            rest = rest - piece.astype(jnp.float32)
        turned = (turned * ROTATE_SCALE).reshape(blocks, count_head, tokens, HD)
        token = lax.broadcasted_iota(jnp.int32, (tokens, HD), 0)
        for s in range(count_head):
            position = lax.rem(me - s + count_head, count_head) * tokens + token
            for i in range(blocks):
                outs[s][i, :, lanes] = jnp.where(
                    position < tokens_ref[shard * blocks + i], turned[i, s], 0.0
                ).astype(jnp.bfloat16)


def attend(block_tokens, bias, start, queries, owns, slots, count_head, count_tm, stacked):
    _, blocks, tokens, size = owns[0].shape[-4:]
    one = (blocks, tokens, size)
    shapes = [(count_head,) + one] if stacked else [one] * count_head
    counts = (count_head, count_tm, len(queries), len(owns), len(slots))
    vmem = pl.BlockSpec(memory_space=pltpu.VMEM)
    return pl.pallas_call(
        functools.partial(attend_kernel, counts, start),
        in_specs=[pl.BlockSpec(memory_space=pltpu.SMEM)]
        + [vmem] * (1 + len(queries) + len(owns) + len(slots)),
        out_specs=[vmem] * len(shapes),
        out_shape=[jax.ShapeDtypeStruct(shape, jnp.bfloat16) for shape in shapes],
        cost_estimate=NO_COST,
        compiler_params=pltpu.CompilerParams(vmem_limit_bytes=VMEM),
    )(block_tokens, bias, *queries, *owns, *slots)


def place_kernel(counts, starts, width_here, *refs):
    count_head = counts[0]
    out_ref, sems = refs[-2:]
    copies = []
    at = 0
    for count, start in zip(counts[1:], starts):
        pieces = by_distance(refs[at : at + count], count_head, 1)
        at += count
        for s, piece in enumerate(pieces):
            column = lax.rem(lax.axis_index("head") + s, count_head) * width_here + start
            copies.append(
                pltpu.make_async_copy(
                    piece,
                    out_ref.at[:, :, pl.ds(pl.multiple_of(column, HD), piece.shape[-1])],
                    sems.at[len(copies)],
                )
            )
            copies[-1].start()
    for copy in copies:
        copy.wait()


def place_pieces(parts, starts, count_head, width_here):
    pieces = [piece for part in parts for piece in part]
    blocks, tokens, _ = pieces[0].shape[-3:]
    counts = (count_head,) + tuple(len(part) for part in parts)
    return pl.pallas_call(
        functools.partial(place_kernel, counts, starts, width_here),
        in_specs=[pl.BlockSpec(memory_space=pl.ANY)] * len(pieces),
        out_specs=pl.BlockSpec(memory_space=pltpu.HBM),
        out_shape=jax.ShapeDtypeStruct((blocks, tokens, count_head * width_here), jnp.bfloat16),
        scratch_shapes=[pltpu.SemaphoreType.DMA((len(parts) * count_head,))],
        compiler_params=pltpu.CompilerParams(vmem_limit_bytes=VMEM),
    )(*pieces)


def shifted(array, axis, distance):
    count = lax.axis_size(axis)
    return lax.ppermute(array, axis, [(i, (i + distance) % count) for i in range(count)])


def exchange(pieces, direction):
    if len(pieces) == 1:
        return [lax.all_to_all(pieces[0], "head", split_axis=0, concat_axis=0, tiled=True)]
    return [pieces[0]] + [
        shifted(piece, "head", direction * s) for s, piece in enumerate(pieces[1:], 1)
    ]


def forward(sent):
    if len(sent) == 1:
        return [lax.all_to_all(sent[0], "tm", split_axis=0, concat_axis=0, tiled=True)]
    return [shifted(block, "tm", distance) for distance, block in enumerate(sent, 1)]


def shards(query_rows, key_rows, value_rows, pair_list, block_tokens):
    count_head = lax.axis_size("head")
    count_tm = lax.axis_size("tm")
    blocks, tokens, width = query_rows.shape
    width_here = width // count_head
    heads = width_here // HD
    cut = (heads + 1) // 2 * HD
    parts = [(0, cut), (cut, width_here - cut)] if heads > 1 else [(0, width_here)]
    sources = [key_rows, value_rows]
    packed = [rotate_pieces(sources, *parts[0], count_head, False, limit=WIDE_VMEM)]
    packed += [rotate_pieces(sources, *part, count_head, False) for part in parts[1:]]
    key_values = [exchange(pieces, 1) for pieces in packed]
    picks, bias = plan(pair_list, block_tokens, packed[-1][0], blocks, count_head, count_tm)
    sent = [
        pick_blocks(picks, owns, count_head, count_tm, at > 0)
        for at, owns in enumerate(key_values)
    ]
    query = rotate_pieces([query_rows], 0, width_here, count_head, False, after=(sent[0][0],))
    queries = exchange(query, 1)
    returned = []
    for (start, _), owns, picked in zip(parts, key_values, sent):
        slots = forward(picked)
        attended = attend(
            block_tokens, bias, start, queries, owns, slots, count_head, count_tm, False
        )
        returned.append(exchange(attended, -1))
    return place_pieces(returned, [start for start, _ in parts], count_head, width_here)


def solution(mesh):
    placed = (
        P(("grp", "tm"), "head", None),
        P(("grp", "tm"), "head", None),
        P(("grp", "tm"), "head", None),
        P("grp", None),
        P("grp"),
    )
    return jax.shard_map(
        shards,
        mesh=mesh,
        in_specs=placed,
        out_specs=P(("grp", "tm"), "head", None),
        check_vma=False,
    )
```

```python
import functools
import math

import jax
import jax.numpy as jnp
from jax import lax
from jax.experimental import pallas as pl
from jax.experimental.pallas import tpu as pltpu
from jax.sharding import PartitionSpec as P

HD = 128
BLK = 64
NEAR_CAP = 2
FAR_CAP = 1
NEG = -1e30
ROTATE_SCALE = 1.0 / math.sqrt(HD)
SCORE_SCALE = 1.0 / math.sqrt(HD)
VMEM = 24 * 1024 * 1024
WIDE_VMEM = 60 * 1024 * 1024
NO_COST = pl.CostEstimate(flops=0, bytes_accessed=0, transcendentals=0)
HIGH_COST = pl.CostEstimate(flops=10**11, bytes_accessed=0, transcendentals=0)
LOG2E = math.log2(math.e)


def sign_matrix():
    common = lax.broadcasted_iota(jnp.int32, (HD, HD), 0) & lax.broadcasted_iota(
        jnp.int32, (HD, HD), 1
    )
    bits = HD.bit_length() - 1
    parity = common
    for bit in range(1, bits):
        parity = parity ^ (common >> bit)
    return jnp.where((parity & 1) == 0, 1.0, -1.0).astype(jnp.bfloat16)


def rows_of(block):
    rows, width = math.prod(block.shape[:-1]), block.shape[-1]
    if block.shape[-2] % 16 == 0:
        return block.reshape(rows, width)
    return block.astype(jnp.float32).reshape(rows, width).astype(block.dtype)


def by_distance(refs, count, direction, axis="head"):
    if len(refs) > 1:
        return list(refs)
    me = lax.axis_index(axis)
    return [refs[0].at[lax.rem(me + direction * s + count, count)] for s in range(count)]


def rotate_kernel(group, count_head, skipped, *refs):
    ids, start, size = group
    count = len(ids)
    sources, outs = refs[:count], by_distance(refs[count + skipped : -2], count_head, 1)
    buffer, sems = refs[-2:]
    blocks, tokens, width = sources[0].shape
    width_here = width // count_head
    me = lax.axis_index("head")
    order = list(range(1, count_head)) + [0]
    copies = {}
    for s in order:
        goal = lax.rem(me + s, count_head)
        column = pl.multiple_of(goal * width_here + start, HD)
        for k, source in enumerate(sources):
            copies[s, k] = pltpu.make_async_copy(
                source.at[:, :, pl.ds(column, size)], buffer.at[s, k], sems.at[s, k]
            )
            copies[s, k].start()
    sign = sign_matrix()
    for s in order:
        for k in range(count):
            copies[s, k].wait()
            flat = rows_of(buffer[s, k])
            heads = [flat[:, at : at + HD] for at in range(0, size, HD)]
            turned = jnp.dot(
                jnp.concatenate(heads, axis=0), sign, preferred_element_type=jnp.float32
            )
            turned = (turned * ROTATE_SCALE).reshape(size // HD, blocks, tokens, HD)
            for h in range(size // HD):
                outs[s][k, :, :, h * HD : (h + 1) * HD] = turned[h].astype(jnp.bfloat16)


def rotate_pieces(sources, start, size, count_head, stacked, after=(), limit=VMEM):
    blocks, tokens, _ = sources[0].shape
    count = len(sources)
    one = (count, blocks, tokens, size)
    shapes = [(count_head,) + one] if stacked else [one] * count_head
    return pl.pallas_call(
        functools.partial(
            rotate_kernel, (tuple(range(count)), start, size), count_head, len(after)
        ),
        in_specs=[pl.BlockSpec(memory_space=pltpu.HBM)] * count
        + [pl.BlockSpec(memory_space=pl.ANY)] * len(after),
        out_specs=[pl.BlockSpec(memory_space=pltpu.VMEM)] * len(shapes),
        out_shape=[jax.ShapeDtypeStruct(shape, jnp.bfloat16) for shape in shapes],
        scratch_shapes=[
            pltpu.VMEM((count_head,) + one, jnp.bfloat16),
            pltpu.SemaphoreType.DMA((count_head, count)),
        ],
        cost_estimate=NO_COST,
        compiler_params=pltpu.CompilerParams(vmem_limit_bytes=limit),
    )(*sources, *after)


def slots_at(distance, count_tm):
    return NEAR_CAP if distance in (1, count_tm - 1) else FAR_CAP


def pick_kernel(count_head, count_tm, own_count, skipped, picks_ref, *refs):
    pieces = by_distance(refs[:own_count], count_head, -1)
    outs = by_distance(refs[own_count + skipped :], count_tm, 1, "tm")[-(count_tm - 1) :]
    shard = lax.axis_index("tm")
    for distance, out in enumerate(outs, 1):
        goal = lax.rem(shard + distance, count_tm)
        for k in range(slots_at(distance, count_tm)):
            pick = picks_ref[NEAR_CAP * goal + k]
            for s in range(count_head):
                out[k, s] = pieces[s][:, pick]


def pick_blocks(picks, owns, count_head, count_tm, stacked, after=(), cost=NO_COST):
    kinds, _, tokens, width = owns[0].shape[-4:]
    one = (count_head, kinds, tokens, width)
    if stacked:
        shapes = [(count_tm, NEAR_CAP) + one]
    else:
        shapes = [(slots_at(distance, count_tm),) + one for distance in range(1, count_tm)]
    vmem = pl.BlockSpec(memory_space=pltpu.VMEM)
    return pl.pallas_call(
        functools.partial(pick_kernel, count_head, count_tm, len(owns), len(after)),
        in_specs=[pl.BlockSpec(memory_space=pltpu.SMEM)]
        + [vmem] * len(owns)
        + [pl.BlockSpec(memory_space=pl.ANY)] * len(after),
        out_specs=[vmem] * len(shapes),
        out_shape=[jax.ShapeDtypeStruct(shape, jnp.bfloat16) for shape in shapes],
        cost_estimate=cost,
        compiler_params=pltpu.CompilerParams(vmem_limit_bytes=VMEM),
    )(picks, *owns, *after)


def remote_rows(count_tm):
    return [
        (distance, k)
        for distance in range(1, count_tm)
        for k in range(slots_at(distance, count_tm))
    ]


def plan_kernel(count_head, count_tm, blocks, pair_ref, tokens_ref, _, picks_ref, bias_ref, named_ref, table_ref, sem):
    total_blocks, columns = pair_ref.shape
    pairs = pair_ref[...]
    lane = lax.broadcasted_iota(jnp.int32, named_ref.shape, 1)
    named = jnp.zeros(named_ref.shape, jnp.int32)
    for c in range(columns):
        named = jnp.where(pairs[:, c : c + 1] == lane, 1, named)
    named_ref[...] = named
    copy = pltpu.make_async_copy(named_ref, table_ref, sem)
    copy.start()
    copy.wait()
    shard = lax.axis_index("tm")
    place = lax.axis_index("head")
    mine = shard * blocks

    def two_picks(wanted):
        picks = [jnp.int32(0)] * NEAR_CAP
        count = jnp.int32(0)
        for j in range(blocks):
            for k in range(NEAR_CAP):
                picks[k] = jnp.where((wanted[j] > 0) & (count == k), j, picks[k])
            count = count + wanted[j]
        return picks, count

    def named_by(rows, column):
        found = table_ref[rows, column]
        for i in range(1, blocks):
            found = found | table_ref[rows + i, column]
        return found

    for d in range(count_tm):
        picks, _ = two_picks([named_by(d * blocks, mine + j) for j in range(blocks)])
        for k in range(NEAR_CAP):
            picks_ref[NEAR_CAP * d + k] = picks[k]

    kept = [[table_ref[mine + i, mine + j] * tokens_ref[mine + j] for j in range(blocks)] for i in range(blocks)]
    arrivals = {}
    for distance, k in remote_rows(count_tm):
        first = lax.rem(shard - distance + count_tm, count_tm) * blocks
        if k == 0:
            arrivals[distance] = two_picks([named_by(mine, first + j) for j in range(blocks)])
        picks, count = arrivals[distance]
        there = first + picks[k]
        live = jnp.where(count > k, tokens_ref[there], 0)
        for i in range(blocks):
            kept[i].append(table_ref[mine + i, there] * live)

    total = bias_ref.shape[1]
    piece_rows = BLK // count_head
    at = lax.broadcasted_iota(jnp.int32, (blocks, total), 1)
    query = lax.broadcasted_iota(jnp.int32, (blocks, total), 0)
    own = at < blocks * BLK
    row = jnp.where(own, lax.rem(lax.div(at, piece_rows), blocks), lax.div(at, BLK))
    piece = jnp.where(own, lax.div(at, blocks * piece_rows), lax.div(lax.rem(at, BLK), piece_rows))
    source = lax.rem(place - piece + count_head, count_head)
    position = source * piece_rows + lax.rem(at, piece_rows)
    limit = jnp.zeros((blocks, total), jnp.int32)
    for r in range(len(kept[0])):
        value = jnp.zeros((blocks, total), jnp.int32)
        for i in range(blocks):
            value = jnp.where(query == i, kept[i][r], value)
        limit = jnp.where(row == r, value, limit)
    bias_ref[...] = jnp.where(position < limit, 0.0, NEG)


def plan(pair_list, block_tokens, after, blocks, count_head, count_tm):
    total_blocks = pair_list.shape[0]
    lanes = -(-total_blocks // 128) * 128
    total = (blocks + len(remote_rows(count_tm))) * BLK
    return pl.pallas_call(
        functools.partial(plan_kernel, count_head, count_tm, blocks),
        in_specs=[
            pl.BlockSpec(memory_space=pltpu.VMEM),
            pl.BlockSpec(memory_space=pltpu.SMEM),
            pl.BlockSpec(memory_space=pl.ANY),
        ],
        out_specs=[pl.BlockSpec(memory_space=pltpu.SMEM), pl.BlockSpec(memory_space=pltpu.VMEM)],
        out_shape=[
            jax.ShapeDtypeStruct((NEAR_CAP * count_tm,), jnp.int32),
            jax.ShapeDtypeStruct((blocks, total), jnp.float32),
        ],
        scratch_shapes=[
            pltpu.VMEM((total_blocks, lanes), jnp.int32),
            pltpu.SMEM((total_blocks, lanes), jnp.int32),
            pltpu.SemaphoreType.DMA,
        ],
        cost_estimate=NO_COST,
        compiler_params=pltpu.CompilerParams(vmem_limit_bytes=VMEM),
    )(pair_list, block_tokens, after)


def attend_kernel(counts, start, tokens_ref, bias_ref, *refs):
    count_head, count_tm, query_count, own_count, slot_count = counts
    at = [query_count, query_count + own_count, query_count + own_count + slot_count]
    queries = by_distance(refs[: at[0]], count_head, -1)
    owns = by_distance(refs[at[0] : at[1]], count_head, -1)
    slots = by_distance(refs[at[1] : at[2]], count_tm, -1, "tm")[-(count_tm - 1) :]
    outs = by_distance(refs[at[2] :], count_head, -1)
    _, blocks, tokens, size = owns[0].shape
    shard = lax.axis_index("tm")
    me = lax.axis_index("head")
    sign = sign_matrix()
    for h in range(size // HD):
        lanes = slice(h * HD, (h + 1) * HD)
        query_lanes = slice(start + h * HD, start + (h + 1) * HD)
        query = jnp.concatenate(
            [rows_of(queries[s][0, i, :, query_lanes]) for i in range(blocks) for s in range(count_head)],
            axis=0,
        )

        def gathered(kind):
            pieces = [rows_of(own[kind, :, :, lanes]) for own in owns]
            pieces += [
                rows_of(slots[distance - 1][k, :, kind, :, lanes])
                for distance, k in remote_rows(count_tm)
            ]
            return jnp.concatenate(pieces, axis=0)

        keys, values = gathered(0), gathered(1)
        total = keys.shape[0]
        dots = lax.dot_general(
            query, keys, (((1,), (1,)), ((), ())), preferred_element_type=jnp.float32
        )
        dots = dots.reshape(blocks, BLK, total) + bias_ref[...][:, None, :]
        peak = jnp.max(dots, axis=-1, keepdims=True)
        weights = jnp.exp2((dots - peak) * (SCORE_SCALE * LOG2E))
        denominator = jnp.sum(weights, axis=-1, keepdims=True).reshape(blocks * BLK, 1)
        weights_half = weights.astype(jnp.bfloat16).reshape(blocks * BLK, total)
        mixed = jnp.dot(weights_half, values, preferred_element_type=jnp.float32) / denominator
        turned = jnp.zeros_like(mixed)
        rest = mixed
        for _ in range(3):
            piece = rest.astype(jnp.bfloat16)
            turned = turned + jnp.dot(piece, sign, preferred_element_type=jnp.float32)
            rest = rest - piece.astype(jnp.float32)
        turned = (turned * ROTATE_SCALE).reshape(blocks, count_head, tokens, HD)
        token = lax.broadcasted_iota(jnp.int32, (tokens, HD), 0)
        for s in range(count_head):
            position = lax.rem(me - s + count_head, count_head) * tokens + token
            for i in range(blocks):
                outs[s][i, :, lanes] = jnp.where(
                    position < tokens_ref[shard * blocks + i], turned[i, s], 0.0
                ).astype(jnp.bfloat16)


def attend(block_tokens, bias, start, queries, owns, slots, count_head, count_tm, stacked):
    _, blocks, tokens, size = owns[0].shape[-4:]
    one = (blocks, tokens, size)
    shapes = [(count_head,) + one] if stacked else [one] * count_head
    counts = (count_head, count_tm, len(queries), len(owns), len(slots))
    vmem = pl.BlockSpec(memory_space=pltpu.VMEM)
    return pl.pallas_call(
        functools.partial(attend_kernel, counts, start),
        in_specs=[pl.BlockSpec(memory_space=pltpu.SMEM)]
        + [vmem] * (1 + len(queries) + len(owns) + len(slots)),
        out_specs=[vmem] * len(shapes),
        out_shape=[jax.ShapeDtypeStruct(shape, jnp.bfloat16) for shape in shapes],
        cost_estimate=NO_COST,
        compiler_params=pltpu.CompilerParams(vmem_limit_bytes=VMEM),
    )(block_tokens, bias, *queries, *owns, *slots)


def place_kernel(counts, starts, width_here, *refs):
    count_head = counts[0]
    out_ref, sems = refs[-2:]
    copies = []
    at = 0
    for count, start in zip(counts[1:], starts):
        pieces = by_distance(refs[at : at + count], count_head, 1)
        at += count
        for s, piece in enumerate(pieces):
            column = lax.rem(lax.axis_index("head") + s, count_head) * width_here + start
            copies.append(
                pltpu.make_async_copy(
                    piece,
                    out_ref.at[:, :, pl.ds(pl.multiple_of(column, HD), piece.shape[-1])],
                    sems.at[len(copies)],
                )
            )
            copies[-1].start()
    for copy in copies:
        copy.wait()


def place_pieces(parts, starts, count_head, width_here):
    pieces = [piece for part in parts for piece in part]
    blocks, tokens, _ = pieces[0].shape[-3:]
    counts = (count_head,) + tuple(len(part) for part in parts)
    return pl.pallas_call(
        functools.partial(place_kernel, counts, starts, width_here),
        in_specs=[pl.BlockSpec(memory_space=pl.ANY)] * len(pieces),
        out_specs=pl.BlockSpec(memory_space=pltpu.HBM),
        out_shape=jax.ShapeDtypeStruct((blocks, tokens, count_head * width_here), jnp.bfloat16),
        scratch_shapes=[pltpu.SemaphoreType.DMA((len(parts) * count_head,))],
        compiler_params=pltpu.CompilerParams(vmem_limit_bytes=VMEM),
    )(*pieces)


def shifted(array, axis, distance):
    count = lax.axis_size(axis)
    return lax.ppermute(array, axis, [(i, (i + distance) % count) for i in range(count)])


def exchange(pieces, direction):
    if len(pieces) == 1:
        return [lax.all_to_all(pieces[0], "head", split_axis=0, concat_axis=0, tiled=True)]
    return [pieces[0]] + [
        shifted(piece, "head", direction * s) for s, piece in enumerate(pieces[1:], 1)
    ]


def forward(sent):
    if len(sent) == 1:
        return [lax.all_to_all(sent[0], "tm", split_axis=0, concat_axis=0, tiled=True)]
    return [shifted(block, "tm", distance) for distance, block in enumerate(sent, 1)]


def shards(query_rows, key_rows, value_rows, pair_list, block_tokens):
    count_head = lax.axis_size("head")
    count_tm = lax.axis_size("tm")
    blocks, tokens, width = query_rows.shape
    width_here = width // count_head
    heads = width_here // HD
    cut = (heads + 1) // 2 * HD
    parts = [(0, cut), (cut, width_here - cut)] if heads > 1 else [(0, width_here)]
    sources = [key_rows, value_rows]
    packed = [rotate_pieces(sources, *parts[0], count_head, False, limit=WIDE_VMEM)]
    for part in parts[1:]:
        packed.append(
            rotate_pieces(sources, *part, count_head, False, after=(packed[-1][0],))
        )
    key_values = [exchange(pieces, 1) for pieces in packed]
    picks, bias = plan(pair_list, block_tokens, packed[-1][0], blocks, count_head, count_tm)
    sent = [pick_blocks(picks, key_values[0], count_head, count_tm, True)]
    for owns in key_values[1:]:
        sent.append(
            pick_blocks(
                picks, owns, count_head, count_tm, True, after=(sent[-1][0],), cost=HIGH_COST
            )
        )
    query = rotate_pieces([query_rows], 0, width_here, count_head, False, after=(sent[0][0],))
    queries = exchange(query, 1)
    returned = []
    for (start, _), owns, picked in zip(parts, key_values, sent):
        slots = forward(picked)
        attended = attend(
            block_tokens, bias, start, queries, owns, slots, count_head, count_tm, False
        )
        returned.append(exchange(attended, -1))
    return place_pieces(returned, [start for start, _ in parts], count_head, width_here)


def solution(mesh):
    placed = (
        P(("grp", "tm"), "head", None),
        P(("grp", "tm"), "head", None),
        P(("grp", "tm"), "head", None),
        P("grp", None),
        P("grp"),
    )
    return jax.shard_map(
        shards,
        mesh=mesh,
        in_specs=placed,
        out_specs=P(("grp", "tm"), "head", None),
        check_vma=False,
    )
```

```python
import functools
import math

import jax
import jax.numpy as jnp
from jax import lax
from jax.experimental import pallas as pl
from jax.experimental.pallas import tpu as pltpu
from jax.sharding import PartitionSpec as P

HD = 128
BLK = 64
NEAR_CAP = 2
FAR_CAP = 1
NEG = -1e30
ROTATE_SCALE = 1.0 / math.sqrt(HD)
SCORE_SCALE = 1.0 / math.sqrt(HD)
VMEM = 24 * 1024 * 1024
WIDE_VMEM = 60 * 1024 * 1024
NO_COST = pl.CostEstimate(flops=0, bytes_accessed=0, transcendentals=0)
HIGH_COST = pl.CostEstimate(flops=10**11, bytes_accessed=0, transcendentals=0)
LOG2E = math.log2(math.e)


def sign_matrix():
    common = lax.broadcasted_iota(jnp.int32, (HD, HD), 0) & lax.broadcasted_iota(
        jnp.int32, (HD, HD), 1
    )
    bits = HD.bit_length() - 1
    parity = common
    for bit in range(1, bits):
        parity = parity ^ (common >> bit)
    return jnp.where((parity & 1) == 0, 1.0, -1.0).astype(jnp.bfloat16)


def rows_of(block):
    rows, width = math.prod(block.shape[:-1]), block.shape[-1]
    if block.shape[-2] % 16 == 0:
        return block.reshape(rows, width)
    return block.astype(jnp.float32).reshape(rows, width).astype(block.dtype)


def by_distance(refs, count, direction, axis="head"):
    if len(refs) > 1:
        return list(refs)
    me = lax.axis_index(axis)
    return [refs[0].at[lax.rem(me + direction * s + count, count)] for s in range(count)]


def rotate_kernel(group, count_head, skipped, *refs):
    ids, start, size = group
    count = len(ids)
    sources, outs = refs[:count], by_distance(refs[count + skipped : -2], count_head, 1)
    buffer, sems = refs[-2:]
    blocks, tokens, width = sources[0].shape
    width_here = width // count_head
    me = lax.axis_index("head")
    order = list(range(1, count_head)) + [0]
    copies = {}
    for s in order:
        goal = lax.rem(me + s, count_head)
        column = pl.multiple_of(goal * width_here + start, HD)
        for k, source in enumerate(sources):
            copies[s, k] = pltpu.make_async_copy(
                source.at[:, :, pl.ds(column, size)], buffer.at[s, k], sems.at[s, k]
            )
            copies[s, k].start()
    sign = sign_matrix()
    for s in order:
        for k in range(count):
            copies[s, k].wait()
            flat = rows_of(buffer[s, k])
            heads = [flat[:, at : at + HD] for at in range(0, size, HD)]
            turned = jnp.dot(
                jnp.concatenate(heads, axis=0), sign, preferred_element_type=jnp.float32
            )
            turned = (turned * ROTATE_SCALE).reshape(size // HD, blocks, tokens, HD)
            for h in range(size // HD):
                outs[s][k, :, :, h * HD : (h + 1) * HD] = turned[h].astype(jnp.bfloat16)


def rotate_pieces(sources, start, size, count_head, stacked, after=(), limit=VMEM):
    blocks, tokens, _ = sources[0].shape
    count = len(sources)
    one = (count, blocks, tokens, size)
    shapes = [(count_head,) + one] if stacked else [one] * count_head
    return pl.pallas_call(
        functools.partial(
            rotate_kernel, (tuple(range(count)), start, size), count_head, len(after)
        ),
        in_specs=[pl.BlockSpec(memory_space=pltpu.HBM)] * count
        + [pl.BlockSpec(memory_space=pl.ANY)] * len(after),
        out_specs=[pl.BlockSpec(memory_space=pltpu.VMEM)] * len(shapes),
        out_shape=[jax.ShapeDtypeStruct(shape, jnp.bfloat16) for shape in shapes],
        scratch_shapes=[
            pltpu.VMEM((count_head,) + one, jnp.bfloat16),
            pltpu.SemaphoreType.DMA((count_head, count)),
        ],
        cost_estimate=NO_COST,
        compiler_params=pltpu.CompilerParams(vmem_limit_bytes=limit),
    )(*sources, *after)


def slots_at(distance, count_tm):
    return NEAR_CAP if distance in (1, count_tm - 1) else FAR_CAP


def pick_kernel(count_head, count_tm, own_count, skipped, picks_ref, *refs):
    pieces = by_distance(refs[:own_count], count_head, -1)
    outs = by_distance(refs[own_count + skipped :], count_tm, 1, "tm")[-(count_tm - 1) :]
    shard = lax.axis_index("tm")
    for distance, out in enumerate(outs, 1):
        goal = lax.rem(shard + distance, count_tm)
        for k in range(slots_at(distance, count_tm)):
            pick = picks_ref[NEAR_CAP * goal + k]
            for s in range(count_head):
                out[k, s] = pieces[s][:, pick]


def pick_blocks(picks, owns, count_head, count_tm, stacked, after=(), cost=NO_COST):
    kinds, _, tokens, width = owns[0].shape[-4:]
    one = (count_head, kinds, tokens, width)
    if stacked:
        shapes = [(count_tm, NEAR_CAP) + one]
    else:
        shapes = [(slots_at(distance, count_tm),) + one for distance in range(1, count_tm)]
    vmem = pl.BlockSpec(memory_space=pltpu.VMEM)
    return pl.pallas_call(
        functools.partial(pick_kernel, count_head, count_tm, len(owns), len(after)),
        in_specs=[pl.BlockSpec(memory_space=pltpu.SMEM)]
        + [vmem] * len(owns)
        + [pl.BlockSpec(memory_space=pl.ANY)] * len(after),
        out_specs=[vmem] * len(shapes),
        out_shape=[jax.ShapeDtypeStruct(shape, jnp.bfloat16) for shape in shapes],
        cost_estimate=cost,
        compiler_params=pltpu.CompilerParams(vmem_limit_bytes=VMEM),
    )(picks, *owns, *after)


def remote_rows(count_tm):
    return [
        (distance, k)
        for distance in range(1, count_tm)
        for k in range(slots_at(distance, count_tm))
    ]


def plan_kernel(count_head, count_tm, blocks, pair_ref, tokens_ref, _, picks_ref, bias_ref, named_ref, table_ref, sem):
    total_blocks, columns = pair_ref.shape
    pairs = pair_ref[...]
    lane = lax.broadcasted_iota(jnp.int32, named_ref.shape, 1)
    named = jnp.zeros(named_ref.shape, jnp.int32)
    for c in range(columns):
        named = jnp.where(pairs[:, c : c + 1] == lane, 1, named)
    named_ref[...] = named
    copy = pltpu.make_async_copy(named_ref, table_ref, sem)
    copy.start()
    copy.wait()
    shard = lax.axis_index("tm")
    place = lax.axis_index("head")
    mine = shard * blocks

    def two_picks(wanted):
        picks = [jnp.int32(0)] * NEAR_CAP
        count = jnp.int32(0)
        for j in range(blocks):
            for k in range(NEAR_CAP):
                picks[k] = jnp.where((wanted[j] > 0) & (count == k), j, picks[k])
            count = count + wanted[j]
        return picks, count

    def named_by(rows, column):
        found = table_ref[rows, column]
        for i in range(1, blocks):
            found = found | table_ref[rows + i, column]
        return found

    for d in range(count_tm):
        picks, _ = two_picks([named_by(d * blocks, mine + j) for j in range(blocks)])
        for k in range(NEAR_CAP):
            picks_ref[NEAR_CAP * d + k] = picks[k]

    kept = [[table_ref[mine + i, mine + j] * tokens_ref[mine + j] for j in range(blocks)] for i in range(blocks)]
    arrivals = {}
    for distance, k in remote_rows(count_tm):
        first = lax.rem(shard - distance + count_tm, count_tm) * blocks
        if k == 0:
            arrivals[distance] = two_picks([named_by(mine, first + j) for j in range(blocks)])
        picks, count = arrivals[distance]
        there = first + picks[k]
        live = jnp.where(count > k, tokens_ref[there], 0)
        for i in range(blocks):
            kept[i].append(table_ref[mine + i, there] * live)

    total = bias_ref.shape[1]
    piece_rows = BLK // count_head
    at = lax.broadcasted_iota(jnp.int32, (blocks, total), 1)
    query = lax.broadcasted_iota(jnp.int32, (blocks, total), 0)
    own = at < blocks * BLK
    row = jnp.where(own, lax.rem(lax.div(at, piece_rows), blocks), lax.div(at, BLK))
    piece = jnp.where(own, lax.div(at, blocks * piece_rows), lax.div(lax.rem(at, BLK), piece_rows))
    source = lax.rem(place - piece + count_head, count_head)
    position = source * piece_rows + lax.rem(at, piece_rows)
    limit = jnp.zeros((blocks, total), jnp.int32)
    for r in range(len(kept[0])):
        value = jnp.zeros((blocks, total), jnp.int32)
        for i in range(blocks):
            value = jnp.where(query == i, kept[i][r], value)
        limit = jnp.where(row == r, value, limit)
    bias_ref[...] = jnp.where(position < limit, 0.0, NEG)


def plan(pair_list, block_tokens, after, blocks, count_head, count_tm):
    total_blocks = pair_list.shape[0]
    lanes = -(-total_blocks // 128) * 128
    total = (blocks + len(remote_rows(count_tm))) * BLK
    return pl.pallas_call(
        functools.partial(plan_kernel, count_head, count_tm, blocks),
        in_specs=[
            pl.BlockSpec(memory_space=pltpu.VMEM),
            pl.BlockSpec(memory_space=pltpu.SMEM),
            pl.BlockSpec(memory_space=pl.ANY),
        ],
        out_specs=[pl.BlockSpec(memory_space=pltpu.SMEM), pl.BlockSpec(memory_space=pltpu.VMEM)],
        out_shape=[
            jax.ShapeDtypeStruct((NEAR_CAP * count_tm,), jnp.int32),
            jax.ShapeDtypeStruct((blocks, total), jnp.float32),
        ],
        scratch_shapes=[
            pltpu.VMEM((total_blocks, lanes), jnp.int32),
            pltpu.SMEM((total_blocks, lanes), jnp.int32),
            pltpu.SemaphoreType.DMA,
        ],
        cost_estimate=NO_COST,
        compiler_params=pltpu.CompilerParams(vmem_limit_bytes=VMEM),
    )(pair_list, block_tokens, after)


def attend_kernel(counts, start, tokens_ref, bias_ref, *refs):
    count_head, count_tm, query_count, own_count, slot_count, skipped = counts
    at = [query_count, query_count + own_count, query_count + own_count + slot_count]
    queries = by_distance(refs[: at[0]], count_head, -1)
    owns = by_distance(refs[at[0] : at[1]], count_head, -1)
    slots = by_distance(refs[at[1] : at[2]], count_tm, -1, "tm")[-(count_tm - 1) :]
    outs = by_distance(refs[at[2] + skipped :], count_head, -1)
    _, blocks, tokens, size = owns[0].shape
    shard = lax.axis_index("tm")
    me = lax.axis_index("head")
    sign = sign_matrix()
    for h in range(size // HD):
        lanes = slice(h * HD, (h + 1) * HD)
        query_lanes = slice(start + h * HD, start + (h + 1) * HD)
        query = jnp.concatenate(
            [rows_of(queries[s][0, i, :, query_lanes]) for i in range(blocks) for s in range(count_head)],
            axis=0,
        )

        def gathered(kind):
            pieces = [rows_of(own[kind, :, :, lanes]) for own in owns]
            pieces += [
                rows_of(slots[distance - 1][k, :, kind, :, lanes])
                for distance, k in remote_rows(count_tm)
            ]
            return jnp.concatenate(pieces, axis=0)

        keys, values = gathered(0), gathered(1)
        total = keys.shape[0]
        dots = lax.dot_general(
            query, keys, (((1,), (1,)), ((), ())), preferred_element_type=jnp.float32
        )
        dots = dots.reshape(blocks, BLK, total) + bias_ref[...][:, None, :]
        peak = jnp.max(dots, axis=-1, keepdims=True)
        weights = jnp.exp2((dots - peak) * (SCORE_SCALE * LOG2E))
        denominator = jnp.sum(weights, axis=-1, keepdims=True).reshape(blocks * BLK, 1)
        weights_half = weights.astype(jnp.bfloat16).reshape(blocks * BLK, total)
        mixed = jnp.dot(weights_half, values, preferred_element_type=jnp.float32) / denominator
        turned = jnp.zeros_like(mixed)
        rest = mixed
        for _ in range(3):
            piece = rest.astype(jnp.bfloat16)
            turned = turned + jnp.dot(piece, sign, preferred_element_type=jnp.float32)
            rest = rest - piece.astype(jnp.float32)
        turned = (turned * ROTATE_SCALE).reshape(blocks, count_head, tokens, HD)
        token = lax.broadcasted_iota(jnp.int32, (tokens, HD), 0)
        for s in range(count_head):
            position = lax.rem(me - s + count_head, count_head) * tokens + token
            for i in range(blocks):
                outs[s][i, :, lanes] = jnp.where(
                    position < tokens_ref[shard * blocks + i], turned[i, s], 0.0
                ).astype(jnp.bfloat16)


def attend(block_tokens, bias, start, queries, owns, slots, count_head, count_tm, after, cost):
    _, blocks, tokens, size = owns[0].shape[-4:]
    shapes = [(blocks, tokens, size)] * count_head
    counts = (count_head, count_tm, len(queries), len(owns), len(slots), len(after))
    vmem = pl.BlockSpec(memory_space=pltpu.VMEM)
    return pl.pallas_call(
        functools.partial(attend_kernel, counts, start),
        in_specs=[pl.BlockSpec(memory_space=pltpu.SMEM)]
        + [vmem] * (1 + len(queries) + len(owns) + len(slots))
        + [pl.BlockSpec(memory_space=pl.ANY)] * len(after),
        out_specs=[vmem] * len(shapes),
        out_shape=[jax.ShapeDtypeStruct(shape, jnp.bfloat16) for shape in shapes],
        cost_estimate=cost,
        compiler_params=pltpu.CompilerParams(vmem_limit_bytes=VMEM),
    )(block_tokens, bias, *queries, *owns, *slots, *after)


def place_kernel(counts, starts, width_here, *refs):
    count_head = counts[0]
    out_ref, sems = refs[-2:]
    copies = []
    at = 0
    for count, start in zip(counts[1:], starts):
        pieces = by_distance(refs[at : at + count], count_head, 1)
        at += count
        for s, piece in enumerate(pieces):
            column = lax.rem(lax.axis_index("head") + s, count_head) * width_here + start
            copies.append(
                pltpu.make_async_copy(
                    piece,
                    out_ref.at[:, :, pl.ds(pl.multiple_of(column, HD), piece.shape[-1])],
                    sems.at[len(copies)],
                )
            )
            copies[-1].start()
    for copy in copies:
        copy.wait()


def place_pieces(parts, starts, count_head, width_here):
    pieces = [piece for part in parts for piece in part]
    blocks, tokens, _ = pieces[0].shape[-3:]
    counts = (count_head,) + tuple(len(part) for part in parts)
    return pl.pallas_call(
        functools.partial(place_kernel, counts, starts, width_here),
        in_specs=[pl.BlockSpec(memory_space=pl.ANY)] * len(pieces),
        out_specs=pl.BlockSpec(memory_space=pltpu.HBM),
        out_shape=jax.ShapeDtypeStruct((blocks, tokens, count_head * width_here), jnp.bfloat16),
        scratch_shapes=[pltpu.SemaphoreType.DMA((len(parts) * count_head,))],
        compiler_params=pltpu.CompilerParams(vmem_limit_bytes=VMEM),
    )(*pieces)


def shifted(array, axis, distance):
    count = lax.axis_size(axis)
    return lax.ppermute(array, axis, [(i, (i + distance) % count) for i in range(count)])


def exchange(pieces, direction):
    if len(pieces) == 1:
        return [lax.all_to_all(pieces[0], "head", split_axis=0, concat_axis=0, tiled=True)]
    return [pieces[0]] + [
        shifted(piece, "head", direction * s) for s, piece in enumerate(pieces[1:], 1)
    ]


def forward(sent):
    if len(sent) == 1:
        return [lax.all_to_all(sent[0], "tm", split_axis=0, concat_axis=0, tiled=True)]
    return [shifted(block, "tm", distance) for distance, block in enumerate(sent, 1)]


def shards(query_rows, key_rows, value_rows, pair_list, block_tokens):
    count_head = lax.axis_size("head")
    count_tm = lax.axis_size("tm")
    blocks, tokens, width = query_rows.shape
    width_here = width // count_head
    heads = width_here // HD
    cut = (heads + 1) // 2 * HD
    parts = [(0, cut), (cut, width_here - cut)] if heads > 1 else [(0, width_here)]
    sources = [key_rows, value_rows]
    packed = [rotate_pieces(sources, *parts[0], count_head, False, limit=WIDE_VMEM)]
    for part in parts[1:]:
        packed.append(
            rotate_pieces(sources, *part, count_head, False, after=(packed[-1][0],))
        )
    key_values = [exchange(pieces, 1) for pieces in packed]
    picks, bias = plan(pair_list, block_tokens, packed[-1][0], blocks, count_head, count_tm)
    sent = [pick_blocks(picks, key_values[0], count_head, count_tm, True)]
    for owns in key_values[1:]:
        sent.append(
            pick_blocks(
                picks, owns, count_head, count_tm, True, after=(sent[-1][0],), cost=HIGH_COST
            )
        )
    query = rotate_pieces([query_rows], 0, width_here, count_head, False, after=(sent[0][0],))
    queries = exchange(query, 1)
    returned, after = [], ()
    for at, (owns, picked) in enumerate(zip(key_values, sent)):
        cost = NO_COST if at == len(parts) - 1 else HIGH_COST
        slots, start = forward(picked), parts[at][0]
        attended = attend(
            block_tokens, bias, start, queries, owns, slots, count_head, count_tm, after, cost
        )
        after = (attended[0],)
        returned.append(exchange(attended, -1))
    return place_pieces(returned, [start for start, _ in parts], count_head, width_here)


def solution(mesh):
    placed = (
        P(("grp", "tm"), "head", None),
        P(("grp", "tm"), "head", None),
        P(("grp", "tm"), "head", None),
        P("grp", None),
        P("grp"),
    )
    return jax.shard_map(
        shards,
        mesh=mesh,
        in_specs=placed,
        out_specs=P(("grp", "tm"), "head", None),
        check_vma=False,
    )
```

```python
import functools
import math

import jax
import jax.numpy as jnp
from jax import lax
from jax.experimental import pallas as pl
from jax.experimental.pallas import tpu as pltpu
from jax.sharding import PartitionSpec as P

HD = 128
BLK = 64
NEAR_CAP = 2
FAR_CAP = 1
NEG = -1e30
ROTATE_SCALE = 1.0 / math.sqrt(HD)
SCORE_SCALE = 1.0 / math.sqrt(HD)
VMEM = 24 * 1024 * 1024
WIDE_VMEM = 60 * 1024 * 1024
TOKEN = jax.ShapeDtypeStruct((1,), jnp.int32)
TOKEN_SPEC = pl.BlockSpec(memory_space=pltpu.SMEM)
NO_COST = pl.CostEstimate(flops=0, bytes_accessed=0, transcendentals=0)
HIGH_COST = pl.CostEstimate(flops=10**11, bytes_accessed=0, transcendentals=0)
LOG2E = math.log2(math.e)


def sign_matrix():
    common = lax.broadcasted_iota(jnp.int32, (HD, HD), 0) & lax.broadcasted_iota(
        jnp.int32, (HD, HD), 1
    )
    bits = HD.bit_length() - 1
    parity = common
    for bit in range(1, bits):
        parity = parity ^ (common >> bit)
    return jnp.where((parity & 1) == 0, 1.0, -1.0).astype(jnp.bfloat16)


def rows_of(block):
    rows, width = math.prod(block.shape[:-1]), block.shape[-1]
    if block.shape[-2] % 16 == 0:
        return block.reshape(rows, width)
    return block.astype(jnp.float32).reshape(rows, width).astype(block.dtype)


def by_distance(refs, count, direction, axis="head"):
    if len(refs) > 1:
        return list(refs)
    me = lax.axis_index(axis)
    return [refs[0].at[lax.rem(me + direction * s + count, count)] for s in range(count)]


def rotate_kernel(group, count_head, skipped, *refs):
    ids, start, size = group
    count = len(ids)
    sources, outs = refs[:count], by_distance(refs[count + skipped : -3], count_head, 1)
    token, buffer, sems = refs[-3:]
    token[0] = 0
    blocks, tokens, width = sources[0].shape
    width_here = width // count_head
    me = lax.axis_index("head")
    order = list(range(1, count_head)) + [0]
    copies = {}
    for s in order:
        goal = lax.rem(me + s, count_head)
        column = pl.multiple_of(goal * width_here + start, HD)
        for k, source in enumerate(sources):
            copies[s, k] = pltpu.make_async_copy(
                source.at[:, :, pl.ds(column, size)], buffer.at[s, k], sems.at[s, k]
            )
            copies[s, k].start()
    sign = sign_matrix()
    for s in order:
        for k in range(count):
            copies[s, k].wait()
            flat = rows_of(buffer[s, k])
            heads = [flat[:, at : at + HD] for at in range(0, size, HD)]
            turned = jnp.dot(
                jnp.concatenate(heads, axis=0), sign, preferred_element_type=jnp.float32
            )
            turned = (turned * ROTATE_SCALE).reshape(size // HD, blocks, tokens, HD)
            for h in range(size // HD):
                outs[s][k, :, :, h * HD : (h + 1) * HD] = turned[h].astype(jnp.bfloat16)


def rotate_pieces(sources, start, size, count_head, stacked, after=(), limit=VMEM):
    blocks, tokens, _ = sources[0].shape
    count = len(sources)
    one = (count, blocks, tokens, size)
    shapes = [(count_head,) + one] if stacked else [one] * count_head
    *pieces, token = pl.pallas_call(
        functools.partial(
            rotate_kernel, (tuple(range(count)), start, size), count_head, len(after)
        ),
        in_specs=[pl.BlockSpec(memory_space=pltpu.HBM)] * count
        + [TOKEN_SPEC] * len(after),
        out_specs=[pl.BlockSpec(memory_space=pltpu.VMEM)] * len(shapes) + [TOKEN_SPEC],
        out_shape=[jax.ShapeDtypeStruct(shape, jnp.bfloat16) for shape in shapes] + [TOKEN],
        scratch_shapes=[
            pltpu.VMEM((count_head,) + one, jnp.bfloat16),
            pltpu.SemaphoreType.DMA((count_head, count)),
        ],
        cost_estimate=NO_COST,
        compiler_params=pltpu.CompilerParams(vmem_limit_bytes=limit),
    )(*sources, *after)
    return pieces, token


def pick_kernel(count_head, count_tm, own_count, skipped, picks_ref, *refs):
    pieces = by_distance(refs[:own_count], count_head, -1)
    first_ref, next_ref, prev_ref, token = refs[own_count + skipped :]
    shard = lax.axis_index("tm")
    token[0] = 0
    upward = jnp.minimum(shard + 1, count_tm - 1)
    downward = jnp.maximum(shard - 1, 0)
    for s in range(count_head):
        for goal in range(count_tm):
            first_ref[goal, s] = pieces[s][:, picks_ref[NEAR_CAP * goal]]
        next_ref[s] = pieces[s][:, picks_ref[NEAR_CAP * upward + 1]]
        prev_ref[s] = pieces[s][:, picks_ref[NEAR_CAP * downward + 1]]


def pick_blocks(picks, owns, count_head, count_tm, after=(), cost=NO_COST):
    kinds, _, tokens, width = owns[0].shape[-4:]
    one = (count_head, kinds, tokens, width)
    shapes = [(count_tm,) + one, one, one]
    vmem = pl.BlockSpec(memory_space=pltpu.VMEM)
    *sent, token = pl.pallas_call(
        functools.partial(pick_kernel, count_head, count_tm, len(owns), len(after)),
        in_specs=[pl.BlockSpec(memory_space=pltpu.SMEM)]
        + [vmem] * len(owns)
        + [TOKEN_SPEC] * len(after),
        out_specs=[vmem] * len(shapes) + [TOKEN_SPEC],
        out_shape=[jax.ShapeDtypeStruct(shape, jnp.bfloat16) for shape in shapes] + [TOKEN],
        cost_estimate=cost,
        compiler_params=pltpu.CompilerParams(vmem_limit_bytes=VMEM),
    )(picks, *owns, *after)
    return sent, token


def remote_rows(count_tm):
    return [(distance, 0) for distance in range(1, count_tm)] + [(1, 1), (-1, 1)]


def split(value, by):
    if by & (by - 1) == 0:
        return value >> (by.bit_length() - 1), value & (by - 1)
    return lax.div(value, by), lax.rem(value, by)


def plan_kernel(count_head, count_tm, blocks, pair_ref, tokens_ref, _, picks_ref, bias_ref, named_ref, table_ref, sem):
    total_blocks, columns = pair_ref.shape
    pairs = pair_ref[...]
    lane = lax.broadcasted_iota(jnp.int32, named_ref.shape, 1)
    named = jnp.zeros(named_ref.shape, jnp.int32)
    for c in range(columns):
        named = jnp.where(pairs[:, c : c + 1] == lane, 1, named)
    named_ref[...] = named
    copy = pltpu.make_async_copy(named_ref, table_ref, sem)
    copy.start()
    copy.wait()
    shard = lax.axis_index("tm")
    place = lax.axis_index("head")
    mine = shard * blocks

    def two_picks(wanted):
        picks = [jnp.int32(0)] * NEAR_CAP
        count = jnp.int32(0)
        for j in range(blocks):
            for k in range(NEAR_CAP):
                picks[k] = jnp.where((wanted[j] > 0) & (count == k), j, picks[k])
            count = count + wanted[j]
        return picks, count

    def named_by(rows, column):
        found = table_ref[rows, column]
        for i in range(1, blocks):
            found = found | table_ref[rows + i, column]
        return found

    for d in range(count_tm):
        picks, _ = two_picks([named_by(d * blocks, mine + j) for j in range(blocks)])
        for k in range(NEAR_CAP):
            picks_ref[NEAR_CAP * d + k] = picks[k]

    kept = [[table_ref[mine + i, mine + j] * tokens_ref[mine + j] for j in range(blocks)] for i in range(blocks)]
    arrivals = {}
    for distance, k in remote_rows(count_tm):
        sender = lax.rem(shard - distance + count_tm, count_tm)
        if k == 0:
            arrivals[distance] = two_picks([named_by(mine, sender * blocks + j) for j in range(blocks)])
        picks, count = arrivals[distance % count_tm]
        there = sender * blocks + picks[k]
        valid = count > k
        if k > 0:
            valid = valid & (sender == shard - distance)
        live = jnp.where(valid, tokens_ref[there], 0)
        for i in range(blocks):
            kept[i].append(table_ref[mine + i, there] * live)

    total = bias_ref.shape[1]
    piece_rows = BLK // count_head
    at = lax.broadcasted_iota(jnp.int32, (blocks, total), 1)
    query = lax.broadcasted_iota(jnp.int32, (blocks, total), 0)
    own = at < blocks * BLK
    group, token = split(at, piece_rows)
    own_piece, own_block = split(group, blocks)
    far_row, far_group = split(group, count_head)
    row = jnp.where(own, own_block, far_row)
    piece = jnp.where(own, own_piece, far_group)
    source = jnp.where(piece > place, place - piece + count_head, place - piece)
    position = source * piece_rows + token
    limit = jnp.zeros((blocks, total), jnp.int32)
    for r in range(len(kept[0])):
        value = jnp.zeros((blocks, total), jnp.int32)
        for i in range(blocks):
            value = jnp.where(query == i, kept[i][r], value)
        limit = jnp.where(row == r, value, limit)
    bias_ref[...] = jnp.where(position < limit, 0.0, NEG)


def plan(pair_list, block_tokens, after, blocks, count_head, count_tm):
    total_blocks = pair_list.shape[0]
    lanes = -(-total_blocks // 128) * 128
    total = (blocks + len(remote_rows(count_tm))) * BLK
    return pl.pallas_call(
        functools.partial(plan_kernel, count_head, count_tm, blocks),
        in_specs=[
            pl.BlockSpec(memory_space=pltpu.VMEM),
            pl.BlockSpec(memory_space=pltpu.SMEM),
            TOKEN_SPEC,
        ],
        out_specs=[pl.BlockSpec(memory_space=pltpu.SMEM), pl.BlockSpec(memory_space=pltpu.VMEM)],
        out_shape=[
            jax.ShapeDtypeStruct((NEAR_CAP * count_tm,), jnp.int32),
            jax.ShapeDtypeStruct((blocks, total), jnp.float32),
        ],
        scratch_shapes=[
            pltpu.VMEM((total_blocks, lanes), jnp.int32),
            pltpu.SMEM((total_blocks, lanes), jnp.int32),
            pltpu.SemaphoreType.DMA,
        ],
        cost_estimate=NO_COST,
        compiler_params=pltpu.CompilerParams(vmem_limit_bytes=VMEM),
    )(pair_list, block_tokens, after)


def attend_kernel(counts, start, tokens_ref, bias_ref, *refs):
    count_head, count_tm, query_count, own_count, skipped = counts
    at = [query_count, query_count + own_count]
    queries = by_distance(refs[: at[0]], count_head, -1)
    owns = by_distance(refs[at[0] : at[1]], count_head, -1)
    first_ref, before_ref, after_ref = refs[at[1] : at[1] + 3]
    outs = by_distance(refs[at[1] + 3 + skipped : -1], count_head, -1)
    refs[-1][0] = 0
    _, blocks, tokens, size = owns[0].shape
    shard = lax.axis_index("tm")
    me = lax.axis_index("head")
    sign = sign_matrix()
    for h in range(size // HD):
        lanes = slice(h * HD, (h + 1) * HD)
        query_lanes = slice(start + h * HD, start + (h + 1) * HD)
        query = jnp.concatenate(
            [rows_of(queries[s][0, i, :, query_lanes]) for i in range(blocks) for s in range(count_head)],
            axis=0,
        )

        def gathered(kind):
            pieces = [rows_of(own[kind, :, :, lanes]) for own in owns]
            pieces += [
                rows_of(first_ref[lax.rem(shard - d + count_tm, count_tm), :, kind, :, lanes])
                for d, k in remote_rows(count_tm)
                if k == 0
            ]
            pieces += [rows_of(ref[:, kind, :, lanes]) for ref in (before_ref, after_ref)]
            return jnp.concatenate(pieces, axis=0)

        keys, values = gathered(0), gathered(1)
        total = keys.shape[0]
        dots = lax.dot_general(
            query, keys, (((1,), (1,)), ((), ())), preferred_element_type=jnp.float32
        )
        dots = dots.reshape(blocks, BLK, total) + bias_ref[...][:, None, :]
        peak = jnp.max(dots, axis=-1, keepdims=True)
        weights = jnp.exp2((dots - peak) * (SCORE_SCALE * LOG2E))
        denominator = jnp.sum(weights, axis=-1, keepdims=True).reshape(blocks * BLK, 1)
        weights_half = weights.astype(jnp.bfloat16).reshape(blocks * BLK, total)
        mixed = jnp.dot(weights_half, values, preferred_element_type=jnp.float32) / denominator
        turned = jnp.zeros_like(mixed)
        rest = mixed
        for _ in range(3):
            piece = rest.astype(jnp.bfloat16)
            turned = turned + jnp.dot(piece, sign, preferred_element_type=jnp.float32)
            rest = rest - piece.astype(jnp.float32)
        turned = (turned * ROTATE_SCALE).reshape(blocks, count_head, tokens, HD)
        token = lax.broadcasted_iota(jnp.int32, (tokens, HD), 0)
        for s in range(count_head):
            position = lax.rem(me - s + count_head, count_head) * tokens + token
            for i in range(blocks):
                outs[s][i, :, lanes] = jnp.where(
                    position < tokens_ref[shard * blocks + i], turned[i, s], 0.0
                ).astype(jnp.bfloat16)


def attend(block_tokens, bias, start, queries, owns, slots, count_head, count_tm, after, cost):
    _, blocks, tokens, size = owns[0].shape[-4:]
    shapes = [(blocks, tokens, size)] * count_head
    counts = (count_head, count_tm, len(queries), len(owns), len(after))
    vmem = pl.BlockSpec(memory_space=pltpu.VMEM)
    *attended, token = pl.pallas_call(
        functools.partial(attend_kernel, counts, start),
        in_specs=[pl.BlockSpec(memory_space=pltpu.SMEM)]
        + [vmem] * (1 + len(queries) + len(owns) + len(slots))
        + [TOKEN_SPEC] * len(after),
        out_specs=[vmem] * len(shapes) + [TOKEN_SPEC],
        out_shape=[jax.ShapeDtypeStruct(shape, jnp.bfloat16) for shape in shapes] + [TOKEN],
        cost_estimate=cost,
        compiler_params=pltpu.CompilerParams(vmem_limit_bytes=VMEM),
    )(block_tokens, bias, *queries, *owns, *slots, *after)
    return attended, token


def place_kernel(counts, starts, width_here, *refs):
    count_head = counts[0]
    out_ref, sems = refs[-2:]
    copies = []
    at = 0
    for count, start in zip(counts[1:], starts):
        pieces = by_distance(refs[at : at + count], count_head, 1)
        at += count
        for s, piece in enumerate(pieces):
            column = lax.rem(lax.axis_index("head") + s, count_head) * width_here + start
            copies.append(
                pltpu.make_async_copy(
                    piece,
                    out_ref.at[:, :, pl.ds(pl.multiple_of(column, HD), piece.shape[-1])],
                    sems.at[len(copies)],
                )
            )
            copies[-1].start()
    for copy in copies:
        copy.wait()


def place_pieces(parts, starts, count_head, width_here):
    pieces = [piece for part in parts for piece in part]
    blocks, tokens, _ = pieces[0].shape[-3:]
    counts = (count_head,) + tuple(len(part) for part in parts)
    return pl.pallas_call(
        functools.partial(place_kernel, counts, starts, width_here),
        in_specs=[pl.BlockSpec(memory_space=pl.ANY)] * len(pieces),
        out_specs=pl.BlockSpec(memory_space=pltpu.HBM),
        out_shape=jax.ShapeDtypeStruct((blocks, tokens, count_head * width_here), jnp.bfloat16),
        scratch_shapes=[pltpu.SemaphoreType.DMA((len(parts) * count_head,))],
        compiler_params=pltpu.CompilerParams(vmem_limit_bytes=VMEM),
    )(*pieces)


def shifted(array, axis, distance):
    count = lax.axis_size(axis)
    return lax.ppermute(array, axis, [(i, (i + distance) % count) for i in range(count)])


def exchange(pieces, direction):
    if len(pieces) == 1:
        return [lax.all_to_all(pieces[0], "head", split_axis=0, concat_axis=0, tiled=True)]
    return [pieces[0]] + [
        shifted(piece, "head", direction * s) for s, piece in enumerate(pieces[1:], 1)
    ]


def forward(sent):
    first, to_next, to_prev = sent
    count = lax.axis_size("tm")
    upward = [(i, i + 1) for i in range(count - 1)]
    downward = [(i + 1, i) for i in range(count - 1)]
    return (
        lax.all_to_all(first, "tm", split_axis=0, concat_axis=0, tiled=True),
        lax.ppermute(to_next, "tm", upward),
        lax.ppermute(to_prev, "tm", downward),
    )


def shards(query_rows, key_rows, value_rows, pair_list, block_tokens):
    count_head = lax.axis_size("head")
    count_tm = lax.axis_size("tm")
    blocks, tokens, width = query_rows.shape
    width_here = width // count_head
    heads = width_here // HD
    cut = (heads + 1) // 2 * HD
    parts = [(0, cut), (cut, width_here - cut)] if heads > 1 else [(0, width_here)]
    sources = [key_rows, value_rows]
    packed, after, limit = [], (), WIDE_VMEM
    for start, size in parts:
        pieces, token = rotate_pieces(sources, start, size, count_head, False, after, limit)
        packed.append(pieces)
        after, limit = (token,), VMEM
    key_values = [exchange(pieces, 1) for pieces in packed]
    picks, bias = plan(pair_list, block_tokens, token, blocks, count_head, count_tm)
    sent, after, cost = [], (), NO_COST
    for owns in key_values:
        picked, token = pick_blocks(picks, owns, count_head, count_tm, after, cost)
        sent.append(picked)
        if not after:
            query, _ = rotate_pieces([query_rows], 0, width_here, count_head, False, (token,))
        after, cost = (token,), HIGH_COST
    queries = exchange(query, 1)
    returned, after = [], ()
    for at, (owns, picked) in enumerate(zip(key_values, sent)):
        cost = NO_COST if at == len(parts) - 1 else HIGH_COST
        slots, start = forward(picked), parts[at][0]
        attended, token = attend(
            block_tokens, bias, start, queries, owns, slots, count_head, count_tm, after, cost
        )
        after = (token,)
        returned.append(exchange(attended, -1))
    return place_pieces(returned, [start for start, _ in parts], count_head, width_here)


def solution(mesh):
    placed = (
        P(("grp", "tm"), "head", None),
        P(("grp", "tm"), "head", None),
        P(("grp", "tm"), "head", None),
        P("grp", None),
        P("grp"),
    )
    return jax.shard_map(
        shards,
        mesh=mesh,
        in_specs=placed,
        out_specs=P(("grp", "tm"), "head", None),
        check_vma=False,
    )
```

```python
import functools
import math

import jax
import jax.numpy as jnp
from jax import lax
from jax.experimental import pallas as pl
from jax.experimental.pallas import tpu as pltpu
from jax.sharding import PartitionSpec as P

HD = 128
BLK = 64
NEAR_CAP = 2
FAR_CAP = 1
NEG = -1e30
ROTATE_SCALE = 1.0 / math.sqrt(HD)
SCORE_SCALE = 1.0 / math.sqrt(HD)
VMEM = 24 * 1024 * 1024
WIDE_VMEM = 60 * 1024 * 1024
TOKEN = jax.ShapeDtypeStruct((8, 128), jnp.float32)
NO_COST = pl.CostEstimate(flops=0, bytes_accessed=0, transcendentals=0)
HIGH_COST = pl.CostEstimate(flops=10**11, bytes_accessed=0, transcendentals=0)
LOG2E = math.log2(math.e)


def sign_matrix():
    common = lax.broadcasted_iota(jnp.int32, (HD, HD), 0) & lax.broadcasted_iota(
        jnp.int32, (HD, HD), 1
    )
    bits = HD.bit_length() - 1
    parity = common
    for bit in range(1, bits):
        parity = parity ^ (common >> bit)
    return jnp.where((parity & 1) == 0, 1.0, -1.0).astype(jnp.bfloat16)


def rows_of(block):
    rows, width = math.prod(block.shape[:-1]), block.shape[-1]
    if block.shape[-2] % 16 == 0:
        return block.reshape(rows, width)
    return block.astype(jnp.float32).reshape(rows, width).astype(block.dtype)


def by_distance(refs, count, direction, axis="head"):
    if len(refs) > 1:
        return list(refs)
    me = lax.axis_index(axis)
    return [refs[0].at[lax.rem(me + direction * s + count, count)] for s in range(count)]


def rotate_kernel(group, count_head, skipped, *refs):
    ids, start, size = group
    count = len(ids)
    sources, outs = refs[:count], by_distance(refs[count + skipped : -3], count_head, 1)
    token, buffer, sems = refs[-3:]
    token[...] = jnp.zeros_like(token)
    blocks, tokens, width = sources[0].shape
    width_here = width // count_head
    me = lax.axis_index("head")
    order = list(range(1, count_head)) + [0]
    copies = {}
    for s in order:
        goal = lax.rem(me + s, count_head)
        column = pl.multiple_of(goal * width_here + start, HD)
        for k, source in enumerate(sources):
            copies[s, k] = pltpu.make_async_copy(
                source.at[:, :, pl.ds(column, size)], buffer.at[s, k], sems.at[s, k]
            )
            copies[s, k].start()
    sign = sign_matrix()
    for s in order:
        for k in range(count):
            copies[s, k].wait()
            flat = rows_of(buffer[s, k])
            heads = [flat[:, at : at + HD] for at in range(0, size, HD)]
            turned = jnp.dot(
                jnp.concatenate(heads, axis=0), sign, preferred_element_type=jnp.float32
            )
            turned = (turned * ROTATE_SCALE).reshape(size // HD, blocks, tokens, HD)
            for h in range(size // HD):
                outs[s][k, :, :, h * HD : (h + 1) * HD] = turned[h].astype(jnp.bfloat16)


def rotate_pieces(sources, start, size, count_head, stacked, after=(), limit=VMEM):
    blocks, tokens, _ = sources[0].shape
    count = len(sources)
    one = (count, blocks, tokens, size)
    shapes = [(count_head,) + one] if stacked else [one] * count_head
    *pieces, token = pl.pallas_call(
        functools.partial(
            rotate_kernel, (tuple(range(count)), start, size), count_head, len(after)
        ),
        in_specs=[pl.BlockSpec(memory_space=pltpu.HBM)] * count
        + [pl.BlockSpec(memory_space=pl.ANY)] * len(after),
        out_specs=[pl.BlockSpec(memory_space=pltpu.VMEM)] * (len(shapes) + 1),
        out_shape=[jax.ShapeDtypeStruct(shape, jnp.bfloat16) for shape in shapes] + [TOKEN],
        scratch_shapes=[
            pltpu.VMEM((count_head,) + one, jnp.bfloat16),
            pltpu.SemaphoreType.DMA((count_head, count)),
        ],
        cost_estimate=NO_COST,
        compiler_params=pltpu.CompilerParams(vmem_limit_bytes=limit),
    )(*sources, *after)
    return pieces, token


def slots_at(distance, count_tm):
    return NEAR_CAP if distance in (1, count_tm - 1) else FAR_CAP


def pick_kernel(count_head, count_tm, own_count, skipped, picks_ref, *refs):
    pieces = by_distance(refs[:own_count], count_head, -1)
    outs = by_distance(refs[own_count + skipped :], count_tm, 1, "tm")[-(count_tm - 1) :]
    shard = lax.axis_index("tm")
    for distance, out in enumerate(outs, 1):
        goal = lax.rem(shard + distance, count_tm)
        for k in range(slots_at(distance, count_tm)):
            pick = picks_ref[NEAR_CAP * goal + k]
            for s in range(count_head):
                out[k, s] = pieces[s][:, pick]


def pick_blocks(picks, owns, count_head, count_tm, stacked, after=(), cost=NO_COST):
    kinds, _, tokens, width = owns[0].shape[-4:]
    one = (count_head, kinds, tokens, width)
    if stacked:
        shapes = [(count_tm, NEAR_CAP) + one]
    else:
        shapes = [(slots_at(distance, count_tm),) + one for distance in range(1, count_tm)]
    vmem = pl.BlockSpec(memory_space=pltpu.VMEM)
    return pl.pallas_call(
        functools.partial(pick_kernel, count_head, count_tm, len(owns), len(after)),
        in_specs=[pl.BlockSpec(memory_space=pltpu.SMEM)]
        + [vmem] * len(owns)
        + [pl.BlockSpec(memory_space=pl.ANY)] * len(after),
        out_specs=[vmem] * len(shapes),
        out_shape=[jax.ShapeDtypeStruct(shape, jnp.bfloat16) for shape in shapes],
        cost_estimate=cost,
        compiler_params=pltpu.CompilerParams(vmem_limit_bytes=VMEM),
    )(picks, *owns, *after)


def remote_rows(count_tm):
    return [
        (distance, k)
        for distance in range(1, count_tm)
        for k in range(slots_at(distance, count_tm))
    ]


def split(value, by):
    if by & (by - 1) == 0:
        return value >> (by.bit_length() - 1), value & (by - 1)
    return lax.div(value, by), lax.rem(value, by)


def plan_kernel(count_head, count_tm, blocks, pair_ref, tokens_ref, _, picks_ref, bias_ref, named_ref, table_ref, sem):
    total_blocks, columns = pair_ref.shape
    pairs = pair_ref[...]
    lane = lax.broadcasted_iota(jnp.int32, named_ref.shape, 1)
    named = jnp.zeros(named_ref.shape, jnp.int32)
    for c in range(columns):
        named = jnp.where(pairs[:, c : c + 1] == lane, 1, named)
    named_ref[...] = named
    copy = pltpu.make_async_copy(named_ref, table_ref, sem)
    copy.start()
    copy.wait()
    shard = lax.axis_index("tm")
    place = lax.axis_index("head")
    mine = shard * blocks

    def two_picks(wanted):
        picks = [jnp.int32(0)] * NEAR_CAP
        count = jnp.int32(0)
        for j in range(blocks):
            for k in range(NEAR_CAP):
                picks[k] = jnp.where((wanted[j] > 0) & (count == k), j, picks[k])
            count = count + wanted[j]
        return picks, count

    def named_by(rows, column):
        found = table_ref[rows, column]
        for i in range(1, blocks):
            found = found | table_ref[rows + i, column]
        return found

    for d in range(count_tm):
        picks, _ = two_picks([named_by(d * blocks, mine + j) for j in range(blocks)])
        for k in range(NEAR_CAP):
            picks_ref[NEAR_CAP * d + k] = picks[k]

    kept = [[table_ref[mine + i, mine + j] * tokens_ref[mine + j] for j in range(blocks)] for i in range(blocks)]
    arrivals = {}
    for distance, k in remote_rows(count_tm):
        first = lax.rem(shard - distance + count_tm, count_tm) * blocks
        if k == 0:
            arrivals[distance] = two_picks([named_by(mine, first + j) for j in range(blocks)])
        picks, count = arrivals[distance]
        there = first + picks[k]
        live = jnp.where(count > k, tokens_ref[there], 0)
        for i in range(blocks):
            kept[i].append(table_ref[mine + i, there] * live)

    total = bias_ref.shape[1]
    piece_rows = BLK // count_head
    at = lax.broadcasted_iota(jnp.int32, (blocks, total), 1)
    query = lax.broadcasted_iota(jnp.int32, (blocks, total), 0)
    own = at < blocks * BLK
    group, token = split(at, piece_rows)
    own_piece, own_block = split(group, blocks)
    far_row, far_group = split(group, count_head)
    row = jnp.where(own, own_block, far_row)
    piece = jnp.where(own, own_piece, far_group)
    source = jnp.where(piece > place, place - piece + count_head, place - piece)
    position = source * piece_rows + token
    limit = jnp.zeros((blocks, total), jnp.int32)
    for r in range(len(kept[0])):
        value = jnp.zeros((blocks, total), jnp.int32)
        for i in range(blocks):
            value = jnp.where(query == i, kept[i][r], value)
        limit = jnp.where(row == r, value, limit)
    bias_ref[...] = jnp.where(position < limit, 0.0, NEG)


def plan(pair_list, block_tokens, after, blocks, count_head, count_tm):
    total_blocks = pair_list.shape[0]
    lanes = -(-total_blocks // 128) * 128
    total = (blocks + len(remote_rows(count_tm))) * BLK
    return pl.pallas_call(
        functools.partial(plan_kernel, count_head, count_tm, blocks),
        in_specs=[
            pl.BlockSpec(memory_space=pltpu.VMEM),
            pl.BlockSpec(memory_space=pltpu.SMEM),
            pl.BlockSpec(memory_space=pl.ANY),
        ],
        out_specs=[pl.BlockSpec(memory_space=pltpu.SMEM), pl.BlockSpec(memory_space=pltpu.VMEM)],
        out_shape=[
            jax.ShapeDtypeStruct((NEAR_CAP * count_tm,), jnp.int32),
            jax.ShapeDtypeStruct((blocks, total), jnp.float32),
        ],
        scratch_shapes=[
            pltpu.VMEM((total_blocks, lanes), jnp.int32),
            pltpu.SMEM((total_blocks, lanes), jnp.int32),
            pltpu.SemaphoreType.DMA,
        ],
        cost_estimate=NO_COST,
        compiler_params=pltpu.CompilerParams(vmem_limit_bytes=VMEM),
    )(pair_list, block_tokens, after)


def attend_kernel(counts, start, tokens_ref, bias_ref, *refs):
    count_head, count_tm, query_count, own_count, slot_count, skipped = counts
    at = [query_count, query_count + own_count, query_count + own_count + slot_count]
    queries = by_distance(refs[: at[0]], count_head, -1)
    owns = by_distance(refs[at[0] : at[1]], count_head, -1)
    slots = by_distance(refs[at[1] : at[2]], count_tm, -1, "tm")[-(count_tm - 1) :]
    outs = by_distance(refs[at[2] + skipped :], count_head, -1)
    _, blocks, tokens, size = owns[0].shape
    shard = lax.axis_index("tm")
    me = lax.axis_index("head")
    sign = sign_matrix()
    for h in range(size // HD):
        lanes = slice(h * HD, (h + 1) * HD)
        query_lanes = slice(start + h * HD, start + (h + 1) * HD)
        query = jnp.concatenate(
            [rows_of(queries[s][0, i, :, query_lanes]) for i in range(blocks) for s in range(count_head)],
            axis=0,
        )

        def gathered(kind):
            pieces = [rows_of(own[kind, :, :, lanes]) for own in owns]
            pieces += [
                rows_of(slots[distance - 1][k, :, kind, :, lanes])
                for distance, k in remote_rows(count_tm)
            ]
            return jnp.concatenate(pieces, axis=0)

        keys, values = gathered(0), gathered(1)
        total = keys.shape[0]
        dots = lax.dot_general(
            query, keys, (((1,), (1,)), ((), ())), preferred_element_type=jnp.float32
        )
        dots = dots.reshape(blocks, BLK, total) + bias_ref[...][:, None, :]
        peak = jnp.max(dots, axis=-1, keepdims=True)
        weights = jnp.exp2((dots - peak) * (SCORE_SCALE * LOG2E))
        denominator = jnp.sum(weights, axis=-1, keepdims=True).reshape(blocks * BLK, 1)
        weights_half = weights.astype(jnp.bfloat16).reshape(blocks * BLK, total)
        mixed = jnp.dot(weights_half, values, preferred_element_type=jnp.float32) / denominator
        turned = jnp.zeros_like(mixed)
        rest = mixed
        for _ in range(3):
            piece = rest.astype(jnp.bfloat16)
            turned = turned + jnp.dot(piece, sign, preferred_element_type=jnp.float32)
            rest = rest - piece.astype(jnp.float32)
        turned = (turned * ROTATE_SCALE).reshape(blocks, count_head, tokens, HD)
        token = lax.broadcasted_iota(jnp.int32, (tokens, HD), 0)
        for s in range(count_head):
            position = lax.rem(me - s + count_head, count_head) * tokens + token
            for i in range(blocks):
                outs[s][i, :, lanes] = jnp.where(
                    position < tokens_ref[shard * blocks + i], turned[i, s], 0.0
                ).astype(jnp.bfloat16)


def attend(block_tokens, bias, start, queries, owns, slots, count_head, count_tm, after, cost):
    _, blocks, tokens, size = owns[0].shape[-4:]
    shapes = [(blocks, tokens, size)] * count_head
    counts = (count_head, count_tm, len(queries), len(owns), len(slots), len(after))
    vmem = pl.BlockSpec(memory_space=pltpu.VMEM)
    return pl.pallas_call(
        functools.partial(attend_kernel, counts, start),
        in_specs=[pl.BlockSpec(memory_space=pltpu.SMEM)]
        + [vmem] * (1 + len(queries) + len(owns) + len(slots))
        + [pl.BlockSpec(memory_space=pl.ANY)] * len(after),
        out_specs=[vmem] * len(shapes),
        out_shape=[jax.ShapeDtypeStruct(shape, jnp.bfloat16) for shape in shapes],
        cost_estimate=cost,
        compiler_params=pltpu.CompilerParams(vmem_limit_bytes=VMEM),
    )(block_tokens, bias, *queries, *owns, *slots, *after)


def place_kernel(counts, starts, width_here, *refs):
    count_head = counts[0]
    out_ref, sems = refs[-2:]
    copies = []
    at = 0
    for count, start in zip(counts[1:], starts):
        pieces = by_distance(refs[at : at + count], count_head, 1)
        at += count
        for s, piece in enumerate(pieces):
            column = lax.rem(lax.axis_index("head") + s, count_head) * width_here + start
            copies.append(
                pltpu.make_async_copy(
                    piece,
                    out_ref.at[:, :, pl.ds(pl.multiple_of(column, HD), piece.shape[-1])],
                    sems.at[len(copies)],
                )
            )
            copies[-1].start()
    for copy in copies:
        copy.wait()


def place_pieces(parts, starts, count_head, width_here):
    pieces = [piece for part in parts for piece in part]
    blocks, tokens, _ = pieces[0].shape[-3:]
    counts = (count_head,) + tuple(len(part) for part in parts)
    return pl.pallas_call(
        functools.partial(place_kernel, counts, starts, width_here),
        in_specs=[pl.BlockSpec(memory_space=pl.ANY)] * len(pieces),
        out_specs=pl.BlockSpec(memory_space=pltpu.HBM),
        out_shape=jax.ShapeDtypeStruct((blocks, tokens, count_head * width_here), jnp.bfloat16),
        scratch_shapes=[pltpu.SemaphoreType.DMA((len(parts) * count_head,))],
        compiler_params=pltpu.CompilerParams(vmem_limit_bytes=VMEM),
    )(*pieces)


def shifted(array, axis, distance):
    count = lax.axis_size(axis)
    return lax.ppermute(array, axis, [(i, (i + distance) % count) for i in range(count)])


def exchange(pieces, direction):
    if len(pieces) == 1:
        return [lax.all_to_all(pieces[0], "head", split_axis=0, concat_axis=0, tiled=True)]
    return [pieces[0]] + [
        shifted(piece, "head", direction * s) for s, piece in enumerate(pieces[1:], 1)
    ]


def forward(sent):
    if len(sent) == 1:
        return [lax.all_to_all(sent[0], "tm", split_axis=0, concat_axis=0, tiled=True)]
    return [shifted(block, "tm", distance) for distance, block in enumerate(sent, 1)]


def shards(query_rows, key_rows, value_rows, pair_list, block_tokens):
    count_head = lax.axis_size("head")
    count_tm = lax.axis_size("tm")
    blocks, tokens, width = query_rows.shape
    width_here = width // count_head
    heads = width_here // HD
    cut = (heads + 1) // 2 * HD
    parts = [(0, cut), (cut, width_here - cut)] if heads > 1 else [(0, width_here)]
    sources = [key_rows, value_rows]
    pieces, token = rotate_pieces(sources, *parts[0], count_head, False, limit=WIDE_VMEM)
    packed = [pieces]
    picks, bias = plan(pair_list, block_tokens, token, blocks, count_head, count_tm)
    for part in parts[1:]:
        pieces, token = rotate_pieces(sources, *part, count_head, False, after=(bias, token))
        packed.append(pieces)
    key_values = [exchange(pieces, 1) for pieces in packed]
    sent = [pick_blocks(picks, key_values[0], count_head, count_tm, False)]
    for owns in key_values[1:]:
        sent.append(
            pick_blocks(
                picks, owns, count_head, count_tm, False, after=(sent[-1][0],), cost=HIGH_COST
            )
        )
    query, _ = rotate_pieces([query_rows], 0, width_here, count_head, False, after=(sent[0][0],))
    queries = exchange(query, 1)
    returned, after = [], ()
    for at, (owns, picked) in enumerate(zip(key_values, sent)):
        cost = NO_COST if at == len(parts) - 1 else HIGH_COST
        slots, start = forward(picked), parts[at][0]
        attended = attend(
            block_tokens, bias, start, queries, owns, slots, count_head, count_tm, after, cost
        )
        after = (attended[0],)
        returned.append(exchange(attended, -1))
    return place_pieces(returned, [start for start, _ in parts], count_head, width_here)


def solution(mesh):
    placed = (
        P(("grp", "tm"), "head", None),
        P(("grp", "tm"), "head", None),
        P(("grp", "tm"), "head", None),
        P("grp", None),
        P("grp"),
    )
    return jax.shard_map(
        shards,
        mesh=mesh,
        in_specs=placed,
        out_specs=P(("grp", "tm"), "head", None),
        check_vma=False,
    )
```

```python
import functools
import math

import jax
import jax.numpy as jnp
from jax import lax
from jax.experimental import pallas as pl
from jax.experimental.pallas import tpu as pltpu
from jax.sharding import PartitionSpec as P

HD = 128
BLK = 64
NEAR_CAP = 2
FAR_CAP = 1
NEG = -1e30
ROTATE_SCALE = 1.0 / math.sqrt(HD)
SCORE_SCALE = 1.0 / math.sqrt(HD)
VMEM = 24 * 1024 * 1024
WIDE_VMEM = 60 * 1024 * 1024
TOKEN = jax.ShapeDtypeStruct((8, 128), jnp.float32)
NO_COST = pl.CostEstimate(flops=0, bytes_accessed=0, transcendentals=0)
HIGH_COST = pl.CostEstimate(flops=10**11, bytes_accessed=0, transcendentals=0)
LOG2E = math.log2(math.e)


def sign_matrix():
    common = lax.broadcasted_iota(jnp.int32, (HD, HD), 0) & lax.broadcasted_iota(
        jnp.int32, (HD, HD), 1
    )
    bits = HD.bit_length() - 1
    parity = common
    for bit in range(1, bits):
        parity = parity ^ (common >> bit)
    return jnp.where((parity & 1) == 0, 1.0, -1.0).astype(jnp.bfloat16)


def rows_of(block):
    rows, width = math.prod(block.shape[:-1]), block.shape[-1]
    if block.shape[-2] % 16 == 0:
        return block.reshape(rows, width)
    return block.astype(jnp.float32).reshape(rows, width).astype(block.dtype)


def fields_of(message):
    at, fields = 0, []
    for source, start, size in message:
        fields.append((source, start, size, at))
        at += size
    return fields, at


def rotate_kernel(message, sources, count_head, skipped, *refs):
    fields, total = fields_of(message)
    ins = dict(zip(sources, refs))
    outs, (token, buffer, sems) = refs[len(sources) + skipped : -3], refs[-3:]
    token[...] = jnp.zeros_like(token)
    blocks, tokens, width = refs[0].shape
    width_here = width // count_head
    me = lax.axis_index("head")
    order = list(range(1, count_head)) + [0]
    copies = {}
    for s in order:
        goal = lax.rem(me + s, count_head)
        for f, (source, start, size, at) in enumerate(fields):
            column = pl.multiple_of(goal * width_here + start, HD)
            copies[s, f] = pltpu.make_async_copy(
                ins[source].at[:, :, pl.ds(column, size)],
                buffer.at[s, :, :, pl.ds(at, size)],
                sems.at[s, f],
            )
            copies[s, f].start()
    sign = sign_matrix()
    for s in order:
        for f, (_, _, size, start) in enumerate(fields):
            copies[s, f].wait()
            flat = rows_of(buffer[s, :, :, start : start + size])
            heads = [flat[:, at : at + HD] for at in range(0, size, HD)]
            turned = jnp.dot(
                jnp.concatenate(heads, axis=0), sign, preferred_element_type=jnp.float32
            )
            turned = (turned * ROTATE_SCALE).reshape(size // HD, blocks, tokens, HD)
            for h in range(size // HD):
                at = start + h * HD
                outs[s][:, :, at : at + HD] = turned[h].astype(jnp.bfloat16)


def rotate_pieces(arrays, message, count_head, after=(), limit=VMEM):
    blocks, tokens, _ = arrays[0].shape
    fields, total = fields_of(message)
    sources = sorted({source for source, _, _ in message})
    one = (blocks, tokens, total)
    *pieces, token = pl.pallas_call(
        functools.partial(rotate_kernel, message, sources, count_head, len(after)),
        in_specs=[pl.BlockSpec(memory_space=pltpu.HBM)] * len(sources)
        + [pl.BlockSpec(memory_space=pl.ANY)] * len(after),
        out_specs=[pl.BlockSpec(memory_space=pltpu.VMEM)] * (count_head + 1),
        out_shape=[jax.ShapeDtypeStruct(one, jnp.bfloat16)] * count_head + [TOKEN],
        scratch_shapes=[
            pltpu.VMEM((count_head,) + one, jnp.bfloat16),
            pltpu.SemaphoreType.DMA((count_head, len(fields))),
        ],
        cost_estimate=NO_COST,
        compiler_params=pltpu.CompilerParams(vmem_limit_bytes=limit),
    )(*[arrays[source] for source in sources], *after)
    return pieces, token


def slots_at(distance, count_tm):
    return NEAR_CAP if distance in (1, count_tm - 1) else FAR_CAP


def pick_kernel(count_head, count_tm, lanes, skipped, picks_ref, *refs):
    pieces, outs = refs[:count_head], refs[count_head + skipped :]
    shard = lax.axis_index("tm")
    for distance, out in enumerate(outs, 1):
        goal = lax.rem(shard + distance, count_tm)
        for k in range(slots_at(distance, count_tm)):
            pick = picks_ref[NEAR_CAP * goal + k]
            for s in range(count_head):
                out[k, s] = pieces[s][pick, :, lanes[0] : lanes[1]]


def pick_blocks(picks, pieces, lanes, count_tm, after, cost):
    count_head = len(pieces)
    one = (count_head, pieces[0].shape[1], lanes[1] - lanes[0])
    vmem = pl.BlockSpec(memory_space=pltpu.VMEM)
    return pl.pallas_call(
        functools.partial(pick_kernel, count_head, count_tm, lanes, len(after)),
        in_specs=[pl.BlockSpec(memory_space=pltpu.SMEM)]
        + [vmem] * count_head
        + [pl.BlockSpec(memory_space=pl.ANY)] * len(after),
        out_specs=[vmem] * (count_tm - 1),
        out_shape=[
            jax.ShapeDtypeStruct((slots_at(distance, count_tm),) + one, jnp.bfloat16)
            for distance in range(1, count_tm)
        ],
        cost_estimate=cost,
        compiler_params=pltpu.CompilerParams(vmem_limit_bytes=VMEM),
    )(picks, *pieces, *after)


def remote_rows(count_tm):
    return [
        (distance, k)
        for distance in range(1, count_tm)
        for k in range(slots_at(distance, count_tm))
    ]


def split(value, by):
    if by & (by - 1) == 0:
        return value >> (by.bit_length() - 1), value & (by - 1)
    return lax.div(value, by), lax.rem(value, by)


def plan_kernel(count_head, count_tm, blocks, pair_ref, tokens_ref, _, picks_ref, bias_ref, named_ref, table_ref, sem):
    total_blocks, columns = pair_ref.shape
    pairs = pair_ref[...]
    lane = lax.broadcasted_iota(jnp.int32, named_ref.shape, 1)
    named = jnp.zeros(named_ref.shape, jnp.int32)
    for c in range(columns):
        named = jnp.where(pairs[:, c : c + 1] == lane, 1, named)
    named_ref[...] = named
    copy = pltpu.make_async_copy(named_ref, table_ref, sem)
    copy.start()
    copy.wait()
    shard = lax.axis_index("tm")
    place = lax.axis_index("head")
    mine = shard * blocks

    def two_picks(wanted):
        picks = [jnp.int32(0)] * NEAR_CAP
        count = jnp.int32(0)
        for j in range(blocks):
            for k in range(NEAR_CAP):
                picks[k] = jnp.where((wanted[j] > 0) & (count == k), j, picks[k])
            count = count + wanted[j]
        return picks, count

    def named_by(rows, column):
        found = table_ref[rows, column]
        for i in range(1, blocks):
            found = found | table_ref[rows + i, column]
        return found

    for d in range(count_tm):
        picks, _ = two_picks([named_by(d * blocks, mine + j) for j in range(blocks)])
        for k in range(NEAR_CAP):
            picks_ref[NEAR_CAP * d + k] = picks[k]

    kept = [[table_ref[mine + i, mine + j] * tokens_ref[mine + j] for j in range(blocks)] for i in range(blocks)]
    arrivals = {}
    for distance, k in remote_rows(count_tm):
        first = lax.rem(shard - distance + count_tm, count_tm) * blocks
        if k == 0:
            arrivals[distance] = two_picks([named_by(mine, first + j) for j in range(blocks)])
        picks, count = arrivals[distance]
        there = first + picks[k]
        live = jnp.where(count > k, tokens_ref[there], 0)
        for i in range(blocks):
            kept[i].append(table_ref[mine + i, there] * live)

    total = bias_ref.shape[1]
    piece_rows = BLK // count_head
    at = lax.broadcasted_iota(jnp.int32, (blocks, total), 1)
    query = lax.broadcasted_iota(jnp.int32, (blocks, total), 0)
    own = at < blocks * BLK
    group, token = split(at, piece_rows)
    own_piece, own_block = split(group, blocks)
    far_row, far_group = split(group, count_head)
    row = jnp.where(own, own_block, far_row)
    piece = jnp.where(own, own_piece, far_group)
    source = jnp.where(piece > place, place - piece + count_head, place - piece)
    position = source * piece_rows + token
    limit = jnp.zeros((blocks, total), jnp.int32)
    for r in range(len(kept[0])):
        value = jnp.zeros((blocks, total), jnp.int32)
        for i in range(blocks):
            value = jnp.where(query == i, kept[i][r], value)
        limit = jnp.where(row == r, value, limit)
    bias_ref[...] = jnp.where(position < limit, 0.0, NEG)


def plan(pair_list, block_tokens, after, blocks, count_head, count_tm):
    total_blocks = pair_list.shape[0]
    lanes = -(-total_blocks // 128) * 128
    total = (blocks + len(remote_rows(count_tm))) * BLK
    return pl.pallas_call(
        functools.partial(plan_kernel, count_head, count_tm, blocks),
        in_specs=[
            pl.BlockSpec(memory_space=pltpu.VMEM),
            pl.BlockSpec(memory_space=pltpu.SMEM),
            pl.BlockSpec(memory_space=pl.ANY),
        ],
        out_specs=[pl.BlockSpec(memory_space=pltpu.SMEM), pl.BlockSpec(memory_space=pltpu.VMEM)],
        out_shape=[
            jax.ShapeDtypeStruct((NEAR_CAP * count_tm,), jnp.int32),
            jax.ShapeDtypeStruct((blocks, total), jnp.float32),
        ],
        scratch_shapes=[
            pltpu.VMEM((total_blocks, lanes), jnp.int32),
            pltpu.SMEM((total_blocks, lanes), jnp.int32),
            pltpu.SemaphoreType.DMA,
        ],
        cost_estimate=NO_COST,
        compiler_params=pltpu.CompilerParams(vmem_limit_bytes=VMEM),
    )(pair_list, block_tokens, after)


def attend_kernel(counts, at, size, tokens_ref, bias_ref, *refs):
    count_head, count_tm, skipped = counts
    query_at, key_at = at
    queries, owns = refs[:count_head], refs[count_head : 2 * count_head]
    slots = refs[2 * count_head : 2 * count_head + count_tm - 1]
    outs = refs[2 * count_head + count_tm - 1 + skipped :]
    blocks, tokens, _ = owns[0].shape
    shard = lax.axis_index("tm")
    me = lax.axis_index("head")
    sign = sign_matrix()
    for h in range(size // HD):
        lanes = slice(h * HD, (h + 1) * HD)
        query_lanes = slice(query_at + h * HD, query_at + (h + 1) * HD)
        query = jnp.concatenate(
            [rows_of(queries[s][i, :, query_lanes]) for i in range(blocks) for s in range(count_head)],
            axis=0,
        )

        def gathered(kind):
            first = kind * size + h * HD
            own_lanes = slice(key_at + first, key_at + first + HD)
            pieces = [rows_of(own[:, :, own_lanes]) for own in owns]
            pieces += [
                rows_of(slots[distance - 1][k, :, :, first : first + HD])
                for distance, k in remote_rows(count_tm)
            ]
            return jnp.concatenate(pieces, axis=0)

        keys, values = gathered(0), gathered(1)
        total = keys.shape[0]
        dots = lax.dot_general(
            query, keys, (((1,), (1,)), ((), ())), preferred_element_type=jnp.float32
        )
        dots = dots.reshape(blocks, BLK, total) + bias_ref[...][:, None, :]
        peak = jnp.max(dots, axis=-1, keepdims=True)
        weights = jnp.exp2((dots - peak) * (SCORE_SCALE * LOG2E))
        denominator = jnp.sum(weights, axis=-1, keepdims=True).reshape(blocks * BLK, 1)
        weights_half = weights.astype(jnp.bfloat16).reshape(blocks * BLK, total)
        mixed = jnp.dot(weights_half, values, preferred_element_type=jnp.float32) / denominator
        turned = jnp.zeros_like(mixed)
        rest = mixed
        for _ in range(3):
            piece = rest.astype(jnp.bfloat16)
            turned = turned + jnp.dot(piece, sign, preferred_element_type=jnp.float32)
            rest = rest - piece.astype(jnp.float32)
        turned = (turned * ROTATE_SCALE).reshape(blocks, count_head, tokens, HD)
        token = lax.broadcasted_iota(jnp.int32, (tokens, HD), 0)
        for s in range(count_head):
            position = lax.rem(me - s + count_head, count_head) * tokens + token
            for i in range(blocks):
                outs[s][i, :, lanes] = jnp.where(
                    position < tokens_ref[shard * blocks + i], turned[i, s], 0.0
                ).astype(jnp.bfloat16)


def attend(block_tokens, bias, queries, query_at, owns, key_at, slots, size, after, cost):
    count_head, count_tm = len(owns), len(slots) + 1
    blocks, tokens, _ = owns[0].shape
    vmem = pl.BlockSpec(memory_space=pltpu.VMEM)
    return pl.pallas_call(
        functools.partial(
            attend_kernel, (count_head, count_tm, len(after)), (query_at, key_at), size
        ),
        in_specs=[pl.BlockSpec(memory_space=pltpu.SMEM)]
        + [vmem] * (2 * count_head + count_tm)
        + [pl.BlockSpec(memory_space=pl.ANY)] * len(after),
        out_specs=[vmem] * count_head,
        out_shape=[jax.ShapeDtypeStruct((blocks, tokens, size), jnp.bfloat16)] * count_head,
        cost_estimate=cost,
        compiler_params=pltpu.CompilerParams(vmem_limit_bytes=VMEM),
    )(block_tokens, bias, *queries, *owns, *slots, *after)


def place_kernel(count_head, starts, width_here, *refs):
    pieces, out_ref, sems = refs[:-2], refs[-2], refs[-1]
    me = lax.axis_index("head")
    copies = []
    for at, piece in enumerate(pieces):
        part, s = at // count_head, at % count_head
        column = lax.rem(me + s, count_head) * width_here + starts[part]
        copies.append(
            pltpu.make_async_copy(
                piece,
                out_ref.at[:, :, pl.ds(pl.multiple_of(column, HD), piece.shape[-1])],
                sems.at[at],
            )
        )
        copies[-1].start()
    for copy in copies:
        copy.wait()


def place_pieces(parts, starts, width_here):
    count_head = len(parts[0])
    pieces = [piece for part in parts for piece in part]
    blocks, tokens, _ = pieces[0].shape
    return pl.pallas_call(
        functools.partial(place_kernel, count_head, starts, width_here),
        in_specs=[pl.BlockSpec(memory_space=pl.ANY)] * len(pieces),
        out_specs=pl.BlockSpec(memory_space=pltpu.HBM),
        out_shape=jax.ShapeDtypeStruct((blocks, tokens, count_head * width_here), jnp.bfloat16),
        scratch_shapes=[pltpu.SemaphoreType.DMA((len(pieces),))],
        compiler_params=pltpu.CompilerParams(vmem_limit_bytes=VMEM),
    )(*pieces)


def shifted(array, axis, distance):
    count = lax.axis_size(axis)
    return lax.ppermute(array, axis, [(i, (i + distance) % count) for i in range(count)])


def exchange(pieces, direction):
    return [pieces[0]] + [
        shifted(piece, "head", direction * s) for s, piece in enumerate(pieces[1:], 1)
    ]


def forward(sent):
    return [shifted(block, "tm", distance) for distance, block in enumerate(sent, 1)]


def shards(query_rows, key_rows, value_rows, pair_list, block_tokens):
    count_head = lax.axis_size("head")
    count_tm = lax.axis_size("tm")
    blocks, tokens, width = query_rows.shape
    width_here = width // count_head
    heads = width_here // HD
    cut = (2 * heads + 2) // 3 * HD
    parts = [(0, cut), (cut, width_here - cut)] if heads > 1 else [(0, width_here)]
    arrays = [query_rows, key_rows, value_rows]
    messages = []
    for at, part in enumerate(parts):
        message = [(1,) + part, (2,) + part]
        messages.append(message + ([(0,) + parts[at - 1]] if at else []))
    messages.append([(0,) + parts[-1]])
    key_at = [0] * len(parts)
    query_at = [2 * size for _, size in parts[1:]] + [0]

    pieces, token = rotate_pieces(arrays, messages[0], count_head, limit=WIDE_VMEM)
    packed = [pieces]
    picks, bias = plan(pair_list, block_tokens, token, blocks, count_head, count_tm)
    after = (bias,)
    for message in messages[1:-1]:
        pieces, token = rotate_pieces(arrays, message, count_head, after)
        packed.append(pieces)
        after = (token,)
    received = [exchange(pieces, 1) for pieces in packed]
    sent, after = [], ()
    for at, (_, size) in enumerate(parts):
        lanes = (key_at[at], key_at[at] + 2 * size)
        cost = HIGH_COST if at else NO_COST
        sent.append(pick_blocks(picks, received[at], lanes, count_tm, after, cost))
        after = (sent[-1][0],)
        if not at:
            pieces, _ = rotate_pieces(arrays, messages[-1], count_head, after)
    received.append(exchange(pieces, 1))
    returned, after = [], ()
    for at, (_, size) in enumerate(parts):
        cost = NO_COST if at == len(parts) - 1 else HIGH_COST
        attended = attend(
            block_tokens, bias, received[at + 1], query_at[at], received[at], key_at[at],
            forward(sent[at]), size, after, cost,
        )
        after = (attended[0],)
        returned.append(exchange(attended, -1))
    return place_pieces(returned, [start for start, _ in parts], width_here)


def solution(mesh):
    placed = (
        P(("grp", "tm"), "head", None),
        P(("grp", "tm"), "head", None),
        P(("grp", "tm"), "head", None),
        P("grp", None),
        P("grp"),
    )
    return jax.shard_map(
        shards,
        mesh=mesh,
        in_specs=placed,
        out_specs=P(("grp", "tm"), "head", None),
        check_vma=False,
    )
```

```python
import functools
import math

import jax
import jax.numpy as jnp
from jax import lax
from jax.experimental import pallas as pl
from jax.experimental.pallas import tpu as pltpu
from jax.sharding import PartitionSpec as P

HD = 128
BLK = 64
NEAR_CAP = 2
FAR_CAP = 1
NEG = -1e30
ROTATE_SCALE = 1.0 / math.sqrt(HD)
SCORE_SCALE = 1.0 / math.sqrt(HD)
VMEM = 24 * 1024 * 1024
WIDE_VMEM = 60 * 1024 * 1024
TOKEN = jax.ShapeDtypeStruct((8, 128), jnp.float32)
NO_COST = pl.CostEstimate(flops=0, bytes_accessed=0, transcendentals=0)
HIGH_COST = pl.CostEstimate(flops=10**11, bytes_accessed=0, transcendentals=0)
LOG2E = math.log2(math.e)


def sign_matrix():
    common = lax.broadcasted_iota(jnp.int32, (HD, HD), 0) & lax.broadcasted_iota(
        jnp.int32, (HD, HD), 1
    )
    bits = HD.bit_length() - 1
    parity = common
    for bit in range(1, bits):
        parity = parity ^ (common >> bit)
    return jnp.where((parity & 1) == 0, 1.0, -1.0).astype(jnp.bfloat16)


def rows_of(block):
    rows, width = math.prod(block.shape[:-1]), block.shape[-1]
    if block.shape[-2] % 16 == 0:
        return block.reshape(rows, width)
    return block.astype(jnp.float32).reshape(rows, width).astype(block.dtype)


def fields_of(message):
    at, fields = 0, []
    for source, start, size in message:
        fields.append((source, start, size, at))
        at += size
    return fields, at


def rotate_kernel(message, sources, count_head, skipped, *refs):
    fields, total = fields_of(message)
    ins = dict(zip(sources, refs))
    outs, (token, buffer, sems) = refs[len(sources) + skipped : -3], refs[-3:]
    token[...] = jnp.zeros_like(token)
    blocks, tokens, width = refs[0].shape
    width_here = width // count_head
    me = lax.axis_index("head")
    order = list(range(1, count_head)) + [0]
    copies = {}
    for s in order:
        goal = lax.rem(me + s, count_head)
        for f, (source, start, size, at) in enumerate(fields):
            column = pl.multiple_of(goal * width_here + start, HD)
            copies[s, f] = pltpu.make_async_copy(
                ins[source].at[:, :, pl.ds(column, size)],
                buffer.at[s, :, :, pl.ds(at, size)],
                sems.at[s, f],
            )
            copies[s, f].start()
    sign = sign_matrix()
    for s in order:
        for f, (_, _, size, start) in enumerate(fields):
            copies[s, f].wait()
            flat = rows_of(buffer[s, :, :, start : start + size])
            heads = [flat[:, at : at + HD] for at in range(0, size, HD)]
            turned = jnp.dot(
                jnp.concatenate(heads, axis=0), sign, preferred_element_type=jnp.float32
            )
            turned = (turned * ROTATE_SCALE).reshape(size // HD, blocks, tokens, HD)
            for h in range(size // HD):
                at = start + h * HD
                outs[s][:, :, at : at + HD] = turned[h].astype(jnp.bfloat16)


def rotate_pieces(arrays, message, count_head, after=(), limit=VMEM):
    blocks, tokens, _ = arrays[0].shape
    fields, total = fields_of(message)
    sources = sorted({source for source, _, _ in message})
    one = (blocks, tokens, total)
    *pieces, token = pl.pallas_call(
        functools.partial(rotate_kernel, message, sources, count_head, len(after)),
        in_specs=[pl.BlockSpec(memory_space=pltpu.HBM)] * len(sources)
        + [pl.BlockSpec(memory_space=pl.ANY)] * len(after),
        out_specs=[pl.BlockSpec(memory_space=pltpu.VMEM)] * (count_head + 1),
        out_shape=[jax.ShapeDtypeStruct(one, jnp.bfloat16)] * count_head + [TOKEN],
        scratch_shapes=[
            pltpu.VMEM((count_head,) + one, jnp.bfloat16),
            pltpu.SemaphoreType.DMA((count_head, len(fields))),
        ],
        cost_estimate=NO_COST,
        compiler_params=pltpu.CompilerParams(vmem_limit_bytes=limit),
    )(*[arrays[source] for source in sources], *after)
    return pieces, token


def slots_at(distance, count_tm):
    return NEAR_CAP if distance in (1, count_tm - 1) else FAR_CAP


def pick_kernel(count_head, count_tm, lanes, skipped, picks_ref, *refs):
    pieces, outs = refs[:count_head], refs[count_head + skipped :]
    shard = lax.axis_index("tm")
    for distance, out in enumerate(outs, 1):
        goal = lax.rem(shard + distance, count_tm)
        for k in range(slots_at(distance, count_tm)):
            pick = picks_ref[NEAR_CAP * goal + k]
            for s in range(count_head):
                out[k, s] = pieces[s][pick, :, lanes[0] : lanes[1]]


def pick_blocks(picks, pieces, lanes, count_tm, after, cost):
    count_head = len(pieces)
    one = (count_head, pieces[0].shape[1], lanes[1] - lanes[0])
    vmem = pl.BlockSpec(memory_space=pltpu.VMEM)
    return pl.pallas_call(
        functools.partial(pick_kernel, count_head, count_tm, lanes, len(after)),
        in_specs=[pl.BlockSpec(memory_space=pltpu.SMEM)]
        + [vmem] * count_head
        + [pl.BlockSpec(memory_space=pl.ANY)] * len(after),
        out_specs=[vmem] * (count_tm - 1),
        out_shape=[
            jax.ShapeDtypeStruct((slots_at(distance, count_tm),) + one, jnp.bfloat16)
            for distance in range(1, count_tm)
        ],
        cost_estimate=cost,
        compiler_params=pltpu.CompilerParams(vmem_limit_bytes=VMEM),
    )(picks, *pieces, *after)


def remote_rows(count_tm):
    return [
        (distance, k)
        for distance in range(1, count_tm)
        for k in range(slots_at(distance, count_tm))
    ]


def split(value, by):
    if by & (by - 1) == 0:
        return value >> (by.bit_length() - 1), value & (by - 1)
    return lax.div(value, by), lax.rem(value, by)


def plan_kernel(count_head, count_tm, blocks, pair_ref, tokens_ref, _, picks_ref, bias_ref, named_ref, table_ref, sem):
    total_blocks, columns = pair_ref.shape
    pairs = pair_ref[...]
    lane = lax.broadcasted_iota(jnp.int32, named_ref.shape, 1)
    named = jnp.zeros(named_ref.shape, jnp.int32)
    for c in range(columns):
        named = jnp.where(pairs[:, c : c + 1] == lane, 1, named)
    named_ref[...] = named
    copy = pltpu.make_async_copy(named_ref, table_ref, sem)
    copy.start()
    copy.wait()
    shard = lax.axis_index("tm")
    place = lax.axis_index("head")
    mine = shard * blocks

    def two_picks(wanted):
        picks = [jnp.int32(0)] * NEAR_CAP
        count = jnp.int32(0)
        for j in range(blocks):
            for k in range(NEAR_CAP):
                picks[k] = jnp.where((wanted[j] > 0) & (count == k), j, picks[k])
            count = count + wanted[j]
        return picks, count

    def named_by(rows, column):
        found = table_ref[rows, column]
        for i in range(1, blocks):
            found = found | table_ref[rows + i, column]
        return found

    for d in range(count_tm):
        picks, _ = two_picks([named_by(d * blocks, mine + j) for j in range(blocks)])
        for k in range(NEAR_CAP):
            picks_ref[NEAR_CAP * d + k] = picks[k]

    kept = [[table_ref[mine + i, mine + j] * tokens_ref[mine + j] for j in range(blocks)] for i in range(blocks)]
    arrivals = {}
    for distance, k in remote_rows(count_tm):
        first = lax.rem(shard - distance + count_tm, count_tm) * blocks
        if k == 0:
            arrivals[distance] = two_picks([named_by(mine, first + j) for j in range(blocks)])
        picks, count = arrivals[distance]
        there = first + picks[k]
        live = jnp.where(count > k, tokens_ref[there], 0)
        for i in range(blocks):
            kept[i].append(table_ref[mine + i, there] * live)

    total = bias_ref.shape[1]
    piece_rows = BLK // count_head
    at = lax.broadcasted_iota(jnp.int32, (blocks, total), 1)
    query = lax.broadcasted_iota(jnp.int32, (blocks, total), 0)
    own = at < blocks * BLK
    group, token = split(at, piece_rows)
    own_piece, own_block = split(group, blocks)
    far_row, far_group = split(group, count_head)
    row = jnp.where(own, own_block, far_row)
    piece = jnp.where(own, own_piece, far_group)
    source = jnp.where(piece > place, place - piece + count_head, place - piece)
    position = source * piece_rows + token
    limit = jnp.zeros((blocks, total), jnp.int32)
    for r in range(len(kept[0])):
        value = jnp.zeros((blocks, total), jnp.int32)
        for i in range(blocks):
            value = jnp.where(query == i, kept[i][r], value)
        limit = jnp.where(row == r, value, limit)
    bias_ref[...] = jnp.where(position < limit, 0.0, NEG)


def plan(pair_list, block_tokens, after, blocks, count_head, count_tm):
    total_blocks = pair_list.shape[0]
    lanes = -(-total_blocks // 128) * 128
    total = (blocks + len(remote_rows(count_tm))) * BLK
    return pl.pallas_call(
        functools.partial(plan_kernel, count_head, count_tm, blocks),
        in_specs=[
            pl.BlockSpec(memory_space=pltpu.VMEM),
            pl.BlockSpec(memory_space=pltpu.SMEM),
            pl.BlockSpec(memory_space=pl.ANY),
        ],
        out_specs=[pl.BlockSpec(memory_space=pltpu.SMEM), pl.BlockSpec(memory_space=pltpu.VMEM)],
        out_shape=[
            jax.ShapeDtypeStruct((NEAR_CAP * count_tm,), jnp.int32),
            jax.ShapeDtypeStruct((blocks, total), jnp.float32),
        ],
        scratch_shapes=[
            pltpu.VMEM((total_blocks, lanes), jnp.int32),
            pltpu.SMEM((total_blocks, lanes), jnp.int32),
            pltpu.SemaphoreType.DMA,
        ],
        cost_estimate=NO_COST,
        compiler_params=pltpu.CompilerParams(vmem_limit_bytes=VMEM),
    )(pair_list, block_tokens, after)


def attend_kernel(counts, at, size, tokens_ref, bias_ref, *refs):
    count_head, count_tm, skipped = counts
    query_at, key_at = at
    queries, owns = refs[:count_head], refs[count_head : 2 * count_head]
    slots = refs[2 * count_head : 2 * count_head + count_tm - 1]
    outs = refs[2 * count_head + count_tm - 1 + skipped :]
    blocks, tokens, _ = owns[0].shape
    shard = lax.axis_index("tm")
    me = lax.axis_index("head")
    sign = sign_matrix()
    for h in range(size // HD):
        lanes = slice(h * HD, (h + 1) * HD)
        query_lanes = slice(query_at + h * HD, query_at + (h + 1) * HD)
        query = jnp.concatenate(
            [rows_of(queries[s][i, :, query_lanes]) for i in range(blocks) for s in range(count_head)],
            axis=0,
        )

        def gathered(kind):
            first = kind * size + h * HD
            own_lanes = slice(key_at + first, key_at + first + HD)
            pieces = [rows_of(own[:, :, own_lanes]) for own in owns]
            pieces += [
                rows_of(slots[distance - 1][k, :, :, first : first + HD])
                for distance, k in remote_rows(count_tm)
            ]
            return jnp.concatenate(pieces, axis=0)

        keys, values = gathered(0), gathered(1)
        total = keys.shape[0]
        dots = lax.dot_general(
            query, keys, (((1,), (1,)), ((), ())), preferred_element_type=jnp.float32
        )
        dots = dots.reshape(blocks, BLK, total) + bias_ref[...][:, None, :]
        peak = jnp.max(dots, axis=-1, keepdims=True)
        weights = jnp.exp2((dots - peak) * (SCORE_SCALE * LOG2E))
        denominator = jnp.sum(weights, axis=-1, keepdims=True).reshape(blocks * BLK, 1)
        weights_half = weights.astype(jnp.bfloat16).reshape(blocks * BLK, total)
        mixed = jnp.dot(weights_half, values, preferred_element_type=jnp.float32) / denominator
        turned = jnp.zeros_like(mixed)
        rest = mixed
        for _ in range(3):
            piece = rest.astype(jnp.bfloat16)
            turned = turned + jnp.dot(piece, sign, preferred_element_type=jnp.float32)
            rest = rest - piece.astype(jnp.float32)
        turned = (turned * ROTATE_SCALE).reshape(blocks, count_head, tokens, HD)
        token = lax.broadcasted_iota(jnp.int32, (tokens, HD), 0)
        for s in range(count_head):
            position = lax.rem(me - s + count_head, count_head) * tokens + token
            for i in range(blocks):
                outs[s][i, :, lanes] = jnp.where(
                    position < tokens_ref[shard * blocks + i], turned[i, s], 0.0
                ).astype(jnp.bfloat16)


def attend(block_tokens, bias, queries, query_at, owns, key_at, slots, size, after, cost):
    count_head, count_tm = len(owns), len(slots) + 1
    blocks, tokens, _ = owns[0].shape
    vmem = pl.BlockSpec(memory_space=pltpu.VMEM)
    return pl.pallas_call(
        functools.partial(
            attend_kernel, (count_head, count_tm, len(after)), (query_at, key_at), size
        ),
        in_specs=[pl.BlockSpec(memory_space=pltpu.SMEM)]
        + [vmem] * (2 * count_head + count_tm)
        + [pl.BlockSpec(memory_space=pl.ANY)] * len(after),
        out_specs=[vmem] * count_head,
        out_shape=[jax.ShapeDtypeStruct((blocks, tokens, size), jnp.bfloat16)] * count_head,
        cost_estimate=cost,
        compiler_params=pltpu.CompilerParams(vmem_limit_bytes=VMEM),
    )(block_tokens, bias, *queries, *owns, *slots, *after)


def place_kernel(count_head, starts, width_here, *refs):
    pieces, out_ref, sems = refs[:-2], refs[-2], refs[-1]
    me = lax.axis_index("head")
    copies = []
    for at, piece in enumerate(pieces):
        part, s = at // count_head, at % count_head
        column = lax.rem(me + s, count_head) * width_here + starts[part]
        copies.append(
            pltpu.make_async_copy(
                piece,
                out_ref.at[:, :, pl.ds(pl.multiple_of(column, HD), piece.shape[-1])],
                sems.at[at],
            )
        )
        copies[-1].start()
    for copy in copies:
        copy.wait()


def place_pieces(parts, starts, width_here):
    count_head = len(parts[0])
    pieces = [piece for part in parts for piece in part]
    blocks, tokens, _ = pieces[0].shape
    return pl.pallas_call(
        functools.partial(place_kernel, count_head, starts, width_here),
        in_specs=[pl.BlockSpec(memory_space=pl.ANY)] * len(pieces),
        out_specs=pl.BlockSpec(memory_space=pltpu.HBM),
        out_shape=jax.ShapeDtypeStruct((blocks, tokens, count_head * width_here), jnp.bfloat16),
        scratch_shapes=[pltpu.SemaphoreType.DMA((len(pieces),))],
        compiler_params=pltpu.CompilerParams(vmem_limit_bytes=VMEM),
    )(*pieces)


def shifted(array, axis, distance):
    count = lax.axis_size(axis)
    return lax.ppermute(array, axis, [(i, (i + distance) % count) for i in range(count)])


def exchange(pieces, direction):
    return [pieces[0]] + [
        shifted(piece, "head", direction * s) for s, piece in enumerate(pieces[1:], 1)
    ]


def forward(sent):
    return [shifted(block, "tm", distance) for distance, block in enumerate(sent, 1)]


def shards(query_rows, key_rows, value_rows, pair_list, block_tokens):
    count_head = lax.axis_size("head")
    count_tm = lax.axis_size("tm")
    blocks, tokens, width = query_rows.shape
    width_here = width // count_head
    heads = width_here // HD
    cut = (heads + 1) // 2 * HD
    parts = [(0, cut), (cut, width_here - cut)] if heads > 1 else [(0, width_here)]
    arrays = [query_rows, key_rows, value_rows]
    messages = []
    for at, part in enumerate(parts):
        message = [(1,) + part, (2,) + part]
        messages.append(message + ([(0,) + parts[at - 1]] if at else []))
    messages.append([(0,) + parts[-1]])
    key_at = [0] * len(parts)
    query_at = [2 * size for _, size in parts[1:]] + [0]

    pieces, token = rotate_pieces(arrays, messages[0], count_head, limit=WIDE_VMEM)
    packed = [pieces]
    picks, bias = plan(pair_list, block_tokens, token, blocks, count_head, count_tm)
    after = (bias,)
    for message in messages[1:-1]:
        pieces, token = rotate_pieces(arrays, message, count_head, after)
        packed.append(pieces)
        after = (token,)
    received = [exchange(pieces, 1) for pieces in packed]
    sent, after = [], ()
    for at, (_, size) in enumerate(parts):
        lanes = (key_at[at], key_at[at] + 2 * size)
        cost = HIGH_COST if at else NO_COST
        sent.append(pick_blocks(picks, received[at], lanes, count_tm, after, cost))
        after = (sent[-1][0],)
        if not at:
            pieces, _ = rotate_pieces(arrays, messages[-1], count_head, after)
    received.append(exchange(pieces, 1))
    returned, after = [], ()
    for at, (_, size) in enumerate(parts):
        cost = NO_COST if at == len(parts) - 1 else HIGH_COST
        attended = attend(
            block_tokens, bias, received[at + 1], query_at[at], received[at], key_at[at],
            forward(sent[at]), size, after, cost,
        )
        after = (attended[0],)
        returned.append(exchange(attended, -1))
    return place_pieces(returned, [start for start, _ in parts], width_here)


def solution(mesh):
    placed = (
        P(("grp", "tm"), "head", None),
        P(("grp", "tm"), "head", None),
        P(("grp", "tm"), "head", None),
        P("grp", None),
        P("grp"),
    )
    return jax.shard_map(
        shards,
        mesh=mesh,
        in_specs=placed,
        out_specs=P(("grp", "tm"), "head", None),
        check_vma=False,
    )
```

```python
import functools
import math

import jax
import jax.numpy as jnp
from jax import lax
from jax.experimental import pallas as pl
from jax.experimental.pallas import tpu as pltpu
from jax.sharding import PartitionSpec as P

HD = 128
BLK = 64
NEAR_CAP = 2
FAR_CAP = 1
NEG = -1e30
ROTATE_SCALE = 1.0 / math.sqrt(HD)
SCORE_SCALE = 1.0 / math.sqrt(HD)
VMEM = 24 * 1024 * 1024
WIDE_VMEM = 60 * 1024 * 1024
TOKEN = jax.ShapeDtypeStruct((8, 128), jnp.float32)
NO_COST = pl.CostEstimate(flops=0, bytes_accessed=0, transcendentals=0)
HIGH_COST = pl.CostEstimate(flops=10**11, bytes_accessed=0, transcendentals=0)
LOG2E = math.log2(math.e)


def sign_matrix():
    common = lax.broadcasted_iota(jnp.int32, (HD, HD), 0) & lax.broadcasted_iota(
        jnp.int32, (HD, HD), 1
    )
    bits = HD.bit_length() - 1
    parity = common
    for bit in range(1, bits):
        parity = parity ^ (common >> bit)
    return jnp.where((parity & 1) == 0, 1.0, -1.0).astype(jnp.bfloat16)


def rows_of(block):
    rows, width = math.prod(block.shape[:-1]), block.shape[-1]
    if block.shape[-2] % 16 == 0:
        return block.reshape(rows, width)
    return block.astype(jnp.float32).reshape(rows, width).astype(block.dtype)


def fields_of(message):
    at, fields = 0, []
    for source, start, size in message:
        fields.append((source, start, size, at))
        at += size
    return fields, at


def rotate_kernel(message, sources, count_head, skipped, *refs):
    fields, total = fields_of(message)
    ins = dict(zip(sources, refs))
    outs, (token, buffer, sems) = refs[len(sources) + skipped : -3], refs[-3:]
    token[...] = jnp.zeros_like(token)
    blocks, tokens, width = refs[0].shape
    width_here = width // count_head
    me = lax.axis_index("head")
    order = list(range(1, count_head)) + [0]
    copies = {}
    for s in order:
        goal = lax.rem(me + s, count_head)
        for f, (source, start, size, at) in enumerate(fields):
            column = pl.multiple_of(goal * width_here + start, HD)
            copies[s, f] = pltpu.make_async_copy(
                ins[source].at[:, :, pl.ds(column, size)],
                buffer.at[s, :, :, pl.ds(at, size)],
                sems.at[s, f],
            )
            copies[s, f].start()
    sign = sign_matrix()
    for s in order:
        for f, (_, _, size, start) in enumerate(fields):
            copies[s, f].wait()
            flat = rows_of(buffer[s, :, :, start : start + size])
            heads = [flat[:, at : at + HD] for at in range(0, size, HD)]
            turned = jnp.dot(
                jnp.concatenate(heads, axis=0), sign, preferred_element_type=jnp.float32
            )
            turned = (turned * ROTATE_SCALE).reshape(size // HD, blocks, tokens, HD)
            for h in range(size // HD):
                at = start + h * HD
                outs[s][:, :, at : at + HD] = turned[h].astype(jnp.bfloat16)


def rotate_pieces(arrays, message, count_head, after=(), limit=VMEM):
    blocks, tokens, _ = arrays[0].shape
    fields, total = fields_of(message)
    sources = sorted({source for source, _, _ in message})
    one = (blocks, tokens, total)
    *pieces, token = pl.pallas_call(
        functools.partial(rotate_kernel, message, sources, count_head, len(after)),
        in_specs=[pl.BlockSpec(memory_space=pltpu.HBM)] * len(sources)
        + [pl.BlockSpec(memory_space=pl.ANY)] * len(after),
        out_specs=[pl.BlockSpec(memory_space=pltpu.VMEM)] * (count_head + 1),
        out_shape=[jax.ShapeDtypeStruct(one, jnp.bfloat16)] * count_head + [TOKEN],
        scratch_shapes=[
            pltpu.VMEM((count_head,) + one, jnp.bfloat16),
            pltpu.SemaphoreType.DMA((count_head, len(fields))),
        ],
        cost_estimate=NO_COST,
        compiler_params=pltpu.CompilerParams(vmem_limit_bytes=limit),
    )(*[arrays[source] for source in sources], *after)
    return pieces, token


def slots_at(distance, count_tm):
    return NEAR_CAP if distance in (1, count_tm - 1) else FAR_CAP


def pick_kernel(count_head, count_tm, lanes, skipped, picks_ref, *refs):
    pieces, outs = refs[:count_head], refs[count_head + skipped :]
    shard = lax.axis_index("tm")
    for distance, out in enumerate(outs, 1):
        goal = lax.rem(shard + distance, count_tm)
        for k in range(slots_at(distance, count_tm)):
            pick = picks_ref[NEAR_CAP * goal + k]
            for s in range(count_head):
                out[k, s] = pieces[s][pick, :, lanes[0] : lanes[1]]


def pick_blocks(picks, pieces, lanes, count_tm, after):
    count_head = len(pieces)
    one = (count_head, pieces[0].shape[1], lanes[1] - lanes[0])
    vmem = pl.BlockSpec(memory_space=pltpu.VMEM)
    return pl.pallas_call(
        functools.partial(pick_kernel, count_head, count_tm, lanes, len(after)),
        in_specs=[pl.BlockSpec(memory_space=pltpu.SMEM)]
        + [vmem] * count_head
        + [pl.BlockSpec(memory_space=pl.ANY)] * len(after),
        out_specs=[vmem] * (count_tm - 1),
        out_shape=[
            jax.ShapeDtypeStruct((slots_at(distance, count_tm),) + one, jnp.bfloat16)
            for distance in range(1, count_tm)
        ],
        cost_estimate=HIGH_COST,
        compiler_params=pltpu.CompilerParams(vmem_limit_bytes=VMEM),
    )(picks, *pieces, *after)


def remote_rows(count_tm):
    return [
        (distance, k)
        for distance in range(1, count_tm)
        for k in range(slots_at(distance, count_tm))
    ]


def split(value, by):
    if by & (by - 1) == 0:
        return value >> (by.bit_length() - 1), value & (by - 1)
    return lax.div(value, by), lax.rem(value, by)


def plan_kernel(count_head, count_tm, blocks, pair_ref, tokens_ref, _, picks_ref, bias_ref, named_ref, table_ref, sem):
    total_blocks, columns = pair_ref.shape
    pairs = pair_ref[...]
    lane = lax.broadcasted_iota(jnp.int32, named_ref.shape, 1)
    named = jnp.zeros(named_ref.shape, jnp.int32)
    for c in range(columns):
        named = jnp.where(pairs[:, c : c + 1] == lane, 1, named)
    named_ref[...] = named
    copy = pltpu.make_async_copy(named_ref, table_ref, sem)
    copy.start()
    copy.wait()
    shard = lax.axis_index("tm")
    place = lax.axis_index("head")
    mine = shard * blocks

    def two_picks(wanted):
        picks = [jnp.int32(0)] * NEAR_CAP
        count = jnp.int32(0)
        for j in range(blocks):
            for k in range(NEAR_CAP):
                picks[k] = jnp.where((wanted[j] > 0) & (count == k), j, picks[k])
            count = count + wanted[j]
        return picks, count

    def named_by(rows, column):
        found = table_ref[rows, column]
        for i in range(1, blocks):
            found = found | table_ref[rows + i, column]
        return found

    for d in range(count_tm):
        picks, _ = two_picks([named_by(d * blocks, mine + j) for j in range(blocks)])
        for k in range(NEAR_CAP):
            picks_ref[NEAR_CAP * d + k] = picks[k]

    kept = [[table_ref[mine + i, mine + j] * tokens_ref[mine + j] for j in range(blocks)] for i in range(blocks)]
    arrivals = {}
    for distance, k in remote_rows(count_tm):
        first = lax.rem(shard - distance + count_tm, count_tm) * blocks
        if k == 0:
            arrivals[distance] = two_picks([named_by(mine, first + j) for j in range(blocks)])
        picks, count = arrivals[distance]
        there = first + picks[k]
        live = jnp.where(count > k, tokens_ref[there], 0)
        for i in range(blocks):
            kept[i].append(table_ref[mine + i, there] * live)

    total = bias_ref.shape[1]
    piece_rows = BLK // count_head
    at = lax.broadcasted_iota(jnp.int32, (blocks, total), 1)
    query = lax.broadcasted_iota(jnp.int32, (blocks, total), 0)
    own = at < blocks * BLK
    group, token = split(at, piece_rows)
    own_piece, own_block = split(group, blocks)
    far_row, far_group = split(group, count_head)
    row = jnp.where(own, own_block, far_row)
    piece = jnp.where(own, own_piece, far_group)
    source = jnp.where(piece > place, place - piece + count_head, place - piece)
    position = source * piece_rows + token
    limit = jnp.zeros((blocks, total), jnp.int32)
    for r in range(len(kept[0])):
        value = jnp.zeros((blocks, total), jnp.int32)
        for i in range(blocks):
            value = jnp.where(query == i, kept[i][r], value)
        limit = jnp.where(row == r, value, limit)
    bias_ref[...] = jnp.where(position < limit, 0.0, NEG)


def plan(pair_list, block_tokens, after, blocks, count_head, count_tm):
    total_blocks = pair_list.shape[0]
    lanes = -(-total_blocks // 128) * 128
    total = (blocks + len(remote_rows(count_tm))) * BLK
    return pl.pallas_call(
        functools.partial(plan_kernel, count_head, count_tm, blocks),
        in_specs=[
            pl.BlockSpec(memory_space=pltpu.VMEM),
            pl.BlockSpec(memory_space=pltpu.SMEM),
            pl.BlockSpec(memory_space=pl.ANY),
        ],
        out_specs=[pl.BlockSpec(memory_space=pltpu.SMEM), pl.BlockSpec(memory_space=pltpu.VMEM)],
        out_shape=[
            jax.ShapeDtypeStruct((NEAR_CAP * count_tm,), jnp.int32),
            jax.ShapeDtypeStruct((blocks, total), jnp.float32),
        ],
        scratch_shapes=[
            pltpu.VMEM((total_blocks, lanes), jnp.int32),
            pltpu.SMEM((total_blocks, lanes), jnp.int32),
            pltpu.SemaphoreType.DMA,
        ],
        cost_estimate=NO_COST,
        compiler_params=pltpu.CompilerParams(vmem_limit_bytes=VMEM),
    )(pair_list, block_tokens, after)


def attend_kernel(counts, at, size, tokens_ref, bias_ref, *refs):
    count_head, count_tm, skipped = counts
    query_at, key_at = at
    queries, owns = refs[:count_head], refs[count_head : 2 * count_head]
    slots = refs[2 * count_head : 2 * count_head + count_tm - 1]
    outs = refs[2 * count_head + count_tm - 1 + skipped :]
    blocks, tokens, _ = owns[0].shape
    shard = lax.axis_index("tm")
    me = lax.axis_index("head")
    sign = sign_matrix()
    for h in range(size // HD):
        lanes = slice(h * HD, (h + 1) * HD)
        query_lanes = slice(query_at + h * HD, query_at + (h + 1) * HD)
        query = jnp.concatenate(
            [rows_of(queries[s][i, :, query_lanes]) for i in range(blocks) for s in range(count_head)],
            axis=0,
        )

        def gathered(kind):
            first = kind * size + h * HD
            own_lanes = slice(key_at + first, key_at + first + HD)
            pieces = [rows_of(own[:, :, own_lanes]) for own in owns]
            pieces += [
                rows_of(slots[distance - 1][k, :, :, first : first + HD])
                for distance, k in remote_rows(count_tm)
            ]
            return jnp.concatenate(pieces, axis=0)

        keys, values = gathered(0), gathered(1)
        total = keys.shape[0]
        dots = lax.dot_general(
            query, keys, (((1,), (1,)), ((), ())), preferred_element_type=jnp.float32
        )
        dots = dots.reshape(blocks, BLK, total) + bias_ref[...][:, None, :]
        peak = jnp.max(dots, axis=-1, keepdims=True)
        weights = jnp.exp2((dots - peak) * (SCORE_SCALE * LOG2E))
        denominator = jnp.sum(weights, axis=-1, keepdims=True).reshape(blocks * BLK, 1)
        weights_half = weights.astype(jnp.bfloat16).reshape(blocks * BLK, total)
        mixed = jnp.dot(weights_half, values, preferred_element_type=jnp.float32) / denominator
        turned = jnp.zeros_like(mixed)
        rest = mixed
        for _ in range(3):
            piece = rest.astype(jnp.bfloat16)
            turned = turned + jnp.dot(piece, sign, preferred_element_type=jnp.float32)
            rest = rest - piece.astype(jnp.float32)
        turned = (turned * ROTATE_SCALE).reshape(blocks, count_head, tokens, HD)
        token = lax.broadcasted_iota(jnp.int32, (tokens, HD), 0)
        for s in range(count_head):
            position = lax.rem(me - s + count_head, count_head) * tokens + token
            for i in range(blocks):
                outs[s][i, :, lanes] = jnp.where(
                    position < tokens_ref[shard * blocks + i], turned[i, s], 0.0
                ).astype(jnp.bfloat16)


def attend(block_tokens, bias, queries, query_at, owns, key_at, slots, size, after, cost):
    count_head, count_tm = len(owns), len(slots) + 1
    blocks, tokens, _ = owns[0].shape
    vmem = pl.BlockSpec(memory_space=pltpu.VMEM)
    return pl.pallas_call(
        functools.partial(
            attend_kernel, (count_head, count_tm, len(after)), (query_at, key_at), size
        ),
        in_specs=[pl.BlockSpec(memory_space=pltpu.SMEM)]
        + [vmem] * (2 * count_head + count_tm)
        + [pl.BlockSpec(memory_space=pl.ANY)] * len(after),
        out_specs=[vmem] * count_head,
        out_shape=[jax.ShapeDtypeStruct((blocks, tokens, size), jnp.bfloat16)] * count_head,
        cost_estimate=cost,
        compiler_params=pltpu.CompilerParams(vmem_limit_bytes=VMEM),
    )(block_tokens, bias, *queries, *owns, *slots, *after)


def place_kernel(count_head, starts, width_here, *refs):
    pieces, out_ref, sems = refs[:-2], refs[-2], refs[-1]
    me = lax.axis_index("head")
    copies = []
    for at, piece in enumerate(pieces):
        part, s = at // count_head, at % count_head
        column = lax.rem(me + s, count_head) * width_here + starts[part]
        copies.append(
            pltpu.make_async_copy(
                piece,
                out_ref.at[:, :, pl.ds(pl.multiple_of(column, HD), piece.shape[-1])],
                sems.at[at],
            )
        )
        copies[-1].start()
    for copy in copies:
        copy.wait()


def place_pieces(parts, starts, width_here):
    count_head = len(parts[0])
    pieces = [piece for part in parts for piece in part]
    blocks, tokens, _ = pieces[0].shape
    return pl.pallas_call(
        functools.partial(place_kernel, count_head, starts, width_here),
        in_specs=[pl.BlockSpec(memory_space=pl.ANY)] * len(pieces),
        out_specs=pl.BlockSpec(memory_space=pltpu.HBM),
        out_shape=jax.ShapeDtypeStruct((blocks, tokens, count_head * width_here), jnp.bfloat16),
        scratch_shapes=[pltpu.SemaphoreType.DMA((len(pieces),))],
        compiler_params=pltpu.CompilerParams(vmem_limit_bytes=VMEM),
    )(*pieces)


def shifted(array, axis, distance):
    count = lax.axis_size(axis)
    return lax.ppermute(array, axis, [(i, (i + distance) % count) for i in range(count)])


def exchange(pieces, direction):
    return [pieces[0]] + [
        shifted(piece, "head", direction * s) for s, piece in enumerate(pieces[1:], 1)
    ]


def forward(sent):
    return [shifted(block, "tm", distance) for distance, block in enumerate(sent, 1)]


def shards(query_rows, key_rows, value_rows, pair_list, block_tokens):
    count_head = lax.axis_size("head")
    count_tm = lax.axis_size("tm")
    blocks, tokens, width = query_rows.shape
    width_here = width // count_head
    heads = width_here // HD
    cut = (heads + 1) // 2 * HD
    parts = [(0, cut), (cut, width_here - cut)] if heads > 1 else [(0, width_here)]
    arrays = [query_rows, key_rows, value_rows]
    messages = []
    for at, part in enumerate(parts):
        message = [(1,) + part, (2,) + part]
        messages.append(message + ([(0,) + parts[at - 1]] if at else []))
    messages.append([(0,) + parts[-1]])
    key_at = [0] * len(parts)
    query_at = [2 * size for _, size in parts[1:]] + [0]

    pieces, token = rotate_pieces(arrays, messages[0], count_head, limit=WIDE_VMEM)
    packed = [pieces]
    picks, bias = plan(pair_list, block_tokens, token, blocks, count_head, count_tm)
    after = (bias,)
    for message in messages[1:-1]:
        pieces, token = rotate_pieces(arrays, message, count_head, after)
        packed.append(pieces)
        after = (token,)
    received = [exchange(pieces, 1) for pieces in packed]
    sent, after = [], ()
    for at, (_, size) in enumerate(parts):
        lanes = (key_at[at], key_at[at] + 2 * size)
        sent.append(pick_blocks(picks, received[at], lanes, count_tm, after))
        after = (sent[-1][0],)
        if not at:
            pieces, _ = rotate_pieces(arrays, messages[-1], count_head, after)
    received.append(exchange(pieces, 1))
    returned, after = [], ()
    for at, (_, size) in enumerate(parts):
        cost = NO_COST if at == len(parts) - 1 else HIGH_COST
        attended = attend(
            block_tokens, bias, received[at + 1], query_at[at], received[at], key_at[at],
            forward(sent[at]), size, after, cost,
        )
        after = (attended[0],)
        returned.append(exchange(attended, -1))
    return place_pieces(returned, [start for start, _ in parts], width_here)


def solution(mesh):
    placed = (
        P(("grp", "tm"), "head", None),
        P(("grp", "tm"), "head", None),
        P(("grp", "tm"), "head", None),
        P("grp", None),
        P("grp"),
    )
    return jax.shard_map(
        shards,
        mesh=mesh,
        in_specs=placed,
        out_specs=P(("grp", "tm"), "head", None),
        check_vma=False,
    )
```

```python
import functools
import math

import jax
import jax.numpy as jnp
from jax import lax
from jax.experimental import pallas as pl
from jax.experimental.pallas import tpu as pltpu
from jax.sharding import PartitionSpec as P

HD = 128
BLK = 64
NEAR_CAP = 2
FAR_CAP = 1
NEG = -1e30
ROTATE_SCALE = 1.0 / math.sqrt(HD)
SCORE_SCALE = 1.0 / math.sqrt(HD)
VMEM = 24 * 1024 * 1024
WIDE_VMEM = 60 * 1024 * 1024
TOKEN = jax.ShapeDtypeStruct((8, 128), jnp.float32)
NO_COST = pl.CostEstimate(flops=0, bytes_accessed=0, transcendentals=0)
HIGH_COST = pl.CostEstimate(flops=10**11, bytes_accessed=0, transcendentals=0)
LOG2E = math.log2(math.e)


def sign_matrix():
    common = lax.broadcasted_iota(jnp.int32, (HD, HD), 0) & lax.broadcasted_iota(
        jnp.int32, (HD, HD), 1
    )
    bits = HD.bit_length() - 1
    parity = common
    for bit in range(1, bits):
        parity = parity ^ (common >> bit)
    return jnp.where((parity & 1) == 0, 1.0, -1.0).astype(jnp.bfloat16)


def rows_of(block):
    rows, width = math.prod(block.shape[:-1]), block.shape[-1]
    if block.shape[-2] % 16 == 0:
        return block.reshape(rows, width)
    return block.astype(jnp.float32).reshape(rows, width).astype(block.dtype)


def fields_of(message):
    at, fields = 0, []
    for source, start, size in message:
        fields.append((source, start, size, at))
        at += size
    return fields, at


def by_distance(refs, count, direction):
    if len(refs) > 1:
        return list(refs)
    me = lax.axis_index("head")
    return [refs[0].at[lax.rem(me + direction * s + count, count)] for s in range(count)]


def rotate_kernel(message, sources, count_head, skipped, *refs):
    fields, total = fields_of(message)
    ins = dict(zip(sources, refs))
    outs = by_distance(refs[len(sources) + skipped : -3], count_head, 1)
    token, buffer, sems = refs[-3:]
    token[...] = jnp.zeros_like(token)
    blocks, tokens, width = refs[0].shape
    width_here = width // count_head
    me = lax.axis_index("head")
    order = list(range(1, count_head)) + [0]
    copies = {}
    for s in order:
        goal = lax.rem(me + s, count_head)
        for f, (source, start, size, at) in enumerate(fields):
            column = pl.multiple_of(goal * width_here + start, HD)
            copies[s, f] = pltpu.make_async_copy(
                ins[source].at[:, :, pl.ds(column, size)],
                buffer.at[s, :, :, pl.ds(at, size)],
                sems.at[s, f],
            )
            copies[s, f].start()
    sign = sign_matrix()
    for s in order:
        for f, (_, _, size, start) in enumerate(fields):
            copies[s, f].wait()
            flat = rows_of(buffer[s, :, :, start : start + size])
            heads = [flat[:, at : at + HD] for at in range(0, size, HD)]
            turned = jnp.dot(
                jnp.concatenate(heads, axis=0), sign, preferred_element_type=jnp.float32
            )
            turned = (turned * ROTATE_SCALE).reshape(size // HD, blocks, tokens, HD)
            for h in range(size // HD):
                at = start + h * HD
                outs[s][:, :, at : at + HD] = turned[h].astype(jnp.bfloat16)


def rotate_pieces(arrays, message, count_head, after=(), limit=VMEM, stacked=False):
    blocks, tokens, _ = arrays[0].shape
    fields, total = fields_of(message)
    sources = sorted({source for source, _, _ in message})
    one = (blocks, tokens, total)
    shapes = [(count_head,) + one] if stacked else [one] * count_head
    *pieces, token = pl.pallas_call(
        functools.partial(rotate_kernel, message, sources, count_head, len(after)),
        in_specs=[pl.BlockSpec(memory_space=pltpu.HBM)] * len(sources)
        + [pl.BlockSpec(memory_space=pl.ANY)] * len(after),
        out_specs=[pl.BlockSpec(memory_space=pltpu.VMEM)] * (len(shapes) + 1),
        out_shape=[jax.ShapeDtypeStruct(shape, jnp.bfloat16) for shape in shapes] + [TOKEN],
        scratch_shapes=[
            pltpu.VMEM((count_head,) + one, jnp.bfloat16),
            pltpu.SemaphoreType.DMA((count_head, len(fields))),
        ],
        cost_estimate=NO_COST,
        compiler_params=pltpu.CompilerParams(vmem_limit_bytes=limit),
    )(*[arrays[source] for source in sources], *after)
    return pieces, token


def slots_at(distance, count_tm):
    return NEAR_CAP if distance in (1, count_tm - 1) else FAR_CAP


def pick_kernel(count_head, count_tm, lanes, skipped, picks_ref, *refs):
    pieces, outs = refs[:count_head], refs[count_head + skipped :]
    shard = lax.axis_index("tm")
    for distance, out in enumerate(outs, 1):
        goal = lax.rem(shard + distance, count_tm)
        for k in range(slots_at(distance, count_tm)):
            pick = picks_ref[NEAR_CAP * goal + k]
            for s in range(count_head):
                out[k, s] = pieces[s][pick, :, lanes[0] : lanes[1]]


def pick_blocks(picks, pieces, lanes, count_tm, after):
    count_head = len(pieces)
    one = (count_head, pieces[0].shape[1], lanes[1] - lanes[0])
    vmem = pl.BlockSpec(memory_space=pltpu.VMEM)
    return pl.pallas_call(
        functools.partial(pick_kernel, count_head, count_tm, lanes, len(after)),
        in_specs=[pl.BlockSpec(memory_space=pltpu.SMEM)]
        + [vmem] * count_head
        + [pl.BlockSpec(memory_space=pl.ANY)] * len(after),
        out_specs=[vmem] * (count_tm - 1),
        out_shape=[
            jax.ShapeDtypeStruct((slots_at(distance, count_tm),) + one, jnp.bfloat16)
            for distance in range(1, count_tm)
        ],
        cost_estimate=HIGH_COST,
        compiler_params=pltpu.CompilerParams(vmem_limit_bytes=VMEM),
    )(picks, *pieces, *after)


def remote_rows(count_tm):
    return [
        (distance, k)
        for distance in range(1, count_tm)
        for k in range(slots_at(distance, count_tm))
    ]


def split(value, by):
    if by & (by - 1) == 0:
        return value >> (by.bit_length() - 1), value & (by - 1)
    return lax.div(value, by), lax.rem(value, by)


def plan_kernel(count_head, count_tm, blocks, pair_ref, tokens_ref, _, picks_ref, bias_ref, named_ref, table_ref, sem):
    total_blocks, columns = pair_ref.shape
    pairs = pair_ref[...]
    lane = lax.broadcasted_iota(jnp.int32, named_ref.shape, 1)
    named = jnp.zeros(named_ref.shape, jnp.int32)
    for c in range(columns):
        named = jnp.where(pairs[:, c : c + 1] == lane, 1, named)
    named_ref[...] = named
    copy = pltpu.make_async_copy(named_ref, table_ref, sem)
    copy.start()
    copy.wait()
    shard = lax.axis_index("tm")
    place = lax.axis_index("head")
    mine = shard * blocks

    def two_picks(wanted):
        picks = [jnp.int32(0)] * NEAR_CAP
        count = jnp.int32(0)
        for j in range(blocks):
            for k in range(NEAR_CAP):
                picks[k] = jnp.where((wanted[j] > 0) & (count == k), j, picks[k])
            count = count + wanted[j]
        return picks, count

    def named_by(rows, column):
        found = table_ref[rows, column]
        for i in range(1, blocks):
            found = found | table_ref[rows + i, column]
        return found

    for d in range(count_tm):
        picks, _ = two_picks([named_by(d * blocks, mine + j) for j in range(blocks)])
        for k in range(NEAR_CAP):
            picks_ref[NEAR_CAP * d + k] = picks[k]

    kept = [[table_ref[mine + i, mine + j] * tokens_ref[mine + j] for j in range(blocks)] for i in range(blocks)]
    arrivals = {}
    for distance, k in remote_rows(count_tm):
        first = lax.rem(shard - distance + count_tm, count_tm) * blocks
        if k == 0:
            arrivals[distance] = two_picks([named_by(mine, first + j) for j in range(blocks)])
        picks, count = arrivals[distance]
        there = first + picks[k]
        live = jnp.where(count > k, tokens_ref[there], 0)
        for i in range(blocks):
            kept[i].append(table_ref[mine + i, there] * live)

    total = bias_ref.shape[1]
    piece_rows = BLK // count_head
    at = lax.broadcasted_iota(jnp.int32, (blocks, total), 1)
    query = lax.broadcasted_iota(jnp.int32, (blocks, total), 0)
    own = at < blocks * BLK
    group, token = split(at, piece_rows)
    own_piece, own_block = split(group, blocks)
    far_row, far_group = split(group, count_head)
    row = jnp.where(own, own_block, far_row)
    piece = jnp.where(own, own_piece, far_group)
    source = jnp.where(piece > place, place - piece + count_head, place - piece)
    position = source * piece_rows + token
    limit = jnp.zeros((blocks, total), jnp.int32)
    for r in range(len(kept[0])):
        value = jnp.zeros((blocks, total), jnp.int32)
        for i in range(blocks):
            value = jnp.where(query == i, kept[i][r], value)
        limit = jnp.where(row == r, value, limit)
    bias_ref[...] = jnp.where(position < limit, 0.0, NEG)


def plan(pair_list, block_tokens, after, blocks, count_head, count_tm):
    total_blocks = pair_list.shape[0]
    lanes = -(-total_blocks // 128) * 128
    total = (blocks + len(remote_rows(count_tm))) * BLK
    return pl.pallas_call(
        functools.partial(plan_kernel, count_head, count_tm, blocks),
        in_specs=[
            pl.BlockSpec(memory_space=pltpu.VMEM),
            pl.BlockSpec(memory_space=pltpu.SMEM),
            pl.BlockSpec(memory_space=pl.ANY),
        ],
        out_specs=[pl.BlockSpec(memory_space=pltpu.SMEM), pl.BlockSpec(memory_space=pltpu.VMEM)],
        out_shape=[
            jax.ShapeDtypeStruct((NEAR_CAP * count_tm,), jnp.int32),
            jax.ShapeDtypeStruct((blocks, total), jnp.float32),
        ],
        scratch_shapes=[
            pltpu.VMEM((total_blocks, lanes), jnp.int32),
            pltpu.SMEM((total_blocks, lanes), jnp.int32),
            pltpu.SemaphoreType.DMA,
        ],
        cost_estimate=NO_COST,
        compiler_params=pltpu.CompilerParams(vmem_limit_bytes=VMEM),
    )(pair_list, block_tokens, after)


def attend_kernel(counts, at, size, tokens_ref, bias_ref, *refs):
    count_head, count_tm, query_count, skipped = counts
    query_at, key_at = at
    queries, refs = by_distance(refs[:query_count], count_head, -1), refs[query_count:]
    owns, slots = refs[:count_head], refs[count_head : count_head + count_tm - 1]
    outs = refs[count_head + count_tm - 1 + skipped :]
    blocks, tokens, _ = owns[0].shape
    shard = lax.axis_index("tm")
    me = lax.axis_index("head")
    sign = sign_matrix()
    for h in range(size // HD):
        lanes = slice(h * HD, (h + 1) * HD)
        query_lanes = slice(query_at + h * HD, query_at + (h + 1) * HD)
        query = jnp.concatenate(
            [rows_of(queries[s][i, :, query_lanes]) for i in range(blocks) for s in range(count_head)],
            axis=0,
        )

        def gathered(kind):
            first = kind * size + h * HD
            own_lanes = slice(key_at + first, key_at + first + HD)
            pieces = [rows_of(own[:, :, own_lanes]) for own in owns]
            pieces += [
                rows_of(slots[distance - 1][k, :, :, first : first + HD])
                for distance, k in remote_rows(count_tm)
            ]
            return jnp.concatenate(pieces, axis=0)

        keys, values = gathered(0), gathered(1)
        total = keys.shape[0]
        dots = lax.dot_general(
            query, keys, (((1,), (1,)), ((), ())), preferred_element_type=jnp.float32
        )
        dots = dots.reshape(blocks, BLK, total) + bias_ref[...][:, None, :]
        peak = jnp.max(dots, axis=-1, keepdims=True)
        weights = jnp.exp2((dots - peak) * (SCORE_SCALE * LOG2E))
        denominator = jnp.sum(weights, axis=-1, keepdims=True).reshape(blocks * BLK, 1)
        weights_half = weights.astype(jnp.bfloat16).reshape(blocks * BLK, total)
        mixed = jnp.dot(weights_half, values, preferred_element_type=jnp.float32) / denominator
        turned = jnp.zeros_like(mixed)
        rest = mixed
        for _ in range(3):
            piece = rest.astype(jnp.bfloat16)
            turned = turned + jnp.dot(piece, sign, preferred_element_type=jnp.float32)
            rest = rest - piece.astype(jnp.float32)
        turned = (turned * ROTATE_SCALE).reshape(blocks, count_head, tokens, HD)
        token = lax.broadcasted_iota(jnp.int32, (tokens, HD), 0)
        for s in range(count_head):
            position = lax.rem(me - s + count_head, count_head) * tokens + token
            for i in range(blocks):
                outs[s][i, :, lanes] = jnp.where(
                    position < tokens_ref[shard * blocks + i], turned[i, s], 0.0
                ).astype(jnp.bfloat16)


def attend(block_tokens, bias, queries, query_at, owns, key_at, slots, size, after, cost):
    count_head, count_tm = len(owns), len(slots) + 1
    blocks, tokens, _ = owns[0].shape
    vmem = pl.BlockSpec(memory_space=pltpu.VMEM)
    return pl.pallas_call(
        functools.partial(
            attend_kernel,
            (count_head, count_tm, len(queries), len(after)),
            (query_at, key_at),
            size,
        ),
        in_specs=[pl.BlockSpec(memory_space=pltpu.SMEM)]
        + [vmem] * (len(queries) + count_head + count_tm)
        + [pl.BlockSpec(memory_space=pl.ANY)] * len(after),
        out_specs=[vmem] * count_head,
        out_shape=[jax.ShapeDtypeStruct((blocks, tokens, size), jnp.bfloat16)] * count_head,
        cost_estimate=cost,
        compiler_params=pltpu.CompilerParams(vmem_limit_bytes=VMEM),
    )(block_tokens, bias, *queries, *owns, *slots, *after)


def place_kernel(count_head, starts, width_here, *refs):
    pieces, out_ref, sems = refs[:-2], refs[-2], refs[-1]
    me = lax.axis_index("head")
    copies = []
    for at, piece in enumerate(pieces):
        part, s = at // count_head, at % count_head
        column = lax.rem(me + s, count_head) * width_here + starts[part]
        copies.append(
            pltpu.make_async_copy(
                piece,
                out_ref.at[:, :, pl.ds(pl.multiple_of(column, HD), piece.shape[-1])],
                sems.at[at],
            )
        )
        copies[-1].start()
    for copy in copies:
        copy.wait()


def place_pieces(parts, starts, width_here):
    count_head = len(parts[0])
    pieces = [piece for part in parts for piece in part]
    blocks, tokens, _ = pieces[0].shape
    return pl.pallas_call(
        functools.partial(place_kernel, count_head, starts, width_here),
        in_specs=[pl.BlockSpec(memory_space=pl.ANY)] * len(pieces),
        out_specs=pl.BlockSpec(memory_space=pltpu.HBM),
        out_shape=jax.ShapeDtypeStruct((blocks, tokens, count_head * width_here), jnp.bfloat16),
        scratch_shapes=[pltpu.SemaphoreType.DMA((len(pieces),))],
        compiler_params=pltpu.CompilerParams(vmem_limit_bytes=VMEM),
    )(*pieces)


def shifted(array, axis, distance):
    count = lax.axis_size(axis)
    return lax.ppermute(array, axis, [(i, (i + distance) % count) for i in range(count)])


def exchange(pieces, direction):
    return [pieces[0]] + [
        shifted(piece, "head", direction * s) for s, piece in enumerate(pieces[1:], 1)
    ]


def forward(sent):
    return [shifted(block, "tm", distance) for distance, block in enumerate(sent, 1)]


def shards(query_rows, key_rows, value_rows, pair_list, block_tokens):
    count_head = lax.axis_size("head")
    count_tm = lax.axis_size("tm")
    blocks, tokens, width = query_rows.shape
    width_here = width // count_head
    heads = width_here // HD
    cut = (heads + 1) // 2 * HD
    parts = [(0, cut), (cut, width_here - cut)] if heads > 1 else [(0, width_here)]
    arrays = [query_rows, key_rows, value_rows]
    messages = [[(1,) + part, (2,) + part] for part in parts]
    pieces, token = rotate_pieces(arrays, messages[0], count_head, limit=WIDE_VMEM)
    packed = [pieces]
    picks, bias = plan(pair_list, block_tokens, token, blocks, count_head, count_tm)
    after = (bias,)
    for message in messages[1:]:
        pieces, token = rotate_pieces(arrays, message, count_head, after)
        packed.append(pieces)
        after = (token,)
    received = [exchange(pieces, 1) for pieces in packed]
    sent, after = [], ()
    for owns, (_, size) in zip(received, parts):
        sent.append(pick_blocks(picks, owns, (0, 2 * size), count_tm, after))
        after = (sent[-1][0],)
    message = [(0, 0, width_here)]
    (query,), _ = rotate_pieces(arrays, message, count_head, (sent[0][0],), stacked=True)
    query = lax.all_to_all(query, "head", split_axis=0, concat_axis=0, tiled=True)
    returned, after = [], ()
    for at, (start, size) in enumerate(parts):
        cost = NO_COST if at == len(parts) - 1 else HIGH_COST
        attended = attend(
            block_tokens, bias, [query], start, received[at], 0, forward(sent[at]), size, after, cost
        )
        after = (attended[0],)
        returned.append(exchange(attended, -1))
    return place_pieces(returned, [start for start, _ in parts], width_here)


def solution(mesh):
    placed = (
        P(("grp", "tm"), "head", None),
        P(("grp", "tm"), "head", None),
        P(("grp", "tm"), "head", None),
        P("grp", None),
        P("grp"),
    )
    return jax.shard_map(
        shards,
        mesh=mesh,
        in_specs=placed,
        out_specs=P(("grp", "tm"), "head", None),
        check_vma=False,
    )
```

```python
import functools
import math

import jax
import jax.numpy as jnp
from jax import lax
from jax.experimental import pallas as pl
from jax.experimental.pallas import tpu as pltpu
from jax.sharding import PartitionSpec as P

HD = 128
BLK = 64
NEAR_CAP = 2
FAR_CAP = 1
NEG = -1e30
ROTATE_SCALE = 1.0 / math.sqrt(HD)
SCORE_SCALE = 1.0 / math.sqrt(HD)
VMEM = 24 * 1024 * 1024
WIDE_VMEM = 60 * 1024 * 1024
TOKEN = jax.ShapeDtypeStruct((8, 128), jnp.float32)
NO_COST = pl.CostEstimate(flops=0, bytes_accessed=0, transcendentals=0)
HIGH_COST = pl.CostEstimate(flops=10**11, bytes_accessed=0, transcendentals=0)
LOG2E = math.log2(math.e)


def sign_matrix():
    common = lax.broadcasted_iota(jnp.int32, (HD, HD), 0) & lax.broadcasted_iota(
        jnp.int32, (HD, HD), 1
    )
    bits = HD.bit_length() - 1
    parity = common
    for bit in range(1, bits):
        parity = parity ^ (common >> bit)
    return jnp.where((parity & 1) == 0, 1.0, -1.0).astype(jnp.bfloat16)


def rows_of(block):
    rows, width = math.prod(block.shape[:-1]), block.shape[-1]
    if block.shape[-2] % 16 == 0:
        return block.reshape(rows, width)
    return block.astype(jnp.float32).reshape(rows, width).astype(block.dtype)


def fields_of(message):
    at, fields = 0, []
    for source, start, size in message:
        fields.append((source, start, size, at))
        at += size
    return fields, at


def by_distance(refs, count, direction):
    if len(refs) > 1:
        return list(refs)
    me = lax.axis_index("head")
    return [refs[0].at[lax.rem(me + direction * s + count, count)] for s in range(count)]


def rotate_kernel(message, sources, count_head, skipped, *refs):
    fields, total = fields_of(message)
    ins = dict(zip(sources, refs))
    outs = by_distance(refs[len(sources) + skipped : -3], count_head, 1)
    token, buffer, sems = refs[-3:]
    token[...] = jnp.zeros_like(token)
    blocks, tokens, width = refs[0].shape
    width_here = width // count_head
    me = lax.axis_index("head")
    order = list(range(1, count_head)) + [0]
    copies = {}
    for s in order:
        goal = lax.rem(me + s, count_head)
        for f, (source, start, size, at) in enumerate(fields):
            column = pl.multiple_of(goal * width_here + start, HD)
            copies[s, f] = pltpu.make_async_copy(
                ins[source].at[:, :, pl.ds(column, size)],
                buffer.at[s, :, :, pl.ds(at, size)],
                sems.at[s, f],
            )
            copies[s, f].start()
    sign = sign_matrix()
    for s in order:
        for f, (_, _, size, start) in enumerate(fields):
            copies[s, f].wait()
            flat = rows_of(buffer[s, :, :, start : start + size])
            heads = [flat[:, at : at + HD] for at in range(0, size, HD)]
            turned = jnp.dot(
                jnp.concatenate(heads, axis=0), sign, preferred_element_type=jnp.float32
            )
            turned = (turned * ROTATE_SCALE).reshape(size // HD, blocks, tokens, HD)
            for h in range(size // HD):
                at = start + h * HD
                outs[s][:, :, at : at + HD] = turned[h].astype(jnp.bfloat16)


def rotate_pieces(arrays, message, count_head, after=(), limit=VMEM, stacked=False):
    blocks, tokens, _ = arrays[0].shape
    fields, total = fields_of(message)
    sources = sorted({source for source, _, _ in message})
    one = (blocks, tokens, total)
    shapes = [(count_head,) + one] if stacked else [one] * count_head
    *pieces, token = pl.pallas_call(
        functools.partial(rotate_kernel, message, sources, count_head, len(after)),
        in_specs=[pl.BlockSpec(memory_space=pltpu.HBM)] * len(sources)
        + [pl.BlockSpec(memory_space=pl.ANY)] * len(after),
        out_specs=[pl.BlockSpec(memory_space=pltpu.VMEM)] * (len(shapes) + 1),
        out_shape=[jax.ShapeDtypeStruct(shape, jnp.bfloat16) for shape in shapes] + [TOKEN],
        scratch_shapes=[
            pltpu.VMEM((count_head,) + one, jnp.bfloat16),
            pltpu.SemaphoreType.DMA((count_head, len(fields))),
        ],
        cost_estimate=NO_COST,
        compiler_params=pltpu.CompilerParams(vmem_limit_bytes=limit),
    )(*[arrays[source] for source in sources], *after)
    return pieces, token


def slots_at(distance, count_tm):
    return NEAR_CAP if distance in (1, count_tm - 1) else FAR_CAP


def pick_kernel(count_head, count_tm, lanes, skipped, picks_ref, *refs):
    pieces, outs = refs[:count_head], refs[count_head + skipped :]
    shard = lax.axis_index("tm")
    for distance, out in enumerate(outs, 1):
        goal = lax.rem(shard + distance, count_tm)
        for k in range(slots_at(distance, count_tm)):
            pick = picks_ref[NEAR_CAP * goal + k]
            for s in range(count_head):
                out[k, s] = pieces[s][pick, :, lanes[0] : lanes[1]]


def pick_blocks(picks, pieces, lanes, count_tm, after):
    count_head = len(pieces)
    one = (count_head, pieces[0].shape[1], lanes[1] - lanes[0])
    vmem = pl.BlockSpec(memory_space=pltpu.VMEM)
    return pl.pallas_call(
        functools.partial(pick_kernel, count_head, count_tm, lanes, len(after)),
        in_specs=[pl.BlockSpec(memory_space=pltpu.SMEM)]
        + [vmem] * count_head
        + [pl.BlockSpec(memory_space=pl.ANY)] * len(after),
        out_specs=[vmem] * (count_tm - 1),
        out_shape=[
            jax.ShapeDtypeStruct((slots_at(distance, count_tm),) + one, jnp.bfloat16)
            for distance in range(1, count_tm)
        ],
        cost_estimate=HIGH_COST,
        compiler_params=pltpu.CompilerParams(vmem_limit_bytes=VMEM),
    )(picks, *pieces, *after)


def remote_rows(count_tm):
    return [
        (distance, k)
        for distance in range(1, count_tm)
        for k in range(slots_at(distance, count_tm))
    ]


def split(value, by):
    if by & (by - 1) == 0:
        return value >> (by.bit_length() - 1), value & (by - 1)
    return lax.div(value, by), lax.rem(value, by)


def plan_kernel(count_head, count_tm, blocks, pair_ref, tokens_ref, _, picks_ref, bias_ref, named_ref, table_ref, sem):
    total_blocks, columns = pair_ref.shape
    pairs = pair_ref[...]
    lane = lax.broadcasted_iota(jnp.int32, named_ref.shape, 1)
    named = jnp.zeros(named_ref.shape, jnp.int32)
    for c in range(columns):
        named = jnp.where(pairs[:, c : c + 1] == lane, 1, named)
    named_ref[...] = named
    copy = pltpu.make_async_copy(named_ref, table_ref, sem)
    copy.start()
    copy.wait()
    shard = lax.axis_index("tm")
    place = lax.axis_index("head")
    mine = shard * blocks

    def two_picks(wanted):
        picks = [jnp.int32(0)] * NEAR_CAP
        count = jnp.int32(0)
        for j in range(blocks):
            for k in range(NEAR_CAP):
                picks[k] = jnp.where((wanted[j] > 0) & (count == k), j, picks[k])
            count = count + wanted[j]
        return picks, count

    def named_by(rows, column):
        found = table_ref[rows, column]
        for i in range(1, blocks):
            found = found | table_ref[rows + i, column]
        return found

    for d in range(count_tm):
        picks, _ = two_picks([named_by(d * blocks, mine + j) for j in range(blocks)])
        for k in range(NEAR_CAP):
            picks_ref[NEAR_CAP * d + k] = picks[k]

    kept = [[table_ref[mine + i, mine + j] * tokens_ref[mine + j] for j in range(blocks)] for i in range(blocks)]
    arrivals = {}
    for distance, k in remote_rows(count_tm):
        first = lax.rem(shard - distance + count_tm, count_tm) * blocks
        if k == 0:
            arrivals[distance] = two_picks([named_by(mine, first + j) for j in range(blocks)])
        picks, count = arrivals[distance]
        there = first + picks[k]
        live = jnp.where(count > k, tokens_ref[there], 0)
        for i in range(blocks):
            kept[i].append(table_ref[mine + i, there] * live)

    total = bias_ref.shape[1]
    piece_rows = BLK // count_head
    at = lax.broadcasted_iota(jnp.int32, (blocks, total), 1)
    query = lax.broadcasted_iota(jnp.int32, (blocks, total), 0)
    own = at < blocks * BLK
    group, token = split(at, piece_rows)
    own_piece, own_block = split(group, blocks)
    far_row, far_group = split(group, count_head)
    row = jnp.where(own, own_block, far_row)
    piece = jnp.where(own, own_piece, far_group)
    source = jnp.where(piece > place, place - piece + count_head, place - piece)
    position = source * piece_rows + token
    limit = jnp.zeros((blocks, total), jnp.int32)
    for r in range(len(kept[0])):
        value = jnp.zeros((blocks, total), jnp.int32)
        for i in range(blocks):
            value = jnp.where(query == i, kept[i][r], value)
        limit = jnp.where(row == r, value, limit)
    bias_ref[...] = jnp.where(position < limit, 0.0, NEG)


def plan(pair_list, block_tokens, after, blocks, count_head, count_tm):
    total_blocks = pair_list.shape[0]
    lanes = -(-total_blocks // 128) * 128
    total = (blocks + len(remote_rows(count_tm))) * BLK
    return pl.pallas_call(
        functools.partial(plan_kernel, count_head, count_tm, blocks),
        in_specs=[
            pl.BlockSpec(memory_space=pltpu.VMEM),
            pl.BlockSpec(memory_space=pltpu.SMEM),
            pl.BlockSpec(memory_space=pl.ANY),
        ],
        out_specs=[pl.BlockSpec(memory_space=pltpu.SMEM), pl.BlockSpec(memory_space=pltpu.VMEM)],
        out_shape=[
            jax.ShapeDtypeStruct((NEAR_CAP * count_tm,), jnp.int32),
            jax.ShapeDtypeStruct((blocks, total), jnp.float32),
        ],
        scratch_shapes=[
            pltpu.VMEM((total_blocks, lanes), jnp.int32),
            pltpu.SMEM((total_blocks, lanes), jnp.int32),
            pltpu.SemaphoreType.DMA,
        ],
        cost_estimate=NO_COST,
        compiler_params=pltpu.CompilerParams(vmem_limit_bytes=VMEM),
    )(pair_list, block_tokens, after)


def attend_kernel(counts, at, size, tokens_ref, bias_ref, *refs):
    count_head, count_tm, query_count, skipped = counts
    query_at, key_at = at
    queries, refs = by_distance(refs[:query_count], count_head, -1), refs[query_count:]
    owns, slots = refs[:count_head], refs[count_head : count_head + count_tm - 1]
    outs = refs[count_head + count_tm - 1 + skipped :]
    blocks, tokens, _ = owns[0].shape
    shard = lax.axis_index("tm")
    me = lax.axis_index("head")
    sign = sign_matrix()
    for h in range(size // HD):
        lanes = slice(h * HD, (h + 1) * HD)
        query_lanes = slice(query_at + h * HD, query_at + (h + 1) * HD)
        query = jnp.concatenate(
            [rows_of(queries[s][i, :, query_lanes]) for i in range(blocks) for s in range(count_head)],
            axis=0,
        )

        def gathered(kind):
            first = kind * size + h * HD
            own_lanes = slice(key_at + first, key_at + first + HD)
            pieces = [rows_of(own[:, :, own_lanes]) for own in owns]
            pieces += [
                rows_of(slots[distance - 1][k, :, :, first : first + HD])
                for distance, k in remote_rows(count_tm)
            ]
            return jnp.concatenate(pieces, axis=0)

        keys, values = gathered(0), gathered(1)
        total = keys.shape[0]
        dots = lax.dot_general(
            query, keys, (((1,), (1,)), ((), ())), preferred_element_type=jnp.float32
        )
        dots = dots.reshape(blocks, BLK, total) + bias_ref[...][:, None, :]
        peak = jnp.max(dots, axis=-1, keepdims=True)
        weights = jnp.exp2((dots - peak) * (SCORE_SCALE * LOG2E))
        denominator = jnp.sum(weights, axis=-1, keepdims=True).reshape(blocks * BLK, 1)
        weights_half = weights.astype(jnp.bfloat16).reshape(blocks * BLK, total)
        mixed = jnp.dot(weights_half, values, preferred_element_type=jnp.float32) / denominator
        turned = jnp.zeros_like(mixed)
        rest = mixed
        for _ in range(3):
            piece = rest.astype(jnp.bfloat16)
            turned = turned + jnp.dot(piece, sign, preferred_element_type=jnp.float32)
            rest = rest - piece.astype(jnp.float32)
        turned = (turned * ROTATE_SCALE).reshape(blocks, count_head, tokens, HD)
        token = lax.broadcasted_iota(jnp.int32, (tokens, HD), 0)
        for s in range(count_head):
            position = lax.rem(me - s + count_head, count_head) * tokens + token
            for i in range(blocks):
                outs[s][i, :, lanes] = jnp.where(
                    position < tokens_ref[shard * blocks + i], turned[i, s], 0.0
                ).astype(jnp.bfloat16)


def attend(block_tokens, bias, queries, query_at, owns, key_at, slots, size, after, cost):
    count_head, count_tm = len(owns), len(slots) + 1
    blocks, tokens, _ = owns[0].shape
    vmem = pl.BlockSpec(memory_space=pltpu.VMEM)
    return pl.pallas_call(
        functools.partial(
            attend_kernel,
            (count_head, count_tm, len(queries), len(after)),
            (query_at, key_at),
            size,
        ),
        in_specs=[pl.BlockSpec(memory_space=pltpu.SMEM)]
        + [vmem] * (len(queries) + count_head + count_tm)
        + [pl.BlockSpec(memory_space=pl.ANY)] * len(after),
        out_specs=[vmem] * count_head,
        out_shape=[jax.ShapeDtypeStruct((blocks, tokens, size), jnp.bfloat16)] * count_head,
        cost_estimate=cost,
        compiler_params=pltpu.CompilerParams(vmem_limit_bytes=VMEM),
    )(block_tokens, bias, *queries, *owns, *slots, *after)


def place_kernel(count_head, starts, width_here, *refs):
    pieces, out_ref, sems = refs[:-2], refs[-2], refs[-1]
    me = lax.axis_index("head")
    copies = []
    for at, piece in enumerate(pieces):
        part, s = at // count_head, at % count_head
        column = lax.rem(me + s, count_head) * width_here + starts[part]
        copies.append(
            pltpu.make_async_copy(
                piece,
                out_ref.at[:, :, pl.ds(pl.multiple_of(column, HD), piece.shape[-1])],
                sems.at[at],
            )
        )
        copies[-1].start()
    for copy in copies:
        copy.wait()


def place_pieces(parts, starts, width_here):
    count_head = len(parts[0])
    pieces = [piece for part in parts for piece in part]
    blocks, tokens, _ = pieces[0].shape
    return pl.pallas_call(
        functools.partial(place_kernel, count_head, starts, width_here),
        in_specs=[pl.BlockSpec(memory_space=pl.ANY)] * len(pieces),
        out_specs=pl.BlockSpec(memory_space=pltpu.HBM),
        out_shape=jax.ShapeDtypeStruct((blocks, tokens, count_head * width_here), jnp.bfloat16),
        scratch_shapes=[pltpu.SemaphoreType.DMA((len(pieces),))],
        compiler_params=pltpu.CompilerParams(vmem_limit_bytes=VMEM),
    )(*pieces)


def shifted(array, axis, distance):
    count = lax.axis_size(axis)
    return lax.ppermute(array, axis, [(i, (i + distance) % count) for i in range(count)])


def exchange(pieces, direction):
    return [pieces[0]] + [
        shifted(piece, "head", direction * s) for s, piece in enumerate(pieces[1:], 1)
    ]


def forward(sent):
    return [shifted(block, "tm", distance) for distance, block in enumerate(sent, 1)]


def shards(query_rows, key_rows, value_rows, pair_list, block_tokens):
    count_head = lax.axis_size("head")
    count_tm = lax.axis_size("tm")
    blocks, tokens, width = query_rows.shape
    width_here = width // count_head
    heads = width_here // HD
    cut = (heads + 1) // 2 * HD
    parts = [(0, cut), (cut, width_here - cut)] if heads > 1 else [(0, width_here)]
    arrays = [query_rows, key_rows, value_rows]
    messages = []
    for at, part in enumerate(parts):
        message = [(1,) + part, (2,) + part]
        messages.append(message + ([(0,) + parts[at - 1]] if at else []))
    query_at = [2 * size for _, size in parts[1:]] + [0]
    pieces, token = rotate_pieces(arrays, messages[0], count_head, limit=WIDE_VMEM)
    packed = [pieces]
    picks, bias = plan(pair_list, block_tokens, token, blocks, count_head, count_tm)
    after = (bias,)
    for message in messages[1:]:
        pieces, token = rotate_pieces(arrays, message, count_head, after)
        packed.append(pieces)
        after = (token,)
    received = [exchange(pieces, 1) for pieces in packed]
    sent, after = [], ()
    for owns, (_, size) in zip(received, parts):
        sent.append(pick_blocks(picks, owns, (0, 2 * size), count_tm, after))
        after = (sent[-1][0],)
    message = [(0,) + parts[-1]]
    (query,), _ = rotate_pieces(arrays, message, count_head, (sent[0][0],), stacked=True)
    query = lax.all_to_all(query, "head", split_axis=0, concat_axis=0, tiled=True)
    queries = received[1:] + [[query]]
    returned, after = [], ()
    for at, (_, size) in enumerate(parts):
        attended = attend(
            block_tokens, bias, queries[at], query_at[at], received[at], 0,
            forward(sent[at]), size, after, NO_COST,
        )
        after = (attended[0],)
        returned.append(exchange(attended, -1))
    return place_pieces(returned, [start for start, _ in parts], width_here)


def solution(mesh):
    placed = (
        P(("grp", "tm"), "head", None),
        P(("grp", "tm"), "head", None),
        P(("grp", "tm"), "head", None),
        P("grp", None),
        P("grp"),
    )
    return jax.shard_map(
        shards,
        mesh=mesh,
        in_specs=placed,
        out_specs=P(("grp", "tm"), "head", None),
        check_vma=False,
    )
```

```python
import functools
import math

import jax
import jax.numpy as jnp
from jax import lax
from jax.experimental import pallas as pl
from jax.experimental.pallas import tpu as pltpu
from jax.sharding import PartitionSpec as P

HD = 128
BLK = 64
NEAR_CAP = 2
FAR_CAP = 1
NEG = -1e30
ROTATE_SCALE = 1.0 / math.sqrt(HD)
SCORE_SCALE = 1.0 / math.sqrt(HD)
VMEM = 24 * 1024 * 1024
WIDE_VMEM = 60 * 1024 * 1024
TOKEN = jax.ShapeDtypeStruct((8, 128), jnp.float32)
NO_COST = pl.CostEstimate(flops=0, bytes_accessed=0, transcendentals=0)
HIGH_COST = pl.CostEstimate(flops=10**11, bytes_accessed=0, transcendentals=0)
LOG2E = math.log2(math.e)


def sign_matrix():
    common = lax.broadcasted_iota(jnp.int32, (HD, HD), 0) & lax.broadcasted_iota(
        jnp.int32, (HD, HD), 1
    )
    bits = HD.bit_length() - 1
    parity = common
    for bit in range(1, bits):
        parity = parity ^ (common >> bit)
    return jnp.where((parity & 1) == 0, 1.0, -1.0).astype(jnp.bfloat16)


def rows_of(block):
    rows, width = math.prod(block.shape[:-1]), block.shape[-1]
    if block.shape[-2] % 16 == 0:
        return block.reshape(rows, width)
    return block.astype(jnp.float32).reshape(rows, width).astype(block.dtype)


def fields_of(message):
    at, fields = 0, []
    for source, start, size in message:
        fields.append((source, start, size, at))
        at += size
    return fields, at


def by_distance(refs, count, direction):
    if len(refs) > 1:
        return list(refs)
    me = lax.axis_index("head")
    return [refs[0].at[lax.rem(me + direction * s + count, count)] for s in range(count)]


def rotate_kernel(message, sources, count_head, skipped, *refs):
    fields, total = fields_of(message)
    ins = dict(zip(sources, refs))
    outs = by_distance(refs[len(sources) + skipped : -3], count_head, 1)
    token, buffer, sems = refs[-3:]
    token[...] = jnp.zeros_like(token)
    blocks, tokens, width = refs[0].shape
    width_here = width // count_head
    me = lax.axis_index("head")
    order = list(range(1, count_head)) + [0]
    copies = {}
    for s in order:
        goal = lax.rem(me + s, count_head)
        for f, (source, start, size, at) in enumerate(fields):
            column = pl.multiple_of(goal * width_here + start, HD)
            copies[s, f] = pltpu.make_async_copy(
                ins[source].at[:, :, pl.ds(column, size)],
                buffer.at[s, :, :, pl.ds(at, size)],
                sems.at[s, f],
            )
            copies[s, f].start()
    sign = sign_matrix()
    for s in order:
        for f, (_, _, size, start) in enumerate(fields):
            copies[s, f].wait()
            flat = rows_of(buffer[s, :, :, start : start + size])
            heads = [flat[:, at : at + HD] for at in range(0, size, HD)]
            turned = jnp.dot(
                jnp.concatenate(heads, axis=0), sign, preferred_element_type=jnp.float32
            )
            turned = (turned * ROTATE_SCALE).reshape(size // HD, blocks, tokens, HD)
            for h in range(size // HD):
                at = start + h * HD
                outs[s][:, :, at : at + HD] = turned[h].astype(jnp.bfloat16)


def rotate_pieces(arrays, message, count_head, after=(), limit=VMEM, stacked=False):
    blocks, tokens, _ = arrays[0].shape
    fields, total = fields_of(message)
    sources = sorted({source for source, _, _ in message})
    one = (blocks, tokens, total)
    shapes = [(count_head,) + one] if stacked else [one] * count_head
    *pieces, token = pl.pallas_call(
        functools.partial(rotate_kernel, message, sources, count_head, len(after)),
        in_specs=[pl.BlockSpec(memory_space=pltpu.HBM)] * len(sources)
        + [pl.BlockSpec(memory_space=pl.ANY)] * len(after),
        out_specs=[pl.BlockSpec(memory_space=pltpu.VMEM)] * (len(shapes) + 1),
        out_shape=[jax.ShapeDtypeStruct(shape, jnp.bfloat16) for shape in shapes] + [TOKEN],
        scratch_shapes=[
            pltpu.VMEM((count_head,) + one, jnp.bfloat16),
            pltpu.SemaphoreType.DMA((count_head, len(fields))),
        ],
        cost_estimate=NO_COST,
        compiler_params=pltpu.CompilerParams(vmem_limit_bytes=limit),
    )(*[arrays[source] for source in sources], *after)
    return pieces, token


def slots_at(distance, count_tm):
    return NEAR_CAP if distance in (1, count_tm - 1) else FAR_CAP


def pick_kernel(count_head, count_tm, lanes, skipped, picks_ref, *refs):
    pieces, outs = refs[:count_head], refs[count_head + skipped :]
    shard = lax.axis_index("tm")
    for distance, out in enumerate(outs, 1):
        goal = lax.rem(shard + distance, count_tm)
        for k in range(slots_at(distance, count_tm)):
            pick = picks_ref[NEAR_CAP * goal + k]
            for s in range(count_head):
                out[k, s] = pieces[s][pick, :, lanes[0] : lanes[1]]


def pick_blocks(picks, pieces, lanes, count_tm, after):
    count_head = len(pieces)
    one = (count_head, pieces[0].shape[1], lanes[1] - lanes[0])
    vmem = pl.BlockSpec(memory_space=pltpu.VMEM)
    return pl.pallas_call(
        functools.partial(pick_kernel, count_head, count_tm, lanes, len(after)),
        in_specs=[pl.BlockSpec(memory_space=pltpu.SMEM)]
        + [vmem] * count_head
        + [pl.BlockSpec(memory_space=pl.ANY)] * len(after),
        out_specs=[vmem] * (count_tm - 1),
        out_shape=[
            jax.ShapeDtypeStruct((slots_at(distance, count_tm),) + one, jnp.bfloat16)
            for distance in range(1, count_tm)
        ],
        cost_estimate=HIGH_COST,
        compiler_params=pltpu.CompilerParams(vmem_limit_bytes=VMEM),
    )(picks, *pieces, *after)


def remote_rows(count_tm):
    return [
        (distance, k)
        for distance in range(1, count_tm)
        for k in range(slots_at(distance, count_tm))
    ]


def split(value, by):
    if by & (by - 1) == 0:
        return value >> (by.bit_length() - 1), value & (by - 1)
    return lax.div(value, by), lax.rem(value, by)


def plan_kernel(count_head, count_tm, blocks, pair_ref, tokens_ref, _, picks_ref, bias_ref, named_ref, table_ref, sem):
    total_blocks, columns = pair_ref.shape
    pairs = pair_ref[...]
    lane = lax.broadcasted_iota(jnp.int32, named_ref.shape, 1)
    named = jnp.zeros(named_ref.shape, jnp.int32)
    for c in range(columns):
        named = jnp.where(pairs[:, c : c + 1] == lane, 1, named)
    named_ref[...] = named
    copy = pltpu.make_async_copy(named_ref, table_ref, sem)
    copy.start()
    copy.wait()
    shard = lax.axis_index("tm")
    place = lax.axis_index("head")
    mine = shard * blocks

    def two_picks(wanted):
        picks = [jnp.int32(0)] * NEAR_CAP
        count = jnp.int32(0)
        for j in range(blocks):
            for k in range(NEAR_CAP):
                picks[k] = jnp.where((wanted[j] > 0) & (count == k), j, picks[k])
            count = count + wanted[j]
        return picks, count

    def named_by(rows, column):
        found = table_ref[rows, column]
        for i in range(1, blocks):
            found = found | table_ref[rows + i, column]
        return found

    for d in range(count_tm):
        picks, _ = two_picks([named_by(d * blocks, mine + j) for j in range(blocks)])
        for k in range(NEAR_CAP):
            picks_ref[NEAR_CAP * d + k] = picks[k]

    kept = [[table_ref[mine + i, mine + j] * tokens_ref[mine + j] for j in range(blocks)] for i in range(blocks)]
    arrivals = {}
    for distance, k in remote_rows(count_tm):
        first = lax.rem(shard - distance + count_tm, count_tm) * blocks
        if k == 0:
            arrivals[distance] = two_picks([named_by(mine, first + j) for j in range(blocks)])
        picks, count = arrivals[distance]
        there = first + picks[k]
        live = jnp.where(count > k, tokens_ref[there], 0)
        for i in range(blocks):
            kept[i].append(table_ref[mine + i, there] * live)

    total = bias_ref.shape[1]
    piece_rows = BLK // count_head
    at = lax.broadcasted_iota(jnp.int32, (blocks, total), 1)
    query = lax.broadcasted_iota(jnp.int32, (blocks, total), 0)
    own = at < blocks * BLK
    group, token = split(at, piece_rows)
    own_piece, own_block = split(group, blocks)
    far_row, far_group = split(group, count_head)
    row = jnp.where(own, own_block, far_row)
    piece = jnp.where(own, own_piece, far_group)
    source = jnp.where(piece > place, place - piece + count_head, place - piece)
    position = source * piece_rows + token
    limit = jnp.zeros((blocks, total), jnp.int32)
    for r in range(len(kept[0])):
        value = jnp.zeros((blocks, total), jnp.int32)
        for i in range(blocks):
            value = jnp.where(query == i, kept[i][r], value)
        limit = jnp.where(row == r, value, limit)
    bias_ref[...] = jnp.where(position < limit, 0.0, NEG)


def plan(pair_list, block_tokens, after, blocks, count_head, count_tm):
    total_blocks = pair_list.shape[0]
    lanes = -(-total_blocks // 128) * 128
    total = (blocks + len(remote_rows(count_tm))) * BLK
    return pl.pallas_call(
        functools.partial(plan_kernel, count_head, count_tm, blocks),
        in_specs=[
            pl.BlockSpec(memory_space=pltpu.VMEM),
            pl.BlockSpec(memory_space=pltpu.SMEM),
            pl.BlockSpec(memory_space=pl.ANY),
        ],
        out_specs=[pl.BlockSpec(memory_space=pltpu.SMEM), pl.BlockSpec(memory_space=pltpu.VMEM)],
        out_shape=[
            jax.ShapeDtypeStruct((NEAR_CAP * count_tm,), jnp.int32),
            jax.ShapeDtypeStruct((blocks, total), jnp.float32),
        ],
        scratch_shapes=[
            pltpu.VMEM((total_blocks, lanes), jnp.int32),
            pltpu.SMEM((total_blocks, lanes), jnp.int32),
            pltpu.SemaphoreType.DMA,
        ],
        cost_estimate=NO_COST,
        compiler_params=pltpu.CompilerParams(vmem_limit_bytes=VMEM),
    )(pair_list, block_tokens, after)


def attend_kernel(counts, at, size, tokens_ref, bias_ref, *refs):
    count_head, count_tm, query_count, skipped = counts
    query_at, key_at = at
    queries, refs = by_distance(refs[:query_count], count_head, -1), refs[query_count:]
    owns, slots = refs[:count_head], refs[count_head : count_head + count_tm - 1]
    outs = by_distance(refs[count_head + count_tm - 1 + skipped :], count_head, -1)
    blocks, tokens, _ = owns[0].shape
    shard = lax.axis_index("tm")
    me = lax.axis_index("head")
    sign = sign_matrix()
    for h in range(size // HD):
        lanes = slice(h * HD, (h + 1) * HD)
        query_lanes = slice(query_at + h * HD, query_at + (h + 1) * HD)
        query = jnp.concatenate(
            [rows_of(queries[s][i, :, query_lanes]) for i in range(blocks) for s in range(count_head)],
            axis=0,
        )

        def gathered(kind):
            first = kind * size + h * HD
            own_lanes = slice(key_at + first, key_at + first + HD)
            pieces = [rows_of(own[:, :, own_lanes]) for own in owns]
            pieces += [
                rows_of(slots[distance - 1][k, :, :, first : first + HD])
                for distance, k in remote_rows(count_tm)
            ]
            return jnp.concatenate(pieces, axis=0)

        keys, values = gathered(0), gathered(1)
        total = keys.shape[0]
        dots = lax.dot_general(
            query, keys, (((1,), (1,)), ((), ())), preferred_element_type=jnp.float32
        )
        dots = dots.reshape(blocks, BLK, total) + bias_ref[...][:, None, :]
        peak = jnp.max(dots, axis=-1, keepdims=True)
        weights = jnp.exp2((dots - peak) * (SCORE_SCALE * LOG2E))
        denominator = jnp.sum(weights, axis=-1, keepdims=True).reshape(blocks * BLK, 1)
        weights_half = weights.astype(jnp.bfloat16).reshape(blocks * BLK, total)
        mixed = jnp.dot(weights_half, values, preferred_element_type=jnp.float32) / denominator
        turned = jnp.zeros_like(mixed)
        rest = mixed
        for _ in range(3):
            piece = rest.astype(jnp.bfloat16)
            turned = turned + jnp.dot(piece, sign, preferred_element_type=jnp.float32)
            rest = rest - piece.astype(jnp.float32)
        turned = (turned * ROTATE_SCALE).reshape(blocks, count_head, tokens, HD)
        token = lax.broadcasted_iota(jnp.int32, (tokens, HD), 0)
        for s in range(count_head):
            position = lax.rem(me - s + count_head, count_head) * tokens + token
            for i in range(blocks):
                outs[s][i, :, lanes] = jnp.where(
                    position < tokens_ref[shard * blocks + i], turned[i, s], 0.0
                ).astype(jnp.bfloat16)


def attend(block_tokens, bias, queries, query_at, owns, key_at, slots, size, after, cost, stacked):
    count_head, count_tm = len(owns), len(slots) + 1
    blocks, tokens, _ = owns[0].shape
    one = (blocks, tokens, size)
    shapes = [(count_head,) + one] if stacked else [one] * count_head
    vmem = pl.BlockSpec(memory_space=pltpu.VMEM)
    return pl.pallas_call(
        functools.partial(
            attend_kernel,
            (count_head, count_tm, len(queries), len(after)),
            (query_at, key_at),
            size,
        ),
        in_specs=[pl.BlockSpec(memory_space=pltpu.SMEM)]
        + [vmem] * (len(queries) + count_head + count_tm)
        + [pl.BlockSpec(memory_space=pl.ANY)] * len(after),
        out_specs=[vmem] * len(shapes),
        out_shape=[jax.ShapeDtypeStruct(shape, jnp.bfloat16) for shape in shapes],
        cost_estimate=cost,
        compiler_params=pltpu.CompilerParams(vmem_limit_bytes=VMEM),
    )(block_tokens, bias, *queries, *owns, *slots, *after)


def place_kernel(count_head, counts, starts, width_here, *refs):
    out_ref, sems = refs[-2:]
    me = lax.axis_index("head")
    copies, at = [], 0
    for count, start in zip(counts, starts):
        pieces = by_distance(refs[at : at + count], count_head, 1)
        at += count
        for s, piece in enumerate(pieces):
            column = lax.rem(me + s, count_head) * width_here + start
            copies.append(
                pltpu.make_async_copy(
                    piece,
                    out_ref.at[:, :, pl.ds(pl.multiple_of(column, HD), piece.shape[-1])],
                    sems.at[len(copies)],
                )
            )
            copies[-1].start()
    for copy in copies:
        copy.wait()


def place_pieces(parts, starts, count_head, width_here):
    pieces = [piece for part in parts for piece in part]
    blocks, tokens, _ = pieces[0].shape[-3:]
    counts = [len(part) for part in parts]
    return pl.pallas_call(
        functools.partial(place_kernel, count_head, counts, starts, width_here),
        in_specs=[pl.BlockSpec(memory_space=pl.ANY)] * len(pieces),
        out_specs=pl.BlockSpec(memory_space=pltpu.HBM),
        out_shape=jax.ShapeDtypeStruct((blocks, tokens, count_head * width_here), jnp.bfloat16),
        scratch_shapes=[pltpu.SemaphoreType.DMA((len(parts) * count_head,))],
        compiler_params=pltpu.CompilerParams(vmem_limit_bytes=VMEM),
    )(*pieces)


def shifted(array, axis, distance):
    count = lax.axis_size(axis)
    return lax.ppermute(array, axis, [(i, (i + distance) % count) for i in range(count)])


def exchange(pieces, direction):
    if len(pieces) == 1:
        return [lax.all_to_all(pieces[0], "head", split_axis=0, concat_axis=0, tiled=True)]
    return [pieces[0]] + [
        shifted(piece, "head", direction * s) for s, piece in enumerate(pieces[1:], 1)
    ]


def forward(sent):
    return [shifted(block, "tm", distance) for distance, block in enumerate(sent, 1)]


def shards(query_rows, key_rows, value_rows, pair_list, block_tokens):
    count_head = lax.axis_size("head")
    count_tm = lax.axis_size("tm")
    blocks, tokens, width = query_rows.shape
    width_here = width // count_head
    heads = width_here // HD
    cut = (heads + 1) // 2 * HD
    parts = [(0, cut), (cut, width_here - cut)] if heads > 1 else [(0, width_here)]
    arrays = [query_rows, key_rows, value_rows]
    messages = []
    for at, part in enumerate(parts):
        message = [(1,) + part, (2,) + part]
        messages.append(message + ([(0,) + parts[at - 1]] if at else []))
    query_at = [2 * size for _, size in parts[1:]] + [0]
    pieces, token = rotate_pieces(arrays, messages[0], count_head, limit=WIDE_VMEM)
    packed = [pieces]
    picks, bias = plan(pair_list, block_tokens, token, blocks, count_head, count_tm)
    after = (bias,)
    for message in messages[1:]:
        pieces, token = rotate_pieces(arrays, message, count_head, after)
        packed.append(pieces)
        after = (token,)
    received = [exchange(pieces, 1) for pieces in packed]
    sent, after = [], ()
    for owns, (_, size) in zip(received, parts):
        sent.append(pick_blocks(picks, owns, (0, 2 * size), count_tm, after))
        after = (sent[-1][0],)
    message = [(0,) + parts[-1]]
    query, _ = rotate_pieces(arrays, message, count_head, (sent[0][0],), stacked=True)
    queries = received[1:] + [exchange(query, 1)]
    returned, after = [], ()
    for at, (_, size) in enumerate(parts):
        last = at == len(parts) - 1
        attended = attend(
            block_tokens, bias, queries[at], query_at[at], received[at], 0,
            forward(sent[at]), size, after, HIGH_COST if last else NO_COST, not last,
        )
        after = (attended[0],)
        returned.append(exchange(attended, -1))
    return place_pieces(returned, [start for start, _ in parts], count_head, width_here)


def solution(mesh):
    placed = (
        P(("grp", "tm"), "head", None),
        P(("grp", "tm"), "head", None),
        P(("grp", "tm"), "head", None),
        P("grp", None),
        P("grp"),
    )
    return jax.shard_map(
        shards,
        mesh=mesh,
        in_specs=placed,
        out_specs=P(("grp", "tm"), "head", None),
        check_vma=False,
    )
```

```python
import functools
import math

import jax
import jax.numpy as jnp
from jax import lax
from jax.experimental import pallas as pl
from jax.experimental.pallas import tpu as pltpu
from jax.sharding import PartitionSpec as P

HD = 128
BLK = 64
NEAR_CAP = 2
FAR_CAP = 1
NEG = -1e30
ROTATE_SCALE = 1.0 / math.sqrt(HD)
SCORE_SCALE = 1.0 / math.sqrt(HD)
VMEM = 24 * 1024 * 1024
WIDE_VMEM = 60 * 1024 * 1024
TOKEN = jax.ShapeDtypeStruct((8, 128), jnp.float32)
NO_COST = pl.CostEstimate(flops=0, bytes_accessed=0, transcendentals=0)
HIGH_COST = pl.CostEstimate(flops=10**11, bytes_accessed=0, transcendentals=0)
LOG2E = math.log2(math.e)


def sign_matrix():
    common = lax.broadcasted_iota(jnp.int32, (HD, HD), 0) & lax.broadcasted_iota(
        jnp.int32, (HD, HD), 1
    )
    bits = HD.bit_length() - 1
    parity = common
    for bit in range(1, bits):
        parity = parity ^ (common >> bit)
    return jnp.where((parity & 1) == 0, 1.0, -1.0).astype(jnp.bfloat16)


def rows_of(block):
    rows, width = math.prod(block.shape[:-1]), block.shape[-1]
    if block.shape[-2] % 16 == 0:
        return block.reshape(rows, width)
    return block.astype(jnp.float32).reshape(rows, width).astype(block.dtype)


def fields_of(message):
    at, fields = 0, []
    for source, start, size in message:
        fields.append((source, start, size, at))
        at += size
    return fields, at


def by_distance(refs, count, direction):
    if len(refs) > 1:
        return list(refs)
    me = lax.axis_index("head")
    return [refs[0].at[lax.rem(me + direction * s + count, count)] for s in range(count)]


def rotate_kernel(message, sources, count_head, skipped, *refs):
    fields, total = fields_of(message)
    ins = dict(zip(sources, refs))
    outs = by_distance(refs[len(sources) + skipped : -5], count_head, 1)
    token, buffer, sems, turned_ref, out_sems = refs[-5:]
    token[...] = jnp.zeros_like(token)
    leaving = []
    blocks, tokens, width = refs[0].shape
    width_here = width // count_head
    me = lax.axis_index("head")
    order = list(range(1, count_head)) + [0]
    copies = {}
    for s in order:
        goal = lax.rem(me + s, count_head)
        for f, (source, start, size, at) in enumerate(fields):
            column = pl.multiple_of(goal * width_here + start, HD)
            copies[s, f] = pltpu.make_async_copy(
                ins[source].at[:, :, pl.ds(column, size)],
                buffer.at[s, :, :, pl.ds(at, size)],
                sems.at[s, f],
            )
            copies[s, f].start()
    sign = sign_matrix()
    for s in order:
        for f, (_, _, size, start) in enumerate(fields):
            copies[s, f].wait()
            flat = rows_of(buffer[s, :, :, start : start + size])
            heads = [flat[:, at : at + HD] for at in range(0, size, HD)]
            turned = jnp.dot(
                jnp.concatenate(heads, axis=0), sign, preferred_element_type=jnp.float32
            )
            turned = (turned * ROTATE_SCALE).reshape(size // HD, blocks, tokens, HD)
            for h in range(size // HD):
                at = start + h * HD
                turned_ref[s, :, :, at : at + HD] = turned[h].astype(jnp.bfloat16)
        leaving.append(pltpu.make_async_copy(turned_ref.at[s], outs[s], out_sems.at[s]))
        leaving[-1].start()
    for copy in leaving:
        copy.wait()


def rotate_pieces(arrays, message, count_head, after=(), limit=VMEM, stacked=False):
    blocks, tokens, _ = arrays[0].shape
    fields, total = fields_of(message)
    sources = sorted({source for source, _, _ in message})
    one = (blocks, tokens, total)
    shapes = [(count_head,) + one] if stacked else [one] * count_head
    *pieces, token = pl.pallas_call(
        functools.partial(rotate_kernel, message, sources, count_head, len(after)),
        in_specs=[pl.BlockSpec(memory_space=pltpu.HBM)] * len(sources)
        + [pl.BlockSpec(memory_space=pl.ANY)] * len(after),
        out_specs=[pl.BlockSpec(memory_space=pl.ANY)] * len(shapes)
        + [pl.BlockSpec(memory_space=pltpu.VMEM)],
        out_shape=[jax.ShapeDtypeStruct(shape, jnp.bfloat16) for shape in shapes] + [TOKEN],
        scratch_shapes=[
            pltpu.VMEM((count_head,) + one, jnp.bfloat16),
            pltpu.SemaphoreType.DMA((count_head, len(fields))),
            pltpu.VMEM((count_head,) + one, jnp.bfloat16),
            pltpu.SemaphoreType.DMA((count_head,)),
        ],
        cost_estimate=NO_COST,
        compiler_params=pltpu.CompilerParams(vmem_limit_bytes=limit),
    )(*[arrays[source] for source in sources], *after)
    return pieces, token


def slots_at(distance, count_tm):
    return NEAR_CAP if distance in (1, count_tm - 1) else FAR_CAP


def pick_kernel(count_head, count_tm, lanes, skipped, picks_ref, *refs):
    pieces, outs = refs[:count_head], refs[count_head + skipped :]
    shard = lax.axis_index("tm")
    for distance, out in enumerate(outs, 1):
        goal = lax.rem(shard + distance, count_tm)
        for k in range(slots_at(distance, count_tm)):
            pick = picks_ref[NEAR_CAP * goal + k]
            for s in range(count_head):
                out[k, s] = pieces[s][pick, :, lanes[0] : lanes[1]]


def pick_blocks(picks, pieces, lanes, count_tm, after):
    count_head = len(pieces)
    one = (count_head, pieces[0].shape[1], lanes[1] - lanes[0])
    vmem = pl.BlockSpec(memory_space=pltpu.VMEM)
    return pl.pallas_call(
        functools.partial(pick_kernel, count_head, count_tm, lanes, len(after)),
        in_specs=[pl.BlockSpec(memory_space=pltpu.SMEM)]
        + [vmem] * count_head
        + [pl.BlockSpec(memory_space=pl.ANY)] * len(after),
        out_specs=[vmem] * (count_tm - 1),
        out_shape=[
            jax.ShapeDtypeStruct((slots_at(distance, count_tm),) + one, jnp.bfloat16)
            for distance in range(1, count_tm)
        ],
        cost_estimate=HIGH_COST,
        compiler_params=pltpu.CompilerParams(vmem_limit_bytes=VMEM),
    )(picks, *pieces, *after)


def remote_rows(count_tm):
    return [
        (distance, k)
        for distance in range(1, count_tm)
        for k in range(slots_at(distance, count_tm))
    ]


def split(value, by):
    if by & (by - 1) == 0:
        return value >> (by.bit_length() - 1), value & (by - 1)
    return lax.div(value, by), lax.rem(value, by)


def plan_kernel(count_head, count_tm, blocks, pair_ref, tokens_ref, _, picks_ref, bias_ref, named_ref, table_ref, sem):
    total_blocks, columns = pair_ref.shape
    pairs = pair_ref[...]
    lane = lax.broadcasted_iota(jnp.int32, named_ref.shape, 1)
    named = jnp.zeros(named_ref.shape, jnp.int32)
    for c in range(columns):
        named = jnp.where(pairs[:, c : c + 1] == lane, 1, named)
    named_ref[...] = named
    copy = pltpu.make_async_copy(named_ref, table_ref, sem)
    copy.start()
    copy.wait()
    shard = lax.axis_index("tm")
    place = lax.axis_index("head")
    mine = shard * blocks

    def two_picks(wanted):
        picks = [jnp.int32(0)] * NEAR_CAP
        count = jnp.int32(0)
        for j in range(blocks):
            for k in range(NEAR_CAP):
                picks[k] = jnp.where((wanted[j] > 0) & (count == k), j, picks[k])
            count = count + wanted[j]
        return picks, count

    def named_by(rows, column):
        found = table_ref[rows, column]
        for i in range(1, blocks):
            found = found | table_ref[rows + i, column]
        return found

    for d in range(count_tm):
        picks, _ = two_picks([named_by(d * blocks, mine + j) for j in range(blocks)])
        for k in range(NEAR_CAP):
            picks_ref[NEAR_CAP * d + k] = picks[k]

    kept = [[table_ref[mine + i, mine + j] * tokens_ref[mine + j] for j in range(blocks)] for i in range(blocks)]
    arrivals = {}
    for distance, k in remote_rows(count_tm):
        first = lax.rem(shard - distance + count_tm, count_tm) * blocks
        if k == 0:
            arrivals[distance] = two_picks([named_by(mine, first + j) for j in range(blocks)])
        picks, count = arrivals[distance]
        there = first + picks[k]
        live = jnp.where(count > k, tokens_ref[there], 0)
        for i in range(blocks):
            kept[i].append(table_ref[mine + i, there] * live)

    total = bias_ref.shape[1]
    piece_rows = BLK // count_head
    at = lax.broadcasted_iota(jnp.int32, (blocks, total), 1)
    query = lax.broadcasted_iota(jnp.int32, (blocks, total), 0)
    own = at < blocks * BLK
    group, token = split(at, piece_rows)
    own_piece, own_block = split(group, blocks)
    far_row, far_group = split(group, count_head)
    row = jnp.where(own, own_block, far_row)
    piece = jnp.where(own, own_piece, far_group)
    source = jnp.where(piece > place, place - piece + count_head, place - piece)
    position = source * piece_rows + token
    limit = jnp.zeros((blocks, total), jnp.int32)
    for r in range(len(kept[0])):
        value = jnp.zeros((blocks, total), jnp.int32)
        for i in range(blocks):
            value = jnp.where(query == i, kept[i][r], value)
        limit = jnp.where(row == r, value, limit)
    bias_ref[...] = jnp.where(position < limit, 0.0, NEG)


def plan(pair_list, block_tokens, after, blocks, count_head, count_tm):
    total_blocks = pair_list.shape[0]
    lanes = -(-total_blocks // 128) * 128
    total = (blocks + len(remote_rows(count_tm))) * BLK
    return pl.pallas_call(
        functools.partial(plan_kernel, count_head, count_tm, blocks),
        in_specs=[
            pl.BlockSpec(memory_space=pltpu.VMEM),
            pl.BlockSpec(memory_space=pltpu.SMEM),
            pl.BlockSpec(memory_space=pl.ANY),
        ],
        out_specs=[pl.BlockSpec(memory_space=pltpu.SMEM), pl.BlockSpec(memory_space=pltpu.VMEM)],
        out_shape=[
            jax.ShapeDtypeStruct((NEAR_CAP * count_tm,), jnp.int32),
            jax.ShapeDtypeStruct((blocks, total), jnp.float32),
        ],
        scratch_shapes=[
            pltpu.VMEM((total_blocks, lanes), jnp.int32),
            pltpu.SMEM((total_blocks, lanes), jnp.int32),
            pltpu.SemaphoreType.DMA,
        ],
        cost_estimate=NO_COST,
        compiler_params=pltpu.CompilerParams(vmem_limit_bytes=VMEM),
    )(pair_list, block_tokens, after)


def attend_kernel(counts, at, size, tokens_ref, bias_ref, *refs):
    count_head, count_tm, query_count, skipped = counts
    query_at, key_at = at
    queries, refs = by_distance(refs[:query_count], count_head, -1), refs[query_count:]
    owns, slots = refs[:count_head], refs[count_head : count_head + count_tm - 1]
    outs = refs[count_head + count_tm - 1 + skipped :]
    blocks, tokens, _ = owns[0].shape
    shard = lax.axis_index("tm")
    me = lax.axis_index("head")
    heads = size // HD
    bias = bias_ref[...][:, None, :]

    def gathered(kind, h):
        first = kind * size + h * HD
        own_lanes = slice(key_at + first, key_at + first + HD)
        pieces = [rows_of(own[:, :, own_lanes]) for own in owns]
        pieces += [
            rows_of(slots[distance - 1][k, :, :, first : first + HD])
            for distance, k in remote_rows(count_tm)
        ]
        return jnp.concatenate(pieces, axis=0)

    def products(h):
        lanes = slice(query_at + h * HD, query_at + (h + 1) * HD)
        query = jnp.concatenate(
            [rows_of(queries[s][i, :, lanes]) for i in range(blocks) for s in range(count_head)],
            axis=0,
        )
        return lax.dot_general(
            query, gathered(0, h), (((1,), (1,)), ((), ())), preferred_element_type=jnp.float32
        )

    dots, mixed = products(0), []
    for h in range(heads):
        ahead = products(h + 1) if h + 1 < heads else None
        dots = dots.reshape(blocks, BLK, -1) + bias
        peak = jnp.max(dots, axis=-1, keepdims=True)
        weights = jnp.exp2((dots - peak) * (SCORE_SCALE * LOG2E))
        inverse = 1.0 / jnp.sum(weights, axis=-1, keepdims=True)
        weights_half = weights.astype(jnp.bfloat16).reshape(blocks * BLK, -1)
        rows = jnp.dot(weights_half, gathered(1, h), preferred_element_type=jnp.float32)
        mixed.append(rows * inverse.reshape(blocks * BLK, 1))
        dots = ahead
    mixed = jnp.concatenate(mixed, axis=0)
    sign = sign_matrix()
    high = mixed.astype(jnp.bfloat16)
    low = (mixed - high.astype(jnp.float32)).astype(jnp.bfloat16)
    turned = jnp.dot(high, sign, preferred_element_type=jnp.float32)
    turned = turned + jnp.dot(low, sign, preferred_element_type=jnp.float32)
    turned = (turned * ROTATE_SCALE).reshape(heads, blocks, count_head, tokens, HD)
    token = lax.broadcasted_iota(jnp.int32, (tokens, HD), 0)
    for s in range(count_head):
        position = lax.rem(me - s + count_head, count_head) * tokens + token
        for i in range(blocks):
            live = position < tokens_ref[shard * blocks + i]
            for h in range(heads):
                outs[s][i, :, h * HD : (h + 1) * HD] = jnp.where(
                    live, turned[h, i, s], 0.0
                ).astype(jnp.bfloat16)


def attend(block_tokens, bias, queries, query_at, owns, key_at, slots, size, after, cost):
    count_head, count_tm = len(owns), len(slots) + 1
    blocks, tokens, _ = owns[0].shape
    vmem = pl.BlockSpec(memory_space=pltpu.VMEM)
    return pl.pallas_call(
        functools.partial(
            attend_kernel,
            (count_head, count_tm, len(queries), len(after)),
            (query_at, key_at),
            size,
        ),
        in_specs=[pl.BlockSpec(memory_space=pltpu.SMEM)]
        + [vmem] * (len(queries) + count_head + count_tm)
        + [pl.BlockSpec(memory_space=pl.ANY)] * len(after),
        out_specs=[vmem] * count_head,
        out_shape=[jax.ShapeDtypeStruct((blocks, tokens, size), jnp.bfloat16)] * count_head,
        cost_estimate=cost,
        compiler_params=pltpu.CompilerParams(vmem_limit_bytes=VMEM),
    )(block_tokens, bias, *queries, *owns, *slots, *after)


def place_kernel(count_head, starts, width_here, *refs):
    pieces, out_ref, sems = refs[:-2], refs[-2], refs[-1]
    me = lax.axis_index("head")
    copies = []
    for at, piece in enumerate(pieces):
        part, s = at // count_head, at % count_head
        column = lax.rem(me + s, count_head) * width_here + starts[part]
        copies.append(
            pltpu.make_async_copy(
                piece,
                out_ref.at[:, :, pl.ds(pl.multiple_of(column, HD), piece.shape[-1])],
                sems.at[at],
            )
        )
        copies[-1].start()
    for copy in copies:
        copy.wait()


def place_pieces(parts, starts, width_here):
    count_head = len(parts[0])
    pieces = [piece for part in parts for piece in part]
    blocks, tokens, _ = pieces[0].shape
    return pl.pallas_call(
        functools.partial(place_kernel, count_head, starts, width_here),
        in_specs=[pl.BlockSpec(memory_space=pl.ANY)] * len(pieces),
        out_specs=pl.BlockSpec(memory_space=pltpu.HBM),
        out_shape=jax.ShapeDtypeStruct((blocks, tokens, count_head * width_here), jnp.bfloat16),
        scratch_shapes=[pltpu.SemaphoreType.DMA((len(pieces),))],
        compiler_params=pltpu.CompilerParams(vmem_limit_bytes=VMEM),
    )(*pieces)


def shifted(array, axis, distance):
    count = lax.axis_size(axis)
    return lax.ppermute(array, axis, [(i, (i + distance) % count) for i in range(count)])


def exchange(pieces, direction):
    return [pieces[0]] + [
        shifted(piece, "head", direction * s) for s, piece in enumerate(pieces[1:], 1)
    ]


def forward(sent):
    return [shifted(block, "tm", distance) for distance, block in enumerate(sent, 1)]


def shards(query_rows, key_rows, value_rows, pair_list, block_tokens):
    count_head = lax.axis_size("head")
    count_tm = lax.axis_size("tm")
    blocks, tokens, width = query_rows.shape
    width_here = width // count_head
    heads = width_here // HD
    cut = (heads + 1) // 2 * HD
    parts = [(0, cut), (cut, width_here - cut)] if heads > 1 else [(0, width_here)]
    arrays = [query_rows, key_rows, value_rows]
    messages = []
    for at, part in enumerate(parts):
        message = [(1,) + part, (2,) + part]
        messages.append(message + ([(0,) + parts[at - 1]] if at else []))
    query_at = [2 * size for _, size in parts[1:]] + [0]
    pieces, token = rotate_pieces(arrays, messages[0], count_head, limit=WIDE_VMEM)
    packed = [pieces]
    picks, bias = plan(pair_list, block_tokens, token, blocks, count_head, count_tm)
    after = (bias,)
    for message in messages[1:]:
        pieces, token = rotate_pieces(arrays, message, count_head, after)
        packed.append(pieces)
        after = (token,)
    received = [exchange(pieces, 1) for pieces in packed]
    sent, after = [], ()
    for owns, (_, size) in zip(received, parts):
        sent.append(pick_blocks(picks, owns, (0, 2 * size), count_tm, after))
        after = (sent[-1][0],)
    message = [(0,) + parts[-1]]
    (query,), _ = rotate_pieces(arrays, message, count_head, (sent[0][0],), stacked=True)
    query = lax.all_to_all(query, "head", split_axis=0, concat_axis=0, tiled=True)
    queries = received[1:] + [[query]]
    returned, after = [], ()
    for at, (_, size) in enumerate(parts):
        attended = attend(
            block_tokens, bias, queries[at], query_at[at], received[at], 0,
            forward(sent[at]), size, after, NO_COST,
        )
        after = (attended[0],)
        returned.append(exchange(attended, -1))
    return place_pieces(returned, [start for start, _ in parts], width_here)


def solution(mesh):
    placed = (
        P(("grp", "tm"), "head", None),
        P(("grp", "tm"), "head", None),
        P(("grp", "tm"), "head", None),
        P("grp", None),
        P("grp"),
    )
    return jax.shard_map(
        shards,
        mesh=mesh,
        in_specs=placed,
        out_specs=P(("grp", "tm"), "head", None),
        check_vma=False,
    )
```

```python
import functools
import math

import jax
import jax.numpy as jnp
from jax import lax
from jax.experimental import pallas as pl
from jax.experimental.pallas import tpu as pltpu
from jax.sharding import PartitionSpec as P

HD = 128
BLK = 64
NEAR_CAP = 2
FAR_CAP = 1
NEG = -1e30
ROTATE_SCALE = 1.0 / math.sqrt(HD)
SCORE_SCALE = 1.0 / math.sqrt(HD)
VMEM = 24 * 1024 * 1024
WIDE_VMEM = 60 * 1024 * 1024
TOKEN = jax.ShapeDtypeStruct((8, 128), jnp.float32)
NO_COST = pl.CostEstimate(flops=0, bytes_accessed=0, transcendentals=0)
HIGH_COST = pl.CostEstimate(flops=10**11, bytes_accessed=0, transcendentals=0)
LOG2E = math.log2(math.e)


def sign_matrix():
    common = lax.broadcasted_iota(jnp.int32, (HD, HD), 0) & lax.broadcasted_iota(
        jnp.int32, (HD, HD), 1
    )
    bits = HD.bit_length() - 1
    parity = common
    for bit in range(1, bits):
        parity = parity ^ (common >> bit)
    return jnp.where((parity & 1) == 0, 1.0, -1.0).astype(jnp.bfloat16)


def rows_of(block):
    rows, width = math.prod(block.shape[:-1]), block.shape[-1]
    if block.shape[-2] % 16 == 0:
        return block.reshape(rows, width)
    return block.astype(jnp.float32).reshape(rows, width).astype(block.dtype)


def fields_of(message):
    at, fields = 0, []
    for source, start, size in message:
        fields.append((source, start, size, at))
        at += size
    return fields, at


def by_distance(refs, count, direction):
    if len(refs) > 1:
        return list(refs)
    me = lax.axis_index("head")
    return [refs[0].at[lax.rem(me + direction * s + count, count)] for s in range(count)]


def rotate_kernel(message, sources, count_head, skipped, *refs):
    fields, total = fields_of(message)
    ins = dict(zip(sources, refs))
    outs = by_distance(refs[len(sources) + skipped : -3], count_head, 1)
    token, buffer, sems = refs[-3:]
    token[...] = jnp.zeros_like(token)
    blocks, tokens, width = refs[0].shape
    width_here = width // count_head
    me = lax.axis_index("head")
    order = list(range(1, count_head)) + [0]
    copies = {}
    for s in order:
        goal = lax.rem(me + s, count_head)
        for f, (source, start, size, at) in enumerate(fields):
            column = pl.multiple_of(goal * width_here + start, HD)
            copies[s, f] = pltpu.make_async_copy(
                ins[source].at[:, :, pl.ds(column, size)],
                buffer.at[s, :, :, pl.ds(at, size)],
                sems.at[s, f],
            )
            copies[s, f].start()
    sign = sign_matrix()
    for s in order:
        for f, (_, _, size, start) in enumerate(fields):
            copies[s, f].wait()
            flat = rows_of(buffer[s, :, :, start : start + size])
            heads = [flat[:, at : at + HD] for at in range(0, size, HD)]
            turned = jnp.dot(
                jnp.concatenate(heads, axis=0), sign, preferred_element_type=jnp.float32
            )
            turned = (turned * ROTATE_SCALE).reshape(size // HD, blocks, tokens, HD)
            for h in range(size // HD):
                at = start + h * HD
                outs[s][:, :, at : at + HD] = turned[h].astype(jnp.bfloat16)


def rotate_pieces(arrays, message, count_head, after=(), limit=VMEM, stacked=False):
    blocks, tokens, _ = arrays[0].shape
    fields, total = fields_of(message)
    sources = sorted({source for source, _, _ in message})
    one = (blocks, tokens, total)
    shapes = [(count_head,) + one] if stacked else [one] * count_head
    *pieces, token = pl.pallas_call(
        functools.partial(rotate_kernel, message, sources, count_head, len(after)),
        in_specs=[pl.BlockSpec(memory_space=pltpu.HBM)] * len(sources)
        + [pl.BlockSpec(memory_space=pl.ANY)] * len(after),
        out_specs=[pl.BlockSpec(memory_space=pltpu.VMEM)] * (len(shapes) + 1),
        out_shape=[jax.ShapeDtypeStruct(shape, jnp.bfloat16) for shape in shapes] + [TOKEN],
        scratch_shapes=[
            pltpu.VMEM((count_head,) + one, jnp.bfloat16),
            pltpu.SemaphoreType.DMA((count_head, len(fields))),
        ],
        cost_estimate=NO_COST,
        compiler_params=pltpu.CompilerParams(vmem_limit_bytes=limit),
    )(*[arrays[source] for source in sources], *after)
    return pieces, token


def slots_at(distance, count_tm):
    return NEAR_CAP if distance in (1, count_tm - 1) else FAR_CAP


def pick_kernel(count_head, count_tm, lanes, skipped, picks_ref, *refs):
    pieces, outs = refs[:count_head], refs[count_head + skipped :]
    shard = lax.axis_index("tm")
    for distance, out in enumerate(outs, 1):
        goal = lax.rem(shard + distance, count_tm)
        for k in range(slots_at(distance, count_tm)):
            pick = picks_ref[NEAR_CAP * goal + k]
            for s in range(count_head):
                out[k, s] = pieces[s][pick, :, lanes[0] : lanes[1]]


def pick_blocks(picks, pieces, lanes, count_tm, after):
    count_head = len(pieces)
    one = (count_head, pieces[0].shape[1], lanes[1] - lanes[0])
    vmem = pl.BlockSpec(memory_space=pltpu.VMEM)
    return pl.pallas_call(
        functools.partial(pick_kernel, count_head, count_tm, lanes, len(after)),
        in_specs=[pl.BlockSpec(memory_space=pltpu.SMEM)]
        + [vmem] * count_head
        + [pl.BlockSpec(memory_space=pl.ANY)] * len(after),
        out_specs=[vmem] * (count_tm - 1),
        out_shape=[
            jax.ShapeDtypeStruct((slots_at(distance, count_tm),) + one, jnp.bfloat16)
            for distance in range(1, count_tm)
        ],
        cost_estimate=HIGH_COST,
        compiler_params=pltpu.CompilerParams(vmem_limit_bytes=VMEM),
    )(picks, *pieces, *after)


def remote_rows(count_tm):
    return [
        (distance, k)
        for distance in range(1, count_tm)
        for k in range(slots_at(distance, count_tm))
    ]


def split(value, by):
    if by & (by - 1) == 0:
        return value >> (by.bit_length() - 1), value & (by - 1)
    return lax.div(value, by), lax.rem(value, by)


def plan_kernel(count_head, count_tm, blocks, pair_ref, tokens_ref, _, picks_ref, bias_ref, named_ref, table_ref, sem):
    total_blocks, columns = pair_ref.shape
    pairs = pair_ref[...]
    lane = lax.broadcasted_iota(jnp.int32, named_ref.shape, 1)
    named = jnp.zeros(named_ref.shape, jnp.int32)
    for c in range(columns):
        named = jnp.where(pairs[:, c : c + 1] == lane, 1, named)
    named_ref[...] = named
    copy = pltpu.make_async_copy(named_ref, table_ref, sem)
    copy.start()
    copy.wait()
    shard = lax.axis_index("tm")
    place = lax.axis_index("head")
    mine = shard * blocks

    def two_picks(wanted):
        picks = [jnp.int32(0)] * NEAR_CAP
        count = jnp.int32(0)
        for j in range(blocks):
            for k in range(NEAR_CAP):
                picks[k] = jnp.where((wanted[j] > 0) & (count == k), j, picks[k])
            count = count + wanted[j]
        return picks, count

    def named_by(rows, column):
        found = table_ref[rows, column]
        for i in range(1, blocks):
            found = found | table_ref[rows + i, column]
        return found

    for d in range(count_tm):
        picks, _ = two_picks([named_by(d * blocks, mine + j) for j in range(blocks)])
        for k in range(NEAR_CAP):
            picks_ref[NEAR_CAP * d + k] = picks[k]

    kept = [[table_ref[mine + i, mine + j] * tokens_ref[mine + j] for j in range(blocks)] for i in range(blocks)]
    arrivals = {}
    for distance, k in remote_rows(count_tm):
        first = lax.rem(shard - distance + count_tm, count_tm) * blocks
        if k == 0:
            arrivals[distance] = two_picks([named_by(mine, first + j) for j in range(blocks)])
        picks, count = arrivals[distance]
        there = first + picks[k]
        live = jnp.where(count > k, tokens_ref[there], 0)
        for i in range(blocks):
            kept[i].append(table_ref[mine + i, there] * live)

    total = bias_ref.shape[1]
    piece_rows = BLK // count_head
    at = lax.broadcasted_iota(jnp.int32, (blocks, total), 1)
    query = lax.broadcasted_iota(jnp.int32, (blocks, total), 0)
    own = at < blocks * BLK
    group, token = split(at, piece_rows)
    own_piece, own_block = split(group, blocks)
    far_row, far_group = split(group, count_head)
    row = jnp.where(own, own_block, far_row)
    piece = jnp.where(own, own_piece, far_group)
    source = jnp.where(piece > place, place - piece + count_head, place - piece)
    position = source * piece_rows + token
    limit = jnp.zeros((blocks, total), jnp.int32)
    for r in range(len(kept[0])):
        value = jnp.zeros((blocks, total), jnp.int32)
        for i in range(blocks):
            value = jnp.where(query == i, kept[i][r], value)
        limit = jnp.where(row == r, value, limit)
    bias_ref[...] = jnp.where(position < limit, 0.0, NEG)


def plan(pair_list, block_tokens, after, blocks, count_head, count_tm):
    total_blocks = pair_list.shape[0]
    lanes = -(-total_blocks // 128) * 128
    total = (blocks + len(remote_rows(count_tm))) * BLK
    return pl.pallas_call(
        functools.partial(plan_kernel, count_head, count_tm, blocks),
        in_specs=[
            pl.BlockSpec(memory_space=pltpu.VMEM),
            pl.BlockSpec(memory_space=pltpu.SMEM),
            pl.BlockSpec(memory_space=pl.ANY),
        ],
        out_specs=[pl.BlockSpec(memory_space=pltpu.SMEM), pl.BlockSpec(memory_space=pltpu.VMEM)],
        out_shape=[
            jax.ShapeDtypeStruct((NEAR_CAP * count_tm,), jnp.int32),
            jax.ShapeDtypeStruct((blocks, total), jnp.float32),
        ],
        scratch_shapes=[
            pltpu.VMEM((total_blocks, lanes), jnp.int32),
            pltpu.SMEM((total_blocks, lanes), jnp.int32),
            pltpu.SemaphoreType.DMA,
        ],
        cost_estimate=NO_COST,
        compiler_params=pltpu.CompilerParams(vmem_limit_bytes=VMEM),
    )(pair_list, block_tokens, after)


def attend_kernel(counts, sizes, distances, tokens_ref, bias_ref, query_ref, *refs):
    count_head, count_tm = counts
    queries = by_distance([query_ref], count_head, -1)
    per_part = count_head + count_tm - 1
    parts = [refs[p * per_part : (p + 1) * per_part] for p in range(len(sizes))]
    outs = refs[len(sizes) * per_part :][-len(distances) :]
    blocks, tokens, _ = outs[0].shape
    rows = len(distances) * tokens
    shard = lax.axis_index("tm")
    me = lax.axis_index("head")
    bias = bias_ref[...][:, None, :]
    place_of = [(p, h) for p, size in enumerate(sizes) for h in range(size // HD)]

    def gathered(kind, head):
        p, h = place_of[head]
        first = kind * sizes[p] + h * HD
        lanes = slice(first, first + HD)
        pieces = [rows_of(own[:, :, lanes]) for own in parts[p][:count_head]]
        pieces += [
            rows_of(parts[p][count_head + distance - 1][k, :, :, lanes])
            for distance, k in remote_rows(count_tm)
        ]
        return jnp.concatenate(pieces, axis=0)

    def products(head):
        lanes = slice(head * HD, (head + 1) * HD)
        query = jnp.concatenate(
            [rows_of(queries[s][i, :, lanes]) for i in range(blocks) for s in distances], axis=0
        )
        return lax.dot_general(
            query, gathered(0, head), (((1,), (1,)), ((), ())), preferred_element_type=jnp.float32
        )

    heads = len(place_of)
    dots, mixed = products(0), []
    for h in range(heads):
        ahead = products(h + 1) if h + 1 < heads else None
        dots = dots.reshape(blocks, rows, -1) + bias
        peak = jnp.max(dots, axis=-1, keepdims=True)
        weights = jnp.exp2((dots - peak) * (SCORE_SCALE * LOG2E))
        inverse = 1.0 / jnp.sum(weights, axis=-1, keepdims=True)
        weights_half = weights.astype(jnp.bfloat16).reshape(blocks * rows, -1)
        part = jnp.dot(weights_half, gathered(1, h), preferred_element_type=jnp.float32)
        mixed.append(part * inverse.reshape(blocks * rows, 1))
        dots = ahead
    mixed = jnp.concatenate(mixed, axis=0)
    sign = sign_matrix()
    high = mixed.astype(jnp.bfloat16)
    low = (mixed - high.astype(jnp.float32)).astype(jnp.bfloat16)
    turned = jnp.dot(high, sign, preferred_element_type=jnp.float32)
    turned = turned + jnp.dot(low, sign, preferred_element_type=jnp.float32)
    turned = (turned * ROTATE_SCALE).reshape(heads, blocks, len(distances), tokens, HD)
    token = lax.broadcasted_iota(jnp.int32, (tokens, HD), 0)
    for at, s in enumerate(distances):
        position = lax.rem(me - s + count_head, count_head) * tokens + token
        for i in range(blocks):
            live = position < tokens_ref[shard * blocks + i]
            for h in range(heads):
                outs[at][i, :, h * HD : (h + 1) * HD] = jnp.where(
                    live, turned[h, i, at], 0.0
                ).astype(jnp.bfloat16)


def attend(block_tokens, bias, query, parts, sizes, distances, after, cost):
    count_head, count_tm = query.shape[0], len(parts[0][1]) + 1
    operands = [ref for owns, slots in parts for ref in owns + slots]
    vmem = pl.BlockSpec(memory_space=pltpu.VMEM)
    return pl.pallas_call(
        functools.partial(attend_kernel, (count_head, count_tm), sizes, distances),
        in_specs=[pl.BlockSpec(memory_space=pltpu.SMEM)]
        + [vmem] * (2 + len(operands))
        + [pl.BlockSpec(memory_space=pl.ANY)] * len(after),
        out_specs=[vmem] * len(distances),
        out_shape=[jax.ShapeDtypeStruct(query.shape[1:], jnp.bfloat16)] * len(distances),
        cost_estimate=cost,
        compiler_params=pltpu.CompilerParams(vmem_limit_bytes=VMEM),
    )(block_tokens, bias, query, *operands, *after)


def place_kernel(width_here, *refs):
    pieces, out_ref, sems = refs[:-2], refs[-2], refs[-1]
    me = lax.axis_index("head")
    copies = []
    for s, piece in enumerate(pieces):
        column = pl.multiple_of(lax.rem(me + s, len(pieces)) * width_here, HD)
        copies.append(
            pltpu.make_async_copy(
                piece, out_ref.at[:, :, pl.ds(column, width_here)], sems.at[s]
            )
        )
        copies[-1].start()
    for copy in copies:
        copy.wait()


def place_pieces(pieces):
    blocks, tokens, width_here = pieces[0].shape
    return pl.pallas_call(
        functools.partial(place_kernel, width_here),
        in_specs=[pl.BlockSpec(memory_space=pl.ANY)] * len(pieces),
        out_specs=pl.BlockSpec(memory_space=pltpu.HBM),
        out_shape=jax.ShapeDtypeStruct((blocks, tokens, len(pieces) * width_here), jnp.bfloat16),
        scratch_shapes=[pltpu.SemaphoreType.DMA((len(pieces),))],
        compiler_params=pltpu.CompilerParams(vmem_limit_bytes=VMEM),
    )(*pieces)


def shifted(array, axis, distance):
    count = lax.axis_size(axis)
    return lax.ppermute(array, axis, [(i, (i + distance) % count) for i in range(count)])


def exchange(pieces, direction):
    return [pieces[0]] + [
        shifted(piece, "head", direction * s) for s, piece in enumerate(pieces[1:], 1)
    ]


def forward(sent):
    return [shifted(block, "tm", distance) for distance, block in enumerate(sent, 1)]


def shards(query_rows, key_rows, value_rows, pair_list, block_tokens):
    count_head = lax.axis_size("head")
    count_tm = lax.axis_size("tm")
    blocks, tokens, width = query_rows.shape
    width_here = width // count_head
    heads = width_here // HD
    cut = (heads + 1) // 2 * HD
    parts = [(0, cut), (cut, width_here - cut)] if heads > 1 else [(0, width_here)]
    arrays = [query_rows, key_rows, value_rows]
    packed, after, limit = [], (), WIDE_VMEM
    for part in parts:
        message = [(1,) + part, (2,) + part]
        pieces, token = rotate_pieces(arrays, message, count_head, after, limit)
        packed.append(pieces)
        after, limit = (token,), VMEM
    received = [exchange(pieces, 1) for pieces in packed]
    picks, bias = plan(pair_list, block_tokens, token, blocks, count_head, count_tm)
    sent, after = [], ()
    for owns, (_, size) in zip(received, parts):
        sent.append(pick_blocks(picks, owns, (0, 2 * size), count_tm, after))
        after = (sent[-1][0],)
    message = [(0, 0, width_here)]
    (query,), _ = rotate_pieces(arrays, message, count_head, (sent[0][0],), stacked=True)
    query = lax.all_to_all(query, "head", split_axis=0, concat_axis=0, tiled=True)
    inputs = [(owns, forward(picked)) for owns, picked in zip(received, sent)]
    sizes = [size for _, size in parts]
    leaving = attend(
        block_tokens, bias, query, inputs, sizes, list(range(1, count_head)), (), NO_COST
    )
    staying = attend(block_tokens, bias, query, inputs, sizes, [0], (leaving[0],), NO_COST)
    return place_pieces(exchange(staying + leaving, -1))


def solution(mesh):
    placed = (
        P(("grp", "tm"), "head", None),
        P(("grp", "tm"), "head", None),
        P(("grp", "tm"), "head", None),
        P("grp", None),
        P("grp"),
    )
    return jax.shard_map(
        shards,
        mesh=mesh,
        in_specs=placed,
        out_specs=P(("grp", "tm"), "head", None),
        check_vma=False,
    )
```

```python
import functools
import math

import jax
import jax.numpy as jnp
from jax import lax
from jax.experimental import pallas as pl
from jax.experimental.pallas import tpu as pltpu
from jax.sharding import PartitionSpec as P

HD = 128
BLK = 64
NEAR_CAP = 2
FAR_CAP = 1
NEG = -1e30
ROTATE_SCALE = 1.0 / math.sqrt(HD)
SCORE_SCALE = 1.0 / math.sqrt(HD)
VMEM = 24 * 1024 * 1024
WIDE_VMEM = 60 * 1024 * 1024
TOKEN = jax.ShapeDtypeStruct((8, 128), jnp.float32)
NO_COST = pl.CostEstimate(flops=0, bytes_accessed=0, transcendentals=0)
HIGH_COST = pl.CostEstimate(flops=10**11, bytes_accessed=0, transcendentals=0)
LOG2E = math.log2(math.e)


def sign_matrix():
    common = lax.broadcasted_iota(jnp.int32, (HD, HD), 0) & lax.broadcasted_iota(
        jnp.int32, (HD, HD), 1
    )
    bits = HD.bit_length() - 1
    parity = common
    for bit in range(1, bits):
        parity = parity ^ (common >> bit)
    return jnp.where((parity & 1) == 0, 1.0, -1.0).astype(jnp.bfloat16)


def rows_of(block):
    rows, width = math.prod(block.shape[:-1]), block.shape[-1]
    if block.shape[-2] % 16 == 0:
        return block.reshape(rows, width)
    return block.astype(jnp.float32).reshape(rows, width).astype(block.dtype)


def fields_of(message):
    at, fields = 0, []
    for source, start, size in message:
        fields.append((source, start, size, at))
        at += size
    return fields, at


def by_distance(refs, count, direction):
    if len(refs) > 1:
        return list(refs)
    me = lax.axis_index("head")
    return [refs[0].at[lax.rem(me + direction * s + count, count)] for s in range(count)]


def rotate_kernel(message, sources, count_head, skipped, *refs):
    fields, total = fields_of(message)
    ins = dict(zip(sources, refs))
    outs = by_distance(refs[len(sources) + skipped : -3], count_head, 1)
    token, buffer, sems = refs[-3:]
    token[...] = jnp.zeros_like(token)
    blocks, tokens, width = refs[0].shape
    width_here = width // count_head
    me = lax.axis_index("head")
    order = list(range(1, count_head)) + [0]
    copies = {}
    for s in order:
        goal = lax.rem(me + s, count_head)
        for f, (source, start, size, at) in enumerate(fields):
            column = pl.multiple_of(goal * width_here + start, HD)
            copies[s, f] = pltpu.make_async_copy(
                ins[source].at[:, :, pl.ds(column, size)],
                buffer.at[s, :, :, pl.ds(at, size)],
                sems.at[s, f],
            )
            copies[s, f].start()
    sign = sign_matrix()
    for s in order:
        for f, (_, _, size, start) in enumerate(fields):
            copies[s, f].wait()
            flat = rows_of(buffer[s, :, :, start : start + size])
            heads = [flat[:, at : at + HD] for at in range(0, size, HD)]
            turned = jnp.dot(
                jnp.concatenate(heads, axis=0), sign, preferred_element_type=jnp.float32
            )
            turned = (turned * ROTATE_SCALE).reshape(size // HD, blocks, tokens, HD)
            for h in range(size // HD):
                at = start + h * HD
                outs[s][:, :, at : at + HD] = turned[h].astype(jnp.bfloat16)


def rotate_pieces(arrays, message, count_head, after=(), limit=VMEM, stacked=False):
    blocks, tokens, _ = arrays[0].shape
    fields, total = fields_of(message)
    sources = sorted({source for source, _, _ in message})
    one = (blocks, tokens, total)
    shapes = [(count_head,) + one] if stacked else [one] * count_head
    *pieces, token = pl.pallas_call(
        functools.partial(rotate_kernel, message, sources, count_head, len(after)),
        in_specs=[pl.BlockSpec(memory_space=pltpu.HBM)] * len(sources)
        + [pl.BlockSpec(memory_space=pl.ANY)] * len(after),
        out_specs=[pl.BlockSpec(memory_space=pltpu.VMEM)] * (len(shapes) + 1),
        out_shape=[jax.ShapeDtypeStruct(shape, jnp.bfloat16) for shape in shapes] + [TOKEN],
        scratch_shapes=[
            pltpu.VMEM((count_head,) + one, jnp.bfloat16),
            pltpu.SemaphoreType.DMA((count_head, len(fields))),
        ],
        cost_estimate=NO_COST,
        compiler_params=pltpu.CompilerParams(vmem_limit_bytes=limit),
    )(*[arrays[source] for source in sources], *after)
    return pieces, token


def slots_at(distance, count_tm):
    return NEAR_CAP if distance in (1, count_tm - 1) else FAR_CAP


def pick_kernel(count_head, count_tm, lanes, skipped, picks_ref, *refs):
    pieces, outs = refs[:count_head], refs[count_head + skipped :]
    shard = lax.axis_index("tm")
    for distance, out in enumerate(outs, 1):
        goal = lax.rem(shard + distance, count_tm)
        for k in range(slots_at(distance, count_tm)):
            pick = picks_ref[NEAR_CAP * goal + k]
            for s in range(count_head):
                out[k, s] = pieces[s][pick, :, lanes[0] : lanes[1]]


def pick_blocks(picks, pieces, lanes, count_tm, after):
    count_head = len(pieces)
    one = (count_head, pieces[0].shape[1], lanes[1] - lanes[0])
    vmem = pl.BlockSpec(memory_space=pltpu.VMEM)
    return pl.pallas_call(
        functools.partial(pick_kernel, count_head, count_tm, lanes, len(after)),
        in_specs=[pl.BlockSpec(memory_space=pltpu.SMEM)]
        + [vmem] * count_head
        + [pl.BlockSpec(memory_space=pl.ANY)] * len(after),
        out_specs=[vmem] * (count_tm - 1),
        out_shape=[
            jax.ShapeDtypeStruct((slots_at(distance, count_tm),) + one, jnp.bfloat16)
            for distance in range(1, count_tm)
        ],
        cost_estimate=HIGH_COST,
        compiler_params=pltpu.CompilerParams(vmem_limit_bytes=VMEM),
    )(picks, *pieces, *after)


def remote_rows(count_tm):
    return [
        (distance, k)
        for distance in range(1, count_tm)
        for k in range(slots_at(distance, count_tm))
    ]


def split(value, by):
    if by & (by - 1) == 0:
        return value >> (by.bit_length() - 1), value & (by - 1)
    return lax.div(value, by), lax.rem(value, by)


def plan_kernel(count_head, count_tm, blocks, pair_ref, tokens_ref, _, picks_ref, bias_ref, named_ref, table_ref, sem):
    total_blocks, columns = pair_ref.shape
    pairs = pair_ref[...]
    lane = lax.broadcasted_iota(jnp.int32, named_ref.shape, 1)
    named = jnp.zeros(named_ref.shape, jnp.int32)
    for c in range(columns):
        named = jnp.where(pairs[:, c : c + 1] == lane, 1, named)
    named_ref[...] = named
    copy = pltpu.make_async_copy(named_ref, table_ref, sem)
    copy.start()
    copy.wait()
    shard = lax.axis_index("tm")
    place = lax.axis_index("head")
    mine = shard * blocks

    def two_picks(wanted):
        picks = [jnp.int32(0)] * NEAR_CAP
        count = jnp.int32(0)
        for j in range(blocks):
            for k in range(NEAR_CAP):
                picks[k] = jnp.where((wanted[j] > 0) & (count == k), j, picks[k])
            count = count + wanted[j]
        return picks, count

    def named_by(rows, column):
        found = table_ref[rows, column]
        for i in range(1, blocks):
            found = found | table_ref[rows + i, column]
        return found

    for d in range(count_tm):
        picks, _ = two_picks([named_by(d * blocks, mine + j) for j in range(blocks)])
        for k in range(NEAR_CAP):
            picks_ref[NEAR_CAP * d + k] = picks[k]

    kept = [[table_ref[mine + i, mine + j] * tokens_ref[mine + j] for j in range(blocks)] for i in range(blocks)]
    arrivals = {}
    for distance, k in remote_rows(count_tm):
        first = lax.rem(shard - distance + count_tm, count_tm) * blocks
        if k == 0:
            arrivals[distance] = two_picks([named_by(mine, first + j) for j in range(blocks)])
        picks, count = arrivals[distance]
        there = first + picks[k]
        live = jnp.where(count > k, tokens_ref[there], 0)
        for i in range(blocks):
            kept[i].append(table_ref[mine + i, there] * live)

    total = bias_ref.shape[1]
    piece_rows = BLK // count_head
    at = lax.broadcasted_iota(jnp.int32, (blocks, total), 1)
    query = lax.broadcasted_iota(jnp.int32, (blocks, total), 0)
    own = at < blocks * BLK
    group, token = split(at, piece_rows)
    own_piece, own_block = split(group, blocks)
    far_row, far_group = split(group, count_head)
    row = jnp.where(own, own_block, far_row)
    piece = jnp.where(own, own_piece, far_group)
    source = jnp.where(piece > place, place - piece + count_head, place - piece)
    position = source * piece_rows + token
    limit = jnp.zeros((blocks, total), jnp.int32)
    for r in range(len(kept[0])):
        value = jnp.zeros((blocks, total), jnp.int32)
        for i in range(blocks):
            value = jnp.where(query == i, kept[i][r], value)
        limit = jnp.where(row == r, value, limit)
    bias_ref[...] = jnp.where(position < limit, 0.0, NEG)


def plan(pair_list, block_tokens, after, blocks, count_head, count_tm):
    total_blocks = pair_list.shape[0]
    lanes = -(-total_blocks // 128) * 128
    total = (blocks + len(remote_rows(count_tm))) * BLK
    return pl.pallas_call(
        functools.partial(plan_kernel, count_head, count_tm, blocks),
        in_specs=[
            pl.BlockSpec(memory_space=pltpu.VMEM),
            pl.BlockSpec(memory_space=pltpu.SMEM),
            pl.BlockSpec(memory_space=pl.ANY),
        ],
        out_specs=[pl.BlockSpec(memory_space=pltpu.SMEM), pl.BlockSpec(memory_space=pltpu.VMEM)],
        out_shape=[
            jax.ShapeDtypeStruct((NEAR_CAP * count_tm,), jnp.int32),
            jax.ShapeDtypeStruct((blocks, total), jnp.float32),
        ],
        scratch_shapes=[
            pltpu.VMEM((total_blocks, lanes), jnp.int32),
            pltpu.SMEM((total_blocks, lanes), jnp.int32),
            pltpu.SemaphoreType.DMA,
        ],
        cost_estimate=NO_COST,
        compiler_params=pltpu.CompilerParams(vmem_limit_bytes=VMEM),
    )(pair_list, block_tokens, after)


def attend_kernel(counts, sizes, distances, tokens_ref, bias_ref, query_ref, *refs):
    count_head, count_tm = counts
    queries = by_distance([query_ref], count_head, -1)
    per_part = count_head + count_tm - 1
    parts = [refs[p * per_part : (p + 1) * per_part] for p in range(len(sizes))]
    outs = refs[len(sizes) * per_part :][-len(distances) :]
    blocks, tokens, _ = outs[0].shape
    rows = len(distances) * tokens
    shard = lax.axis_index("tm")
    me = lax.axis_index("head")
    bias = bias_ref[...][:, None, :]
    place_of = [(p, h) for p, size in enumerate(sizes) for h in range(size // HD)]

    def gathered(kind, head):
        p, h = place_of[head]
        first = kind * sizes[p] + h * HD
        lanes = slice(first, first + HD)
        pieces = [rows_of(own[:, :, lanes]) for own in parts[p][:count_head]]
        pieces += [
            rows_of(parts[p][count_head + distance - 1][k, :, :, lanes])
            for distance, k in remote_rows(count_tm)
        ]
        return jnp.concatenate(pieces, axis=0)

    def products(head):
        lanes = slice(head * HD, (head + 1) * HD)
        query = jnp.concatenate(
            [rows_of(queries[s][i, :, lanes]) for i in range(blocks) for s in distances], axis=0
        )
        return lax.dot_general(
            query, gathered(0, head), (((1,), (1,)), ((), ())), preferred_element_type=jnp.float32
        )

    heads = len(place_of)
    dots, mixed = products(0), []
    for h in range(heads):
        ahead = products(h + 1) if h + 1 < heads else None
        dots = dots.reshape(blocks, rows, -1) + bias
        peak = jnp.max(dots, axis=-1, keepdims=True)
        weights = jnp.exp2((dots - peak) * (SCORE_SCALE * LOG2E))
        inverse = 1.0 / jnp.sum(weights, axis=-1, keepdims=True)
        weights_half = weights.astype(jnp.bfloat16).reshape(blocks * rows, -1)
        part = jnp.dot(weights_half, gathered(1, h), preferred_element_type=jnp.float32)
        mixed.append(part * inverse.reshape(blocks * rows, 1))
        dots = ahead
    mixed = jnp.concatenate(mixed, axis=0)
    sign = sign_matrix()
    high = mixed.astype(jnp.bfloat16)
    low = (mixed - high.astype(jnp.float32)).astype(jnp.bfloat16)
    turned = jnp.dot(high, sign, preferred_element_type=jnp.float32)
    turned = turned + jnp.dot(low, sign, preferred_element_type=jnp.float32)
    turned = (turned * ROTATE_SCALE).reshape(heads, blocks, len(distances), tokens, HD)
    token = lax.broadcasted_iota(jnp.int32, (tokens, HD), 0)
    for at, s in enumerate(distances):
        position = lax.rem(me - s + count_head, count_head) * tokens + token
        for i in range(blocks):
            live = position < tokens_ref[shard * blocks + i]
            for h in range(heads):
                outs[at][i, :, h * HD : (h + 1) * HD] = jnp.where(
                    live, turned[h, i, at], 0.0
                ).astype(jnp.bfloat16)


def attend(block_tokens, bias, query, parts, sizes, distances, after, cost):
    count_head, count_tm = query.shape[0], len(parts[0][1]) + 1
    operands = [ref for owns, slots in parts for ref in owns + slots]
    vmem = pl.BlockSpec(memory_space=pltpu.VMEM)
    return pl.pallas_call(
        functools.partial(attend_kernel, (count_head, count_tm), sizes, distances),
        in_specs=[pl.BlockSpec(memory_space=pltpu.SMEM)]
        + [vmem] * (2 + len(operands))
        + [pl.BlockSpec(memory_space=pl.ANY)] * len(after),
        out_specs=[vmem] * len(distances),
        out_shape=[jax.ShapeDtypeStruct(query.shape[1:], jnp.bfloat16)] * len(distances),
        cost_estimate=cost,
        compiler_params=pltpu.CompilerParams(vmem_limit_bytes=VMEM),
    )(block_tokens, bias, query, *operands, *after)


def place_kernel(width_here, *refs):
    pieces, out_ref, sems = refs[:-2], refs[-2], refs[-1]
    me = lax.axis_index("head")
    copies = []
    for s, piece in enumerate(pieces):
        column = pl.multiple_of(lax.rem(me + s, len(pieces)) * width_here, HD)
        copies.append(
            pltpu.make_async_copy(
                piece, out_ref.at[:, :, pl.ds(column, width_here)], sems.at[s]
            )
        )
        copies[-1].start()
    for copy in copies:
        copy.wait()


def place_pieces(pieces):
    blocks, tokens, width_here = pieces[0].shape
    return pl.pallas_call(
        functools.partial(place_kernel, width_here),
        in_specs=[pl.BlockSpec(memory_space=pl.ANY)] * len(pieces),
        out_specs=pl.BlockSpec(memory_space=pltpu.HBM),
        out_shape=jax.ShapeDtypeStruct((blocks, tokens, len(pieces) * width_here), jnp.bfloat16),
        scratch_shapes=[pltpu.SemaphoreType.DMA((len(pieces),))],
        compiler_params=pltpu.CompilerParams(vmem_limit_bytes=VMEM),
    )(*pieces)


def shifted(array, axis, distance):
    count = lax.axis_size(axis)
    return lax.ppermute(array, axis, [(i, (i + distance) % count) for i in range(count)])


def exchange(pieces, direction):
    return [pieces[0]] + [
        shifted(piece, "head", direction * s) for s, piece in enumerate(pieces[1:], 1)
    ]


def forward(sent):
    return [shifted(block, "tm", distance) for distance, block in enumerate(sent, 1)]


def shards(query_rows, key_rows, value_rows, pair_list, block_tokens):
    count_head = lax.axis_size("head")
    count_tm = lax.axis_size("tm")
    blocks, tokens, width = query_rows.shape
    width_here = width // count_head
    heads = width_here // HD
    cut = (heads + 1) // 2 * HD
    parts = [(0, cut), (cut, width_here - cut)] if heads > 1 else [(0, width_here)]
    arrays = [query_rows, key_rows, value_rows]
    packed, after, limit = [], (), WIDE_VMEM
    for part in parts:
        message = [(1,) + part, (2,) + part]
        pieces, token = rotate_pieces(arrays, message, count_head, after, limit)
        packed.append(pieces)
        after, limit = (token,), VMEM
    received = [exchange(pieces, 1) for pieces in packed]
    picks, bias = plan(pair_list, block_tokens, token, blocks, count_head, count_tm)
    inputs, after = [], ()
    for owns, (_, size) in zip(received, parts):
        sent = pick_blocks(picks, owns, (0, 2 * size), count_tm, after)
        if not inputs:
            (query,), _ = rotate_pieces(
                arrays, [(0, 0, width_here)], count_head, (sent[0],), stacked=True
            )
        inputs.append((owns, forward(sent)))
        after = inputs[-1][1]
    query = lax.all_to_all(query, "head", split_axis=0, concat_axis=0, tiled=True)
    sizes = [size for _, size in parts]
    leaving = attend(
        block_tokens, bias, query, inputs, sizes, list(range(1, count_head)), (), NO_COST
    )
    staying = attend(block_tokens, bias, query, inputs, sizes, [0], (leaving[0],), NO_COST)
    return place_pieces(exchange(staying + leaving, -1))


def solution(mesh):
    placed = (
        P(("grp", "tm"), "head", None),
        P(("grp", "tm"), "head", None),
        P(("grp", "tm"), "head", None),
        P("grp", None),
        P("grp"),
    )
    return jax.shard_map(
        shards,
        mesh=mesh,
        in_specs=placed,
        out_specs=P(("grp", "tm"), "head", None),
        check_vma=False,
    )
```

```python
import functools
import math

import jax
import jax.numpy as jnp
from jax import lax
from jax.experimental import pallas as pl
from jax.experimental.pallas import tpu as pltpu
from jax.sharding import PartitionSpec as P

HD = 128
BLK = 64
NEAR_CAP = 2
FAR_CAP = 1
NEG = -1e30
ROTATE_SCALE = 1.0 / math.sqrt(HD)
SCORE_SCALE = 1.0 / math.sqrt(HD)
VMEM = 24 * 1024 * 1024
WIDE_VMEM = 60 * 1024 * 1024
TOKEN = jax.ShapeDtypeStruct((8, 128), jnp.float32)
NO_COST = pl.CostEstimate(flops=0, bytes_accessed=0, transcendentals=0)
HIGH_COST = pl.CostEstimate(flops=10**11, bytes_accessed=0, transcendentals=0)
LOG2E = math.log2(math.e)


def sign_matrix():
    common = lax.broadcasted_iota(jnp.int32, (HD, HD), 0) & lax.broadcasted_iota(
        jnp.int32, (HD, HD), 1
    )
    bits = HD.bit_length() - 1
    parity = common
    for bit in range(1, bits):
        parity = parity ^ (common >> bit)
    return jnp.where((parity & 1) == 0, 1.0, -1.0).astype(jnp.bfloat16)


def rows_of(block):
    rows, width = math.prod(block.shape[:-1]), block.shape[-1]
    if block.shape[-2] % 16 == 0:
        return block.reshape(rows, width)
    return block.astype(jnp.float32).reshape(rows, width).astype(block.dtype)


def fields_of(message):
    at, fields = 0, []
    for source, start, size in message:
        fields.append((source, start, size, at))
        at += size
    return fields, at


def by_distance(refs, count, direction):
    if len(refs) > 1:
        return list(refs)
    me = lax.axis_index("head")
    return [refs[0].at[lax.rem(me + direction * s + count, count)] for s in range(count)]


def rotate_kernel(message, sources, count_head, skipped, *refs):
    fields, total = fields_of(message)
    ins = dict(zip(sources, refs))
    outs = by_distance(refs[len(sources) + skipped : -3], count_head, 1)
    token, buffer, sems = refs[-3:]
    token[...] = jnp.zeros_like(token)
    blocks, tokens, width = refs[0].shape
    width_here = width // count_head
    me = lax.axis_index("head")
    order = list(range(1, count_head)) + [0]
    copies = {}
    for s in order:
        goal = lax.rem(me + s, count_head)
        for f, (source, start, size, at) in enumerate(fields):
            column = pl.multiple_of(goal * width_here + start, HD)
            copies[s, f] = pltpu.make_async_copy(
                ins[source].at[:, :, pl.ds(column, size)],
                buffer.at[s, :, :, pl.ds(at, size)],
                sems.at[s, f],
            )
            copies[s, f].start()
    sign = sign_matrix()
    for s in order:
        for f, (_, _, size, start) in enumerate(fields):
            copies[s, f].wait()
            flat = rows_of(buffer[s, :, :, start : start + size])
            heads = [flat[:, at : at + HD] for at in range(0, size, HD)]
            turned = jnp.dot(
                jnp.concatenate(heads, axis=0), sign, preferred_element_type=jnp.float32
            )
            turned = (turned * ROTATE_SCALE).reshape(size // HD, blocks, tokens, HD)
            for h in range(size // HD):
                at = start + h * HD
                outs[s][:, :, at : at + HD] = turned[h].astype(jnp.bfloat16)


def rotate_pieces(arrays, message, count_head, after=(), limit=VMEM, stacked=False):
    blocks, tokens, _ = arrays[0].shape
    fields, total = fields_of(message)
    sources = sorted({source for source, _, _ in message})
    one = (blocks, tokens, total)
    shapes = [(count_head,) + one] if stacked else [one] * count_head
    *pieces, token = pl.pallas_call(
        functools.partial(rotate_kernel, message, sources, count_head, len(after)),
        in_specs=[pl.BlockSpec(memory_space=pltpu.HBM)] * len(sources)
        + [pl.BlockSpec(memory_space=pl.ANY)] * len(after),
        out_specs=[pl.BlockSpec(memory_space=pltpu.VMEM)] * (len(shapes) + 1),
        out_shape=[jax.ShapeDtypeStruct(shape, jnp.bfloat16) for shape in shapes] + [TOKEN],
        scratch_shapes=[
            pltpu.VMEM((count_head,) + one, jnp.bfloat16),
            pltpu.SemaphoreType.DMA((count_head, len(fields))),
        ],
        cost_estimate=NO_COST,
        compiler_params=pltpu.CompilerParams(vmem_limit_bytes=limit),
    )(*[arrays[source] for source in sources], *after)
    return pieces, token


def slots_at(distance, count_tm):
    return NEAR_CAP if distance in (1, count_tm - 1) else FAR_CAP


def pick_kernel(count_head, count_tm, lanes, skipped, picks_ref, *refs):
    pieces, outs = refs[:count_head], refs[count_head + skipped :]
    shard = lax.axis_index("tm")
    for distance, out in enumerate(outs, 1):
        goal = lax.rem(shard + distance, count_tm)
        for k in range(slots_at(distance, count_tm)):
            pick = picks_ref[NEAR_CAP * goal + k]
            for s in range(count_head):
                out[k, s] = pieces[s][pick, :, lanes[0] : lanes[1]]


def pick_blocks(picks, pieces, lanes, count_tm, after):
    count_head = len(pieces)
    one = (count_head, pieces[0].shape[1], lanes[1] - lanes[0])
    vmem = pl.BlockSpec(memory_space=pltpu.VMEM)
    return pl.pallas_call(
        functools.partial(pick_kernel, count_head, count_tm, lanes, len(after)),
        in_specs=[pl.BlockSpec(memory_space=pltpu.SMEM)]
        + [vmem] * count_head
        + [pl.BlockSpec(memory_space=pl.ANY)] * len(after),
        out_specs=[vmem] * (count_tm - 1),
        out_shape=[
            jax.ShapeDtypeStruct((slots_at(distance, count_tm),) + one, jnp.bfloat16)
            for distance in range(1, count_tm)
        ],
        cost_estimate=HIGH_COST,
        compiler_params=pltpu.CompilerParams(vmem_limit_bytes=VMEM),
    )(picks, *pieces, *after)


def remote_rows(count_tm):
    return [
        (distance, k)
        for distance in range(1, count_tm)
        for k in range(slots_at(distance, count_tm))
    ]


def split(value, by):
    if by & (by - 1) == 0:
        return value >> (by.bit_length() - 1), value & (by - 1)
    return lax.div(value, by), lax.rem(value, by)


def plan_kernel(count_head, count_tm, blocks, pair_ref, tokens_ref, _, picks_ref, bias_ref, named_ref, table_ref, sem):
    total_blocks, columns = pair_ref.shape
    pairs = pair_ref[...]
    lane = lax.broadcasted_iota(jnp.int32, named_ref.shape, 1)
    named = jnp.zeros(named_ref.shape, jnp.int32)
    for c in range(columns):
        named = jnp.where(pairs[:, c : c + 1] == lane, 1, named)
    named_ref[...] = named
    copy = pltpu.make_async_copy(named_ref, table_ref, sem)
    copy.start()
    copy.wait()
    shard = lax.axis_index("tm")
    place = lax.axis_index("head")
    mine = shard * blocks

    def two_picks(wanted):
        picks = [jnp.int32(0)] * NEAR_CAP
        count = jnp.int32(0)
        for j in range(blocks):
            for k in range(NEAR_CAP):
                picks[k] = jnp.where((wanted[j] > 0) & (count == k), j, picks[k])
            count = count + wanted[j]
        return picks, count

    def named_by(rows, column):
        found = table_ref[rows, column]
        for i in range(1, blocks):
            found = found | table_ref[rows + i, column]
        return found

    for d in range(count_tm):
        picks, _ = two_picks([named_by(d * blocks, mine + j) for j in range(blocks)])
        for k in range(NEAR_CAP):
            picks_ref[NEAR_CAP * d + k] = picks[k]

    kept = [[table_ref[mine + i, mine + j] * tokens_ref[mine + j] for j in range(blocks)] for i in range(blocks)]
    arrivals = {}
    for distance, k in remote_rows(count_tm):
        first = lax.rem(shard - distance + count_tm, count_tm) * blocks
        if k == 0:
            arrivals[distance] = two_picks([named_by(mine, first + j) for j in range(blocks)])
        picks, count = arrivals[distance]
        there = first + picks[k]
        live = jnp.where(count > k, tokens_ref[there], 0)
        for i in range(blocks):
            kept[i].append(table_ref[mine + i, there] * live)

    total = bias_ref.shape[1]
    piece_rows = BLK // count_head
    at = lax.broadcasted_iota(jnp.int32, (blocks, total), 1)
    query = lax.broadcasted_iota(jnp.int32, (blocks, total), 0)
    own = at < blocks * BLK
    group, token = split(at, piece_rows)
    own_piece, own_block = split(group, blocks)
    far_row, far_group = split(group, count_head)
    row = jnp.where(own, own_block, far_row)
    piece = jnp.where(own, own_piece, far_group)
    source = jnp.where(piece > place, place - piece + count_head, place - piece)
    position = source * piece_rows + token
    limit = jnp.zeros((blocks, total), jnp.int32)
    for r in range(len(kept[0])):
        value = jnp.zeros((blocks, total), jnp.int32)
        for i in range(blocks):
            value = jnp.where(query == i, kept[i][r], value)
        limit = jnp.where(row == r, value, limit)
    bias_ref[...] = jnp.where(position < limit, 0.0, NEG)


def plan(pair_list, block_tokens, after, blocks, count_head, count_tm):
    total_blocks = pair_list.shape[0]
    lanes = -(-total_blocks // 128) * 128
    total = (blocks + len(remote_rows(count_tm))) * BLK
    return pl.pallas_call(
        functools.partial(plan_kernel, count_head, count_tm, blocks),
        in_specs=[
            pl.BlockSpec(memory_space=pltpu.VMEM),
            pl.BlockSpec(memory_space=pltpu.SMEM),
            pl.BlockSpec(memory_space=pl.ANY),
        ],
        out_specs=[pl.BlockSpec(memory_space=pltpu.SMEM), pl.BlockSpec(memory_space=pltpu.VMEM)],
        out_shape=[
            jax.ShapeDtypeStruct((NEAR_CAP * count_tm,), jnp.int32),
            jax.ShapeDtypeStruct((blocks, total), jnp.float32),
        ],
        scratch_shapes=[
            pltpu.VMEM((total_blocks, lanes), jnp.int32),
            pltpu.SMEM((total_blocks, lanes), jnp.int32),
            pltpu.SemaphoreType.DMA,
        ],
        cost_estimate=NO_COST,
        compiler_params=pltpu.CompilerParams(vmem_limit_bytes=VMEM),
    )(pair_list, block_tokens, after)


def attend_kernel(counts, sizes, distances, tokens_ref, bias_ref, query_ref, *refs):
    count_head, count_tm = counts
    queries = by_distance([query_ref], count_head, -1)
    per_part = count_head + count_tm - 1
    parts = [refs[p * per_part : (p + 1) * per_part] for p in range(len(sizes))]
    outs = refs[len(sizes) * per_part :][-len(distances) :]
    blocks, tokens, _ = outs[0].shape
    rows = len(distances) * tokens
    shard = lax.axis_index("tm")
    me = lax.axis_index("head")
    bias = bias_ref[...][:, None, :]
    place_of = [(p, h) for p, size in enumerate(sizes) for h in range(size // HD)]

    def gathered(kind, head):
        p, h = place_of[head]
        first = kind * sizes[p] + h * HD
        lanes = slice(first, first + HD)
        pieces = [rows_of(own[:, :, lanes]) for own in parts[p][:count_head]]
        pieces += [
            rows_of(parts[p][count_head + distance - 1][k, :, :, lanes])
            for distance, k in remote_rows(count_tm)
        ]
        return jnp.concatenate(pieces, axis=0)

    def products(head):
        lanes = slice(head * HD, (head + 1) * HD)
        query = jnp.concatenate(
            [rows_of(queries[s][i, :, lanes]) for i in range(blocks) for s in distances], axis=0
        )
        return lax.dot_general(
            query, gathered(0, head), (((1,), (1,)), ((), ())), preferred_element_type=jnp.float32
        )

    heads = len(place_of)
    dots, mixed = products(0), []
    for h in range(heads):
        ahead = products(h + 1) if h + 1 < heads else None
        dots = dots.reshape(blocks, rows, -1) + bias
        peak = jnp.max(dots, axis=-1, keepdims=True)
        weights = jnp.exp2((dots - peak) * (SCORE_SCALE * LOG2E))
        inverse = 1.0 / jnp.sum(weights, axis=-1, keepdims=True)
        weights_half = weights.astype(jnp.bfloat16).reshape(blocks * rows, -1)
        part = jnp.dot(weights_half, gathered(1, h), preferred_element_type=jnp.float32)
        mixed.append(part * inverse.reshape(blocks * rows, 1))
        dots = ahead
    mixed = jnp.concatenate(mixed, axis=0)
    sign = sign_matrix()
    high = mixed.astype(jnp.bfloat16)
    low = (mixed - high.astype(jnp.float32)).astype(jnp.bfloat16)
    turned = jnp.dot(high, sign, preferred_element_type=jnp.float32)
    turned = turned + jnp.dot(low, sign, preferred_element_type=jnp.float32)
    turned = (turned * ROTATE_SCALE).reshape(heads, blocks, len(distances), tokens, HD)
    token = lax.broadcasted_iota(jnp.int32, (tokens, HD), 0)
    for at, s in enumerate(distances):
        position = lax.rem(me - s + count_head, count_head) * tokens + token
        for i in range(blocks):
            live = position < tokens_ref[shard * blocks + i]
            for h in range(heads):
                outs[at][i, :, h * HD : (h + 1) * HD] = jnp.where(
                    live, turned[h, i, at], 0.0
                ).astype(jnp.bfloat16)


def attend(block_tokens, bias, query, parts, sizes, distances, after, cost):
    count_head, count_tm = query.shape[0], len(parts[0][1]) + 1
    operands = [ref for owns, slots in parts for ref in owns + slots]
    vmem = pl.BlockSpec(memory_space=pltpu.VMEM)
    return pl.pallas_call(
        functools.partial(attend_kernel, (count_head, count_tm), sizes, distances),
        in_specs=[pl.BlockSpec(memory_space=pltpu.SMEM)]
        + [vmem] * (2 + len(operands))
        + [pl.BlockSpec(memory_space=pl.ANY)] * len(after),
        out_specs=[vmem] * len(distances),
        out_shape=[jax.ShapeDtypeStruct(query.shape[1:], jnp.bfloat16)] * len(distances),
        cost_estimate=cost,
        compiler_params=pltpu.CompilerParams(vmem_limit_bytes=VMEM),
    )(block_tokens, bias, query, *operands, *after)


def place_kernel(width_here, *refs):
    pieces, out_ref, sems = refs[:-2], refs[-2], refs[-1]
    me = lax.axis_index("head")
    copies = []
    for s, piece in enumerate(pieces):
        column = pl.multiple_of(lax.rem(me + s, len(pieces)) * width_here, HD)
        copies.append(
            pltpu.make_async_copy(
                piece, out_ref.at[:, :, pl.ds(column, width_here)], sems.at[s]
            )
        )
        copies[-1].start()
    for copy in copies:
        copy.wait()


def place_pieces(pieces):
    blocks, tokens, width_here = pieces[0].shape
    return pl.pallas_call(
        functools.partial(place_kernel, width_here),
        in_specs=[pl.BlockSpec(memory_space=pl.ANY)] * len(pieces),
        out_specs=pl.BlockSpec(memory_space=pltpu.HBM),
        out_shape=jax.ShapeDtypeStruct((blocks, tokens, len(pieces) * width_here), jnp.bfloat16),
        scratch_shapes=[pltpu.SemaphoreType.DMA((len(pieces),))],
        compiler_params=pltpu.CompilerParams(vmem_limit_bytes=VMEM),
    )(*pieces)


def shifted(array, axis, distance):
    count = lax.axis_size(axis)
    return lax.ppermute(array, axis, [(i, (i + distance) % count) for i in range(count)])


def exchange(pieces, direction):
    return [pieces[0]] + [
        shifted(piece, "head", direction * s) for s, piece in enumerate(pieces[1:], 1)
    ]


def forward(sent):
    return [shifted(block, "tm", distance) for distance, block in enumerate(sent, 1)]


def shards(query_rows, key_rows, value_rows, pair_list, block_tokens):
    count_head = lax.axis_size("head")
    count_tm = lax.axis_size("tm")
    blocks, tokens, width = query_rows.shape
    width_here = width // count_head
    heads = width_here // HD
    cut = (2 * heads + 2) // 3 * HD
    parts = [(0, cut), (cut, width_here - cut)] if heads > 1 else [(0, width_here)]
    arrays = [query_rows, key_rows, value_rows]
    packed, after, limit = [], (), WIDE_VMEM
    for part in parts:
        message = [(1,) + part, (2,) + part]
        pieces, token = rotate_pieces(arrays, message, count_head, after, limit)
        packed.append(pieces)
        after, limit = (token,), VMEM
    received = [exchange(pieces, 1) for pieces in packed]
    picks, bias = plan(pair_list, block_tokens, token, blocks, count_head, count_tm)
    sent, after = [], ()
    for owns, (_, size) in zip(received, parts):
        sent.append(pick_blocks(picks, owns, (0, 2 * size), count_tm, after))
        after = (sent[-1][0],)
    message = [(0, 0, width_here)]
    (query,), _ = rotate_pieces(arrays, message, count_head, (sent[0][0],), stacked=True)
    query = lax.all_to_all(query, "head", split_axis=0, concat_axis=0, tiled=True)
    inputs = [(owns, forward(picked)) for owns, picked in zip(received, sent)]
    sizes = [size for _, size in parts]
    leaving = attend(
        block_tokens, bias, query, inputs, sizes, list(range(1, count_head)), (), NO_COST
    )
    staying = attend(block_tokens, bias, query, inputs, sizes, [0], (leaving[0],), NO_COST)
    return place_pieces(exchange(staying + leaving, -1))


def solution(mesh):
    placed = (
        P(("grp", "tm"), "head", None),
        P(("grp", "tm"), "head", None),
        P(("grp", "tm"), "head", None),
        P("grp", None),
        P("grp"),
    )
    return jax.shard_map(
        shards,
        mesh=mesh,
        in_specs=placed,
        out_specs=P(("grp", "tm"), "head", None),
        check_vma=False,
    )
```

```python
import functools
import math

import jax
import jax.numpy as jnp
from jax import lax
from jax.experimental import pallas as pl
from jax.experimental.pallas import tpu as pltpu
from jax.sharding import PartitionSpec as P

HD = 128
BLK = 64
NEAR_CAP = 2
FAR_CAP = 1
NEG = -1e30
ROTATE_SCALE = 1.0 / math.sqrt(HD)
SCORE_SCALE = 1.0 / math.sqrt(HD)
VMEM = 24 * 1024 * 1024
WIDE_VMEM = 60 * 1024 * 1024
TOKEN = jax.ShapeDtypeStruct((8, 128), jnp.float32)
NO_COST = pl.CostEstimate(flops=0, bytes_accessed=0, transcendentals=0)
HIGH_COST = pl.CostEstimate(flops=10**11, bytes_accessed=0, transcendentals=0)
LOG2E = math.log2(math.e)


def sign_matrix():
    common = lax.broadcasted_iota(jnp.int32, (HD, HD), 0) & lax.broadcasted_iota(
        jnp.int32, (HD, HD), 1
    )
    bits = HD.bit_length() - 1
    parity = common
    for bit in range(1, bits):
        parity = parity ^ (common >> bit)
    return jnp.where((parity & 1) == 0, 1.0, -1.0).astype(jnp.bfloat16)


def rows_of(block):
    rows, width = math.prod(block.shape[:-1]), block.shape[-1]
    if block.shape[-2] % 16 == 0:
        return block.reshape(rows, width)
    return block.astype(jnp.float32).reshape(rows, width).astype(block.dtype)


def fields_of(message):
    at, fields = 0, []
    for source, start, size in message:
        fields.append((source, start, size, at))
        at += size
    return fields, at


def by_distance(refs, count, direction):
    if len(refs) > 1:
        return list(refs)
    me = lax.axis_index("head")
    return [refs[0].at[lax.rem(me + direction * s + count, count)] for s in range(count)]


def rotate_kernel(message, sources, count_head, skipped, *refs):
    fields, total = fields_of(message)
    ins = dict(zip(sources, refs))
    outs = by_distance(refs[len(sources) + skipped : -3], count_head, 1)
    token, buffer, sems = refs[-3:]
    token[...] = jnp.zeros_like(token)
    blocks, tokens, width = refs[0].shape
    width_here = width // count_head
    me = lax.axis_index("head")
    order = list(range(1, count_head)) + [0]
    copies = {}
    for s in order:
        goal = lax.rem(me + s, count_head)
        for f, (source, start, size, at) in enumerate(fields):
            column = pl.multiple_of(goal * width_here + start, HD)
            copies[s, f] = pltpu.make_async_copy(
                ins[source].at[:, :, pl.ds(column, size)],
                buffer.at[s, :, :, pl.ds(at, size)],
                sems.at[s, f],
            )
            copies[s, f].start()
    sign = sign_matrix()
    for s in order:
        for f, (_, _, size, start) in enumerate(fields):
            copies[s, f].wait()
            flat = rows_of(buffer[s, :, :, start : start + size])
            heads = [flat[:, at : at + HD] for at in range(0, size, HD)]
            turned = jnp.dot(
                jnp.concatenate(heads, axis=0), sign, preferred_element_type=jnp.float32
            )
            turned = (turned * ROTATE_SCALE).reshape(size // HD, blocks, tokens, HD)
            for h in range(size // HD):
                at = start + h * HD
                outs[s][:, :, at : at + HD] = turned[h].astype(jnp.bfloat16)


def rotate_pieces(arrays, message, count_head, after=(), limit=VMEM, stacked=False):
    blocks, tokens, _ = arrays[0].shape
    fields, total = fields_of(message)
    sources = sorted({source for source, _, _ in message})
    one = (blocks, tokens, total)
    shapes = [(count_head,) + one] if stacked else [one] * count_head
    *pieces, token = pl.pallas_call(
        functools.partial(rotate_kernel, message, sources, count_head, len(after)),
        in_specs=[pl.BlockSpec(memory_space=pltpu.HBM)] * len(sources)
        + [pl.BlockSpec(memory_space=pl.ANY)] * len(after),
        out_specs=[pl.BlockSpec(memory_space=pltpu.VMEM)] * (len(shapes) + 1),
        out_shape=[jax.ShapeDtypeStruct(shape, jnp.bfloat16) for shape in shapes] + [TOKEN],
        scratch_shapes=[
            pltpu.VMEM((count_head,) + one, jnp.bfloat16),
            pltpu.SemaphoreType.DMA((count_head, len(fields))),
        ],
        cost_estimate=NO_COST,
        compiler_params=pltpu.CompilerParams(vmem_limit_bytes=limit),
    )(*[arrays[source] for source in sources], *after)
    return pieces, token


def slots_at(distance, count_tm):
    return NEAR_CAP if distance in (1, count_tm - 1) else FAR_CAP


def pick_kernel(count_head, count_tm, lanes, skipped, picks_ref, *refs):
    pieces, outs = refs[:count_head], refs[count_head + skipped :]
    shard = lax.axis_index("tm")
    for distance, out in enumerate(outs, 1):
        goal = lax.rem(shard + distance, count_tm)
        for k in range(slots_at(distance, count_tm)):
            pick = picks_ref[NEAR_CAP * goal + k]
            for s in range(count_head):
                out[k, s] = pieces[s][pick, :, lanes[0] : lanes[1]]


def pick_blocks(picks, pieces, lanes, count_tm, after):
    count_head = len(pieces)
    one = (count_head, pieces[0].shape[1], lanes[1] - lanes[0])
    vmem = pl.BlockSpec(memory_space=pltpu.VMEM)
    return pl.pallas_call(
        functools.partial(pick_kernel, count_head, count_tm, lanes, len(after)),
        in_specs=[pl.BlockSpec(memory_space=pltpu.SMEM)]
        + [vmem] * count_head
        + [pl.BlockSpec(memory_space=pl.ANY)] * len(after),
        out_specs=[vmem] * (count_tm - 1),
        out_shape=[
            jax.ShapeDtypeStruct((slots_at(distance, count_tm),) + one, jnp.bfloat16)
            for distance in range(1, count_tm)
        ],
        cost_estimate=HIGH_COST,
        compiler_params=pltpu.CompilerParams(vmem_limit_bytes=VMEM),
    )(picks, *pieces, *after)


def remote_rows(count_tm):
    return [
        (distance, k)
        for distance in range(1, count_tm)
        for k in range(slots_at(distance, count_tm))
    ]


def split(value, by):
    if by & (by - 1) == 0:
        return value >> (by.bit_length() - 1), value & (by - 1)
    return lax.div(value, by), lax.rem(value, by)


def plan_kernel(count_head, count_tm, blocks, pair_ref, tokens_ref, _, picks_ref, bias_ref, named_ref, table_ref, sem):
    total_blocks, columns = pair_ref.shape
    pairs = pair_ref[...]
    lane = lax.broadcasted_iota(jnp.int32, named_ref.shape, 1)
    named = jnp.zeros(named_ref.shape, jnp.int32)
    for c in range(columns):
        named = jnp.where(pairs[:, c : c + 1] == lane, 1, named)
    named_ref[...] = named
    copy = pltpu.make_async_copy(named_ref, table_ref, sem)
    copy.start()
    copy.wait()
    shard = lax.axis_index("tm")
    place = lax.axis_index("head")
    mine = shard * blocks

    def two_picks(wanted):
        picks = [jnp.int32(0)] * NEAR_CAP
        count = jnp.int32(0)
        for j in range(blocks):
            for k in range(NEAR_CAP):
                picks[k] = jnp.where((wanted[j] > 0) & (count == k), j, picks[k])
            count = count + wanted[j]
        return picks, count

    def named_by(rows, column):
        found = table_ref[rows, column]
        for i in range(1, blocks):
            found = found | table_ref[rows + i, column]
        return found

    for d in range(count_tm):
        picks, _ = two_picks([named_by(d * blocks, mine + j) for j in range(blocks)])
        for k in range(NEAR_CAP):
            picks_ref[NEAR_CAP * d + k] = picks[k]

    kept = [[table_ref[mine + i, mine + j] * tokens_ref[mine + j] for j in range(blocks)] for i in range(blocks)]
    arrivals = {}
    for distance, k in remote_rows(count_tm):
        first = lax.rem(shard - distance + count_tm, count_tm) * blocks
        if k == 0:
            arrivals[distance] = two_picks([named_by(mine, first + j) for j in range(blocks)])
        picks, count = arrivals[distance]
        there = first + picks[k]
        live = jnp.where(count > k, tokens_ref[there], 0)
        for i in range(blocks):
            kept[i].append(table_ref[mine + i, there] * live)

    total = bias_ref.shape[1]
    piece_rows = BLK // count_head
    at = lax.broadcasted_iota(jnp.int32, (blocks, total), 1)
    query = lax.broadcasted_iota(jnp.int32, (blocks, total), 0)
    own = at < blocks * BLK
    group, token = split(at, piece_rows)
    own_piece, own_block = split(group, blocks)
    far_row, far_group = split(group, count_head)
    row = jnp.where(own, own_block, far_row)
    piece = jnp.where(own, own_piece, far_group)
    source = jnp.where(piece > place, place - piece + count_head, place - piece)
    position = source * piece_rows + token
    limit = jnp.zeros((blocks, total), jnp.int32)
    for r in range(len(kept[0])):
        value = jnp.zeros((blocks, total), jnp.int32)
        for i in range(blocks):
            value = jnp.where(query == i, kept[i][r], value)
        limit = jnp.where(row == r, value, limit)
    bias_ref[...] = jnp.where(position < limit, 0.0, NEG)


def plan(pair_list, block_tokens, after, blocks, count_head, count_tm):
    total_blocks = pair_list.shape[0]
    lanes = -(-total_blocks // 128) * 128
    total = (blocks + len(remote_rows(count_tm))) * BLK
    return pl.pallas_call(
        functools.partial(plan_kernel, count_head, count_tm, blocks),
        in_specs=[
            pl.BlockSpec(memory_space=pltpu.VMEM),
            pl.BlockSpec(memory_space=pltpu.SMEM),
            pl.BlockSpec(memory_space=pl.ANY),
        ],
        out_specs=[pl.BlockSpec(memory_space=pltpu.SMEM), pl.BlockSpec(memory_space=pltpu.VMEM)],
        out_shape=[
            jax.ShapeDtypeStruct((NEAR_CAP * count_tm,), jnp.int32),
            jax.ShapeDtypeStruct((blocks, total), jnp.float32),
        ],
        scratch_shapes=[
            pltpu.VMEM((total_blocks, lanes), jnp.int32),
            pltpu.SMEM((total_blocks, lanes), jnp.int32),
            pltpu.SemaphoreType.DMA,
        ],
        cost_estimate=NO_COST,
        compiler_params=pltpu.CompilerParams(vmem_limit_bytes=VMEM),
    )(pair_list, block_tokens, after)


def attend_kernel(counts, sizes, distances, tokens_ref, bias_ref, query_ref, *refs):
    count_head, count_tm = counts
    queries = by_distance([query_ref], count_head, -1)
    per_part = count_head + count_tm - 1
    parts = [refs[p * per_part : (p + 1) * per_part] for p in range(len(sizes))]
    outs = refs[len(sizes) * per_part :][-len(distances) :]
    blocks, tokens, _ = outs[0].shape
    rows = len(distances) * tokens
    shard = lax.axis_index("tm")
    me = lax.axis_index("head")
    bias = bias_ref[...][:, None, :]
    place_of = [(p, h) for p, size in enumerate(sizes) for h in range(size // HD)]

    def gathered(kind, head):
        p, h = place_of[head]
        first = kind * sizes[p] + h * HD
        lanes = slice(first, first + HD)
        pieces = [rows_of(own[:, :, lanes]) for own in parts[p][:count_head]]
        pieces += [
            rows_of(parts[p][count_head + distance - 1][k, :, :, lanes])
            for distance, k in remote_rows(count_tm)
        ]
        return jnp.concatenate(pieces, axis=0)

    def products(head):
        lanes = slice(head * HD, (head + 1) * HD)
        query = jnp.concatenate(
            [rows_of(queries[s][i, :, lanes]) for i in range(blocks) for s in distances], axis=0
        )
        return lax.dot_general(
            query, gathered(0, head), (((1,), (1,)), ((), ())), preferred_element_type=jnp.float32
        )

    heads = len(place_of)
    dots, mixed = products(0), []
    for h in range(heads):
        ahead = products(h + 1) if h + 1 < heads else None
        dots = dots.reshape(blocks, rows, -1) + bias
        peak = jnp.max(dots, axis=-1, keepdims=True)
        weights = jnp.exp2((dots - peak) * (SCORE_SCALE * LOG2E))
        inverse = 1.0 / jnp.sum(weights, axis=-1, keepdims=True)
        weights_half = weights.astype(jnp.bfloat16).reshape(blocks * rows, -1)
        part = jnp.dot(weights_half, gathered(1, h), preferred_element_type=jnp.float32)
        mixed.append(part * inverse.reshape(blocks * rows, 1))
        dots = ahead
    mixed = jnp.concatenate(mixed, axis=0)
    sign = sign_matrix()
    high = mixed.astype(jnp.bfloat16)
    low = (mixed - high.astype(jnp.float32)).astype(jnp.bfloat16)
    turned = jnp.dot(high, sign, preferred_element_type=jnp.float32)
    turned = turned + jnp.dot(low, sign, preferred_element_type=jnp.float32)
    turned = (turned * ROTATE_SCALE).reshape(heads, blocks, len(distances), tokens, HD)
    token = lax.broadcasted_iota(jnp.int32, (tokens, HD), 0)
    for at, s in enumerate(distances):
        position = lax.rem(me - s + count_head, count_head) * tokens + token
        for i in range(blocks):
            live = position < tokens_ref[shard * blocks + i]
            for h in range(heads):
                outs[at][i, :, h * HD : (h + 1) * HD] = jnp.where(
                    live, turned[h, i, at], 0.0
                ).astype(jnp.bfloat16)


def attend(block_tokens, bias, query, parts, sizes, distances, after, cost):
    count_head, count_tm = query.shape[0], len(parts[0][1]) + 1
    operands = [ref for owns, slots in parts for ref in owns + slots]
    vmem = pl.BlockSpec(memory_space=pltpu.VMEM)
    return pl.pallas_call(
        functools.partial(attend_kernel, (count_head, count_tm), sizes, distances),
        in_specs=[pl.BlockSpec(memory_space=pltpu.SMEM)]
        + [vmem] * (2 + len(operands))
        + [pl.BlockSpec(memory_space=pl.ANY)] * len(after),
        out_specs=[vmem] * len(distances),
        out_shape=[jax.ShapeDtypeStruct(query.shape[1:], jnp.bfloat16)] * len(distances),
        cost_estimate=cost,
        compiler_params=pltpu.CompilerParams(vmem_limit_bytes=VMEM),
    )(block_tokens, bias, query, *operands, *after)


def place_kernel(width_here, *refs):
    pieces, out_ref, sems = refs[:-2], refs[-2], refs[-1]
    me = lax.axis_index("head")
    copies = []
    for s, piece in enumerate(pieces):
        column = pl.multiple_of(lax.rem(me + s, len(pieces)) * width_here, HD)
        copies.append(
            pltpu.make_async_copy(
                piece, out_ref.at[:, :, pl.ds(column, width_here)], sems.at[s]
            )
        )
        copies[-1].start()
    for copy in copies:
        copy.wait()


def place_pieces(pieces):
    blocks, tokens, width_here = pieces[0].shape
    return pl.pallas_call(
        functools.partial(place_kernel, width_here),
        in_specs=[pl.BlockSpec(memory_space=pl.ANY)] * len(pieces),
        out_specs=pl.BlockSpec(memory_space=pltpu.HBM),
        out_shape=jax.ShapeDtypeStruct((blocks, tokens, len(pieces) * width_here), jnp.bfloat16),
        scratch_shapes=[pltpu.SemaphoreType.DMA((len(pieces),))],
        compiler_params=pltpu.CompilerParams(vmem_limit_bytes=VMEM),
    )(*pieces)


def shifted(array, axis, distance):
    count = lax.axis_size(axis)
    return lax.ppermute(array, axis, [(i, (i + distance) % count) for i in range(count)])


def exchange(pieces, direction):
    return [pieces[0]] + [
        shifted(piece, "head", direction * s) for s, piece in enumerate(pieces[1:], 1)
    ]


def forward(sent):
    return [shifted(block, "tm", distance) for distance, block in enumerate(sent, 1)]


def shards(query_rows, key_rows, value_rows, pair_list, block_tokens):
    count_head = lax.axis_size("head")
    count_tm = lax.axis_size("tm")
    blocks, tokens, width = query_rows.shape
    width_here = width // count_head
    heads = width_here // HD
    cut = (heads + 1) // 2 * HD
    parts = [(0, cut), (cut, width_here - cut)] if heads > 1 else [(0, width_here)]
    arrays = [query_rows, key_rows, value_rows]
    messages = [[(1,) + part, (2,) + part] for part in parts]
    pieces, token = rotate_pieces(arrays, messages[0], count_head, limit=WIDE_VMEM)
    packed = [pieces]
    picks, bias = plan(pair_list, block_tokens, token, blocks, count_head, count_tm)
    after = (bias,)
    for message in messages[1:]:
        pieces, token = rotate_pieces(arrays, message, count_head, after)
        packed.append(pieces)
        after = (token,)
    received = [exchange(pieces, 1) for pieces in packed]
    sent, after = [], (received[-1][1],)
    for owns, (_, size) in zip(received, parts):
        sent.append(pick_blocks(picks, owns, (0, 2 * size), count_tm, after))
        after = (sent[-1][0],)
    message = [(0, 0, width_here)]
    (query,), _ = rotate_pieces(arrays, message, count_head, (sent[0][0],), stacked=True)
    query = lax.all_to_all(query, "head", split_axis=0, concat_axis=0, tiled=True)
    inputs = [(owns, forward(picked)) for owns, picked in zip(received, sent)]
    sizes = [size for _, size in parts]
    leaving = attend(
        block_tokens, bias, query, inputs, sizes, list(range(1, count_head)), (), NO_COST
    )
    staying = attend(block_tokens, bias, query, inputs, sizes, [0], (leaving[0],), NO_COST)
    return place_pieces(exchange(staying + leaving, -1))


def solution(mesh):
    placed = (
        P(("grp", "tm"), "head", None),
        P(("grp", "tm"), "head", None),
        P(("grp", "tm"), "head", None),
        P("grp", None),
        P("grp"),
    )
    return jax.shard_map(
        shards,
        mesh=mesh,
        in_specs=placed,
        out_specs=P(("grp", "tm"), "head", None),
        check_vma=False,
    )
```

```python
import functools
import math

import jax
import jax.numpy as jnp
from jax import lax
from jax.experimental import pallas as pl
from jax.experimental.pallas import tpu as pltpu
from jax.sharding import PartitionSpec as P

HD = 128
BLK = 64
NEAR_CAP = 2
FAR_CAP = 1
NEG = -1e30
ROTATE_SCALE = 1.0 / math.sqrt(HD)
SCORE_SCALE = 1.0 / math.sqrt(HD)
VMEM = 24 * 1024 * 1024
WIDE_VMEM = 60 * 1024 * 1024
TOKEN = jax.ShapeDtypeStruct((8, 128), jnp.float32)
NO_COST = pl.CostEstimate(flops=0, bytes_accessed=0, transcendentals=0)
HIGH_COST = pl.CostEstimate(flops=10**11, bytes_accessed=0, transcendentals=0)
LOG2E = math.log2(math.e)


def sign_matrix():
    common = lax.broadcasted_iota(jnp.int32, (HD, HD), 0) & lax.broadcasted_iota(
        jnp.int32, (HD, HD), 1
    )
    bits = HD.bit_length() - 1
    parity = common
    for bit in range(1, bits):
        parity = parity ^ (common >> bit)
    return jnp.where((parity & 1) == 0, 1.0, -1.0).astype(jnp.bfloat16)


def rows_of(block):
    rows, width = math.prod(block.shape[:-1]), block.shape[-1]
    if block.shape[-2] % 16 == 0:
        return block.reshape(rows, width)
    return block.astype(jnp.float32).reshape(rows, width).astype(block.dtype)


def fields_of(message):
    at, fields = 0, []
    for source, start, size in message:
        fields.append((source, start, size, at))
        at += size
    return fields, at


def by_distance(refs, count, direction):
    if len(refs) > 1:
        return list(refs)
    me = lax.axis_index("head")
    return [refs[0].at[lax.rem(me + direction * s + count, count)] for s in range(count)]


def rotate_kernel(message, sources, count_head, skipped, *refs):
    fields, total = fields_of(message)
    ins = dict(zip(sources, refs))
    outs = by_distance(refs[len(sources) + skipped : -3], count_head, 1)
    token, buffer, sems = refs[-3:]
    token[...] = jnp.zeros_like(token)
    blocks, tokens, width = refs[0].shape
    width_here = width // count_head
    me = lax.axis_index("head")
    order = list(range(1, count_head)) + [0]
    copies = {}
    for s in order:
        goal = lax.rem(me + s, count_head)
        for f, (source, start, size, at) in enumerate(fields):
            column = pl.multiple_of(goal * width_here + start, HD)
            copies[s, f] = pltpu.make_async_copy(
                ins[source].at[:, :, pl.ds(column, size)],
                buffer.at[s, :, :, pl.ds(at, size)],
                sems.at[s, f],
            )
            copies[s, f].start()
    sign = sign_matrix()
    for s in order:
        for f, (_, _, size, start) in enumerate(fields):
            copies[s, f].wait()
            flat = rows_of(buffer[s, :, :, start : start + size])
            heads = [flat[:, at : at + HD] for at in range(0, size, HD)]
            turned = jnp.dot(
                jnp.concatenate(heads, axis=0), sign, preferred_element_type=jnp.float32
            )
            turned = (turned * ROTATE_SCALE).reshape(size // HD, blocks, tokens, HD)
            for h in range(size // HD):
                at = start + h * HD
                outs[s][:, :, at : at + HD] = turned[h].astype(jnp.bfloat16)


def rotate_pieces(arrays, message, count_head, after=(), limit=VMEM, stacked=False):
    blocks, tokens, _ = arrays[0].shape
    fields, total = fields_of(message)
    sources = sorted({source for source, _, _ in message})
    one = (blocks, tokens, total)
    shapes = [(count_head,) + one] if stacked else [one] * count_head
    *pieces, token = pl.pallas_call(
        functools.partial(rotate_kernel, message, sources, count_head, len(after)),
        in_specs=[pl.BlockSpec(memory_space=pltpu.HBM)] * len(sources)
        + [pl.BlockSpec(memory_space=pl.ANY)] * len(after),
        out_specs=[pl.BlockSpec(memory_space=pltpu.VMEM)] * (len(shapes) + 1),
        out_shape=[jax.ShapeDtypeStruct(shape, jnp.bfloat16) for shape in shapes] + [TOKEN],
        scratch_shapes=[
            pltpu.VMEM((count_head,) + one, jnp.bfloat16),
            pltpu.SemaphoreType.DMA((count_head, len(fields))),
        ],
        cost_estimate=NO_COST,
        compiler_params=pltpu.CompilerParams(vmem_limit_bytes=limit),
    )(*[arrays[source] for source in sources], *after)
    return pieces, token


def slots_at(distance, count_tm):
    return NEAR_CAP if distance in (1, count_tm - 1) else FAR_CAP


def pick_kernel(count_head, count_tm, lanes, skipped, picks_ref, *refs):
    pieces, outs = refs[:count_head], refs[count_head + skipped :]
    shard = lax.axis_index("tm")
    for distance, out in enumerate(outs, 1):
        goal = lax.rem(shard + distance, count_tm)
        for k in range(slots_at(distance, count_tm)):
            pick = picks_ref[NEAR_CAP * goal + k]
            for s in range(count_head):
                out[k, s] = pieces[s][pick, :, lanes[0] : lanes[1]]


def pick_blocks(picks, pieces, lanes, count_tm, after):
    count_head = len(pieces)
    one = (count_head, pieces[0].shape[1], lanes[1] - lanes[0])
    vmem = pl.BlockSpec(memory_space=pltpu.VMEM)
    return pl.pallas_call(
        functools.partial(pick_kernel, count_head, count_tm, lanes, len(after)),
        in_specs=[pl.BlockSpec(memory_space=pltpu.SMEM)]
        + [vmem] * count_head
        + [pl.BlockSpec(memory_space=pl.ANY)] * len(after),
        out_specs=[vmem] * (count_tm - 1),
        out_shape=[
            jax.ShapeDtypeStruct((slots_at(distance, count_tm),) + one, jnp.bfloat16)
            for distance in range(1, count_tm)
        ],
        cost_estimate=HIGH_COST,
        compiler_params=pltpu.CompilerParams(vmem_limit_bytes=VMEM),
    )(picks, *pieces, *after)


def remote_rows(count_tm):
    return [
        (distance, k)
        for distance in range(1, count_tm)
        for k in range(slots_at(distance, count_tm))
    ]


def split(value, by):
    if by & (by - 1) == 0:
        return value >> (by.bit_length() - 1), value & (by - 1)
    return lax.div(value, by), lax.rem(value, by)


def plan_kernel(count_head, count_tm, blocks, pair_ref, tokens_ref, _, picks_ref, bias_ref, named_ref, table_ref, sem):
    total_blocks, columns = pair_ref.shape
    pairs = pair_ref[...]
    lane = lax.broadcasted_iota(jnp.int32, named_ref.shape, 1)
    named = jnp.zeros(named_ref.shape, jnp.int32)
    for c in range(columns):
        named = jnp.where(pairs[:, c : c + 1] == lane, 1, named)
    named_ref[...] = named
    copy = pltpu.make_async_copy(named_ref, table_ref, sem)
    copy.start()
    copy.wait()
    shard = lax.axis_index("tm")
    place = lax.axis_index("head")
    mine = shard * blocks

    def two_picks(wanted):
        picks = [jnp.int32(0)] * NEAR_CAP
        count = jnp.int32(0)
        for j in range(blocks):
            for k in range(NEAR_CAP):
                picks[k] = jnp.where((wanted[j] > 0) & (count == k), j, picks[k])
            count = count + wanted[j]
        return picks, count

    def named_by(rows, column):
        found = table_ref[rows, column]
        for i in range(1, blocks):
            found = found | table_ref[rows + i, column]
        return found

    for d in range(count_tm):
        picks, _ = two_picks([named_by(d * blocks, mine + j) for j in range(blocks)])
        for k in range(NEAR_CAP):
            picks_ref[NEAR_CAP * d + k] = picks[k]

    kept = [[table_ref[mine + i, mine + j] * tokens_ref[mine + j] for j in range(blocks)] for i in range(blocks)]
    arrivals = {}
    for distance, k in remote_rows(count_tm):
        first = lax.rem(shard - distance + count_tm, count_tm) * blocks
        if k == 0:
            arrivals[distance] = two_picks([named_by(mine, first + j) for j in range(blocks)])
        picks, count = arrivals[distance]
        there = first + picks[k]
        live = jnp.where(count > k, tokens_ref[there], 0)
        for i in range(blocks):
            kept[i].append(table_ref[mine + i, there] * live)

    total = bias_ref.shape[1]
    piece_rows = BLK // count_head
    at = lax.broadcasted_iota(jnp.int32, (blocks, total), 1)
    query = lax.broadcasted_iota(jnp.int32, (blocks, total), 0)
    own = at < blocks * BLK
    group, token = split(at, piece_rows)
    own_piece, own_block = split(group, blocks)
    far_row, far_group = split(group, count_head)
    row = jnp.where(own, own_block, far_row)
    piece = jnp.where(own, own_piece, far_group)
    source = jnp.where(piece > place, place - piece + count_head, place - piece)
    position = source * piece_rows + token
    limit = jnp.zeros((blocks, total), jnp.int32)
    for r in range(len(kept[0])):
        value = jnp.zeros((blocks, total), jnp.int32)
        for i in range(blocks):
            value = jnp.where(query == i, kept[i][r], value)
        limit = jnp.where(row == r, value, limit)
    bias_ref[...] = jnp.where(position < limit, 0.0, NEG)


def plan(pair_list, block_tokens, after, blocks, count_head, count_tm):
    total_blocks = pair_list.shape[0]
    lanes = -(-total_blocks // 128) * 128
    total = (blocks + len(remote_rows(count_tm))) * BLK
    return pl.pallas_call(
        functools.partial(plan_kernel, count_head, count_tm, blocks),
        in_specs=[
            pl.BlockSpec(memory_space=pltpu.VMEM),
            pl.BlockSpec(memory_space=pltpu.SMEM),
            pl.BlockSpec(memory_space=pl.ANY),
        ],
        out_specs=[pl.BlockSpec(memory_space=pltpu.SMEM), pl.BlockSpec(memory_space=pltpu.VMEM)],
        out_shape=[
            jax.ShapeDtypeStruct((NEAR_CAP * count_tm,), jnp.int32),
            jax.ShapeDtypeStruct((blocks, total), jnp.float32),
        ],
        scratch_shapes=[
            pltpu.VMEM((total_blocks, lanes), jnp.int32),
            pltpu.SMEM((total_blocks, lanes), jnp.int32),
            pltpu.SemaphoreType.DMA,
        ],
        cost_estimate=NO_COST,
        compiler_params=pltpu.CompilerParams(vmem_limit_bytes=VMEM),
    )(pair_list, block_tokens, after)


def attend_kernel(counts, heads_of, distances, tokens_ref, bias_ref, query_ref, *refs):
    count_head, count_tm = counts
    queries = by_distance([query_ref], count_head, -1)
    per_part = count_head + count_tm - 1
    parts = [refs[p * per_part : (p + 1) * per_part] for p in range(len(heads_of))]
    outs = refs[len(heads_of) * per_part :][-len(distances) :]
    blocks, tokens, _ = outs[0].shape
    rows = len(distances) * tokens
    shard = lax.axis_index("tm")
    me = lax.axis_index("head")
    bias = bias_ref[...][:, None, :]
    place_of = [(p, h) for p, (_, size) in enumerate(heads_of) for h in range(size // HD)]

    def gathered(kind, head):
        p, h = place_of[head]
        first = kind * heads_of[p][1] + h * HD
        lanes = slice(first, first + HD)
        pieces = [rows_of(own[:, :, lanes]) for own in parts[p][:count_head]]
        pieces += [
            rows_of(parts[p][count_head + distance - 1][k, :, :, lanes])
            for distance, k in remote_rows(count_tm)
        ]
        return jnp.concatenate(pieces, axis=0)

    def products(head):
        first = heads_of[0][0] + head * HD
        lanes = slice(first, first + HD)
        query = jnp.concatenate(
            [rows_of(queries[s][i, :, lanes]) for i in range(blocks) for s in distances], axis=0
        )
        return lax.dot_general(
            query, gathered(0, head), (((1,), (1,)), ((), ())), preferred_element_type=jnp.float32
        )

    heads = len(place_of)
    dots, mixed = products(0), []
    for h in range(heads):
        ahead = products(h + 1) if h + 1 < heads else None
        dots = dots.reshape(blocks, rows, -1) + bias
        peak = jnp.max(dots, axis=-1, keepdims=True)
        weights = jnp.exp2((dots - peak) * (SCORE_SCALE * LOG2E))
        inverse = 1.0 / jnp.sum(weights, axis=-1, keepdims=True)
        weights_half = weights.astype(jnp.bfloat16).reshape(blocks * rows, -1)
        part = jnp.dot(weights_half, gathered(1, h), preferred_element_type=jnp.float32)
        mixed.append(part * inverse.reshape(blocks * rows, 1))
        dots = ahead
    mixed = jnp.concatenate(mixed, axis=0)
    sign = sign_matrix()
    high = mixed.astype(jnp.bfloat16)
    low = (mixed - high.astype(jnp.float32)).astype(jnp.bfloat16)
    turned = jnp.dot(high, sign, preferred_element_type=jnp.float32)
    turned = turned + jnp.dot(low, sign, preferred_element_type=jnp.float32)
    turned = (turned * ROTATE_SCALE).reshape(heads, blocks, len(distances), tokens, HD)
    token = lax.broadcasted_iota(jnp.int32, (tokens, HD), 0)
    for at, s in enumerate(distances):
        position = lax.rem(me - s + count_head, count_head) * tokens + token
        for i in range(blocks):
            live = position < tokens_ref[shard * blocks + i]
            for h in range(heads):
                outs[at][i, :, h * HD : (h + 1) * HD] = jnp.where(
                    live, turned[h, i, at], 0.0
                ).astype(jnp.bfloat16)


def attend(block_tokens, bias, query, parts, heads_of, distances, after=(), cost=NO_COST):
    count_head, count_tm = query.shape[0], len(parts[0][1]) + 1
    operands = [ref for owns, slots in parts for ref in owns + slots]
    shape = query.shape[1:3] + (sum(size for _, size in heads_of),)
    vmem = pl.BlockSpec(memory_space=pltpu.VMEM)
    return pl.pallas_call(
        functools.partial(attend_kernel, (count_head, count_tm), heads_of, distances),
        in_specs=[pl.BlockSpec(memory_space=pltpu.SMEM)]
        + [vmem] * (2 + len(operands))
        + [pl.BlockSpec(memory_space=pl.ANY)] * len(after),
        out_specs=[vmem] * len(distances),
        out_shape=[jax.ShapeDtypeStruct(shape, jnp.bfloat16)] * len(distances),
        cost_estimate=cost,
        compiler_params=pltpu.CompilerParams(vmem_limit_bytes=VMEM),
    )(block_tokens, bias, query, *operands, *after)


def place_kernel(places, width_here, *refs):
    pieces, out_ref, sems = refs[:-2], refs[-2], refs[-1]
    me, count = lax.axis_index("head"), lax.axis_size("head")
    copies = []
    for at, (piece, (s, start)) in enumerate(zip(pieces, places)):
        column = pl.multiple_of(lax.rem(me + s, count) * width_here + start, HD)
        copies.append(
            pltpu.make_async_copy(
                piece, out_ref.at[:, :, pl.ds(column, piece.shape[-1])], sems.at[at]
            )
        )
        copies[-1].start()
    for copy in copies:
        copy.wait()


def place_pieces(pieces, places, width_here):
    blocks, tokens, _ = pieces[0].shape
    width = width_here * lax.axis_size("head")
    return pl.pallas_call(
        functools.partial(place_kernel, places, width_here),
        in_specs=[pl.BlockSpec(memory_space=pl.ANY)] * len(pieces),
        out_specs=pl.BlockSpec(memory_space=pltpu.HBM),
        out_shape=jax.ShapeDtypeStruct((blocks, tokens, width), jnp.bfloat16),
        scratch_shapes=[pltpu.SemaphoreType.DMA((len(pieces),))],
        compiler_params=pltpu.CompilerParams(vmem_limit_bytes=VMEM),
    )(*pieces)


def shifted(array, axis, distance):
    count = lax.axis_size(axis)
    return lax.ppermute(array, axis, [(i, (i + distance) % count) for i in range(count)])


def exchange(pieces, direction):
    return [shifted(piece, "head", direction * s) for s, piece in enumerate(pieces, 1)]


def forward(sent):
    return [shifted(block, "tm", distance) for distance, block in enumerate(sent, 1)]


def shards(query_rows, key_rows, value_rows, pair_list, block_tokens):
    count_head = lax.axis_size("head")
    count_tm = lax.axis_size("tm")
    blocks, tokens, width = query_rows.shape
    width_here = width // count_head
    heads = width_here // HD
    cut = (heads + 1) // 2 * HD
    parts = [(0, cut), (cut, width_here - cut)] if heads > 1 else [(0, width_here)]
    arrays = [query_rows, key_rows, value_rows]
    messages = [[(1,) + part, (2,) + part] for part in parts]
    pieces, token = rotate_pieces(arrays, messages[0], count_head, limit=WIDE_VMEM)
    packed = [pieces]
    picks, bias = plan(pair_list, block_tokens, token, blocks, count_head, count_tm)
    after = (bias,)
    for message in messages[1:]:
        pieces, token = rotate_pieces(arrays, message, count_head, after)
        packed.append(pieces)
        after = (token,)
    received = [pieces[:1] + exchange(pieces[1:], 1) for pieces in packed]
    sent, after = [], ()
    for owns, (_, size) in zip(received, parts):
        sent.append(pick_blocks(picks, owns, (0, 2 * size), count_tm, after))
        after = (sent[-1][0],)
    message = [(0, 0, width_here)]
    (query,), _ = rotate_pieces(arrays, message, count_head, (sent[0][0],), stacked=True)
    query = lax.all_to_all(query, "head", split_axis=0, concat_axis=0, tiled=True)
    inputs = [(owns, forward(picked)) for owns, picked in zip(received, sent)]
    distances, after = list(range(1, count_head)), ()
    pieces, places = [], []
    for at, part in enumerate(parts):
        cost = NO_COST if at == len(parts) - 1 else HIGH_COST
        leaving = attend(
            block_tokens, bias, query, [inputs[at]], [part], distances, after, cost
        )
        after = (leaving[0],)
        pieces += exchange(leaving, -1)
        places += [(s, part[0]) for s in distances]
    pieces += attend(block_tokens, bias, query, inputs, parts, [0], after)
    return place_pieces(pieces, places + [(0, 0)], width_here)


def solution(mesh):
    placed = (
        P(("grp", "tm"), "head", None),
        P(("grp", "tm"), "head", None),
        P(("grp", "tm"), "head", None),
        P("grp", None),
        P("grp"),
    )
    return jax.shard_map(
        shards,
        mesh=mesh,
        in_specs=placed,
        out_specs=P(("grp", "tm"), "head", None),
        check_vma=False,
    )
```

```python
import functools
import math

import jax
import jax.numpy as jnp
from jax import lax
from jax.experimental import pallas as pl
from jax.experimental.pallas import tpu as pltpu
from jax.sharding import PartitionSpec as P

HD = 128
BLK = 64
NEAR_CAP = 2
FAR_CAP = 1
NEG = -1e30
ROTATE_SCALE = 1.0 / math.sqrt(HD)
SCORE_SCALE = 1.0 / math.sqrt(HD)
VMEM = 24 * 1024 * 1024
WIDE_VMEM = 60 * 1024 * 1024
TOKEN = jax.ShapeDtypeStruct((8, 128), jnp.float32)
NO_COST = pl.CostEstimate(flops=0, bytes_accessed=0, transcendentals=0)
HIGH_COST = pl.CostEstimate(flops=10**11, bytes_accessed=0, transcendentals=0)
LOG2E = math.log2(math.e)


def sign_matrix():
    common = lax.broadcasted_iota(jnp.int32, (HD, HD), 0) & lax.broadcasted_iota(
        jnp.int32, (HD, HD), 1
    )
    bits = HD.bit_length() - 1
    parity = common
    for bit in range(1, bits):
        parity = parity ^ (common >> bit)
    return jnp.where((parity & 1) == 0, 1.0, -1.0).astype(jnp.bfloat16)


def rows_of(block):
    rows, width = math.prod(block.shape[:-1]), block.shape[-1]
    if block.shape[-2] % 16 == 0:
        return block.reshape(rows, width)
    return block.astype(jnp.float32).reshape(rows, width).astype(block.dtype)


def fields_of(message):
    at, fields = 0, []
    for source, start, size in message:
        fields.append((source, start, size, at))
        at += size
    return fields, at


def by_distance(refs, count, direction):
    if len(refs[0].shape) == 3:
        return list(refs)
    me = lax.axis_index("head")
    return [refs[0].at[lax.rem(me + direction * s + count, count)] for s in range(count)]


def rotate_kernel(message, sources, count_head, distances, skipped, *refs):
    fields, total = fields_of(message)
    ins = dict(zip(sources, refs))
    outs = by_distance(refs[len(sources) + skipped : -3], count_head, 1)
    outs = dict(zip(distances, outs))
    token, buffer, sems = refs[-3:]
    token[...] = jnp.zeros_like(token)
    blocks, tokens, width = refs[0].shape
    width_here = width // count_head
    me = lax.axis_index("head")
    copies = {}
    for at_piece, s in enumerate(distances):
        goal = lax.rem(me + s, count_head)
        for f, (source, start, size, at) in enumerate(fields):
            column = pl.multiple_of(goal * width_here + start, HD)
            copies[s, f] = pltpu.make_async_copy(
                ins[source].at[:, :, pl.ds(column, size)],
                buffer.at[at_piece, :, :, pl.ds(at, size)],
                sems.at[at_piece, f],
            )
            copies[s, f].start()
    sign = sign_matrix()
    for at_piece, s in enumerate(distances):
        for f, (_, _, size, start) in enumerate(fields):
            copies[s, f].wait()
            flat = rows_of(buffer[at_piece, :, :, start : start + size])
            heads = [flat[:, at : at + HD] for at in range(0, size, HD)]
            turned = jnp.dot(
                jnp.concatenate(heads, axis=0), sign, preferred_element_type=jnp.float32
            )
            turned = (turned * ROTATE_SCALE).reshape(size // HD, blocks, tokens, HD)
            for h in range(size // HD):
                at = start + h * HD
                outs[s][:, :, at : at + HD] = turned[h].astype(jnp.bfloat16)


def rotate_pieces(arrays, message, count_head, distances, after=(), limit=VMEM, stacked=False):
    blocks, tokens, _ = arrays[0].shape
    fields, total = fields_of(message)
    sources = sorted({source for source, _, _ in message})
    count = len(distances)
    one = (blocks, tokens, total)
    shapes = [(count,) + one] if stacked else [one] * count
    *pieces, token = pl.pallas_call(
        functools.partial(rotate_kernel, message, sources, count_head, distances, len(after)),
        in_specs=[pl.BlockSpec(memory_space=pltpu.HBM)] * len(sources)
        + [pl.BlockSpec(memory_space=pl.ANY)] * len(after),
        out_specs=[pl.BlockSpec(memory_space=pltpu.VMEM)] * (len(shapes) + 1),
        out_shape=[jax.ShapeDtypeStruct(shape, jnp.bfloat16) for shape in shapes] + [TOKEN],
        scratch_shapes=[
            pltpu.VMEM((count,) + one, jnp.bfloat16),
            pltpu.SemaphoreType.DMA((count, len(fields))),
        ],
        cost_estimate=NO_COST,
        compiler_params=pltpu.CompilerParams(vmem_limit_bytes=limit),
    )(*[arrays[source] for source in sources], *after)
    return pieces, token


def slots_at(distance, count_tm):
    return NEAR_CAP if distance in (1, count_tm - 1) else FAR_CAP


def pick_kernel(count_head, count_tm, lanes, skipped, picks_ref, *refs):
    pieces, outs = refs[:count_head], refs[count_head + skipped :]
    shard = lax.axis_index("tm")
    for distance, out in enumerate(outs, 1):
        goal = lax.rem(shard + distance, count_tm)
        for k in range(slots_at(distance, count_tm)):
            pick = picks_ref[NEAR_CAP * goal + k]
            for s in range(count_head):
                out[k, s] = pieces[s][pick, :, lanes[0] : lanes[1]]


def pick_blocks(picks, pieces, lanes, count_tm, after):
    count_head = len(pieces)
    one = (count_head, pieces[0].shape[1], lanes[1] - lanes[0])
    vmem = pl.BlockSpec(memory_space=pltpu.VMEM)
    return pl.pallas_call(
        functools.partial(pick_kernel, count_head, count_tm, lanes, len(after)),
        in_specs=[pl.BlockSpec(memory_space=pltpu.SMEM)]
        + [vmem] * count_head
        + [pl.BlockSpec(memory_space=pl.ANY)] * len(after),
        out_specs=[vmem] * (count_tm - 1),
        out_shape=[
            jax.ShapeDtypeStruct((slots_at(distance, count_tm),) + one, jnp.bfloat16)
            for distance in range(1, count_tm)
        ],
        cost_estimate=HIGH_COST,
        compiler_params=pltpu.CompilerParams(vmem_limit_bytes=VMEM),
    )(picks, *pieces, *after)


def remote_rows(count_tm):
    return [
        (distance, k)
        for distance in range(1, count_tm)
        for k in range(slots_at(distance, count_tm))
    ]


def split(value, by):
    if by & (by - 1) == 0:
        return value >> (by.bit_length() - 1), value & (by - 1)
    return lax.div(value, by), lax.rem(value, by)


def plan_kernel(count_head, count_tm, blocks, pair_ref, tokens_ref, _, picks_ref, bias_ref, named_ref, table_ref, sem):
    total_blocks, columns = pair_ref.shape
    pairs = pair_ref[...]
    lane = lax.broadcasted_iota(jnp.int32, named_ref.shape, 1)
    named = jnp.zeros(named_ref.shape, jnp.int32)
    for c in range(columns):
        named = jnp.where(pairs[:, c : c + 1] == lane, 1, named)
    named_ref[...] = named
    copy = pltpu.make_async_copy(named_ref, table_ref, sem)
    copy.start()
    copy.wait()
    shard = lax.axis_index("tm")
    place = lax.axis_index("head")
    mine = shard * blocks

    def two_picks(wanted):
        picks = [jnp.int32(0)] * NEAR_CAP
        count = jnp.int32(0)
        for j in range(blocks):
            for k in range(NEAR_CAP):
                picks[k] = jnp.where((wanted[j] > 0) & (count == k), j, picks[k])
            count = count + wanted[j]
        return picks, count

    def named_by(rows, column):
        found = table_ref[rows, column]
        for i in range(1, blocks):
            found = found | table_ref[rows + i, column]
        return found

    for d in range(count_tm):
        picks, _ = two_picks([named_by(d * blocks, mine + j) for j in range(blocks)])
        for k in range(NEAR_CAP):
            picks_ref[NEAR_CAP * d + k] = picks[k]

    kept = [[table_ref[mine + i, mine + j] * tokens_ref[mine + j] for j in range(blocks)] for i in range(blocks)]
    arrivals = {}
    for distance, k in remote_rows(count_tm):
        first = lax.rem(shard - distance + count_tm, count_tm) * blocks
        if k == 0:
            arrivals[distance] = two_picks([named_by(mine, first + j) for j in range(blocks)])
        picks, count = arrivals[distance]
        there = first + picks[k]
        live = jnp.where(count > k, tokens_ref[there], 0)
        for i in range(blocks):
            kept[i].append(table_ref[mine + i, there] * live)

    total = bias_ref.shape[1]
    piece_rows = BLK // count_head
    at = lax.broadcasted_iota(jnp.int32, (blocks, total), 1)
    query = lax.broadcasted_iota(jnp.int32, (blocks, total), 0)
    own = at < blocks * BLK
    group, token = split(at, piece_rows)
    own_piece, own_block = split(group, blocks)
    far_row, far_group = split(group, count_head)
    row = jnp.where(own, own_block, far_row)
    piece = jnp.where(own, own_piece, far_group)
    source = jnp.where(piece > place, place - piece + count_head, place - piece)
    position = source * piece_rows + token
    limit = jnp.zeros((blocks, total), jnp.int32)
    for r in range(len(kept[0])):
        value = jnp.zeros((blocks, total), jnp.int32)
        for i in range(blocks):
            value = jnp.where(query == i, kept[i][r], value)
        limit = jnp.where(row == r, value, limit)
    bias_ref[...] = jnp.where(position < limit, 0.0, NEG)


def plan(pair_list, block_tokens, after, blocks, count_head, count_tm):
    total_blocks = pair_list.shape[0]
    lanes = -(-total_blocks // 128) * 128
    total = (blocks + len(remote_rows(count_tm))) * BLK
    return pl.pallas_call(
        functools.partial(plan_kernel, count_head, count_tm, blocks),
        in_specs=[
            pl.BlockSpec(memory_space=pltpu.VMEM),
            pl.BlockSpec(memory_space=pltpu.SMEM),
            pl.BlockSpec(memory_space=pl.ANY),
        ],
        out_specs=[pl.BlockSpec(memory_space=pltpu.SMEM), pl.BlockSpec(memory_space=pltpu.VMEM)],
        out_shape=[
            jax.ShapeDtypeStruct((NEAR_CAP * count_tm,), jnp.int32),
            jax.ShapeDtypeStruct((blocks, total), jnp.float32),
        ],
        scratch_shapes=[
            pltpu.VMEM((total_blocks, lanes), jnp.int32),
            pltpu.SMEM((total_blocks, lanes), jnp.int32),
            pltpu.SemaphoreType.DMA,
        ],
        cost_estimate=NO_COST,
        compiler_params=pltpu.CompilerParams(vmem_limit_bytes=VMEM),
    )(pair_list, block_tokens, after)


def attend_kernel(counts, heads_of, distances, tokens_ref, bias_ref, query_ref, *refs):
    count_head, count_tm = counts
    queries = by_distance([query_ref], count_head, -1)
    per_part = count_head + count_tm - 1
    parts = [refs[p * per_part : (p + 1) * per_part] for p in range(len(heads_of))]
    outs = refs[len(heads_of) * per_part :][-len(distances) :]
    blocks, tokens, _ = outs[0].shape
    rows = len(distances) * tokens
    shard = lax.axis_index("tm")
    me = lax.axis_index("head")
    bias = bias_ref[...][:, None, :]
    place_of = [(p, h) for p, (_, size) in enumerate(heads_of) for h in range(size // HD)]

    def gathered(kind, head):
        p, h = place_of[head]
        first = kind * heads_of[p][1] + h * HD
        lanes = slice(first, first + HD)
        pieces = [rows_of(own[:, :, lanes]) for own in parts[p][:count_head]]
        pieces += [
            rows_of(parts[p][count_head + distance - 1][k, :, :, lanes])
            for distance, k in remote_rows(count_tm)
        ]
        return jnp.concatenate(pieces, axis=0)

    def products(head):
        first = heads_of[0][0] + head * HD
        lanes = slice(first, first + HD)
        query = jnp.concatenate(
            [rows_of(queries[s][i, :, lanes]) for i in range(blocks) for s in distances], axis=0
        )
        return lax.dot_general(
            query, gathered(0, head), (((1,), (1,)), ((), ())), preferred_element_type=jnp.float32
        )

    heads = len(place_of)
    dots, mixed = products(0), []
    for h in range(heads):
        ahead = products(h + 1) if h + 1 < heads else None
        dots = dots.reshape(blocks, rows, -1) + bias
        peak = jnp.max(dots, axis=-1, keepdims=True)
        weights = jnp.exp2((dots - peak) * (SCORE_SCALE * LOG2E))
        inverse = 1.0 / jnp.sum(weights, axis=-1, keepdims=True)
        weights_half = weights.astype(jnp.bfloat16).reshape(blocks * rows, -1)
        part = jnp.dot(weights_half, gathered(1, h), preferred_element_type=jnp.float32)
        mixed.append(part * inverse.reshape(blocks * rows, 1))
        dots = ahead
    mixed = jnp.concatenate(mixed, axis=0)
    sign = sign_matrix()
    high = mixed.astype(jnp.bfloat16)
    low = (mixed - high.astype(jnp.float32)).astype(jnp.bfloat16)
    turned = jnp.dot(high, sign, preferred_element_type=jnp.float32)
    turned = turned + jnp.dot(low, sign, preferred_element_type=jnp.float32)
    turned = (turned * ROTATE_SCALE).reshape(heads, blocks, len(distances), tokens, HD)
    token = lax.broadcasted_iota(jnp.int32, (tokens, HD), 0)
    for at, s in enumerate(distances):
        position = lax.rem(me - s + count_head, count_head) * tokens + token
        for i in range(blocks):
            live = position < tokens_ref[shard * blocks + i]
            for h in range(heads):
                outs[at][i, :, h * HD : (h + 1) * HD] = jnp.where(
                    live, turned[h, i, at], 0.0
                ).astype(jnp.bfloat16)


def attend(block_tokens, bias, query, parts, heads_of, distances, after=(), cost=NO_COST):
    count_head, count_tm = query.shape[0], len(parts[0][1]) + 1
    operands = [ref for owns, slots in parts for ref in owns + slots]
    shape = query.shape[1:3] + (sum(size for _, size in heads_of),)
    vmem = pl.BlockSpec(memory_space=pltpu.VMEM)
    return pl.pallas_call(
        functools.partial(attend_kernel, (count_head, count_tm), heads_of, distances),
        in_specs=[pl.BlockSpec(memory_space=pltpu.SMEM)]
        + [vmem] * (2 + len(operands))
        + [pl.BlockSpec(memory_space=pl.ANY)] * len(after),
        out_specs=[vmem] * len(distances),
        out_shape=[jax.ShapeDtypeStruct(shape, jnp.bfloat16)] * len(distances),
        cost_estimate=cost,
        compiler_params=pltpu.CompilerParams(vmem_limit_bytes=VMEM),
    )(block_tokens, bias, query, *operands, *after)


def place_kernel(places, width_here, *refs):
    pieces, out_ref, sems = refs[:-2], refs[-2], refs[-1]
    me, count = lax.axis_index("head"), lax.axis_size("head")
    copies = []
    for at, (piece, (s, start)) in enumerate(zip(pieces, places)):
        column = pl.multiple_of(lax.rem(me + s, count) * width_here + start, HD)
        copies.append(
            pltpu.make_async_copy(
                piece, out_ref.at[:, :, pl.ds(column, piece.shape[-1])], sems.at[at]
            )
        )
        copies[-1].start()
    for copy in copies:
        copy.wait()


def place_pieces(pieces, places, width_here):
    blocks, tokens, _ = pieces[0].shape
    width = width_here * lax.axis_size("head")
    return pl.pallas_call(
        functools.partial(place_kernel, places, width_here),
        in_specs=[pl.BlockSpec(memory_space=pl.ANY)] * len(pieces),
        out_specs=pl.BlockSpec(memory_space=pltpu.HBM),
        out_shape=jax.ShapeDtypeStruct((blocks, tokens, width), jnp.bfloat16),
        scratch_shapes=[pltpu.SemaphoreType.DMA((len(pieces),))],
        compiler_params=pltpu.CompilerParams(vmem_limit_bytes=VMEM),
    )(*pieces)


def shifted(array, axis, distance):
    count = lax.axis_size(axis)
    return lax.ppermute(array, axis, [(i, (i + distance) % count) for i in range(count)])


def exchange(pieces, direction):
    return [shifted(piece, "head", direction * s) for s, piece in enumerate(pieces, 1)]


def forward(sent):
    return [shifted(block, "tm", distance) for distance, block in enumerate(sent, 1)]


def shards(query_rows, key_rows, value_rows, pair_list, block_tokens):
    count_head = lax.axis_size("head")
    count_tm = lax.axis_size("tm")
    blocks, tokens, width = query_rows.shape
    width_here = width // count_head
    heads = width_here // HD
    cut = (heads + 1) // 2 * HD
    parts = [(0, cut), (cut, width_here - cut)] if heads > 1 else [(0, width_here)]
    arrays = [query_rows, key_rows, value_rows]
    messages = [[(1,) + part, (2,) + part] for part in parts]
    half = count_head // 2
    others = [s for s in range(1, count_head) if s != half]
    (farthest,), token = rotate_pieces(
        arrays, messages[0], count_head, [half], limit=WIDE_VMEM
    )
    (*near, own), token = rotate_pieces(
        arrays, messages[0], count_head, others + [0], (token,), WIDE_VMEM
    )
    farthest = shifted(farthest, "head", half)
    near = [shifted(piece, "head", s) for s, piece in zip(others, near)]
    received = [[own] + near[: half - 1] + [farthest] + near[half - 1 :]]
    picks, bias = plan(pair_list, block_tokens, token, blocks, count_head, count_tm)
    after = (bias, farthest)
    distances = list(range(1, count_head))
    for message in messages[1:]:
        (*pieces, own), token = rotate_pieces(
            arrays, message, count_head, distances + [0], after
        )
        received.append([own] + exchange(pieces, 1))
        after = (token,)
    sent, after = [], ()
    for owns, (_, size) in zip(received, parts):
        sent.append(pick_blocks(picks, owns, (0, 2 * size), count_tm, after))
        after = (sent[-1][0],)
    message = [(0, 0, width_here)]
    (query,), _ = rotate_pieces(
        arrays, message, count_head, list(range(count_head)), (sent[0][0],), stacked=True
    )
    query = lax.all_to_all(query, "head", split_axis=0, concat_axis=0, tiled=True)
    inputs = [(owns, forward(picked)) for owns, picked in zip(received, sent)]
    after, pieces, places = (), [], []
    for at, part in enumerate(parts):
        cost = NO_COST if at == len(parts) - 1 else HIGH_COST
        leaving = attend(
            block_tokens, bias, query, [inputs[at]], [part], distances, after, cost
        )
        after = (leaving[0],)
        pieces += exchange(leaving, -1)
        places += [(s, part[0]) for s in distances]
    pieces += attend(block_tokens, bias, query, inputs, parts, [0], after)
    return place_pieces(pieces, places + [(0, 0)], width_here)


def solution(mesh):
    placed = (
        P(("grp", "tm"), "head", None),
        P(("grp", "tm"), "head", None),
        P(("grp", "tm"), "head", None),
        P("grp", None),
        P("grp"),
    )
    return jax.shard_map(
        shards,
        mesh=mesh,
        in_specs=placed,
        out_specs=P(("grp", "tm"), "head", None),
        check_vma=False,
    )
```

```python
import functools
import math

import jax
import jax.numpy as jnp
from jax import lax
from jax.experimental import pallas as pl
from jax.experimental.pallas import tpu as pltpu
from jax.sharding import PartitionSpec as P

HD = 128
BLK = 64
NEAR_CAP = 2
FAR_CAP = 1
NEG = -1e30
ROTATE_SCALE = 1.0 / math.sqrt(HD)
SCORE_SCALE = 1.0 / math.sqrt(HD)
VMEM = 24 * 1024 * 1024
WIDE_VMEM = 60 * 1024 * 1024
TOKEN = jax.ShapeDtypeStruct((8, 128), jnp.float32)
NO_COST = pl.CostEstimate(flops=0, bytes_accessed=0, transcendentals=0)
HIGH_COST = pl.CostEstimate(flops=10**11, bytes_accessed=0, transcendentals=0)
LOG2E = math.log2(math.e)


def sign_matrix():
    common = lax.broadcasted_iota(jnp.int32, (HD, HD), 0) & lax.broadcasted_iota(
        jnp.int32, (HD, HD), 1
    )
    bits = HD.bit_length() - 1
    parity = common
    for bit in range(1, bits):
        parity = parity ^ (common >> bit)
    return jnp.where((parity & 1) == 0, 1.0, -1.0).astype(jnp.bfloat16)


def rows_of(block):
    rows, width = math.prod(block.shape[:-1]), block.shape[-1]
    if block.shape[-2] % 16 == 0:
        return block.reshape(rows, width)
    return block.astype(jnp.float32).reshape(rows, width).astype(block.dtype)


def fields_of(message):
    at, fields = 0, []
    for source, start, size in message:
        fields.append((source, start, size, at))
        at += size
    return fields, at


def by_distance(refs, count, direction):
    if len(refs[0].shape) == 3:
        return list(refs)
    me = lax.axis_index("head")
    return [refs[0].at[lax.rem(me + direction * s + count, count)] for s in range(count)]


def rotate_kernel(message, sources, count_head, skipped, *refs):
    fields, total = fields_of(message)
    ins = dict(zip(sources, refs))
    outs = by_distance(refs[len(sources) + skipped : -3], count_head, 1)
    token, buffer, sems = refs[-3:]
    token[...] = jnp.zeros_like(token)
    blocks, tokens, width = refs[0].shape
    width_here = width // count_head
    me = lax.axis_index("head")
    order = list(range(1, count_head)) + [0]
    copies = {}
    for s in order:
        goal = lax.rem(me + s, count_head)
        for f, (source, start, size, at) in enumerate(fields):
            column = pl.multiple_of(goal * width_here + start, HD)
            copies[s, f] = pltpu.make_async_copy(
                ins[source].at[:, :, pl.ds(column, size)],
                buffer.at[s, :, :, pl.ds(at, size)],
                sems.at[s, f],
            )
            copies[s, f].start()
    sign = sign_matrix()
    for s in order:
        for f, (_, _, size, start) in enumerate(fields):
            copies[s, f].wait()
            flat = rows_of(buffer[s, :, :, start : start + size])
            heads = [flat[:, at : at + HD] for at in range(0, size, HD)]
            turned = jnp.dot(
                jnp.concatenate(heads, axis=0), sign, preferred_element_type=jnp.float32
            )
            turned = (turned * ROTATE_SCALE).reshape(size // HD, blocks, tokens, HD)
            for h in range(size // HD):
                at = start + h * HD
                outs[s][:, :, at : at + HD] = turned[h].astype(jnp.bfloat16)


def rotate_pieces(arrays, message, count_head, after=(), limit=VMEM, stacked=False):
    blocks, tokens, _ = arrays[0].shape
    fields, total = fields_of(message)
    sources = sorted({source for source, _, _ in message})
    one = (blocks, tokens, total)
    shapes = [(count_head,) + one] if stacked else [one] * count_head
    *pieces, token = pl.pallas_call(
        functools.partial(rotate_kernel, message, sources, count_head, len(after)),
        in_specs=[pl.BlockSpec(memory_space=pltpu.HBM)] * len(sources)
        + [pl.BlockSpec(memory_space=pl.ANY)] * len(after),
        out_specs=[pl.BlockSpec(memory_space=pltpu.VMEM)] * (len(shapes) + 1),
        out_shape=[jax.ShapeDtypeStruct(shape, jnp.bfloat16) for shape in shapes] + [TOKEN],
        scratch_shapes=[
            pltpu.VMEM((count_head,) + one, jnp.bfloat16),
            pltpu.SemaphoreType.DMA((count_head, len(fields))),
        ],
        cost_estimate=NO_COST,
        compiler_params=pltpu.CompilerParams(vmem_limit_bytes=limit),
    )(*[arrays[source] for source in sources], *after)
    return pieces, token


def slots_at(distance, count_tm):
    return NEAR_CAP if distance in (1, count_tm - 1) else FAR_CAP


def pick_kernel(counts, lanes, picks_ref, *refs):
    count_head, count_tm, own_count, skipped = counts
    pieces = by_distance(refs[:own_count], count_head, -1)
    outs = refs[own_count + skipped :]
    shard = lax.axis_index("tm")
    for distance, out in enumerate(outs, 1):
        goal = lax.rem(shard + distance, count_tm)
        for k in range(slots_at(distance, count_tm)):
            pick = picks_ref[NEAR_CAP * goal + k]
            for s in range(count_head):
                out[k, s] = pieces[s][pick, :, lanes[0] : lanes[1]]


def pick_blocks(picks, pieces, lanes, count_head, count_tm, after):
    one = (count_head, pieces[0].shape[-2], lanes[1] - lanes[0])
    vmem = pl.BlockSpec(memory_space=pltpu.VMEM)
    return pl.pallas_call(
        functools.partial(
            pick_kernel, (count_head, count_tm, len(pieces), len(after)), lanes
        ),
        in_specs=[pl.BlockSpec(memory_space=pltpu.SMEM)]
        + [vmem] * len(pieces)
        + [pl.BlockSpec(memory_space=pl.ANY)] * len(after),
        out_specs=[vmem] * (count_tm - 1),
        out_shape=[
            jax.ShapeDtypeStruct((slots_at(distance, count_tm),) + one, jnp.bfloat16)
            for distance in range(1, count_tm)
        ],
        cost_estimate=HIGH_COST,
        compiler_params=pltpu.CompilerParams(vmem_limit_bytes=VMEM),
    )(picks, *pieces, *after)


def remote_rows(count_tm):
    return [
        (distance, k)
        for distance in range(1, count_tm)
        for k in range(slots_at(distance, count_tm))
    ]


def split(value, by):
    if by & (by - 1) == 0:
        return value >> (by.bit_length() - 1), value & (by - 1)
    return lax.div(value, by), lax.rem(value, by)


def plan_kernel(count_head, count_tm, blocks, pair_ref, tokens_ref, _, picks_ref, bias_ref, named_ref, table_ref, sem):
    total_blocks, columns = pair_ref.shape
    pairs = pair_ref[...]
    lane = lax.broadcasted_iota(jnp.int32, named_ref.shape, 1)
    named = jnp.zeros(named_ref.shape, jnp.int32)
    for c in range(columns):
        named = jnp.where(pairs[:, c : c + 1] == lane, 1, named)
    named_ref[...] = named
    copy = pltpu.make_async_copy(named_ref, table_ref, sem)
    copy.start()
    copy.wait()
    shard = lax.axis_index("tm")
    place = lax.axis_index("head")
    mine = shard * blocks

    def two_picks(wanted):
        picks = [jnp.int32(0)] * NEAR_CAP
        count = jnp.int32(0)
        for j in range(blocks):
            for k in range(NEAR_CAP):
                picks[k] = jnp.where((wanted[j] > 0) & (count == k), j, picks[k])
            count = count + wanted[j]
        return picks, count

    def named_by(rows, column):
        found = table_ref[rows, column]
        for i in range(1, blocks):
            found = found | table_ref[rows + i, column]
        return found

    for d in range(count_tm):
        picks, _ = two_picks([named_by(d * blocks, mine + j) for j in range(blocks)])
        for k in range(NEAR_CAP):
            picks_ref[NEAR_CAP * d + k] = picks[k]

    kept = [[table_ref[mine + i, mine + j] * tokens_ref[mine + j] for j in range(blocks)] for i in range(blocks)]
    arrivals = {}
    for distance, k in remote_rows(count_tm):
        first = lax.rem(shard - distance + count_tm, count_tm) * blocks
        if k == 0:
            arrivals[distance] = two_picks([named_by(mine, first + j) for j in range(blocks)])
        picks, count = arrivals[distance]
        there = first + picks[k]
        live = jnp.where(count > k, tokens_ref[there], 0)
        for i in range(blocks):
            kept[i].append(table_ref[mine + i, there] * live)

    total = bias_ref.shape[1]
    piece_rows = BLK // count_head
    at = lax.broadcasted_iota(jnp.int32, (blocks, total), 1)
    query = lax.broadcasted_iota(jnp.int32, (blocks, total), 0)
    own = at < blocks * BLK
    group, token = split(at, piece_rows)
    own_piece, own_block = split(group, blocks)
    far_row, far_group = split(group, count_head)
    row = jnp.where(own, own_block, far_row)
    piece = jnp.where(own, own_piece, far_group)
    source = jnp.where(piece > place, place - piece + count_head, place - piece)
    position = source * piece_rows + token
    limit = jnp.zeros((blocks, total), jnp.int32)
    for r in range(len(kept[0])):
        value = jnp.zeros((blocks, total), jnp.int32)
        for i in range(blocks):
            value = jnp.where(query == i, kept[i][r], value)
        limit = jnp.where(row == r, value, limit)
    bias_ref[...] = jnp.where(position < limit, 0.0, NEG)


def plan(pair_list, block_tokens, after, blocks, count_head, count_tm):
    total_blocks = pair_list.shape[0]
    lanes = -(-total_blocks // 128) * 128
    total = (blocks + len(remote_rows(count_tm))) * BLK
    return pl.pallas_call(
        functools.partial(plan_kernel, count_head, count_tm, blocks),
        in_specs=[
            pl.BlockSpec(memory_space=pltpu.VMEM),
            pl.BlockSpec(memory_space=pltpu.SMEM),
            pl.BlockSpec(memory_space=pl.ANY),
        ],
        out_specs=[pl.BlockSpec(memory_space=pltpu.SMEM), pl.BlockSpec(memory_space=pltpu.VMEM)],
        out_shape=[
            jax.ShapeDtypeStruct((NEAR_CAP * count_tm,), jnp.int32),
            jax.ShapeDtypeStruct((blocks, total), jnp.float32),
        ],
        scratch_shapes=[
            pltpu.VMEM((total_blocks, lanes), jnp.int32),
            pltpu.SMEM((total_blocks, lanes), jnp.int32),
            pltpu.SemaphoreType.DMA,
        ],
        cost_estimate=NO_COST,
        compiler_params=pltpu.CompilerParams(vmem_limit_bytes=VMEM),
    )(pair_list, block_tokens, after)


def attend_kernel(counts, heads_of, distances, tokens_ref, bias_ref, query_ref, *refs):
    count_head, count_tm, own_counts = counts
    queries = by_distance([query_ref], count_head, -1)
    parts, at = [], 0
    for count in own_counts:
        owns = by_distance(refs[at : at + count], count_head, -1)
        parts.append((owns, refs[at + count : at + count + count_tm - 1]))
        at += count + count_tm - 1
    outs = refs[-len(distances) :]
    blocks, tokens, _ = outs[0].shape
    rows = len(distances) * tokens
    shard = lax.axis_index("tm")
    me = lax.axis_index("head")
    bias = bias_ref[...][:, None, :]
    place_of = [(p, h) for p, (_, size) in enumerate(heads_of) for h in range(size // HD)]

    def gathered(kind, head):
        p, h = place_of[head]
        first = kind * heads_of[p][1] + h * HD
        lanes = slice(first, first + HD)
        owns, slots = parts[p]
        pieces = [rows_of(own[:, :, lanes]) for own in owns]
        pieces += [
            rows_of(slots[distance - 1][k, :, :, lanes])
            for distance, k in remote_rows(count_tm)
        ]
        return jnp.concatenate(pieces, axis=0)

    def products(head):
        first = heads_of[0][0] + head * HD
        lanes = slice(first, first + HD)
        query = jnp.concatenate(
            [rows_of(queries[s][i, :, lanes]) for i in range(blocks) for s in distances], axis=0
        )
        return lax.dot_general(
            query, gathered(0, head), (((1,), (1,)), ((), ())), preferred_element_type=jnp.float32
        )

    heads = len(place_of)
    dots, mixed = products(0), []
    for h in range(heads):
        ahead = products(h + 1) if h + 1 < heads else None
        dots = dots.reshape(blocks, rows, -1) + bias
        peak = jnp.max(dots, axis=-1, keepdims=True)
        weights = jnp.exp2((dots - peak) * (SCORE_SCALE * LOG2E))
        inverse = 1.0 / jnp.sum(weights, axis=-1, keepdims=True)
        weights_half = weights.astype(jnp.bfloat16).reshape(blocks * rows, -1)
        part = jnp.dot(weights_half, gathered(1, h), preferred_element_type=jnp.float32)
        mixed.append(part * inverse.reshape(blocks * rows, 1))
        dots = ahead
    mixed = jnp.concatenate(mixed, axis=0)
    sign = sign_matrix()
    high = mixed.astype(jnp.bfloat16)
    low = (mixed - high.astype(jnp.float32)).astype(jnp.bfloat16)
    turned = jnp.dot(high, sign, preferred_element_type=jnp.float32)
    turned = turned + jnp.dot(low, sign, preferred_element_type=jnp.float32)
    turned = (turned * ROTATE_SCALE).reshape(heads, blocks, len(distances), tokens, HD)
    token = lax.broadcasted_iota(jnp.int32, (tokens, HD), 0)
    for at, s in enumerate(distances):
        position = lax.rem(me - s + count_head, count_head) * tokens + token
        for i in range(blocks):
            live = position < tokens_ref[shard * blocks + i]
            for h in range(heads):
                outs[at][i, :, h * HD : (h + 1) * HD] = jnp.where(
                    live, turned[h, i, at], 0.0
                ).astype(jnp.bfloat16)


def attend(block_tokens, bias, query, parts, heads_of, distances, after=(), cost=NO_COST):
    count_head, count_tm = query.shape[0], len(parts[0][1]) + 1
    operands = [ref for owns, slots in parts for ref in owns + slots]
    counts = (count_head, count_tm, [len(owns) for owns, _ in parts])
    shape = query.shape[1:3] + (sum(size for _, size in heads_of),)
    vmem = pl.BlockSpec(memory_space=pltpu.VMEM)
    return pl.pallas_call(
        functools.partial(attend_kernel, counts, heads_of, distances),
        in_specs=[pl.BlockSpec(memory_space=pltpu.SMEM)]
        + [vmem] * (2 + len(operands))
        + [pl.BlockSpec(memory_space=pl.ANY)] * len(after),
        out_specs=[vmem] * len(distances),
        out_shape=[jax.ShapeDtypeStruct(shape, jnp.bfloat16)] * len(distances),
        cost_estimate=cost,
        compiler_params=pltpu.CompilerParams(vmem_limit_bytes=VMEM),
    )(block_tokens, bias, query, *operands, *after)


def place_kernel(places, width_here, *refs):
    pieces, out_ref, sems = refs[:-2], refs[-2], refs[-1]
    me, count = lax.axis_index("head"), lax.axis_size("head")
    copies = []
    for at, (piece, (s, start)) in enumerate(zip(pieces, places)):
        column = pl.multiple_of(lax.rem(me + s, count) * width_here + start, HD)
        copies.append(
            pltpu.make_async_copy(
                piece, out_ref.at[:, :, pl.ds(column, piece.shape[-1])], sems.at[at]
            )
        )
        copies[-1].start()
    for copy in copies:
        copy.wait()


def place_pieces(pieces, places, width_here):
    blocks, tokens, _ = pieces[0].shape
    width = width_here * lax.axis_size("head")
    return pl.pallas_call(
        functools.partial(place_kernel, places, width_here),
        in_specs=[pl.BlockSpec(memory_space=pl.ANY)] * len(pieces),
        out_specs=pl.BlockSpec(memory_space=pltpu.HBM),
        out_shape=jax.ShapeDtypeStruct((blocks, tokens, width), jnp.bfloat16),
        scratch_shapes=[pltpu.SemaphoreType.DMA((len(pieces),))],
        compiler_params=pltpu.CompilerParams(vmem_limit_bytes=VMEM),
    )(*pieces)


def shifted(array, axis, distance):
    count = lax.axis_size(axis)
    return lax.ppermute(array, axis, [(i, (i + distance) % count) for i in range(count)])


def exchange(pieces, direction):
    return [shifted(piece, "head", direction * s) for s, piece in enumerate(pieces, 1)]


def forward(sent):
    return [shifted(block, "tm", distance) for distance, block in enumerate(sent, 1)]


def shards(query_rows, key_rows, value_rows, pair_list, block_tokens):
    count_head = lax.axis_size("head")
    count_tm = lax.axis_size("tm")
    blocks, tokens, width = query_rows.shape
    width_here = width // count_head
    heads = width_here // HD
    cut = (heads + 1) // 2 * HD
    parts = [(0, cut), (cut, width_here - cut)] if heads > 1 else [(0, width_here)]
    arrays = [query_rows, key_rows, value_rows]
    messages = [[(1,) + part, (2,) + part] for part in parts]
    stacked, token = rotate_pieces(
        arrays, messages[0], count_head, limit=WIDE_VMEM, stacked=True
    )
    received = [[lax.all_to_all(stacked[0], "head", split_axis=0, concat_axis=0, tiled=True)]]
    picks, bias = plan(pair_list, block_tokens, token, blocks, count_head, count_tm)
    after = (bias,)
    for message in messages[1:]:
        pieces, token = rotate_pieces(arrays, message, count_head, after)
        received.append(pieces[:1] + exchange(pieces[1:], 1))
        after = (token,)
    sent, after = [], ()
    for owns, (_, size) in zip(received, parts):
        sent.append(pick_blocks(picks, owns, (0, 2 * size), count_head, count_tm, after))
        after = (sent[-1][0],)
    message = [(0, 0, width_here)]
    (query,), _ = rotate_pieces(arrays, message, count_head, (sent[0][0],), stacked=True)
    query = lax.all_to_all(query, "head", split_axis=0, concat_axis=0, tiled=True)
    inputs = [(owns, forward(picked)) for owns, picked in zip(received, sent)]
    distances, after = list(range(1, count_head)), ()
    pieces, places = [], []
    for at, part in enumerate(parts):
        cost = NO_COST if at == len(parts) - 1 else HIGH_COST
        leaving = attend(
            block_tokens, bias, query, [inputs[at]], [part], distances, after, cost
        )
        after = (leaving[0],)
        pieces += exchange(leaving, -1)
        places += [(s, part[0]) for s in distances]
    pieces += attend(block_tokens, bias, query, inputs, parts, [0], after)
    return place_pieces(pieces, places + [(0, 0)], width_here)


def solution(mesh):
    placed = (
        P(("grp", "tm"), "head", None),
        P(("grp", "tm"), "head", None),
        P(("grp", "tm"), "head", None),
        P("grp", None),
        P("grp"),
    )
    return jax.shard_map(
        shards,
        mesh=mesh,
        in_specs=placed,
        out_specs=P(("grp", "tm"), "head", None),
        check_vma=False,
    )
```

```python
import functools
import math

import jax
import jax.numpy as jnp
from jax import lax
from jax.experimental import pallas as pl
from jax.experimental.pallas import tpu as pltpu
from jax.sharding import PartitionSpec as P

HD = 128
BLK = 64
NEAR_CAP = 2
FAR_CAP = 1
NEG = -1e30
ROTATE_SCALE = 1.0 / math.sqrt(HD)
SCORE_SCALE = 1.0 / math.sqrt(HD)
VMEM = 24 * 1024 * 1024
WIDE_VMEM = 60 * 1024 * 1024
TOKEN = jax.ShapeDtypeStruct((8, 128), jnp.float32)
NO_COST = pl.CostEstimate(flops=0, bytes_accessed=0, transcendentals=0)
HIGH_COST = pl.CostEstimate(flops=10**11, bytes_accessed=0, transcendentals=0)
LOG2E = math.log2(math.e)


def sign_matrix():
    common = lax.broadcasted_iota(jnp.int32, (HD, HD), 0) & lax.broadcasted_iota(
        jnp.int32, (HD, HD), 1
    )
    bits = HD.bit_length() - 1
    parity = common
    for bit in range(1, bits):
        parity = parity ^ (common >> bit)
    return jnp.where((parity & 1) == 0, 1.0, -1.0).astype(jnp.bfloat16)


def rows_of(block):
    rows, width = math.prod(block.shape[:-1]), block.shape[-1]
    if block.shape[-2] % 16 == 0:
        return block.reshape(rows, width)
    return block.astype(jnp.float32).reshape(rows, width).astype(block.dtype)


def fields_of(message):
    at, fields = 0, []
    for source, start, size in message:
        fields.append((source, start, size, at))
        at += size
    return fields, at


def by_distance(refs, count, direction):
    if len(refs[0].shape) == 3:
        return list(refs)
    me = lax.axis_index("head")
    return [refs[0].at[lax.rem(me + direction * s + count, count)] for s in range(count)]


def rotated(block, sign):
    blocks, tokens, size = block.shape
    flat = rows_of(block)
    heads = [flat[:, at : at + HD] for at in range(0, size, HD)]
    turned = jnp.dot(jnp.concatenate(heads, axis=0), sign, preferred_element_type=jnp.float32)
    return (turned * ROTATE_SCALE).reshape(size // HD, blocks, tokens, HD).astype(jnp.bfloat16)


def store_heads(out, start, turned):
    for h in range(turned.shape[0]):
        at = start + h * HD
        out[:, :, at : at + HD] = turned[h]


def rotate_kernel(message, sources, count_head, *refs):
    fields, total = fields_of(message)
    ins = dict(zip(sources, refs))
    outs, (token, buffer, sems) = refs[len(sources) : -3], refs[-3:]
    token[...] = jnp.zeros_like(token)
    width_here = refs[0].shape[2] // count_head
    me = lax.axis_index("head")
    order = list(range(1, count_head)) + [0]
    copies = {}
    for s in order:
        goal = lax.rem(me + s, count_head)
        for f, (source, start, size, at) in enumerate(fields):
            column = pl.multiple_of(goal * width_here + start, HD)
            copies[s, f] = pltpu.make_async_copy(
                ins[source].at[:, :, pl.ds(column, size)],
                buffer.at[s, :, :, pl.ds(at, size)],
                sems.at[s, f],
            )
            copies[s, f].start()
    sign = sign_matrix()
    for s in order:
        for f, (_, _, size, start) in enumerate(fields):
            copies[s, f].wait()
            store_heads(outs[s], start, rotated(buffer[s, :, :, start : start + size], sign))


def rotate_here(fields, ins, outs, distances, count_head, sign):
    width_here = next(iter(ins.values())).shape[2] // count_head
    me = lax.axis_index("head")
    for s in distances:
        goal = lax.rem(me + s, count_head)
        for source, start, size, at in fields:
            column = pl.multiple_of(goal * width_here + start, HD)
            store_heads(outs[s], at, rotated(ins[source][:, :, pl.ds(column, size)], sign))


def stack_kernel(message, source, count_head, source_ref, _, out_ref):
    outs = by_distance([out_ref], count_head, 1)
    fields, _ = fields_of(message)
    places = range(count_head)
    rotate_here(fields, {source: source_ref}, outs, places, count_head, sign_matrix())


def rotate_stacked(arrays, message, count_head, after):
    blocks, tokens, _ = arrays[0].shape
    source, total = message[0][0], fields_of(message)[1]
    vmem = pl.BlockSpec(memory_space=pltpu.VMEM)
    return pl.pallas_call(
        functools.partial(stack_kernel, message, source, count_head),
        in_specs=[vmem, pl.BlockSpec(memory_space=pl.ANY)],
        out_specs=vmem,
        out_shape=jax.ShapeDtypeStruct((count_head, blocks, tokens, total), jnp.bfloat16),
        cost_estimate=NO_COST,
        compiler_params=pltpu.CompilerParams(vmem_limit_bytes=VMEM),
    )(arrays[source], after)


def rotate_pieces(arrays, message, count_head):
    blocks, tokens, _ = arrays[0].shape
    fields, total = fields_of(message)
    sources = sorted({source for source, _, _ in message})
    one = (blocks, tokens, total)
    *pieces, token = pl.pallas_call(
        functools.partial(rotate_kernel, message, sources, count_head),
        in_specs=[pl.BlockSpec(memory_space=pltpu.HBM)] * len(sources),
        out_specs=[pl.BlockSpec(memory_space=pltpu.VMEM)] * (count_head + 1),
        out_shape=[jax.ShapeDtypeStruct(one, jnp.bfloat16)] * count_head + [TOKEN],
        scratch_shapes=[
            pltpu.VMEM((count_head,) + one, jnp.bfloat16),
            pltpu.SemaphoreType.DMA((count_head, len(fields))),
        ],
        cost_estimate=NO_COST,
        compiler_params=pltpu.CompilerParams(vmem_limit_bytes=WIDE_VMEM),
    )(*[arrays[source] for source in sources])
    return pieces, token


def slots_at(distance, count_tm):
    return NEAR_CAP if distance in (1, count_tm - 1) else FAR_CAP


def pick_kernel(count_head, count_tm, lanes, skipped, picks_ref, *refs):
    pieces, outs = refs[:count_head], refs[count_head + skipped :]
    shard = lax.axis_index("tm")
    for distance, out in enumerate(outs, 1):
        goal = lax.rem(shard + distance, count_tm)
        for k in range(slots_at(distance, count_tm)):
            pick = picks_ref[NEAR_CAP * goal + k]
            for s in range(count_head):
                out[k, s] = pieces[s][pick, :, lanes[0] : lanes[1]]


def pick_blocks(picks, pieces, lanes, count_tm, after):
    count_head = len(pieces)
    one = (count_head, pieces[0].shape[1], lanes[1] - lanes[0])
    vmem = pl.BlockSpec(memory_space=pltpu.VMEM)
    return pl.pallas_call(
        functools.partial(pick_kernel, count_head, count_tm, lanes, len(after)),
        in_specs=[pl.BlockSpec(memory_space=pltpu.SMEM)]
        + [vmem] * count_head
        + [pl.BlockSpec(memory_space=pl.ANY)] * len(after),
        out_specs=[vmem] * (count_tm - 1),
        out_shape=[
            jax.ShapeDtypeStruct((slots_at(distance, count_tm),) + one, jnp.bfloat16)
            for distance in range(1, count_tm)
        ],
        cost_estimate=HIGH_COST,
        compiler_params=pltpu.CompilerParams(vmem_limit_bytes=VMEM),
    )(picks, *pieces, *after)


def remote_rows(count_tm):
    return [
        (distance, k)
        for distance in range(1, count_tm)
        for k in range(slots_at(distance, count_tm))
    ]


def split(value, by):
    if by & (by - 1) == 0:
        return value >> (by.bit_length() - 1), value & (by - 1)
    return lax.div(value, by), lax.rem(value, by)


def plan_kernel(messages, count_head, count_tm, blocks, *refs):
    key_ref, value_ref, pair_hbm, tokens_ref, _ = refs[:5]
    picks_ref, bias_ref = refs[5:7]
    pair_ref, named_ref, table_ref, pair_sem, table_sem = refs[-5:]
    outs = refs[7:-5]
    ins = {1: key_ref, 2: value_ref}
    pair_copy = pltpu.make_async_copy(pair_hbm, pair_ref, pair_sem)
    pair_copy.start()
    sign = sign_matrix()
    places = list(range(1, count_head)) + [0]
    jobs = [
        (fields_of(message)[0], outs[m * count_head : (m + 1) * count_head], s)
        for m, message in enumerate(messages)
        for s in places
    ]
    half = len(jobs) // 2
    for fields, pieces, s in jobs[:half]:
        rotate_here(fields, ins, pieces, [s], count_head, sign)
    pair_copy.wait()
    total_blocks, columns = pair_ref.shape
    pairs = pair_ref[...]
    lane = lax.broadcasted_iota(jnp.int32, named_ref.shape, 1)
    named = jnp.zeros(named_ref.shape, jnp.int32)
    for c in range(columns):
        named = jnp.where(pairs[:, c : c + 1] == lane, 1, named)
    named_ref[...] = named
    copy = pltpu.make_async_copy(named_ref, table_ref, table_sem)
    copy.start()
    for fields, pieces, s in jobs[half:]:
        rotate_here(fields, ins, pieces, [s], count_head, sign)
    copy.wait()
    shard = lax.axis_index("tm")
    place = lax.axis_index("head")
    mine = shard * blocks

    def two_picks(wanted):
        picks = [jnp.int32(0)] * NEAR_CAP
        count = jnp.int32(0)
        for j in range(blocks):
            for k in range(NEAR_CAP):
                picks[k] = jnp.where((wanted[j] > 0) & (count == k), j, picks[k])
            count = count + wanted[j]
        return picks, count

    def named_by(rows, column):
        found = table_ref[rows, column]
        for i in range(1, blocks):
            found = found | table_ref[rows + i, column]
        return found

    for d in range(count_tm):
        picks, _ = two_picks([named_by(d * blocks, mine + j) for j in range(blocks)])
        for k in range(NEAR_CAP):
            picks_ref[NEAR_CAP * d + k] = picks[k]

    kept = [[table_ref[mine + i, mine + j] * tokens_ref[mine + j] for j in range(blocks)] for i in range(blocks)]
    arrivals = {}
    for distance, k in remote_rows(count_tm):
        first = lax.rem(shard - distance + count_tm, count_tm) * blocks
        if k == 0:
            arrivals[distance] = two_picks([named_by(mine, first + j) for j in range(blocks)])
        picks, count = arrivals[distance]
        there = first + picks[k]
        live = jnp.where(count > k, tokens_ref[there], 0)
        for i in range(blocks):
            kept[i].append(table_ref[mine + i, there] * live)

    total = bias_ref.shape[1]
    piece_rows = BLK // count_head
    at = lax.broadcasted_iota(jnp.int32, (blocks, total), 1)
    query = lax.broadcasted_iota(jnp.int32, (blocks, total), 0)
    own = at < blocks * BLK
    group, token = split(at, piece_rows)
    own_piece, own_block = split(group, blocks)
    far_row, far_group = split(group, count_head)
    row = jnp.where(own, own_block, far_row)
    piece = jnp.where(own, own_piece, far_group)
    source = jnp.where(piece > place, place - piece + count_head, place - piece)
    position = source * piece_rows + token
    limit = jnp.zeros((blocks, total), jnp.int32)
    for r in range(len(kept[0])):
        value = jnp.zeros((blocks, total), jnp.int32)
        for i in range(blocks):
            value = jnp.where(query == i, kept[i][r], value)
        limit = jnp.where(row == r, value, limit)
    bias_ref[...] = jnp.where(position < limit, 0.0, NEG)


def plan(arrays, messages, pair_list, block_tokens, after, count_head, count_tm):
    blocks, tokens, _ = arrays[0].shape
    total_blocks, columns = pair_list.shape
    lanes = -(-total_blocks // 128) * 128
    total = (blocks + len(remote_rows(count_tm))) * BLK
    vmem = pl.BlockSpec(memory_space=pltpu.VMEM)
    smem = pl.BlockSpec(memory_space=pltpu.SMEM)
    shapes = [
        jax.ShapeDtypeStruct((blocks, tokens, fields_of(message)[1]), jnp.bfloat16)
        for message in messages
        for _ in range(count_head)
    ]
    picks, bias, *pieces = pl.pallas_call(
        functools.partial(plan_kernel, messages, count_head, count_tm, blocks),
        in_specs=[vmem, vmem, pl.BlockSpec(memory_space=pl.ANY), smem]
        + [pl.BlockSpec(memory_space=pl.ANY)],
        out_specs=[smem, vmem] + [vmem] * len(shapes),
        out_shape=[
            jax.ShapeDtypeStruct((NEAR_CAP * count_tm,), jnp.int32),
            jax.ShapeDtypeStruct((blocks, total), jnp.float32),
        ]
        + shapes,
        scratch_shapes=[
            pltpu.VMEM((total_blocks, columns), jnp.int32),
            pltpu.VMEM((total_blocks, lanes), jnp.int32),
            pltpu.SMEM((total_blocks, lanes), jnp.int32),
            pltpu.SemaphoreType.DMA,
            pltpu.SemaphoreType.DMA,
        ],
        cost_estimate=NO_COST,
        compiler_params=pltpu.CompilerParams(vmem_limit_bytes=VMEM),
    )(arrays[1], arrays[2], pair_list, block_tokens, after)
    return picks, bias, [pieces[at : at + count_head] for at in range(0, len(pieces), count_head)]


def attend_kernel(counts, heads_of, distances, tokens_ref, bias_ref, query_ref, *refs):
    count_head, count_tm = counts
    queries = by_distance([query_ref], count_head, -1)
    per_part = count_head + count_tm - 1
    parts = [refs[p * per_part : (p + 1) * per_part] for p in range(len(heads_of))]
    outs = refs[len(heads_of) * per_part :][-len(distances) :]
    blocks, tokens, _ = outs[0].shape
    rows = len(distances) * tokens
    shard = lax.axis_index("tm")
    me = lax.axis_index("head")
    bias = bias_ref[...][:, None, :]
    place_of = [(p, h) for p, (_, size) in enumerate(heads_of) for h in range(size // HD)]

    def gathered(kind, head):
        p, h = place_of[head]
        first = kind * heads_of[p][1] + h * HD
        lanes = slice(first, first + HD)
        pieces = [rows_of(own[:, :, lanes]) for own in parts[p][:count_head]]
        pieces += [
            rows_of(parts[p][count_head + distance - 1][k, :, :, lanes])
            for distance, k in remote_rows(count_tm)
        ]
        return jnp.concatenate(pieces, axis=0)

    def products(head):
        first = heads_of[0][0] + head * HD
        lanes = slice(first, first + HD)
        query = jnp.concatenate(
            [rows_of(queries[s][i, :, lanes]) for i in range(blocks) for s in distances], axis=0
        )
        return lax.dot_general(
            query, gathered(0, head), (((1,), (1,)), ((), ())), preferred_element_type=jnp.float32
        )

    heads = len(place_of)
    dots, mixed = products(0), []
    for h in range(heads):
        ahead = products(h + 1) if h + 1 < heads else None
        dots = dots.reshape(blocks, rows, -1) + bias
        peak = jnp.max(dots, axis=-1, keepdims=True)
        weights = jnp.exp2((dots - peak) * (SCORE_SCALE * LOG2E))
        inverse = 1.0 / jnp.sum(weights, axis=-1, keepdims=True)
        weights_half = weights.astype(jnp.bfloat16).reshape(blocks * rows, -1)
        part = jnp.dot(weights_half, gathered(1, h), preferred_element_type=jnp.float32)
        mixed.append(part * inverse.reshape(blocks * rows, 1))
        dots = ahead
    mixed = jnp.concatenate(mixed, axis=0)
    sign = sign_matrix()
    high = mixed.astype(jnp.bfloat16)
    low = (mixed - high.astype(jnp.float32)).astype(jnp.bfloat16)
    turned = jnp.dot(high, sign, preferred_element_type=jnp.float32)
    turned = turned + jnp.dot(low, sign, preferred_element_type=jnp.float32)
    turned = (turned * ROTATE_SCALE).reshape(heads, blocks, len(distances), tokens, HD)
    token = lax.broadcasted_iota(jnp.int32, (tokens, HD), 0)
    for at, s in enumerate(distances):
        position = lax.rem(me - s + count_head, count_head) * tokens + token
        for i in range(blocks):
            live = position < tokens_ref[shard * blocks + i]
            for h in range(heads):
                outs[at][i, :, h * HD : (h + 1) * HD] = jnp.where(
                    live, turned[h, i, at], 0.0
                ).astype(jnp.bfloat16)


def attend(block_tokens, bias, query, parts, heads_of, distances, after=(), cost=NO_COST):
    count_head, count_tm = query.shape[0], len(parts[0][1]) + 1
    operands = [ref for owns, slots in parts for ref in owns + slots]
    shape = query.shape[1:3] + (sum(size for _, size in heads_of),)
    vmem = pl.BlockSpec(memory_space=pltpu.VMEM)
    return pl.pallas_call(
        functools.partial(attend_kernel, (count_head, count_tm), heads_of, distances),
        in_specs=[pl.BlockSpec(memory_space=pltpu.SMEM)]
        + [vmem] * (2 + len(operands))
        + [pl.BlockSpec(memory_space=pl.ANY)] * len(after),
        out_specs=[vmem] * len(distances),
        out_shape=[jax.ShapeDtypeStruct(shape, jnp.bfloat16)] * len(distances),
        cost_estimate=cost,
        compiler_params=pltpu.CompilerParams(vmem_limit_bytes=VMEM),
    )(block_tokens, bias, query, *operands, *after)


def place_kernel(places, width_here, *refs):
    pieces, out_ref, sems = refs[:-2], refs[-2], refs[-1]
    me, count = lax.axis_index("head"), lax.axis_size("head")
    copies = []
    for at, (piece, (s, start)) in enumerate(zip(pieces, places)):
        column = pl.multiple_of(lax.rem(me + s, count) * width_here + start, HD)
        copies.append(
            pltpu.make_async_copy(
                piece, out_ref.at[:, :, pl.ds(column, piece.shape[-1])], sems.at[at]
            )
        )
        copies[-1].start()
    for copy in copies:
        copy.wait()


def place_pieces(pieces, places, width_here):
    blocks, tokens, _ = pieces[0].shape
    width = width_here * lax.axis_size("head")
    return pl.pallas_call(
        functools.partial(place_kernel, places, width_here),
        in_specs=[pl.BlockSpec(memory_space=pl.ANY)] * len(pieces),
        out_specs=pl.BlockSpec(memory_space=pltpu.HBM),
        out_shape=jax.ShapeDtypeStruct((blocks, tokens, width), jnp.bfloat16),
        scratch_shapes=[pltpu.SemaphoreType.DMA((len(pieces),))],
        compiler_params=pltpu.CompilerParams(vmem_limit_bytes=VMEM),
    )(*pieces)


def shifted(array, axis, distance):
    count = lax.axis_size(axis)
    return lax.ppermute(array, axis, [(i, (i + distance) % count) for i in range(count)])


def exchange(pieces, direction):
    return [shifted(piece, "head", direction * s) for s, piece in enumerate(pieces, 1)]


def forward(sent):
    return [shifted(block, "tm", distance) for distance, block in enumerate(sent, 1)]


def shards(query_rows, key_rows, value_rows, pair_list, block_tokens):
    count_head = lax.axis_size("head")
    count_tm = lax.axis_size("tm")
    blocks, tokens, width = query_rows.shape
    width_here = width // count_head
    heads = width_here // HD
    cut = (heads + 1) // 2 * HD
    parts = [(0, cut), (cut, width_here - cut)] if heads > 1 else [(0, width_here)]
    arrays = [query_rows, key_rows, value_rows]
    messages = [[(1,) + part, (2,) + part] for part in parts]
    pieces, token = rotate_pieces(arrays, messages[0], count_head)
    picks, bias, later = plan(
        arrays, messages[1:], pair_list, block_tokens, token, count_head, count_tm
    )
    received = [piece[:1] + exchange(piece[1:], 1) for piece in [pieces] + later]
    sent, after = [], ()
    for owns, (_, size) in zip(received, parts):
        sent.append(pick_blocks(picks, owns, (0, 2 * size), count_tm, after))
        after = (sent[-1][0],)
    message = [(0, 0, width_here)]
    query = rotate_stacked(arrays, message, count_head, sent[0][0])
    query = lax.all_to_all(query, "head", split_axis=0, concat_axis=0, tiled=True)
    inputs = [(owns, forward(picked)) for owns, picked in zip(received, sent)]
    distances, after = list(range(1, count_head)), ()
    pieces, places = [], []
    for at, part in enumerate(parts):
        cost = NO_COST if at == len(parts) - 1 else HIGH_COST
        leaving = attend(
            block_tokens, bias, query, [inputs[at]], [part], distances, after, cost
        )
        after = (leaving[0],)
        pieces += exchange(leaving, -1)
        places += [(s, part[0]) for s in distances]
    pieces += attend(block_tokens, bias, query, inputs, parts, [0], after)
    return place_pieces(pieces, places + [(0, 0)], width_here)


def solution(mesh):
    placed = (
        P(("grp", "tm"), "head", None),
        P(("grp", "tm"), "head", None),
        P(("grp", "tm"), "head", None),
        P("grp", None),
        P("grp"),
    )
    return jax.shard_map(
        shards,
        mesh=mesh,
        in_specs=placed,
        out_specs=P(("grp", "tm"), "head", None),
        check_vma=False,
    )
```

```python
import functools
import math

import jax
import jax.numpy as jnp
from jax import lax
from jax.experimental import pallas as pl
from jax.experimental.pallas import tpu as pltpu
from jax.sharding import PartitionSpec as P

HD = 128
BLK = 64
NEAR_CAP = 2
FAR_CAP = 1
NEG = -1e30
ROTATE_SCALE = 1.0 / math.sqrt(HD)
SCORE_SCALE = 1.0 / math.sqrt(HD)
VMEM = 24 * 1024 * 1024
WIDE_VMEM = 60 * 1024 * 1024
TOKEN = jax.ShapeDtypeStruct((8, 128), jnp.float32)
NO_COST = pl.CostEstimate(flops=0, bytes_accessed=0, transcendentals=0)
HIGH_COST = pl.CostEstimate(flops=10**11, bytes_accessed=0, transcendentals=0)
LOG2E = math.log2(math.e)


def sign_matrix():
    common = lax.broadcasted_iota(jnp.int32, (HD, HD), 0) & lax.broadcasted_iota(
        jnp.int32, (HD, HD), 1
    )
    bits = HD.bit_length() - 1
    parity = common
    for bit in range(1, bits):
        parity = parity ^ (common >> bit)
    return jnp.where((parity & 1) == 0, 1.0, -1.0).astype(jnp.bfloat16)


def rows_of(block):
    rows, width = math.prod(block.shape[:-1]), block.shape[-1]
    if block.shape[-2] % 16 == 0:
        return block.reshape(rows, width)
    return block.astype(jnp.float32).reshape(rows, width).astype(block.dtype)


def fields_of(message):
    at, fields = 0, []
    for source, start, size in message:
        fields.append((source, start, size, at))
        at += size
    return fields, at


def by_distance(refs, count, direction):
    if len(refs[0].shape) == 3:
        return list(refs)
    me = lax.axis_index("head")
    return [refs[0].at[lax.rem(me + direction * s + count, count)] for s in range(count)]


def rotated(block, sign):
    blocks, tokens, size = block.shape
    flat = rows_of(block)
    heads = [flat[:, at : at + HD] for at in range(0, size, HD)]
    turned = jnp.dot(jnp.concatenate(heads, axis=0), sign, preferred_element_type=jnp.float32)
    return (turned * ROTATE_SCALE).reshape(size // HD, blocks, tokens, HD).astype(jnp.bfloat16)


def store_heads(out, start, turned):
    for h in range(turned.shape[0]):
        at = start + h * HD
        out[:, :, at : at + HD] = turned[h]


def rotate_kernel(message, sources, count_head, *refs):
    fields, total = fields_of(message)
    ins = dict(zip(sources, refs))
    outs, (token, buffer, sems) = refs[len(sources) : -3], refs[-3:]
    token[...] = jnp.zeros_like(token)
    width_here = refs[0].shape[2] // count_head
    me = lax.axis_index("head")
    order = list(range(1, count_head)) + [0]
    copies = {}
    for s in order:
        goal = lax.rem(me + s, count_head)
        for f, (source, start, size, at) in enumerate(fields):
            column = pl.multiple_of(goal * width_here + start, HD)
            copies[s, f] = pltpu.make_async_copy(
                ins[source].at[:, :, pl.ds(column, size)],
                buffer.at[s, :, :, pl.ds(at, size)],
                sems.at[s, f],
            )
            copies[s, f].start()
    sign = sign_matrix()
    for s in order:
        for f, (_, _, size, start) in enumerate(fields):
            copies[s, f].wait()
            store_heads(outs[s], start, rotated(buffer[s, :, :, start : start + size], sign))


def rotate_here(fields, ins, outs, distances, count_head, sign):
    width_here = next(iter(ins.values())).shape[2] // count_head
    me = lax.axis_index("head")
    for s in distances:
        goal = lax.rem(me + s, count_head)
        for source, start, size, at in fields:
            column = pl.multiple_of(goal * width_here + start, HD)
            store_heads(outs[s], at, rotated(ins[source][:, :, pl.ds(column, size)], sign))


def rotate_pieces(arrays, message, count_head):
    blocks, tokens, _ = arrays[0].shape
    fields, total = fields_of(message)
    sources = sorted({source for source, _, _ in message})
    one = (blocks, tokens, total)
    *pieces, token = pl.pallas_call(
        functools.partial(rotate_kernel, message, sources, count_head),
        in_specs=[pl.BlockSpec(memory_space=pltpu.HBM)] * len(sources),
        out_specs=[pl.BlockSpec(memory_space=pltpu.VMEM)] * (count_head + 1),
        out_shape=[jax.ShapeDtypeStruct(one, jnp.bfloat16)] * count_head + [TOKEN],
        scratch_shapes=[
            pltpu.VMEM((count_head,) + one, jnp.bfloat16),
            pltpu.SemaphoreType.DMA((count_head, len(fields))),
        ],
        cost_estimate=NO_COST,
        compiler_params=pltpu.CompilerParams(vmem_limit_bytes=WIDE_VMEM),
    )(*[arrays[source] for source in sources])
    return pieces, token


def slots_at(distance, count_tm):
    return NEAR_CAP if distance in (1, count_tm - 1) else FAR_CAP


def pick_kernel(count_head, count_tm, lanes, skipped, picks_ref, *refs):
    pieces, outs = refs[:count_head], refs[count_head + skipped :]
    shard = lax.axis_index("tm")
    for distance, out in enumerate(outs, 1):
        goal = lax.rem(shard + distance, count_tm)
        for k in range(slots_at(distance, count_tm)):
            pick = picks_ref[NEAR_CAP * goal + k]
            for s in range(count_head):
                out[k, s] = pieces[s][pick, :, lanes[0] : lanes[1]]


def pick_blocks(picks, pieces, lanes, count_tm, after):
    count_head = len(pieces)
    one = (count_head, pieces[0].shape[1], lanes[1] - lanes[0])
    vmem = pl.BlockSpec(memory_space=pltpu.VMEM)
    return pl.pallas_call(
        functools.partial(pick_kernel, count_head, count_tm, lanes, len(after)),
        in_specs=[pl.BlockSpec(memory_space=pltpu.SMEM)]
        + [vmem] * count_head
        + [pl.BlockSpec(memory_space=pl.ANY)] * len(after),
        out_specs=[vmem] * (count_tm - 1),
        out_shape=[
            jax.ShapeDtypeStruct((slots_at(distance, count_tm),) + one, jnp.bfloat16)
            for distance in range(1, count_tm)
        ],
        cost_estimate=HIGH_COST,
        compiler_params=pltpu.CompilerParams(vmem_limit_bytes=VMEM),
    )(picks, *pieces, *after)


def remote_rows(count_tm):
    return [
        (distance, k)
        for distance in range(1, count_tm)
        for k in range(slots_at(distance, count_tm))
    ]


def split(value, by):
    if by & (by - 1) == 0:
        return value >> (by.bit_length() - 1), value & (by - 1)
    return lax.div(value, by), lax.rem(value, by)


def plan_kernel(messages, count_head, count_tm, blocks, *refs):
    *sources, pair_hbm, tokens_ref, _ = refs[:6]
    picks_ref, bias_ref, query_out = refs[6:9]
    pair_ref, named_ref, table_ref, pair_sem, table_sem = refs[-5:]
    outs = refs[9:-5]
    ins = dict(enumerate(sources))
    pair_copy = pltpu.make_async_copy(pair_hbm, pair_ref, pair_sem)
    pair_copy.start()
    sign = sign_matrix()
    places = list(range(1, count_head)) + [0]
    jobs = [
        (fields_of(message)[0], outs[m * count_head : (m + 1) * count_head], s)
        for m, message in enumerate(messages)
        for s in places
    ]
    query_fields = [(0, 0, query_out.shape[-1], 0)]
    jobs += [(query_fields, by_distance([query_out], count_head, 1), s) for s in places]
    half = len(jobs) // 2
    for fields, pieces, s in jobs[:half]:
        rotate_here(fields, ins, pieces, [s], count_head, sign)
    pair_copy.wait()
    total_blocks, columns = pair_ref.shape
    pairs = pair_ref[...]
    lane = lax.broadcasted_iota(jnp.int32, named_ref.shape, 1)
    named = jnp.zeros(named_ref.shape, jnp.int32)
    for c in range(columns):
        named = jnp.where(pairs[:, c : c + 1] == lane, 1, named)
    named_ref[...] = named
    copy = pltpu.make_async_copy(named_ref, table_ref, table_sem)
    copy.start()
    for fields, pieces, s in jobs[half:]:
        rotate_here(fields, ins, pieces, [s], count_head, sign)
    copy.wait()
    shard = lax.axis_index("tm")
    place = lax.axis_index("head")
    mine = shard * blocks

    def two_picks(wanted):
        picks = [jnp.int32(0)] * NEAR_CAP
        count = jnp.int32(0)
        for j in range(blocks):
            for k in range(NEAR_CAP):
                picks[k] = jnp.where((wanted[j] > 0) & (count == k), j, picks[k])
            count = count + wanted[j]
        return picks, count

    def named_by(rows, column):
        found = table_ref[rows, column]
        for i in range(1, blocks):
            found = found | table_ref[rows + i, column]
        return found

    for d in range(count_tm):
        picks, _ = two_picks([named_by(d * blocks, mine + j) for j in range(blocks)])
        for k in range(NEAR_CAP):
            picks_ref[NEAR_CAP * d + k] = picks[k]

    kept = [[table_ref[mine + i, mine + j] * tokens_ref[mine + j] for j in range(blocks)] for i in range(blocks)]
    arrivals = {}
    for distance, k in remote_rows(count_tm):
        first = lax.rem(shard - distance + count_tm, count_tm) * blocks
        if k == 0:
            arrivals[distance] = two_picks([named_by(mine, first + j) for j in range(blocks)])
        picks, count = arrivals[distance]
        there = first + picks[k]
        live = jnp.where(count > k, tokens_ref[there], 0)
        for i in range(blocks):
            kept[i].append(table_ref[mine + i, there] * live)

    total = bias_ref.shape[1]
    piece_rows = BLK // count_head
    at = lax.broadcasted_iota(jnp.int32, (blocks, total), 1)
    query = lax.broadcasted_iota(jnp.int32, (blocks, total), 0)
    own = at < blocks * BLK
    group, token = split(at, piece_rows)
    own_piece, own_block = split(group, blocks)
    far_row, far_group = split(group, count_head)
    row = jnp.where(own, own_block, far_row)
    piece = jnp.where(own, own_piece, far_group)
    source = jnp.where(piece > place, place - piece + count_head, place - piece)
    position = source * piece_rows + token
    limit = jnp.zeros((blocks, total), jnp.int32)
    for r in range(len(kept[0])):
        value = jnp.zeros((blocks, total), jnp.int32)
        for i in range(blocks):
            value = jnp.where(query == i, kept[i][r], value)
        limit = jnp.where(row == r, value, limit)
    bias_ref[...] = jnp.where(position < limit, 0.0, NEG)


def plan(arrays, messages, pair_list, block_tokens, after, count_head, count_tm):
    blocks, tokens, _ = arrays[0].shape
    total_blocks, columns = pair_list.shape
    lanes = -(-total_blocks // 128) * 128
    total = (blocks + len(remote_rows(count_tm))) * BLK
    vmem = pl.BlockSpec(memory_space=pltpu.VMEM)
    smem = pl.BlockSpec(memory_space=pltpu.SMEM)
    stacked = (count_head, blocks, tokens, arrays[0].shape[2] // count_head)
    shapes = [jax.ShapeDtypeStruct(stacked, jnp.bfloat16)] + [
        jax.ShapeDtypeStruct((blocks, tokens, fields_of(message)[1]), jnp.bfloat16)
        for message in messages
        for _ in range(count_head)
    ]
    picks, bias, query, *pieces = pl.pallas_call(
        functools.partial(plan_kernel, messages, count_head, count_tm, blocks),
        in_specs=[vmem] * 3
        + [pl.BlockSpec(memory_space=pl.ANY), smem, pl.BlockSpec(memory_space=pl.ANY)],
        out_specs=[smem, vmem] + [vmem] * len(shapes),
        out_shape=[
            jax.ShapeDtypeStruct((NEAR_CAP * count_tm,), jnp.int32),
            jax.ShapeDtypeStruct((blocks, total), jnp.float32),
        ]
        + shapes,
        scratch_shapes=[
            pltpu.VMEM((total_blocks, columns), jnp.int32),
            pltpu.VMEM((total_blocks, lanes), jnp.int32),
            pltpu.SMEM((total_blocks, lanes), jnp.int32),
            pltpu.SemaphoreType.DMA,
            pltpu.SemaphoreType.DMA,
        ],
        cost_estimate=NO_COST,
        compiler_params=pltpu.CompilerParams(vmem_limit_bytes=VMEM),
    )(*arrays, pair_list, block_tokens, after)
    return picks, bias, query, [pieces[at : at + count_head] for at in range(0, len(pieces), count_head)]


def attend_kernel(counts, heads_of, distances, tokens_ref, bias_ref, query_ref, *refs):
    count_head, count_tm = counts
    queries = by_distance([query_ref], count_head, -1)
    per_part = count_head + count_tm - 1
    parts = [refs[p * per_part : (p + 1) * per_part] for p in range(len(heads_of))]
    outs = refs[len(heads_of) * per_part :][-len(distances) :]
    blocks, tokens, _ = outs[0].shape
    rows = len(distances) * tokens
    shard = lax.axis_index("tm")
    me = lax.axis_index("head")
    bias = bias_ref[...][:, None, :]
    place_of = [(p, h) for p, (_, size) in enumerate(heads_of) for h in range(size // HD)]

    def gathered(kind, head):
        p, h = place_of[head]
        first = kind * heads_of[p][1] + h * HD
        lanes = slice(first, first + HD)
        pieces = [rows_of(own[:, :, lanes]) for own in parts[p][:count_head]]
        pieces += [
            rows_of(parts[p][count_head + distance - 1][k, :, :, lanes])
            for distance, k in remote_rows(count_tm)
        ]
        return jnp.concatenate(pieces, axis=0)

    def products(head):
        first = heads_of[0][0] + head * HD
        lanes = slice(first, first + HD)
        query = jnp.concatenate(
            [rows_of(queries[s][i, :, lanes]) for i in range(blocks) for s in distances], axis=0
        )
        return lax.dot_general(
            query, gathered(0, head), (((1,), (1,)), ((), ())), preferred_element_type=jnp.float32
        )

    heads = len(place_of)
    dots, mixed = products(0), []
    for h in range(heads):
        ahead = products(h + 1) if h + 1 < heads else None
        dots = dots.reshape(blocks, rows, -1) + bias
        peak = jnp.max(dots, axis=-1, keepdims=True)
        weights = jnp.exp2((dots - peak) * (SCORE_SCALE * LOG2E))
        inverse = 1.0 / jnp.sum(weights, axis=-1, keepdims=True)
        weights_half = weights.astype(jnp.bfloat16).reshape(blocks * rows, -1)
        part = jnp.dot(weights_half, gathered(1, h), preferred_element_type=jnp.float32)
        mixed.append(part * inverse.reshape(blocks * rows, 1))
        dots = ahead
    mixed = jnp.concatenate(mixed, axis=0)
    sign = sign_matrix()
    high = mixed.astype(jnp.bfloat16)
    low = (mixed - high.astype(jnp.float32)).astype(jnp.bfloat16)
    turned = jnp.dot(high, sign, preferred_element_type=jnp.float32)
    turned = turned + jnp.dot(low, sign, preferred_element_type=jnp.float32)
    turned = (turned * ROTATE_SCALE).reshape(heads, blocks, len(distances), tokens, HD)
    token = lax.broadcasted_iota(jnp.int32, (tokens, HD), 0)
    for at, s in enumerate(distances):
        position = lax.rem(me - s + count_head, count_head) * tokens + token
        for i in range(blocks):
            live = position < tokens_ref[shard * blocks + i]
            for h in range(heads):
                outs[at][i, :, h * HD : (h + 1) * HD] = jnp.where(
                    live, turned[h, i, at], 0.0
                ).astype(jnp.bfloat16)


def attend(block_tokens, bias, query, parts, heads_of, distances, after=(), cost=NO_COST):
    count_head, count_tm = query.shape[0], len(parts[0][1]) + 1
    operands = [ref for owns, slots in parts for ref in owns + slots]
    shape = query.shape[1:3] + (sum(size for _, size in heads_of),)
    vmem = pl.BlockSpec(memory_space=pltpu.VMEM)
    return pl.pallas_call(
        functools.partial(attend_kernel, (count_head, count_tm), heads_of, distances),
        in_specs=[pl.BlockSpec(memory_space=pltpu.SMEM)]
        + [vmem] * (2 + len(operands))
        + [pl.BlockSpec(memory_space=pl.ANY)] * len(after),
        out_specs=[vmem] * len(distances),
        out_shape=[jax.ShapeDtypeStruct(shape, jnp.bfloat16)] * len(distances),
        cost_estimate=cost,
        compiler_params=pltpu.CompilerParams(vmem_limit_bytes=VMEM),
    )(block_tokens, bias, query, *operands, *after)


def place_kernel(places, width_here, *refs):
    pieces, out_ref, sems = refs[:-2], refs[-2], refs[-1]
    me, count = lax.axis_index("head"), lax.axis_size("head")
    copies = []
    for at, (piece, (s, start)) in enumerate(zip(pieces, places)):
        column = pl.multiple_of(lax.rem(me + s, count) * width_here + start, HD)
        copies.append(
            pltpu.make_async_copy(
                piece, out_ref.at[:, :, pl.ds(column, piece.shape[-1])], sems.at[at]
            )
        )
        copies[-1].start()
    for copy in copies:
        copy.wait()


def place_pieces(pieces, places, width_here):
    blocks, tokens, _ = pieces[0].shape
    width = width_here * lax.axis_size("head")
    return pl.pallas_call(
        functools.partial(place_kernel, places, width_here),
        in_specs=[pl.BlockSpec(memory_space=pl.ANY)] * len(pieces),
        out_specs=pl.BlockSpec(memory_space=pltpu.HBM),
        out_shape=jax.ShapeDtypeStruct((blocks, tokens, width), jnp.bfloat16),
        scratch_shapes=[pltpu.SemaphoreType.DMA((len(pieces),))],
        compiler_params=pltpu.CompilerParams(vmem_limit_bytes=VMEM),
    )(*pieces)


def shifted(array, axis, distance):
    count = lax.axis_size(axis)
    return lax.ppermute(array, axis, [(i, (i + distance) % count) for i in range(count)])


def exchange(pieces, direction):
    return [shifted(piece, "head", direction * s) for s, piece in enumerate(pieces, 1)]


def forward(sent):
    return [shifted(block, "tm", distance) for distance, block in enumerate(sent, 1)]


def shards(query_rows, key_rows, value_rows, pair_list, block_tokens):
    count_head = lax.axis_size("head")
    count_tm = lax.axis_size("tm")
    blocks, tokens, width = query_rows.shape
    width_here = width // count_head
    heads = width_here // HD
    cut = (heads + 1) // 2 * HD
    parts = [(0, cut), (cut, width_here - cut)] if heads > 1 else [(0, width_here)]
    arrays = [query_rows, key_rows, value_rows]
    messages = [[(1,) + part, (2,) + part] for part in parts]
    pieces, token = rotate_pieces(arrays, messages[0], count_head)
    picks, bias, query, later = plan(
        arrays, messages[1:], pair_list, block_tokens, token, count_head, count_tm
    )
    received = [piece[:1] + exchange(piece[1:], 1) for piece in [pieces] + later]
    sent, after = [], ()
    for owns, (_, size) in zip(received, parts):
        sent.append(pick_blocks(picks, owns, (0, 2 * size), count_tm, after))
        after = (sent[-1][0],)
    query = lax.all_to_all(query, "head", split_axis=0, concat_axis=0, tiled=True)
    inputs = [(owns, forward(picked)) for owns, picked in zip(received, sent)]
    distances, after = list(range(1, count_head)), ()
    pieces, places = [], []
    for at, part in enumerate(parts):
        cost = NO_COST if at == len(parts) - 1 else HIGH_COST
        leaving = attend(
            block_tokens, bias, query, [inputs[at]], [part], distances, after, cost
        )
        after = (leaving[0],)
        pieces += exchange(leaving, -1)
        places += [(s, part[0]) for s in distances]
    pieces += attend(block_tokens, bias, query, inputs, parts, [0], after)
    return place_pieces(pieces, places + [(0, 0)], width_here)


def solution(mesh):
    placed = (
        P(("grp", "tm"), "head", None),
        P(("grp", "tm"), "head", None),
        P(("grp", "tm"), "head", None),
        P("grp", None),
        P("grp"),
    )
    return jax.shard_map(
        shards,
        mesh=mesh,
        in_specs=placed,
        out_specs=P(("grp", "tm"), "head", None),
        check_vma=False,
    )
```

```python
import functools
import math

import jax
import jax.numpy as jnp
from jax import lax
from jax.experimental import pallas as pl
from jax.experimental.pallas import tpu as pltpu
from jax.sharding import PartitionSpec as P

HD = 128
BLK = 64
NEAR_CAP = 2
FAR_CAP = 1
NEG = -1e30
ROTATE_SCALE = 1.0 / math.sqrt(HD)
SCORE_SCALE = 1.0 / math.sqrt(HD)
VMEM = 24 * 1024 * 1024
WIDE_VMEM = 60 * 1024 * 1024
TOKEN = jax.ShapeDtypeStruct((8, 128), jnp.float32)
NO_COST = pl.CostEstimate(flops=0, bytes_accessed=0, transcendentals=0)
HIGH_COST = pl.CostEstimate(flops=10**11, bytes_accessed=0, transcendentals=0)
LOG2E = math.log2(math.e)


def sign_matrix():
    common = lax.broadcasted_iota(jnp.int32, (HD, HD), 0) & lax.broadcasted_iota(
        jnp.int32, (HD, HD), 1
    )
    bits = HD.bit_length() - 1
    parity = common
    for bit in range(1, bits):
        parity = parity ^ (common >> bit)
    return jnp.where((parity & 1) == 0, 1.0, -1.0).astype(jnp.bfloat16)


def rows_of(block):
    rows, width = math.prod(block.shape[:-1]), block.shape[-1]
    if block.shape[-2] % 16 == 0:
        return block.reshape(rows, width)
    return block.astype(jnp.float32).reshape(rows, width).astype(block.dtype)


def fields_of(message):
    at, fields = 0, []
    for source, start, size in message:
        fields.append((source, start, size, at))
        at += size
    return fields, at


def by_distance(refs, count, direction):
    if len(refs[0].shape) == 3:
        return list(refs)
    me = lax.axis_index("head")
    return [refs[0].at[lax.rem(me + direction * s + count, count)] for s in range(count)]


def rotated(block, sign):
    blocks, tokens, size = block.shape
    flat = rows_of(block)
    heads = [flat[:, at : at + HD] for at in range(0, size, HD)]
    turned = jnp.dot(jnp.concatenate(heads, axis=0), sign, preferred_element_type=jnp.float32)
    return (turned * ROTATE_SCALE).reshape(size // HD, blocks, tokens, HD).astype(jnp.bfloat16)


def store_heads(out, start, turned):
    for h in range(turned.shape[0]):
        at = start + h * HD
        out[:, :, at : at + HD] = turned[h]


def rotate_kernel(message, sources, count_head, *refs):
    fields, total = fields_of(message)
    ins = dict(zip(sources, refs))
    outs, (token, buffer, sems) = refs[len(sources) : -3], refs[-3:]
    token[...] = jnp.zeros_like(token)
    width_here = refs[0].shape[2] // count_head
    me = lax.axis_index("head")
    order = list(range(1, count_head)) + [0]
    copies = {}
    for s in order:
        goal = lax.rem(me + s, count_head)
        for f, (source, start, size, at) in enumerate(fields):
            column = pl.multiple_of(goal * width_here + start, HD)
            copies[s, f] = pltpu.make_async_copy(
                ins[source].at[:, :, pl.ds(column, size)],
                buffer.at[s, :, :, pl.ds(at, size)],
                sems.at[s, f],
            )
            copies[s, f].start()
    sign = sign_matrix()
    for s in order:
        for f, (_, _, size, start) in enumerate(fields):
            copies[s, f].wait()
            store_heads(outs[s], start, rotated(buffer[s, :, :, start : start + size], sign))


def rotate_here(fields, ins, outs, distances, count_head, sign):
    width_here = next(iter(ins.values())).shape[2] // count_head
    me = lax.axis_index("head")
    for s in distances:
        goal = lax.rem(me + s, count_head)
        for source, start, size, at in fields:
            column = pl.multiple_of(goal * width_here + start, HD)
            store_heads(outs[s], at, rotated(ins[source][:, :, pl.ds(column, size)], sign))


def rotate_pieces(arrays, message, count_head):
    blocks, tokens, _ = arrays[0].shape
    fields, total = fields_of(message)
    sources = sorted({source for source, _, _ in message})
    one = (blocks, tokens, total)
    *pieces, token = pl.pallas_call(
        functools.partial(rotate_kernel, message, sources, count_head),
        in_specs=[pl.BlockSpec(memory_space=pltpu.HBM)] * len(sources),
        out_specs=[pl.BlockSpec(memory_space=pltpu.VMEM)] * (count_head + 1),
        out_shape=[jax.ShapeDtypeStruct(one, jnp.bfloat16)] * count_head + [TOKEN],
        scratch_shapes=[
            pltpu.VMEM((count_head,) + one, jnp.bfloat16),
            pltpu.SemaphoreType.DMA((count_head, len(fields))),
        ],
        cost_estimate=NO_COST,
        compiler_params=pltpu.CompilerParams(vmem_limit_bytes=WIDE_VMEM),
    )(*[arrays[source] for source in sources])
    return pieces, token


def slots_at(distance, count_tm):
    return NEAR_CAP if distance in (1, count_tm - 1) else FAR_CAP


def pick_kernel(count_head, count_tm, lanes, picks_ref, *refs):
    pieces, outs = refs[:count_head], refs[count_head + 1 : count_head + count_tm]
    shard = lax.axis_index("tm")
    for distance, out in enumerate(outs, 1):
        goal = lax.rem(shard + distance, count_tm)
        for k in range(slots_at(distance, count_tm)):
            pick = picks_ref[NEAR_CAP * goal + k]
            for s in range(count_head):
                out[k, s] = pieces[s][pick, :, lanes[0] : lanes[1]]


def pick_blocks(picks, pieces, lanes, count_tm, held, passes):
    count_head = len(pieces)
    one = (count_head, pieces[0].shape[1], lanes[1] - lanes[0])
    vmem, anywhere = pl.BlockSpec(memory_space=pltpu.VMEM), pl.BlockSpec(memory_space=pl.ANY)
    shapes = [
        jax.ShapeDtypeStruct((slots_at(distance, count_tm),) + one, jnp.bfloat16)
        for distance in range(1, count_tm)
    ]
    passed = [jax.ShapeDtypeStruct(held.shape, held.dtype)] if passes else []
    return pl.pallas_call(
        functools.partial(pick_kernel, count_head, count_tm, lanes),
        in_specs=[pl.BlockSpec(memory_space=pltpu.SMEM)] + [vmem] * count_head + [anywhere],
        out_specs=[vmem] * len(shapes) + [anywhere] * len(passed),
        out_shape=shapes + passed,
        input_output_aliases={1 + count_head: len(shapes)} if passes else {},
        cost_estimate=HIGH_COST,
        compiler_params=pltpu.CompilerParams(vmem_limit_bytes=VMEM),
    )(picks, *pieces, held)


def remote_rows(count_tm):
    return [
        (distance, k)
        for distance in range(1, count_tm)
        for k in range(slots_at(distance, count_tm))
    ]


def split(value, by):
    if by & (by - 1) == 0:
        return value >> (by.bit_length() - 1), value & (by - 1)
    return lax.div(value, by), lax.rem(value, by)


def plan_kernel(messages, count_head, count_tm, blocks, *refs):
    *sources, pair_hbm, tokens_ref, _ = refs[:6]
    picks_ref, bias_ref, query_out = refs[6:9]
    pair_ref, named_ref, table_ref, pair_sem, table_sem = refs[-5:]
    outs = refs[9:-5]
    ins = dict(enumerate(sources))
    pair_copy = pltpu.make_async_copy(pair_hbm, pair_ref, pair_sem)
    pair_copy.start()
    sign = sign_matrix()
    places = list(range(1, count_head)) + [0]
    jobs = [
        (fields_of(message)[0], outs[m * count_head : (m + 1) * count_head], s)
        for m, message in enumerate(messages)
        for s in places
    ]
    query_fields = [(0, 0, query_out.shape[-1], 0)]
    jobs += [(query_fields, by_distance([query_out], count_head, 1), s) for s in places]
    half = len(jobs) // 2
    for fields, pieces, s in jobs[:half]:
        rotate_here(fields, ins, pieces, [s], count_head, sign)
    pair_copy.wait()
    total_blocks, columns = pair_ref.shape
    pairs = pair_ref[...]
    lane = lax.broadcasted_iota(jnp.int32, named_ref.shape, 1)
    named = jnp.zeros(named_ref.shape, jnp.int32)
    for c in range(columns):
        named = jnp.where(pairs[:, c : c + 1] == lane, 1, named)
    named_ref[...] = named
    copy = pltpu.make_async_copy(named_ref, table_ref, table_sem)
    copy.start()
    for fields, pieces, s in jobs[half:]:
        rotate_here(fields, ins, pieces, [s], count_head, sign)
    copy.wait()
    shard = lax.axis_index("tm")
    place = lax.axis_index("head")
    mine = shard * blocks

    def two_picks(wanted):
        picks = [jnp.int32(0)] * NEAR_CAP
        count = jnp.int32(0)
        for j in range(blocks):
            for k in range(NEAR_CAP):
                picks[k] = jnp.where((wanted[j] > 0) & (count == k), j, picks[k])
            count = count + wanted[j]
        return picks, count

    def named_by(rows, column):
        found = table_ref[rows, column]
        for i in range(1, blocks):
            found = found | table_ref[rows + i, column]
        return found

    for d in range(count_tm):
        picks, _ = two_picks([named_by(d * blocks, mine + j) for j in range(blocks)])
        for k in range(NEAR_CAP):
            picks_ref[NEAR_CAP * d + k] = picks[k]

    kept = [[table_ref[mine + i, mine + j] * tokens_ref[mine + j] for j in range(blocks)] for i in range(blocks)]
    arrivals = {}
    for distance, k in remote_rows(count_tm):
        first = lax.rem(shard - distance + count_tm, count_tm) * blocks
        if k == 0:
            arrivals[distance] = two_picks([named_by(mine, first + j) for j in range(blocks)])
        picks, count = arrivals[distance]
        there = first + picks[k]
        live = jnp.where(count > k, tokens_ref[there], 0)
        for i in range(blocks):
            kept[i].append(table_ref[mine + i, there] * live)

    total = bias_ref.shape[1]
    piece_rows = BLK // count_head
    at = lax.broadcasted_iota(jnp.int32, (blocks, total), 1)
    query = lax.broadcasted_iota(jnp.int32, (blocks, total), 0)
    own = at < blocks * BLK
    group, token = split(at, piece_rows)
    own_piece, own_block = split(group, blocks)
    far_row, far_group = split(group, count_head)
    row = jnp.where(own, own_block, far_row)
    piece = jnp.where(own, own_piece, far_group)
    source = jnp.where(piece > place, place - piece + count_head, place - piece)
    position = source * piece_rows + token
    limit = jnp.zeros((blocks, total), jnp.int32)
    for r in range(len(kept[0])):
        value = jnp.zeros((blocks, total), jnp.int32)
        for i in range(blocks):
            value = jnp.where(query == i, kept[i][r], value)
        limit = jnp.where(row == r, value, limit)
    bias_ref[...] = jnp.where(position < limit, 0.0, NEG)


def plan(arrays, messages, pair_list, block_tokens, after, count_head, count_tm):
    blocks, tokens, _ = arrays[0].shape
    total_blocks, columns = pair_list.shape
    lanes = -(-total_blocks // 128) * 128
    total = (blocks + len(remote_rows(count_tm))) * BLK
    vmem = pl.BlockSpec(memory_space=pltpu.VMEM)
    smem = pl.BlockSpec(memory_space=pltpu.SMEM)
    stacked = (count_head, blocks, tokens, arrays[0].shape[2] // count_head)
    shapes = [jax.ShapeDtypeStruct(stacked, jnp.bfloat16)] + [
        jax.ShapeDtypeStruct((blocks, tokens, fields_of(message)[1]), jnp.bfloat16)
        for message in messages
        for _ in range(count_head)
    ]
    picks, bias, query, *pieces = pl.pallas_call(
        functools.partial(plan_kernel, messages, count_head, count_tm, blocks),
        in_specs=[vmem] * 3
        + [pl.BlockSpec(memory_space=pl.ANY), smem, pl.BlockSpec(memory_space=pl.ANY)],
        out_specs=[smem, vmem] + [vmem] * len(shapes),
        out_shape=[
            jax.ShapeDtypeStruct((NEAR_CAP * count_tm,), jnp.int32),
            jax.ShapeDtypeStruct((blocks, total), jnp.float32),
        ]
        + shapes,
        scratch_shapes=[
            pltpu.VMEM((total_blocks, columns), jnp.int32),
            pltpu.VMEM((total_blocks, lanes), jnp.int32),
            pltpu.SMEM((total_blocks, lanes), jnp.int32),
            pltpu.SemaphoreType.DMA,
            pltpu.SemaphoreType.DMA,
        ],
        cost_estimate=NO_COST,
        compiler_params=pltpu.CompilerParams(vmem_limit_bytes=VMEM),
    )(*arrays, pair_list, block_tokens, after)
    return picks, bias, query, [pieces[at : at + count_head] for at in range(0, len(pieces), count_head)]


def attend_kernel(counts, heads_of, distances, tokens_ref, bias_ref, query_ref, *refs):
    count_head, count_tm = counts
    queries = by_distance([query_ref], count_head, -1)
    per_part = count_head + count_tm - 1
    parts = [refs[p * per_part : (p + 1) * per_part] for p in range(len(heads_of))]
    outs = refs[len(heads_of) * per_part :][-len(distances) :]
    blocks, tokens, _ = outs[0].shape
    rows = len(distances) * tokens
    shard = lax.axis_index("tm")
    me = lax.axis_index("head")
    bias = bias_ref[...][:, None, :]
    place_of = [(p, h) for p, (_, size) in enumerate(heads_of) for h in range(size // HD)]

    def gathered(kind, head):
        p, h = place_of[head]
        first = kind * heads_of[p][1] + h * HD
        lanes = slice(first, first + HD)
        pieces = [rows_of(own[:, :, lanes]) for own in parts[p][:count_head]]
        pieces += [
            rows_of(parts[p][count_head + distance - 1][k, :, :, lanes])
            for distance, k in remote_rows(count_tm)
        ]
        return jnp.concatenate(pieces, axis=0)

    def products(head):
        first = heads_of[0][0] + head * HD
        lanes = slice(first, first + HD)
        query = jnp.concatenate(
            [rows_of(queries[s][i, :, lanes]) for i in range(blocks) for s in distances], axis=0
        )
        return lax.dot_general(
            query, gathered(0, head), (((1,), (1,)), ((), ())), preferred_element_type=jnp.float32
        )

    heads = len(place_of)
    dots, mixed = products(0), []
    for h in range(heads):
        ahead = products(h + 1) if h + 1 < heads else None
        dots = dots.reshape(blocks, rows, -1) + bias
        peak = jnp.max(dots, axis=-1, keepdims=True)
        weights = jnp.exp2((dots - peak) * (SCORE_SCALE * LOG2E))
        inverse = 1.0 / jnp.sum(weights, axis=-1, keepdims=True)
        weights_half = weights.astype(jnp.bfloat16).reshape(blocks * rows, -1)
        part = jnp.dot(weights_half, gathered(1, h), preferred_element_type=jnp.float32)
        mixed.append(part * inverse.reshape(blocks * rows, 1))
        dots = ahead
    mixed = jnp.concatenate(mixed, axis=0)
    sign = sign_matrix()
    high = mixed.astype(jnp.bfloat16)
    low = (mixed - high.astype(jnp.float32)).astype(jnp.bfloat16)
    turned = jnp.dot(high, sign, preferred_element_type=jnp.float32)
    turned = turned + jnp.dot(low, sign, preferred_element_type=jnp.float32)
    turned = (turned * ROTATE_SCALE).reshape(heads, blocks, len(distances), tokens, HD)
    token = lax.broadcasted_iota(jnp.int32, (tokens, HD), 0)
    for at, s in enumerate(distances):
        position = lax.rem(me - s + count_head, count_head) * tokens + token
        for i in range(blocks):
            live = position < tokens_ref[shard * blocks + i]
            for h in range(heads):
                outs[at][i, :, h * HD : (h + 1) * HD] = jnp.where(
                    live, turned[h, i, at], 0.0
                ).astype(jnp.bfloat16)


def attend(block_tokens, bias, query, parts, heads_of, distances, after=(), cost=NO_COST):
    count_head, count_tm = query.shape[0], len(parts[0][1]) + 1
    operands = [ref for owns, slots in parts for ref in owns + slots]
    shape = query.shape[1:3] + (sum(size for _, size in heads_of),)
    vmem = pl.BlockSpec(memory_space=pltpu.VMEM)
    return pl.pallas_call(
        functools.partial(attend_kernel, (count_head, count_tm), heads_of, distances),
        in_specs=[pl.BlockSpec(memory_space=pltpu.SMEM)]
        + [vmem] * (2 + len(operands))
        + [pl.BlockSpec(memory_space=pl.ANY)] * len(after),
        out_specs=[vmem] * len(distances),
        out_shape=[jax.ShapeDtypeStruct(shape, jnp.bfloat16)] * len(distances),
        cost_estimate=cost,
        compiler_params=pltpu.CompilerParams(vmem_limit_bytes=VMEM),
    )(block_tokens, bias, query, *operands, *after)


def place_kernel(places, width_here, *refs):
    pieces, out_ref, sems = refs[:-2], refs[-2], refs[-1]
    me, count = lax.axis_index("head"), lax.axis_size("head")
    copies = []
    for at, (piece, (s, start)) in enumerate(zip(pieces, places)):
        column = pl.multiple_of(lax.rem(me + s, count) * width_here + start, HD)
        copies.append(
            pltpu.make_async_copy(
                piece, out_ref.at[:, :, pl.ds(column, piece.shape[-1])], sems.at[at]
            )
        )
        copies[-1].start()
    for copy in copies:
        copy.wait()


def place_pieces(pieces, places, width_here):
    blocks, tokens, _ = pieces[0].shape
    width = width_here * lax.axis_size("head")
    return pl.pallas_call(
        functools.partial(place_kernel, places, width_here),
        in_specs=[pl.BlockSpec(memory_space=pl.ANY)] * len(pieces),
        out_specs=pl.BlockSpec(memory_space=pltpu.HBM),
        out_shape=jax.ShapeDtypeStruct((blocks, tokens, width), jnp.bfloat16),
        scratch_shapes=[pltpu.SemaphoreType.DMA((len(pieces),))],
        compiler_params=pltpu.CompilerParams(vmem_limit_bytes=VMEM),
    )(*pieces)


def shifted(array, axis, distance):
    count = lax.axis_size(axis)
    return lax.ppermute(array, axis, [(i, (i + distance) % count) for i in range(count)])


def exchange(pieces, direction):
    return [shifted(piece, "head", direction * s) for s, piece in enumerate(pieces, 1)]


def forward(sent):
    return [shifted(block, "tm", distance) for distance, block in enumerate(sent, 1)]


def shards(query_rows, key_rows, value_rows, pair_list, block_tokens):
    count_head = lax.axis_size("head")
    count_tm = lax.axis_size("tm")
    blocks, tokens, width = query_rows.shape
    width_here = width // count_head
    heads = width_here // HD
    cut = (heads + 1) // 2 * HD
    parts = [(0, cut), (cut, width_here - cut)] if heads > 1 else [(0, width_here)]
    arrays = [query_rows, key_rows, value_rows]
    messages = [[(1,) + part, (2,) + part] for part in parts]
    pieces, token = rotate_pieces(arrays, messages[0], count_head)
    picks, bias, query, later = plan(
        arrays, messages[1:], pair_list, block_tokens, token, count_head, count_tm
    )
    received = [piece[:1] + exchange(piece[1:], 1) for piece in [pieces] + later]
    sent = []
    for owns, (_, size) in zip(received, parts):
        held = sent[-1][0] if sent else query
        picked = pick_blocks(picks, owns, (0, 2 * size), count_tm, held, not sent)
        if not sent:
            *picked, query = picked
        sent.append(list(picked))
    query = lax.all_to_all(query, "head", split_axis=0, concat_axis=0, tiled=True)
    inputs = [(owns, forward(picked)) for owns, picked in zip(received, sent)]
    distances, after = list(range(1, count_head)), ()
    pieces, places = [], []
    for at, part in enumerate(parts):
        cost = NO_COST if at == len(parts) - 1 else HIGH_COST
        leaving = attend(
            block_tokens, bias, query, [inputs[at]], [part], distances, after, cost
        )
        after = (leaving[0],)
        pieces += exchange(leaving, -1)
        places += [(s, part[0]) for s in distances]
    pieces += attend(block_tokens, bias, query, inputs, parts, [0], after)
    return place_pieces(pieces, places + [(0, 0)], width_here)


def solution(mesh):
    placed = (
        P(("grp", "tm"), "head", None),
        P(("grp", "tm"), "head", None),
        P(("grp", "tm"), "head", None),
        P("grp", None),
        P("grp"),
    )
    return jax.shard_map(
        shards,
        mesh=mesh,
        in_specs=placed,
        out_specs=P(("grp", "tm"), "head", None),
        check_vma=False,
    )
```

```python
import functools
import math

import jax
import jax.numpy as jnp
from jax import lax
from jax.experimental import pallas as pl
from jax.experimental.pallas import tpu as pltpu
from jax.sharding import PartitionSpec as P

HD = 128
BLK = 64
NEAR_CAP = 2
FAR_CAP = 1
NEG = -1e30
ROTATE_SCALE = 1.0 / math.sqrt(HD)
SCORE_SCALE = 1.0 / math.sqrt(HD)
VMEM = 24 * 1024 * 1024
WIDE_VMEM = 60 * 1024 * 1024
TOKEN = jax.ShapeDtypeStruct((8, 128), jnp.float32)
NO_COST = pl.CostEstimate(flops=0, bytes_accessed=0, transcendentals=0)
HIGH_COST = pl.CostEstimate(flops=10**11, bytes_accessed=0, transcendentals=0)
LOG2E = math.log2(math.e)


def sign_matrix():
    common = lax.broadcasted_iota(jnp.int32, (HD, HD), 0) & lax.broadcasted_iota(
        jnp.int32, (HD, HD), 1
    )
    bits = HD.bit_length() - 1
    parity = common
    for bit in range(1, bits):
        parity = parity ^ (common >> bit)
    return jnp.where((parity & 1) == 0, 1.0, -1.0).astype(jnp.bfloat16)


def rows_of(block):
    rows, width = math.prod(block.shape[:-1]), block.shape[-1]
    if block.shape[-2] % 16 == 0:
        return block.reshape(rows, width)
    return block.astype(jnp.float32).reshape(rows, width).astype(block.dtype)


def fields_of(message):
    at, fields = 0, []
    for source, start, size in message:
        fields.append((source, start, size, at))
        at += size
    return fields, at


def by_distance(refs, count, direction):
    if len(refs[0].shape) == 3:
        return list(refs)
    me = lax.axis_index("head")
    return [refs[0].at[lax.rem(me + direction * s + count, count)] for s in range(count)]


def rotated(block, sign):
    blocks, tokens, size = block.shape
    flat = rows_of(block)
    heads = [flat[:, at : at + HD] for at in range(0, size, HD)]
    turned = jnp.dot(jnp.concatenate(heads, axis=0), sign, preferred_element_type=jnp.float32)
    return (turned * ROTATE_SCALE).reshape(size // HD, blocks, tokens, HD).astype(jnp.bfloat16)


def store_heads(out, start, turned):
    for h in range(turned.shape[0]):
        at = start + h * HD
        out[:, :, at : at + HD] = turned[h]


def rotate_kernel(message, sources, count_head, *refs):
    fields, total = fields_of(message)
    ins = dict(zip(sources, refs))
    outs, (token, buffer, sems) = refs[len(sources) : -3], refs[-3:]
    token[...] = jnp.zeros_like(token)
    width_here = refs[0].shape[2] // count_head
    me = lax.axis_index("head")
    order = list(range(1, count_head)) + [0]
    copies = {}
    for s in order:
        goal = lax.rem(me + s, count_head)
        for f, (source, start, size, at) in enumerate(fields):
            column = pl.multiple_of(goal * width_here + start, HD)
            copies[s, f] = pltpu.make_async_copy(
                ins[source].at[:, :, pl.ds(column, size)],
                buffer.at[s, :, :, pl.ds(at, size)],
                sems.at[s, f],
            )
            copies[s, f].start()
    sign = sign_matrix()
    for s in order:
        for f, (_, _, size, start) in enumerate(fields):
            copies[s, f].wait()
            store_heads(outs[s], start, rotated(buffer[s, :, :, start : start + size], sign))


def rotate_here(fields, ins, outs, distances, count_head, sign):
    width_here = next(iter(ins.values())).shape[2] // count_head
    me = lax.axis_index("head")
    for s in distances:
        goal = lax.rem(me + s, count_head)
        for source, start, size, at in fields:
            column = pl.multiple_of(goal * width_here + start, HD)
            store_heads(outs[s], at, rotated(ins[source][:, :, pl.ds(column, size)], sign))


def rotate_pieces(arrays, message, count_head):
    blocks, tokens, _ = arrays[0].shape
    fields, total = fields_of(message)
    sources = sorted({source for source, _, _ in message})
    one = (blocks, tokens, total)
    *pieces, token = pl.pallas_call(
        functools.partial(rotate_kernel, message, sources, count_head),
        in_specs=[pl.BlockSpec(memory_space=pltpu.HBM)] * len(sources),
        out_specs=[pl.BlockSpec(memory_space=pltpu.VMEM)] * (count_head + 1),
        out_shape=[jax.ShapeDtypeStruct(one, jnp.bfloat16)] * count_head + [TOKEN],
        scratch_shapes=[
            pltpu.VMEM((count_head,) + one, jnp.bfloat16),
            pltpu.SemaphoreType.DMA((count_head, len(fields))),
        ],
        cost_estimate=NO_COST,
        compiler_params=pltpu.CompilerParams(vmem_limit_bytes=WIDE_VMEM),
    )(*[arrays[source] for source in sources])
    return pieces, token


def slots_at(distance, count_tm):
    return NEAR_CAP if distance in (1, count_tm - 1) else FAR_CAP


def pick_kernel(count_head, count_tm, lanes, picks_ref, *refs):
    pieces, outs = refs[:count_head], refs[count_head + 1 :]
    shard = lax.axis_index("tm")
    for distance, out in enumerate(outs, 1):
        goal = lax.rem(shard + distance, count_tm)
        for k in range(slots_at(distance, count_tm)):
            pick = picks_ref[NEAR_CAP * goal + k]
            for s in range(count_head):
                out[k, s] = pieces[s][pick, :, lanes[0] : lanes[1]]


def pick_blocks(picks, pieces, lanes, count_tm, after):
    count_head = len(pieces)
    one = (count_head, pieces[0].shape[1], lanes[1] - lanes[0])
    vmem = pl.BlockSpec(memory_space=pltpu.VMEM)
    return pl.pallas_call(
        functools.partial(pick_kernel, count_head, count_tm, lanes),
        in_specs=[pl.BlockSpec(memory_space=pltpu.SMEM)]
        + [vmem] * count_head
        + [pl.BlockSpec(memory_space=pl.ANY)],
        out_specs=[vmem] * (count_tm - 1),
        out_shape=[
            jax.ShapeDtypeStruct((slots_at(distance, count_tm),) + one, jnp.bfloat16)
            for distance in range(1, count_tm)
        ],
        cost_estimate=HIGH_COST,
        compiler_params=pltpu.CompilerParams(vmem_limit_bytes=VMEM),
    )(picks, *pieces, after)


def pass_kernel(*refs):
    del refs


def passed_after(array, after):
    anywhere = pl.BlockSpec(memory_space=pl.ANY)
    return pl.pallas_call(
        pass_kernel,
        in_specs=[anywhere] * 2,
        out_specs=anywhere,
        out_shape=jax.ShapeDtypeStruct(array.shape, array.dtype),
        input_output_aliases={0: 0},
        cost_estimate=NO_COST,
        compiler_params=pltpu.CompilerParams(vmem_limit_bytes=VMEM),
    )(array, after)


def remote_rows(count_tm):
    return [
        (distance, k)
        for distance in range(1, count_tm)
        for k in range(slots_at(distance, count_tm))
    ]


def split(value, by):
    if by & (by - 1) == 0:
        return value >> (by.bit_length() - 1), value & (by - 1)
    return lax.div(value, by), lax.rem(value, by)


def plan_kernel(messages, count_head, count_tm, blocks, *refs):
    *sources, pair_hbm, tokens_ref, _ = refs[:6]
    picks_ref, bias_ref, query_out = refs[6:9]
    pair_ref, named_ref, table_ref, pair_sem, table_sem = refs[-5:]
    outs = refs[9:-5]
    ins = dict(enumerate(sources))
    pair_copy = pltpu.make_async_copy(pair_hbm, pair_ref, pair_sem)
    pair_copy.start()
    sign = sign_matrix()
    places = list(range(1, count_head)) + [0]
    jobs = [
        (fields_of(message)[0], outs[m * count_head : (m + 1) * count_head], s)
        for m, message in enumerate(messages)
        for s in places
    ]
    query_fields = [(0, 0, query_out.shape[-1], 0)]
    jobs += [(query_fields, by_distance([query_out], count_head, 1), s) for s in places]
    half = len(jobs) // 2
    for fields, pieces, s in jobs[:half]:
        rotate_here(fields, ins, pieces, [s], count_head, sign)
    pair_copy.wait()
    total_blocks, columns = pair_ref.shape
    pairs = pair_ref[...]
    lane = lax.broadcasted_iota(jnp.int32, named_ref.shape, 1)
    named = jnp.zeros(named_ref.shape, jnp.int32)
    for c in range(columns):
        named = jnp.where(pairs[:, c : c + 1] == lane, 1, named)
    named_ref[...] = named
    copy = pltpu.make_async_copy(named_ref, table_ref, table_sem)
    copy.start()
    for fields, pieces, s in jobs[half:]:
        rotate_here(fields, ins, pieces, [s], count_head, sign)
    copy.wait()
    shard = lax.axis_index("tm")
    place = lax.axis_index("head")
    mine = shard * blocks

    def two_picks(wanted):
        picks = [jnp.int32(0)] * NEAR_CAP
        count = jnp.int32(0)
        for j in range(blocks):
            for k in range(NEAR_CAP):
                picks[k] = jnp.where((wanted[j] > 0) & (count == k), j, picks[k])
            count = count + wanted[j]
        return picks, count

    def named_by(rows, column):
        found = table_ref[rows, column]
        for i in range(1, blocks):
            found = found | table_ref[rows + i, column]
        return found

    for d in range(count_tm):
        picks, _ = two_picks([named_by(d * blocks, mine + j) for j in range(blocks)])
        for k in range(NEAR_CAP):
            picks_ref[NEAR_CAP * d + k] = picks[k]

    kept = [[table_ref[mine + i, mine + j] * tokens_ref[mine + j] for j in range(blocks)] for i in range(blocks)]
    arrivals = {}
    for distance, k in remote_rows(count_tm):
        first = lax.rem(shard - distance + count_tm, count_tm) * blocks
        if k == 0:
            arrivals[distance] = two_picks([named_by(mine, first + j) for j in range(blocks)])
        picks, count = arrivals[distance]
        there = first + picks[k]
        live = jnp.where(count > k, tokens_ref[there], 0)
        for i in range(blocks):
            kept[i].append(table_ref[mine + i, there] * live)

    total = bias_ref.shape[1]
    piece_rows = BLK // count_head
    at = lax.broadcasted_iota(jnp.int32, (blocks, total), 1)
    query = lax.broadcasted_iota(jnp.int32, (blocks, total), 0)
    own = at < blocks * BLK
    group, token = split(at, piece_rows)
    own_piece, own_block = split(group, blocks)
    far_row, far_group = split(group, count_head)
    row = jnp.where(own, own_block, far_row)
    piece = jnp.where(own, own_piece, far_group)
    source = jnp.where(piece > place, place - piece + count_head, place - piece)
    position = source * piece_rows + token
    limit = jnp.zeros((blocks, total), jnp.int32)
    for r in range(len(kept[0])):
        value = jnp.zeros((blocks, total), jnp.int32)
        for i in range(blocks):
            value = jnp.where(query == i, kept[i][r], value)
        limit = jnp.where(row == r, value, limit)
    bias_ref[...] = jnp.where(position < limit, 0.0, NEG)


def plan(arrays, messages, pair_list, block_tokens, after, count_head, count_tm):
    blocks, tokens, _ = arrays[0].shape
    total_blocks, columns = pair_list.shape
    lanes = -(-total_blocks // 128) * 128
    total = (blocks + len(remote_rows(count_tm))) * BLK
    vmem = pl.BlockSpec(memory_space=pltpu.VMEM)
    smem = pl.BlockSpec(memory_space=pltpu.SMEM)
    stacked = (count_head, blocks, tokens, arrays[0].shape[2] // count_head)
    shapes = [jax.ShapeDtypeStruct(stacked, jnp.bfloat16)] + [
        jax.ShapeDtypeStruct((blocks, tokens, fields_of(message)[1]), jnp.bfloat16)
        for message in messages
        for _ in range(count_head)
    ]
    picks, bias, query, *pieces = pl.pallas_call(
        functools.partial(plan_kernel, messages, count_head, count_tm, blocks),
        in_specs=[vmem] * 3
        + [pl.BlockSpec(memory_space=pl.ANY), smem, pl.BlockSpec(memory_space=pl.ANY)],
        out_specs=[smem, vmem] + [vmem] * len(shapes),
        out_shape=[
            jax.ShapeDtypeStruct((NEAR_CAP * count_tm,), jnp.int32),
            jax.ShapeDtypeStruct((blocks, total), jnp.float32),
        ]
        + shapes,
        scratch_shapes=[
            pltpu.VMEM((total_blocks, columns), jnp.int32),
            pltpu.VMEM((total_blocks, lanes), jnp.int32),
            pltpu.SMEM((total_blocks, lanes), jnp.int32),
            pltpu.SemaphoreType.DMA,
            pltpu.SemaphoreType.DMA,
        ],
        cost_estimate=NO_COST,
        compiler_params=pltpu.CompilerParams(vmem_limit_bytes=VMEM),
    )(*arrays, pair_list, block_tokens, after)
    return picks, bias, query, [pieces[at : at + count_head] for at in range(0, len(pieces), count_head)]


def attend_kernel(counts, heads_of, distances, tokens_ref, bias_ref, query_ref, *refs):
    count_head, count_tm = counts
    queries = by_distance([query_ref], count_head, -1)
    per_part = count_head + count_tm - 1
    parts = [refs[p * per_part : (p + 1) * per_part] for p in range(len(heads_of))]
    outs = refs[len(heads_of) * per_part :][-len(distances) :]
    blocks, tokens, _ = outs[0].shape
    rows = len(distances) * tokens
    shard = lax.axis_index("tm")
    me = lax.axis_index("head")
    bias = bias_ref[...][:, None, :]
    place_of = [(p, h) for p, (_, size) in enumerate(heads_of) for h in range(size // HD)]

    def gathered(kind, head):
        p, h = place_of[head]
        first = kind * heads_of[p][1] + h * HD
        lanes = slice(first, first + HD)
        pieces = [rows_of(own[:, :, lanes]) for own in parts[p][:count_head]]
        pieces += [
            rows_of(parts[p][count_head + distance - 1][k, :, :, lanes])
            for distance, k in remote_rows(count_tm)
        ]
        return jnp.concatenate(pieces, axis=0)

    def products(head):
        first = heads_of[0][0] + head * HD
        lanes = slice(first, first + HD)
        query = jnp.concatenate(
            [rows_of(queries[s][i, :, lanes]) for i in range(blocks) for s in distances], axis=0
        )
        return lax.dot_general(
            query, gathered(0, head), (((1,), (1,)), ((), ())), preferred_element_type=jnp.float32
        )

    heads = len(place_of)
    dots, mixed = products(0), []
    for h in range(heads):
        ahead = products(h + 1) if h + 1 < heads else None
        dots = dots.reshape(blocks, rows, -1) + bias
        peak = jnp.max(dots, axis=-1, keepdims=True)
        weights = jnp.exp2((dots - peak) * (SCORE_SCALE * LOG2E))
        inverse = 1.0 / jnp.sum(weights, axis=-1, keepdims=True)
        weights_half = weights.astype(jnp.bfloat16).reshape(blocks * rows, -1)
        part = jnp.dot(weights_half, gathered(1, h), preferred_element_type=jnp.float32)
        mixed.append(part * inverse.reshape(blocks * rows, 1))
        dots = ahead
    mixed = jnp.concatenate(mixed, axis=0)
    sign = sign_matrix()
    high = mixed.astype(jnp.bfloat16)
    low = (mixed - high.astype(jnp.float32)).astype(jnp.bfloat16)
    turned = jnp.dot(high, sign, preferred_element_type=jnp.float32)
    turned = turned + jnp.dot(low, sign, preferred_element_type=jnp.float32)
    turned = (turned * ROTATE_SCALE).reshape(heads, blocks, len(distances), tokens, HD)
    token = lax.broadcasted_iota(jnp.int32, (tokens, HD), 0)
    for at, s in enumerate(distances):
        position = lax.rem(me - s + count_head, count_head) * tokens + token
        for i in range(blocks):
            live = position < tokens_ref[shard * blocks + i]
            for h in range(heads):
                outs[at][i, :, h * HD : (h + 1) * HD] = jnp.where(
                    live, turned[h, i, at], 0.0
                ).astype(jnp.bfloat16)


def attend(block_tokens, bias, query, parts, heads_of, distances, after=(), cost=NO_COST):
    count_head, count_tm = query.shape[0], len(parts[0][1]) + 1
    operands = [ref for owns, slots in parts for ref in owns + slots]
    shape = query.shape[1:3] + (sum(size for _, size in heads_of),)
    vmem = pl.BlockSpec(memory_space=pltpu.VMEM)
    return pl.pallas_call(
        functools.partial(attend_kernel, (count_head, count_tm), heads_of, distances),
        in_specs=[pl.BlockSpec(memory_space=pltpu.SMEM)]
        + [vmem] * (2 + len(operands))
        + [pl.BlockSpec(memory_space=pl.ANY)] * len(after),
        out_specs=[vmem] * len(distances),
        out_shape=[jax.ShapeDtypeStruct(shape, jnp.bfloat16)] * len(distances),
        cost_estimate=cost,
        compiler_params=pltpu.CompilerParams(vmem_limit_bytes=VMEM),
    )(block_tokens, bias, query, *operands, *after)


def place_kernel(places, width_here, *refs):
    pieces, out_ref, sems = refs[:-2], refs[-2], refs[-1]
    me, count = lax.axis_index("head"), lax.axis_size("head")
    copies = []
    for at, (piece, (s, start)) in enumerate(zip(pieces, places)):
        column = pl.multiple_of(lax.rem(me + s, count) * width_here + start, HD)
        copies.append(
            pltpu.make_async_copy(
                piece, out_ref.at[:, :, pl.ds(column, piece.shape[-1])], sems.at[at]
            )
        )
        copies[-1].start()
    for copy in copies:
        copy.wait()


def place_pieces(pieces, places, width_here):
    blocks, tokens, _ = pieces[0].shape
    width = width_here * lax.axis_size("head")
    return pl.pallas_call(
        functools.partial(place_kernel, places, width_here),
        in_specs=[pl.BlockSpec(memory_space=pl.ANY)] * len(pieces),
        out_specs=pl.BlockSpec(memory_space=pltpu.HBM),
        out_shape=jax.ShapeDtypeStruct((blocks, tokens, width), jnp.bfloat16),
        scratch_shapes=[pltpu.SemaphoreType.DMA((len(pieces),))],
        compiler_params=pltpu.CompilerParams(vmem_limit_bytes=VMEM),
    )(*pieces)


def shifted(array, axis, distance):
    count = lax.axis_size(axis)
    return lax.ppermute(array, axis, [(i, (i + distance) % count) for i in range(count)])


def exchange(pieces, direction):
    return [shifted(piece, "head", direction * s) for s, piece in enumerate(pieces, 1)]


def forward(sent):
    return [shifted(block, "tm", distance) for distance, block in enumerate(sent, 1)]


def shards(query_rows, key_rows, value_rows, pair_list, block_tokens):
    count_head = lax.axis_size("head")
    count_tm = lax.axis_size("tm")
    blocks, tokens, width = query_rows.shape
    width_here = width // count_head
    heads = width_here // HD
    cut = (heads + 1) // 2 * HD
    parts = [(0, cut), (cut, width_here - cut)] if heads > 1 else [(0, width_here)]
    arrays = [query_rows, key_rows, value_rows]
    messages = [[(1,) + part, (2,) + part] for part in parts]
    pieces, token = rotate_pieces(arrays, messages[0], count_head)
    picks, bias, query, later = plan(
        arrays, messages[1:], pair_list, block_tokens, token, count_head, count_tm
    )
    received = [piece[:1] + exchange(piece[1:], 1) for piece in [pieces] + later]
    sent, after = [], bias
    for owns, (_, size) in zip(received, parts):
        sent.append(pick_blocks(picks, owns, (0, 2 * size), count_tm, after))
        after = sent[-1][0]
    query = passed_after(query, sent[0][0])
    query = lax.all_to_all(query, "head", split_axis=0, concat_axis=0, tiled=True)
    inputs = [(owns, forward(picked)) for owns, picked in zip(received, sent)]
    distances, after = list(range(1, count_head)), ()
    pieces, places = [], []
    for at, part in enumerate(parts):
        cost = NO_COST if at == len(parts) - 1 else HIGH_COST
        leaving = attend(
            block_tokens, bias, query, [inputs[at]], [part], distances, after, cost
        )
        after = (leaving[0],)
        pieces += exchange(leaving, -1)
        places += [(s, part[0]) for s in distances]
    pieces += attend(block_tokens, bias, query, inputs, parts, [0], after)
    return place_pieces(pieces, places + [(0, 0)], width_here)


def solution(mesh):
    placed = (
        P(("grp", "tm"), "head", None),
        P(("grp", "tm"), "head", None),
        P(("grp", "tm"), "head", None),
        P("grp", None),
        P("grp"),
    )
    return jax.shard_map(
        shards,
        mesh=mesh,
        in_specs=placed,
        out_specs=P(("grp", "tm"), "head", None),
        check_vma=False,
    )
```

```python
import functools
import math

import jax
import jax.numpy as jnp
from jax import lax
from jax.experimental import pallas as pl
from jax.experimental.pallas import tpu as pltpu
from jax.sharding import PartitionSpec as P

HD = 128
BLK = 64
NEAR_CAP = 2
FAR_CAP = 1
NEG = -1e30
ROTATE_SCALE = 1.0 / math.sqrt(HD)
SCORE_SCALE = 1.0 / math.sqrt(HD)
VMEM = 24 * 1024 * 1024
WIDE_VMEM = 60 * 1024 * 1024
TOKEN = jax.ShapeDtypeStruct((8, 128), jnp.float32)
NO_COST = pl.CostEstimate(flops=0, bytes_accessed=0, transcendentals=0)
HIGH_COST = pl.CostEstimate(flops=10**11, bytes_accessed=0, transcendentals=0)
LOG2E = math.log2(math.e)


def sign_matrix():
    common = lax.broadcasted_iota(jnp.int32, (HD, HD), 0) & lax.broadcasted_iota(
        jnp.int32, (HD, HD), 1
    )
    bits = HD.bit_length() - 1
    parity = common
    for bit in range(1, bits):
        parity = parity ^ (common >> bit)
    return jnp.where((parity & 1) == 0, 1.0, -1.0).astype(jnp.bfloat16)


def rows_of(block):
    rows, width = math.prod(block.shape[:-1]), block.shape[-1]
    if block.shape[-2] % 16 == 0:
        return block.reshape(rows, width)
    return block.astype(jnp.float32).reshape(rows, width).astype(block.dtype)


def fields_of(message):
    at, fields = 0, []
    for source, start, size in message:
        fields.append((source, start, size, at))
        at += size
    return fields, at


def by_distance(refs, count, direction):
    if len(refs[0].shape) == 3:
        return list(refs)
    me = lax.axis_index("head")
    return [refs[0].at[lax.rem(me + direction * s + count, count)] for s in range(count)]


def rotated(block, sign):
    blocks, tokens, size = block.shape
    flat = rows_of(block)
    heads = [flat[:, at : at + HD] for at in range(0, size, HD)]
    turned = jnp.dot(jnp.concatenate(heads, axis=0), sign, preferred_element_type=jnp.float32)
    return (turned * ROTATE_SCALE).reshape(size // HD, blocks, tokens, HD).astype(jnp.bfloat16)


def store_heads(out, start, turned):
    for h in range(turned.shape[0]):
        at = start + h * HD
        out[:, :, at : at + HD] = turned[h]


def rotate_kernel(message, sources, count_head, *refs):
    fields, total = fields_of(message)
    ins = dict(zip(sources, refs))
    outs, (token, buffer, sems) = refs[len(sources) : -3], refs[-3:]
    token[...] = jnp.zeros_like(token)
    width_here = refs[0].shape[2] // count_head
    me = lax.axis_index("head")
    order = list(range(1, count_head)) + [0]
    copies = {}
    for s in order:
        goal = lax.rem(me + s, count_head)
        for f, (source, start, size, at) in enumerate(fields):
            column = pl.multiple_of(goal * width_here + start, HD)
            copies[s, f] = pltpu.make_async_copy(
                ins[source].at[:, :, pl.ds(column, size)],
                buffer.at[s, :, :, pl.ds(at, size)],
                sems.at[s, f],
            )
            copies[s, f].start()
    sign = sign_matrix()
    for s in order:
        for f, (_, _, size, start) in enumerate(fields):
            copies[s, f].wait()
            store_heads(outs[s], start, rotated(buffer[s, :, :, start : start + size], sign))


def rotate_here(fields, ins, outs, distances, count_head, sign):
    width_here = next(iter(ins.values())).shape[2] // count_head
    me = lax.axis_index("head")
    for s in distances:
        goal = lax.rem(me + s, count_head)
        for source, start, size, at in fields:
            column = pl.multiple_of(goal * width_here + start, HD)
            store_heads(outs[s], at, rotated(ins[source][:, :, pl.ds(column, size)], sign))


def rotate_pieces(arrays, message, count_head):
    blocks, tokens, _ = arrays[0].shape
    fields, total = fields_of(message)
    sources = sorted({source for source, _, _ in message})
    one = (blocks, tokens, total)
    *pieces, token = pl.pallas_call(
        functools.partial(rotate_kernel, message, sources, count_head),
        in_specs=[pl.BlockSpec(memory_space=pltpu.HBM)] * len(sources),
        out_specs=[pl.BlockSpec(memory_space=pltpu.VMEM)] * (count_head + 1),
        out_shape=[jax.ShapeDtypeStruct(one, jnp.bfloat16)] * count_head + [TOKEN],
        scratch_shapes=[
            pltpu.VMEM((count_head,) + one, jnp.bfloat16),
            pltpu.SemaphoreType.DMA((count_head, len(fields))),
        ],
        cost_estimate=NO_COST,
        compiler_params=pltpu.CompilerParams(vmem_limit_bytes=WIDE_VMEM),
    )(*[arrays[source] for source in sources])
    return pieces, token


def slots_at(distance, count_tm):
    return NEAR_CAP if distance in (1, count_tm - 1) else FAR_CAP


def pick_kernel(count_head, count_tm, lanes, picks_ref, *refs):
    pieces, outs = refs[:count_head], refs[count_head + 1 : count_head + count_tm]
    shard = lax.axis_index("tm")
    for distance, out in enumerate(outs, 1):
        goal = lax.rem(shard + distance, count_tm)
        for k in range(slots_at(distance, count_tm)):
            pick = picks_ref[NEAR_CAP * goal + k]
            for s in range(count_head):
                out[k, s] = pieces[s][pick, :, lanes[0] : lanes[1]]


def pick_blocks(picks, pieces, lanes, count_tm, held, passes):
    count_head = len(pieces)
    one = (count_head, pieces[0].shape[1], lanes[1] - lanes[0])
    vmem, anywhere = pl.BlockSpec(memory_space=pltpu.VMEM), pl.BlockSpec(memory_space=pl.ANY)
    shapes = [
        jax.ShapeDtypeStruct((slots_at(distance, count_tm),) + one, jnp.bfloat16)
        for distance in range(1, count_tm)
    ]
    passed = [jax.ShapeDtypeStruct(held.shape, held.dtype)] if passes else []
    return pl.pallas_call(
        functools.partial(pick_kernel, count_head, count_tm, lanes),
        in_specs=[pl.BlockSpec(memory_space=pltpu.SMEM)] + [vmem] * count_head + [anywhere],
        out_specs=[vmem] * len(shapes) + [anywhere] * len(passed),
        out_shape=shapes + passed,
        input_output_aliases={1 + count_head: len(shapes)} if passes else {},
        cost_estimate=HIGH_COST,
        compiler_params=pltpu.CompilerParams(vmem_limit_bytes=VMEM),
    )(picks, *pieces, held)


def remote_rows(count_tm):
    return [
        (distance, k)
        for distance in range(1, count_tm)
        for k in range(slots_at(distance, count_tm))
    ]


def split(value, by):
    if by & (by - 1) == 0:
        return value >> (by.bit_length() - 1), value & (by - 1)
    return lax.div(value, by), lax.rem(value, by)


def plan_kernel(messages, count_head, count_tm, blocks, *refs):
    *sources, pair_hbm, tokens_ref, _ = refs[:6]
    picks_ref, bias_ref, query_out = refs[6:9]
    pair_ref, named_ref, table_ref, pair_sem, table_sem = refs[-5:]
    outs = refs[9:-5]
    ins = dict(enumerate(sources))
    pair_copy = pltpu.make_async_copy(pair_hbm, pair_ref, pair_sem)
    pair_copy.start()
    sign = sign_matrix()
    places = list(range(1, count_head)) + [0]
    jobs = [
        (fields_of(message)[0], outs[m * count_head : (m + 1) * count_head], s)
        for m, message in enumerate(messages)
        for s in places
    ]
    query_fields = [(0, 0, query_out.shape[-1], 0)]
    jobs += [(query_fields, by_distance([query_out], count_head, 1), s) for s in places]
    half = len(jobs) // 2
    for fields, pieces, s in jobs[:half]:
        rotate_here(fields, ins, pieces, [s], count_head, sign)
    pair_copy.wait()
    total_blocks, columns = pair_ref.shape
    pairs = pair_ref[...]
    lane = lax.broadcasted_iota(jnp.int32, named_ref.shape, 1)
    named = jnp.zeros(named_ref.shape, jnp.int32)
    for c in range(columns):
        named = jnp.where(pairs[:, c : c + 1] == lane, 1, named)
    named_ref[...] = named
    copy = pltpu.make_async_copy(named_ref, table_ref, table_sem)
    copy.start()
    for fields, pieces, s in jobs[half:]:
        rotate_here(fields, ins, pieces, [s], count_head, sign)
    copy.wait()
    shard = lax.axis_index("tm")
    place = lax.axis_index("head")
    mine = shard * blocks

    def two_picks(wanted):
        picks = [jnp.int32(0)] * NEAR_CAP
        count = jnp.int32(0)
        for j in range(blocks):
            for k in range(NEAR_CAP):
                picks[k] = jnp.where((wanted[j] > 0) & (count == k), j, picks[k])
            count = count + wanted[j]
        return picks, count

    def named_by(rows, column):
        found = table_ref[rows, column]
        for i in range(1, blocks):
            found = found | table_ref[rows + i, column]
        return found

    for d in range(count_tm):
        picks, _ = two_picks([named_by(d * blocks, mine + j) for j in range(blocks)])
        for k in range(NEAR_CAP):
            picks_ref[NEAR_CAP * d + k] = picks[k]

    kept = [[table_ref[mine + i, mine + j] * tokens_ref[mine + j] for j in range(blocks)] for i in range(blocks)]
    arrivals = {}
    for distance, k in remote_rows(count_tm):
        first = lax.rem(shard - distance + count_tm, count_tm) * blocks
        if k == 0:
            arrivals[distance] = two_picks([named_by(mine, first + j) for j in range(blocks)])
        picks, count = arrivals[distance]
        there = first + picks[k]
        live = jnp.where(count > k, tokens_ref[there], 0)
        for i in range(blocks):
            kept[i].append(table_ref[mine + i, there] * live)

    total = bias_ref.shape[1]
    piece_rows = BLK // count_head
    at = lax.broadcasted_iota(jnp.int32, (blocks, total), 1)
    query = lax.broadcasted_iota(jnp.int32, (blocks, total), 0)
    own = at < blocks * BLK
    group, token = split(at, piece_rows)
    own_piece, own_block = split(group, blocks)
    far_row, far_group = split(group, count_head)
    row = jnp.where(own, own_block, far_row)
    piece = jnp.where(own, own_piece, far_group)
    source = jnp.where(piece > place, place - piece + count_head, place - piece)
    position = source * piece_rows + token
    limit = jnp.zeros((blocks, total), jnp.int32)
    for r in range(len(kept[0])):
        value = jnp.zeros((blocks, total), jnp.int32)
        for i in range(blocks):
            value = jnp.where(query == i, kept[i][r], value)
        limit = jnp.where(row == r, value, limit)
    bias_ref[...] = jnp.where(position < limit, 0.0, NEG)


def plan(arrays, messages, pair_list, block_tokens, after, count_head, count_tm):
    blocks, tokens, _ = arrays[0].shape
    total_blocks, columns = pair_list.shape
    lanes = -(-total_blocks // 128) * 128
    total = (blocks + len(remote_rows(count_tm))) * BLK
    vmem = pl.BlockSpec(memory_space=pltpu.VMEM)
    smem = pl.BlockSpec(memory_space=pltpu.SMEM)
    stacked = (count_head, blocks, tokens, arrays[0].shape[2] // count_head)
    shapes = [jax.ShapeDtypeStruct(stacked, jnp.bfloat16)] + [
        jax.ShapeDtypeStruct((blocks, tokens, fields_of(message)[1]), jnp.bfloat16)
        for message in messages
        for _ in range(count_head)
    ]
    picks, bias, query, *pieces = pl.pallas_call(
        functools.partial(plan_kernel, messages, count_head, count_tm, blocks),
        in_specs=[vmem] * 3
        + [pl.BlockSpec(memory_space=pl.ANY), smem, pl.BlockSpec(memory_space=pl.ANY)],
        out_specs=[smem, vmem] + [vmem] * len(shapes),
        out_shape=[
            jax.ShapeDtypeStruct((NEAR_CAP * count_tm,), jnp.int32),
            jax.ShapeDtypeStruct((blocks, total), jnp.float32),
        ]
        + shapes,
        scratch_shapes=[
            pltpu.VMEM((total_blocks, columns), jnp.int32),
            pltpu.VMEM((total_blocks, lanes), jnp.int32),
            pltpu.SMEM((total_blocks, lanes), jnp.int32),
            pltpu.SemaphoreType.DMA,
            pltpu.SemaphoreType.DMA,
        ],
        cost_estimate=NO_COST,
        compiler_params=pltpu.CompilerParams(vmem_limit_bytes=VMEM),
    )(*arrays, pair_list, block_tokens, after)
    return picks, bias, query, [pieces[at : at + count_head] for at in range(0, len(pieces), count_head)]


def attend_kernel(counts, heads_of, distances, tokens_ref, bias_ref, query_ref, *refs):
    count_head, count_tm = counts
    queries = by_distance([query_ref], count_head, -1)
    per_part = count_head + count_tm - 1
    parts = [refs[p * per_part : (p + 1) * per_part] for p in range(len(heads_of))]
    outs = refs[len(heads_of) * per_part :][-len(distances) :]
    blocks, tokens, _ = outs[0].shape
    rows = len(distances) * tokens
    shard = lax.axis_index("tm")
    me = lax.axis_index("head")
    bias = bias_ref[...][:, None, :]
    place_of = [(p, h) for p, (_, size) in enumerate(heads_of) for h in range(size // HD)]

    def gathered(kind, head):
        p, h = place_of[head]
        first = kind * heads_of[p][1] + h * HD
        lanes = slice(first, first + HD)
        pieces = [rows_of(own[:, :, lanes]) for own in parts[p][:count_head]]
        pieces += [
            rows_of(parts[p][count_head + distance - 1][k, :, :, lanes])
            for distance, k in remote_rows(count_tm)
        ]
        return jnp.concatenate(pieces, axis=0)

    def products(head):
        first = heads_of[0][0] + head * HD
        lanes = slice(first, first + HD)
        query = jnp.concatenate(
            [rows_of(queries[s][i, :, lanes]) for i in range(blocks) for s in distances], axis=0
        )
        return lax.dot_general(
            query, gathered(0, head), (((1,), (1,)), ((), ())), preferred_element_type=jnp.float32
        )

    heads = len(place_of)
    dots, mixed = products(0), []
    for h in range(heads):
        ahead = products(h + 1) if h + 1 < heads else None
        dots = dots.reshape(blocks, rows, -1) + bias
        peak = jnp.max(dots, axis=-1, keepdims=True)
        weights = jnp.exp2((dots - peak) * (SCORE_SCALE * LOG2E))
        inverse = 1.0 / jnp.sum(weights, axis=-1, keepdims=True)
        weights_half = weights.astype(jnp.bfloat16).reshape(blocks * rows, -1)
        part = jnp.dot(weights_half, gathered(1, h), preferred_element_type=jnp.float32)
        mixed.append(part * inverse.reshape(blocks * rows, 1))
        dots = ahead
    mixed = jnp.concatenate(mixed, axis=0)
    sign = sign_matrix()
    high = mixed.astype(jnp.bfloat16)
    low = (mixed - high.astype(jnp.float32)).astype(jnp.bfloat16)
    turned = jnp.dot(high, sign, preferred_element_type=jnp.float32)
    turned = turned + jnp.dot(low, sign, preferred_element_type=jnp.float32)
    turned = (turned * ROTATE_SCALE).reshape(heads, blocks, len(distances), tokens, HD)
    token = lax.broadcasted_iota(jnp.int32, (tokens, HD), 0)
    for at, s in enumerate(distances):
        position = lax.rem(me - s + count_head, count_head) * tokens + token
        for i in range(blocks):
            live = position < tokens_ref[shard * blocks + i]
            for h in range(heads):
                outs[at][i, :, h * HD : (h + 1) * HD] = jnp.where(
                    live, turned[h, i, at], 0.0
                ).astype(jnp.bfloat16)


def attend(block_tokens, bias, query, parts, heads_of, distances, after=(), cost=NO_COST):
    count_head, count_tm = query.shape[0], len(parts[0][1]) + 1
    operands = [ref for owns, slots in parts for ref in owns + slots]
    shape = query.shape[1:3] + (sum(size for _, size in heads_of),)
    vmem = pl.BlockSpec(memory_space=pltpu.VMEM)
    return pl.pallas_call(
        functools.partial(attend_kernel, (count_head, count_tm), heads_of, distances),
        in_specs=[pl.BlockSpec(memory_space=pltpu.SMEM)]
        + [vmem] * (2 + len(operands))
        + [pl.BlockSpec(memory_space=pl.ANY)] * len(after),
        out_specs=[vmem] * len(distances),
        out_shape=[jax.ShapeDtypeStruct(shape, jnp.bfloat16)] * len(distances),
        cost_estimate=cost,
        compiler_params=pltpu.CompilerParams(vmem_limit_bytes=VMEM),
    )(block_tokens, bias, query, *operands, *after)


def place_kernel(places, width_here, *refs):
    pieces, out_ref, sems = refs[:-2], refs[-2], refs[-1]
    me, count = lax.axis_index("head"), lax.axis_size("head")
    copies = []
    for at, (piece, (s, start)) in enumerate(zip(pieces, places)):
        column = pl.multiple_of(lax.rem(me + s, count) * width_here + start, HD)
        copies.append(
            pltpu.make_async_copy(
                piece, out_ref.at[:, :, pl.ds(column, piece.shape[-1])], sems.at[at]
            )
        )
        copies[-1].start()
    for copy in copies:
        copy.wait()


def place_pieces(pieces, places, width_here):
    blocks, tokens, _ = pieces[0].shape
    width = width_here * lax.axis_size("head")
    return pl.pallas_call(
        functools.partial(place_kernel, places, width_here),
        in_specs=[pl.BlockSpec(memory_space=pl.ANY)] * len(pieces),
        out_specs=pl.BlockSpec(memory_space=pltpu.HBM),
        out_shape=jax.ShapeDtypeStruct((blocks, tokens, width), jnp.bfloat16),
        scratch_shapes=[pltpu.SemaphoreType.DMA((len(pieces),))],
        compiler_params=pltpu.CompilerParams(vmem_limit_bytes=VMEM),
    )(*pieces)


def shifted(array, axis, distance):
    count = lax.axis_size(axis)
    return lax.ppermute(array, axis, [(i, (i + distance) % count) for i in range(count)])


def exchange(pieces, direction):
    return [shifted(piece, "head", direction * s) for s, piece in enumerate(pieces, 1)]


def forward(sent):
    return [shifted(block, "tm", distance) for distance, block in enumerate(sent, 1)]


def shards(query_rows, key_rows, value_rows, pair_list, block_tokens):
    count_head = lax.axis_size("head")
    count_tm = lax.axis_size("tm")
    blocks, tokens, width = query_rows.shape
    width_here = width // count_head
    heads = width_here // HD
    cut = (heads + 1) // 2 * HD
    parts = [(0, cut), (cut, width_here - cut)] if heads > 1 else [(0, width_here)]
    arrays = [query_rows, key_rows, value_rows]
    messages = [[(1,) + part, (2,) + part] for part in parts]
    pieces, token = rotate_pieces(arrays, messages[0], count_head)
    picks, bias, query, later = plan(
        arrays, messages[1:], pair_list, block_tokens, token, count_head, count_tm
    )
    received = [piece[:1] + exchange(piece[1:], 1) for piece in [pieces] + later]
    sent = []
    for owns, (_, size) in zip(received, parts):
        held = sent[-1][0] if sent else query
        picked = pick_blocks(picks, owns, (0, 2 * size), count_tm, held, not sent)
        if not sent:
            *picked, query = picked
        sent.append(list(picked))
    inputs = [(owns, forward(picked)) for owns, picked in zip(received, sent)]
    query = lax.all_to_all(query, "head", split_axis=0, concat_axis=0, tiled=True)
    distances, after = list(range(1, count_head)), ()
    pieces, places = [], []
    for at, part in enumerate(parts):
        cost = NO_COST if at == len(parts) - 1 else HIGH_COST
        leaving = attend(
            block_tokens, bias, query, [inputs[at]], [part], distances, after, cost
        )
        after = (leaving[0],)
        pieces += exchange(leaving, -1)
        places += [(s, part[0]) for s in distances]
    pieces += attend(block_tokens, bias, query, inputs, parts, [0], after)
    return place_pieces(pieces, places + [(0, 0)], width_here)


def solution(mesh):
    placed = (
        P(("grp", "tm"), "head", None),
        P(("grp", "tm"), "head", None),
        P(("grp", "tm"), "head", None),
        P("grp", None),
        P("grp"),
    )
    return jax.shard_map(
        shards,
        mesh=mesh,
        in_specs=placed,
        out_specs=P(("grp", "tm"), "head", None),
        check_vma=False,
    )
```

```python
import functools
import math

import jax
import jax.numpy as jnp
from jax import lax
from jax.experimental import pallas as pl
from jax.experimental.pallas import tpu as pltpu
from jax.sharding import PartitionSpec as P

HD = 128
BLK = 64
NEAR_CAP = 2
FAR_CAP = 1
NEG = -1e30
ROTATE_SCALE = 1.0 / math.sqrt(HD)
SCORE_SCALE = 1.0 / math.sqrt(HD)
VMEM = 24 * 1024 * 1024
WIDE_VMEM = 60 * 1024 * 1024
TOKEN = jax.ShapeDtypeStruct((8, 128), jnp.float32)
NO_COST = pl.CostEstimate(flops=0, bytes_accessed=0, transcendentals=0)
HIGH_COST = pl.CostEstimate(flops=10**11, bytes_accessed=0, transcendentals=0)
LOG2E = math.log2(math.e)


def sign_matrix():
    common = lax.broadcasted_iota(jnp.int32, (HD, HD), 0) & lax.broadcasted_iota(
        jnp.int32, (HD, HD), 1
    )
    bits = HD.bit_length() - 1
    parity = common
    for bit in range(1, bits):
        parity = parity ^ (common >> bit)
    return jnp.where((parity & 1) == 0, 1.0, -1.0).astype(jnp.bfloat16)


def rows_of(block):
    rows, width = math.prod(block.shape[:-1]), block.shape[-1]
    if block.shape[-2] % 16 == 0:
        return block.reshape(rows, width)
    return block.astype(jnp.float32).reshape(rows, width).astype(block.dtype)


def fields_of(message):
    at, fields = 0, []
    for source, start, size in message:
        fields.append((source, start, size, at))
        at += size
    return fields, at


def by_distance(refs, count, direction):
    if len(refs[0].shape) == 3:
        return list(refs)
    me = lax.axis_index("head")
    return [refs[0].at[lax.rem(me + direction * s + count, count)] for s in range(count)]


def rotated(block, sign):
    blocks, tokens, size = block.shape
    flat = rows_of(block)
    heads = [flat[:, at : at + HD] for at in range(0, size, HD)]
    turned = jnp.dot(jnp.concatenate(heads, axis=0), sign, preferred_element_type=jnp.float32)
    return (turned * ROTATE_SCALE).reshape(size // HD, blocks, tokens, HD).astype(jnp.bfloat16)


def store_heads(out, start, turned):
    for h in range(turned.shape[0]):
        at = start + h * HD
        out[:, :, at : at + HD] = turned[h]


def rotate_kernel(message, sources, count_head, *refs):
    fields, total = fields_of(message)
    ins = dict(zip(sources, refs))
    outs, (token, buffer, sems) = refs[len(sources) : -3], refs[-3:]
    token[...] = jnp.zeros_like(token)
    width_here = refs[0].shape[2] // count_head
    me = lax.axis_index("head")
    order = list(range(1, count_head)) + [0]
    copies = {}
    for s in order:
        goal = lax.rem(me + s, count_head)
        for f, (source, start, size, at) in enumerate(fields):
            column = pl.multiple_of(goal * width_here + start, HD)
            copies[s, f] = pltpu.make_async_copy(
                ins[source].at[:, :, pl.ds(column, size)],
                buffer.at[s, :, :, pl.ds(at, size)],
                sems.at[s, f],
            )
            copies[s, f].start()
    sign = sign_matrix()
    for s in order:
        for f, (_, _, size, start) in enumerate(fields):
            copies[s, f].wait()
            store_heads(outs[s], start, rotated(buffer[s, :, :, start : start + size], sign))


def rotate_here(fields, ins, outs, distances, count_head, sign):
    width_here = next(iter(ins.values())).shape[2] // count_head
    me = lax.axis_index("head")
    for s in distances:
        goal = lax.rem(me + s, count_head)
        for source, start, size, at in fields:
            column = pl.multiple_of(goal * width_here + start, HD)
            store_heads(outs[s], at, rotated(ins[source][:, :, pl.ds(column, size)], sign))


def rotate_pieces(arrays, message, count_head):
    blocks, tokens, _ = arrays[0].shape
    fields, total = fields_of(message)
    sources = sorted({source for source, _, _ in message})
    one = (blocks, tokens, total)
    *pieces, token = pl.pallas_call(
        functools.partial(rotate_kernel, message, sources, count_head),
        in_specs=[pl.BlockSpec(memory_space=pltpu.HBM)] * len(sources),
        out_specs=[pl.BlockSpec(memory_space=pltpu.VMEM)] * (count_head + 1),
        out_shape=[jax.ShapeDtypeStruct(one, jnp.bfloat16)] * count_head + [TOKEN],
        scratch_shapes=[
            pltpu.VMEM((count_head,) + one, jnp.bfloat16),
            pltpu.SemaphoreType.DMA((count_head, len(fields))),
        ],
        cost_estimate=NO_COST,
        compiler_params=pltpu.CompilerParams(vmem_limit_bytes=WIDE_VMEM),
    )(*[arrays[source] for source in sources])
    return pieces, token


def routes(count_tm):
    ids = range(count_tm)
    found = [
        (NEAR_CAP, [(i, i + 1) for i in ids[:-1]]),
        (NEAR_CAP, [(i + 1, i) for i in ids[:-1]]),
    ]
    if count_tm > 2:
        found.append((FAR_CAP, [(0, count_tm - 1), (count_tm - 1, 0)]))
    for distance in range(2, count_tm - 1):
        found.append((FAR_CAP, [(i, (i + distance) % count_tm) for i in ids]))
    return found


def partners(count_tm, shard):
    last = count_tm - 1
    upward, downward = jnp.minimum(shard + 1, last), jnp.maximum(shard - 1, 0)
    found = [(upward, downward, shard > 0), (downward, upward, shard < last)]
    if count_tm > 2:
        other = jnp.where(shard == 0, last, 0)
        found.append((other, other, (shard == 0) | (shard == last)))
    for distance in range(2, last):
        goal = lax.rem(shard + distance, count_tm)
        found.append((goal, lax.rem(shard - distance + count_tm, count_tm), shard >= 0))
    return found


def pick_kernel(count_head, count_tm, lanes, picks_ref, *refs):
    pieces, outs = refs[:count_head], refs[count_head + 1 :]
    goals = partners(count_tm, lax.axis_index("tm"))
    for out, (goal, _, _), (slots, _) in zip(outs, goals, routes(count_tm)):
        for k in range(slots):
            pick = picks_ref[NEAR_CAP * goal + k]
            for s in range(count_head):
                out[k, s] = pieces[s][pick, :, lanes[0] : lanes[1]]


def pick_blocks(picks, pieces, lanes, count_tm, held, passes):
    count_head = len(pieces)
    one = (count_head, pieces[0].shape[1], lanes[1] - lanes[0])
    vmem, anywhere = pl.BlockSpec(memory_space=pltpu.VMEM), pl.BlockSpec(memory_space=pl.ANY)
    shapes = [
        jax.ShapeDtypeStruct((slots,) + one, jnp.bfloat16) for slots, _ in routes(count_tm)
    ]
    passed = [jax.ShapeDtypeStruct(held.shape, held.dtype)] if passes else []
    return pl.pallas_call(
        functools.partial(pick_kernel, count_head, count_tm, lanes),
        in_specs=[pl.BlockSpec(memory_space=pltpu.SMEM)] + [vmem] * count_head + [anywhere],
        out_specs=[vmem] * len(shapes) + [anywhere] * len(passed),
        out_shape=shapes + passed,
        input_output_aliases={1 + count_head: len(shapes)} if passes else {},
        cost_estimate=HIGH_COST,
        compiler_params=pltpu.CompilerParams(vmem_limit_bytes=VMEM),
    )(picks, *pieces, held)


def remote_rows(count_tm):
    return [(at, k) for at, (slots, _) in enumerate(routes(count_tm)) for k in range(slots)]


def split(value, by):
    if by & (by - 1) == 0:
        return value >> (by.bit_length() - 1), value & (by - 1)
    return lax.div(value, by), lax.rem(value, by)


def plan_kernel(messages, count_head, count_tm, blocks, *refs):
    *sources, pair_hbm, tokens_ref, _ = refs[:6]
    picks_ref, bias_ref, query_out = refs[6:9]
    pair_ref, named_ref, table_ref, pair_sem, table_sem = refs[-5:]
    outs = refs[9:-5]
    ins = dict(enumerate(sources))
    pair_copy = pltpu.make_async_copy(pair_hbm, pair_ref, pair_sem)
    pair_copy.start()
    sign = sign_matrix()
    places = list(range(1, count_head)) + [0]
    jobs = [
        (fields_of(message)[0], outs[m * count_head : (m + 1) * count_head], s)
        for m, message in enumerate(messages)
        for s in places
    ]
    query_fields = [(0, 0, query_out.shape[-1], 0)]
    jobs += [(query_fields, by_distance([query_out], count_head, 1), s) for s in places]
    half = len(jobs) // 2
    for fields, pieces, s in jobs[:half]:
        rotate_here(fields, ins, pieces, [s], count_head, sign)
    pair_copy.wait()
    total_blocks, columns = pair_ref.shape
    pairs = pair_ref[...]
    lane = lax.broadcasted_iota(jnp.int32, named_ref.shape, 1)
    named = jnp.zeros(named_ref.shape, jnp.int32)
    for c in range(columns):
        named = jnp.where(pairs[:, c : c + 1] == lane, 1, named)
    named_ref[...] = named
    copy = pltpu.make_async_copy(named_ref, table_ref, table_sem)
    copy.start()
    for fields, pieces, s in jobs[half:]:
        rotate_here(fields, ins, pieces, [s], count_head, sign)
    copy.wait()
    shard = lax.axis_index("tm")
    place = lax.axis_index("head")
    mine = shard * blocks

    def two_picks(wanted):
        picks = [jnp.int32(0)] * NEAR_CAP
        count = jnp.int32(0)
        for j in range(blocks):
            for k in range(NEAR_CAP):
                picks[k] = jnp.where((wanted[j] > 0) & (count == k), j, picks[k])
            count = count + wanted[j]
        return picks, count

    def named_by(rows, column):
        found = table_ref[rows, column]
        for i in range(1, blocks):
            found = found | table_ref[rows + i, column]
        return found

    for d in range(count_tm):
        picks, _ = two_picks([named_by(d * blocks, mine + j) for j in range(blocks)])
        for k in range(NEAR_CAP):
            picks_ref[NEAR_CAP * d + k] = picks[k]

    kept = [[table_ref[mine + i, mine + j] * tokens_ref[mine + j] for j in range(blocks)] for i in range(blocks)]
    arrivals = {}
    senders = partners(count_tm, shard)
    for at, k in remote_rows(count_tm):
        _, sender, receives = senders[at]
        first = sender * blocks
        if k == 0:
            arrivals[at] = two_picks([named_by(mine, first + j) for j in range(blocks)])
        picks, count = arrivals[at]
        there = first + picks[k]
        live = jnp.where((count > k) & receives, tokens_ref[there], 0)
        for i in range(blocks):
            kept[i].append(table_ref[mine + i, there] * live)

    total = bias_ref.shape[1]
    piece_rows = BLK // count_head
    at = lax.broadcasted_iota(jnp.int32, (blocks, total), 1)
    query = lax.broadcasted_iota(jnp.int32, (blocks, total), 0)
    own = at < blocks * BLK
    group, token = split(at, piece_rows)
    own_piece, own_block = split(group, blocks)
    far_row, far_group = split(group, count_head)
    row = jnp.where(own, own_block, far_row)
    piece = jnp.where(own, own_piece, far_group)
    source = jnp.where(piece > place, place - piece + count_head, place - piece)
    position = source * piece_rows + token
    limit = jnp.zeros((blocks, total), jnp.int32)
    for r in range(len(kept[0])):
        value = jnp.zeros((blocks, total), jnp.int32)
        for i in range(blocks):
            value = jnp.where(query == i, kept[i][r], value)
        limit = jnp.where(row == r, value, limit)
    bias_ref[...] = jnp.where(position < limit, 0.0, NEG)


def plan(arrays, messages, pair_list, block_tokens, after, count_head, count_tm):
    blocks, tokens, _ = arrays[0].shape
    total_blocks, columns = pair_list.shape
    lanes = -(-total_blocks // 128) * 128
    total = (blocks + len(remote_rows(count_tm))) * BLK
    vmem = pl.BlockSpec(memory_space=pltpu.VMEM)
    smem = pl.BlockSpec(memory_space=pltpu.SMEM)
    stacked = (count_head, blocks, tokens, arrays[0].shape[2] // count_head)
    shapes = [jax.ShapeDtypeStruct(stacked, jnp.bfloat16)] + [
        jax.ShapeDtypeStruct((blocks, tokens, fields_of(message)[1]), jnp.bfloat16)
        for message in messages
        for _ in range(count_head)
    ]
    picks, bias, query, *pieces = pl.pallas_call(
        functools.partial(plan_kernel, messages, count_head, count_tm, blocks),
        in_specs=[vmem] * 3
        + [pl.BlockSpec(memory_space=pl.ANY), smem, pl.BlockSpec(memory_space=pl.ANY)],
        out_specs=[smem, vmem] + [vmem] * len(shapes),
        out_shape=[
            jax.ShapeDtypeStruct((NEAR_CAP * count_tm,), jnp.int32),
            jax.ShapeDtypeStruct((blocks, total), jnp.float32),
        ]
        + shapes,
        scratch_shapes=[
            pltpu.VMEM((total_blocks, columns), jnp.int32),
            pltpu.VMEM((total_blocks, lanes), jnp.int32),
            pltpu.SMEM((total_blocks, lanes), jnp.int32),
            pltpu.SemaphoreType.DMA,
            pltpu.SemaphoreType.DMA,
        ],
        cost_estimate=NO_COST,
        compiler_params=pltpu.CompilerParams(vmem_limit_bytes=VMEM),
    )(*arrays, pair_list, block_tokens, after)
    return picks, bias, query, [pieces[at : at + count_head] for at in range(0, len(pieces), count_head)]


def attend_kernel(counts, heads_of, distances, tokens_ref, bias_ref, query_ref, *refs):
    count_head, count_tm = counts
    queries = by_distance([query_ref], count_head, -1)
    per_part = count_head + len(routes(count_tm))
    parts = [refs[p * per_part : (p + 1) * per_part] for p in range(len(heads_of))]
    outs = refs[len(heads_of) * per_part :][-len(distances) :]
    blocks, tokens, _ = outs[0].shape
    rows = len(distances) * tokens
    shard = lax.axis_index("tm")
    me = lax.axis_index("head")
    bias = bias_ref[...][:, None, :]
    place_of = [(p, h) for p, (_, size) in enumerate(heads_of) for h in range(size // HD)]

    def gathered(kind, head):
        p, h = place_of[head]
        first = kind * heads_of[p][1] + h * HD
        lanes = slice(first, first + HD)
        pieces = [rows_of(own[:, :, lanes]) for own in parts[p][:count_head]]
        pieces += [
            rows_of(parts[p][count_head + at][k, :, :, lanes])
            for at, k in remote_rows(count_tm)
        ]
        return jnp.concatenate(pieces, axis=0)

    def products(head):
        first = heads_of[0][0] + head * HD
        lanes = slice(first, first + HD)
        query = jnp.concatenate(
            [rows_of(queries[s][i, :, lanes]) for i in range(blocks) for s in distances], axis=0
        )
        return lax.dot_general(
            query, gathered(0, head), (((1,), (1,)), ((), ())), preferred_element_type=jnp.float32
        )

    heads = len(place_of)
    dots, mixed = products(0), []
    for h in range(heads):
        ahead = products(h + 1) if h + 1 < heads else None
        dots = dots.reshape(blocks, rows, -1) + bias
        peak = jnp.max(dots, axis=-1, keepdims=True)
        weights = jnp.exp2((dots - peak) * (SCORE_SCALE * LOG2E))
        inverse = 1.0 / jnp.sum(weights, axis=-1, keepdims=True)
        weights_half = weights.astype(jnp.bfloat16).reshape(blocks * rows, -1)
        part = jnp.dot(weights_half, gathered(1, h), preferred_element_type=jnp.float32)
        mixed.append(part * inverse.reshape(blocks * rows, 1))
        dots = ahead
    mixed = jnp.concatenate(mixed, axis=0)
    sign = sign_matrix()
    high = mixed.astype(jnp.bfloat16)
    low = (mixed - high.astype(jnp.float32)).astype(jnp.bfloat16)
    turned = jnp.dot(high, sign, preferred_element_type=jnp.float32)
    turned = turned + jnp.dot(low, sign, preferred_element_type=jnp.float32)
    turned = (turned * ROTATE_SCALE).reshape(heads, blocks, len(distances), tokens, HD)
    token = lax.broadcasted_iota(jnp.int32, (tokens, HD), 0)
    for at, s in enumerate(distances):
        position = lax.rem(me - s + count_head, count_head) * tokens + token
        for i in range(blocks):
            live = position < tokens_ref[shard * blocks + i]
            for h in range(heads):
                outs[at][i, :, h * HD : (h + 1) * HD] = jnp.where(
                    live, turned[h, i, at], 0.0
                ).astype(jnp.bfloat16)


def attend(block_tokens, bias, query, parts, heads_of, distances, after=(), cost=NO_COST):
    count_head, count_tm = query.shape[0], lax.axis_size("tm")
    operands = [ref for owns, slots in parts for ref in owns + slots]
    shape = query.shape[1:3] + (sum(size for _, size in heads_of),)
    vmem = pl.BlockSpec(memory_space=pltpu.VMEM)
    return pl.pallas_call(
        functools.partial(attend_kernel, (count_head, count_tm), heads_of, distances),
        in_specs=[pl.BlockSpec(memory_space=pltpu.SMEM)]
        + [vmem] * (2 + len(operands))
        + [pl.BlockSpec(memory_space=pl.ANY)] * len(after),
        out_specs=[vmem] * len(distances),
        out_shape=[jax.ShapeDtypeStruct(shape, jnp.bfloat16)] * len(distances),
        cost_estimate=cost,
        compiler_params=pltpu.CompilerParams(vmem_limit_bytes=VMEM),
    )(block_tokens, bias, query, *operands, *after)


def place_kernel(places, width_here, *refs):
    pieces, out_ref, sems = refs[:-2], refs[-2], refs[-1]
    me, count = lax.axis_index("head"), lax.axis_size("head")
    copies = []
    for at, (piece, (s, start)) in enumerate(zip(pieces, places)):
        column = pl.multiple_of(lax.rem(me + s, count) * width_here + start, HD)
        copies.append(
            pltpu.make_async_copy(
                piece, out_ref.at[:, :, pl.ds(column, piece.shape[-1])], sems.at[at]
            )
        )
        copies[-1].start()
    for copy in copies:
        copy.wait()


def place_pieces(pieces, places, width_here):
    blocks, tokens, _ = pieces[0].shape
    width = width_here * lax.axis_size("head")
    return pl.pallas_call(
        functools.partial(place_kernel, places, width_here),
        in_specs=[pl.BlockSpec(memory_space=pl.ANY)] * len(pieces),
        out_specs=pl.BlockSpec(memory_space=pltpu.HBM),
        out_shape=jax.ShapeDtypeStruct((blocks, tokens, width), jnp.bfloat16),
        scratch_shapes=[pltpu.SemaphoreType.DMA((len(pieces),))],
        compiler_params=pltpu.CompilerParams(vmem_limit_bytes=VMEM),
    )(*pieces)


def shifted(array, axis, distance):
    count = lax.axis_size(axis)
    return lax.ppermute(array, axis, [(i, (i + distance) % count) for i in range(count)])


def exchange(pieces, direction):
    return [shifted(piece, "head", direction * s) for s, piece in enumerate(pieces, 1)]


def forward(sent):
    ways = routes(lax.axis_size("tm"))
    return [lax.ppermute(block, "tm", way) for block, (_, way) in zip(sent, ways)]


def shards(query_rows, key_rows, value_rows, pair_list, block_tokens):
    count_head = lax.axis_size("head")
    count_tm = lax.axis_size("tm")
    blocks, tokens, width = query_rows.shape
    width_here = width // count_head
    heads = width_here // HD
    cut = (heads + 1) // 2 * HD
    parts = [(0, cut), (cut, width_here - cut)] if heads > 1 else [(0, width_here)]
    arrays = [query_rows, key_rows, value_rows]
    messages = [[(1,) + part, (2,) + part] for part in parts]
    pieces, token = rotate_pieces(arrays, messages[0], count_head)
    picks, bias, query, later = plan(
        arrays, messages[1:], pair_list, block_tokens, token, count_head, count_tm
    )
    received = [piece[:1] + exchange(piece[1:], 1) for piece in [pieces] + later]
    sent = []
    for owns, (_, size) in zip(received, parts):
        held = sent[-1][0] if sent else query
        picked = pick_blocks(picks, owns, (0, 2 * size), count_tm, held, not sent)
        if not sent:
            *picked, query = picked
        sent.append(list(picked))
    query = lax.all_to_all(query, "head", split_axis=0, concat_axis=0, tiled=True)
    inputs = [(owns, forward(picked)) for owns, picked in zip(received, sent)]
    distances, after = list(range(1, count_head)), ()
    pieces, places = [], []
    for at, part in enumerate(parts):
        cost = NO_COST if at == len(parts) - 1 else HIGH_COST
        leaving = attend(
            block_tokens, bias, query, [inputs[at]], [part], distances, after, cost
        )
        after = (leaving[0],)
        pieces += exchange(leaving, -1)
        places += [(s, part[0]) for s in distances]
    pieces += attend(block_tokens, bias, query, inputs, parts, [0], after)
    return place_pieces(pieces, places + [(0, 0)], width_here)


def solution(mesh):
    placed = (
        P(("grp", "tm"), "head", None),
        P(("grp", "tm"), "head", None),
        P(("grp", "tm"), "head", None),
        P("grp", None),
        P("grp"),
    )
    return jax.shard_map(
        shards,
        mesh=mesh,
        in_specs=placed,
        out_specs=P(("grp", "tm"), "head", None),
        check_vma=False,
    )
```

```python
import functools
import math

import jax
import jax.numpy as jnp
from jax import lax
from jax.experimental import pallas as pl
from jax.experimental.pallas import tpu as pltpu
from jax.sharding import PartitionSpec as P

HD = 128
BLK = 64
NEAR_CAP = 2
FAR_CAP = 1
NEG = -1e30
ROTATE_SCALE = 1.0 / math.sqrt(HD)
SCORE_SCALE = 1.0 / math.sqrt(HD)
VMEM = 24 * 1024 * 1024
WIDE_VMEM = 60 * 1024 * 1024
TOKEN = jax.ShapeDtypeStruct((8, 128), jnp.float32)
NO_COST = pl.CostEstimate(flops=0, bytes_accessed=0, transcendentals=0)
HIGH_COST = pl.CostEstimate(flops=10**11, bytes_accessed=0, transcendentals=0)
LOG2E = math.log2(math.e)


def sign_matrix():
    common = lax.broadcasted_iota(jnp.int32, (HD, HD), 0) & lax.broadcasted_iota(
        jnp.int32, (HD, HD), 1
    )
    bits = HD.bit_length() - 1
    parity = common
    for bit in range(1, bits):
        parity = parity ^ (common >> bit)
    return jnp.where((parity & 1) == 0, 1.0, -1.0).astype(jnp.bfloat16)


def rows_of(block):
    rows, width = math.prod(block.shape[:-1]), block.shape[-1]
    if block.shape[-2] % 16 == 0:
        return block.reshape(rows, width)
    return block.astype(jnp.float32).reshape(rows, width).astype(block.dtype)


def fields_of(message):
    at, fields = 0, []
    for source, start, size in message:
        fields.append((source, start, size, at))
        at += size
    return fields, at


def by_distance(refs, count, direction):
    if len(refs[0].shape) == 3:
        return list(refs)
    me = lax.axis_index("head")
    return [refs[0].at[lax.rem(me + direction * s + count, count)] for s in range(count)]


def rotated(block, sign):
    blocks, tokens, size = block.shape
    flat = rows_of(block)
    heads = [flat[:, at : at + HD] for at in range(0, size, HD)]
    turned = jnp.dot(jnp.concatenate(heads, axis=0), sign, preferred_element_type=jnp.float32)
    return (turned * ROTATE_SCALE).reshape(size // HD, blocks, tokens, HD).astype(jnp.bfloat16)


def store_heads(out, start, turned):
    for h in range(turned.shape[0]):
        at = start + h * HD
        out[:, :, at : at + HD] = turned[h]


def rotate_kernel(message, sources, count_head, *refs):
    fields, total = fields_of(message)
    ins = dict(zip(sources, refs))
    outs, (token, buffer, sems) = refs[len(sources) : -3], refs[-3:]
    token[...] = jnp.zeros_like(token)
    width_here = refs[0].shape[2] // count_head
    me = lax.axis_index("head")
    order = list(range(1, count_head)) + [0]
    copies = {}
    for s in order:
        goal = lax.rem(me + s, count_head)
        for f, (source, start, size, at) in enumerate(fields):
            column = pl.multiple_of(goal * width_here + start, HD)
            copies[s, f] = pltpu.make_async_copy(
                ins[source].at[:, :, pl.ds(column, size)],
                buffer.at[s, :, :, pl.ds(at, size)],
                sems.at[s, f],
            )
            copies[s, f].start()
    sign = sign_matrix()
    for s in order:
        for f, (_, _, size, start) in enumerate(fields):
            copies[s, f].wait()
            store_heads(outs[s], start, rotated(buffer[s, :, :, start : start + size], sign))


def rotate_here(fields, ins, outs, distances, count_head, sign):
    width_here = next(iter(ins.values())).shape[2] // count_head
    me = lax.axis_index("head")
    for s in distances:
        goal = lax.rem(me + s, count_head)
        for source, start, size, at in fields:
            column = pl.multiple_of(goal * width_here + start, HD)
            store_heads(outs[s], at, rotated(ins[source][:, :, pl.ds(column, size)], sign))


def rotate_pieces(arrays, message, count_head):
    blocks, tokens, _ = arrays[0].shape
    fields, total = fields_of(message)
    sources = sorted({source for source, _, _ in message})
    one = (blocks, tokens, total)
    *pieces, token = pl.pallas_call(
        functools.partial(rotate_kernel, message, sources, count_head),
        in_specs=[pl.BlockSpec(memory_space=pltpu.HBM)] * len(sources),
        out_specs=[pl.BlockSpec(memory_space=pltpu.VMEM)] * (count_head + 1),
        out_shape=[jax.ShapeDtypeStruct(one, jnp.bfloat16)] * count_head + [TOKEN],
        scratch_shapes=[
            pltpu.VMEM((count_head,) + one, jnp.bfloat16),
            pltpu.SemaphoreType.DMA((count_head, len(fields))),
        ],
        cost_estimate=NO_COST,
        compiler_params=pltpu.CompilerParams(vmem_limit_bytes=WIDE_VMEM),
    )(*[arrays[source] for source in sources])
    return pieces, token


def slots_at(distance, count_tm):
    return NEAR_CAP if distance in (1, count_tm - 1) else FAR_CAP


def pick_kernel(count_head, count_tm, lanes, picks_ref, *refs):
    pieces, outs = refs[:count_head], refs[count_head + 1 : count_head + count_tm]
    shard = lax.axis_index("tm")
    for distance, out in enumerate(outs, 1):
        goal = lax.rem(shard + distance, count_tm)
        for k in range(slots_at(distance, count_tm)):
            pick = picks_ref[NEAR_CAP * goal + k]
            for s in range(count_head):
                out[k, s] = pieces[s][pick, :, lanes[0] : lanes[1]]


def pick_blocks(picks, pieces, lanes, count_tm, held, passes):
    count_head = len(pieces)
    one = (count_head, pieces[0].shape[1], lanes[1] - lanes[0])
    vmem, anywhere = pl.BlockSpec(memory_space=pltpu.VMEM), pl.BlockSpec(memory_space=pl.ANY)
    shapes = [
        jax.ShapeDtypeStruct((slots_at(distance, count_tm),) + one, jnp.bfloat16)
        for distance in range(1, count_tm)
    ]
    passed = [jax.ShapeDtypeStruct(held.shape, held.dtype)] if passes else []
    return pl.pallas_call(
        functools.partial(pick_kernel, count_head, count_tm, lanes),
        in_specs=[pl.BlockSpec(memory_space=pltpu.SMEM)] + [vmem] * count_head + [anywhere],
        out_specs=[vmem] * len(shapes) + [anywhere] * len(passed),
        out_shape=shapes + passed,
        input_output_aliases={1 + count_head: len(shapes)} if passes else {},
        cost_estimate=HIGH_COST,
        compiler_params=pltpu.CompilerParams(vmem_limit_bytes=VMEM),
    )(picks, *pieces, held)


def remote_rows(count_tm):
    return [
        (distance, k)
        for distance in range(1, count_tm)
        for k in range(slots_at(distance, count_tm))
    ]


def split(value, by):
    if by & (by - 1) == 0:
        return value >> (by.bit_length() - 1), value & (by - 1)
    return lax.div(value, by), lax.rem(value, by)


def plan_kernel(messages, count_head, count_tm, blocks, *refs):
    *sources, pair_hbm, tokens_ref, _ = refs[:6]
    picks_ref, bias_ref, query_out = refs[6:9]
    pair_ref, named_ref, table_ref, pair_sem, table_sem = refs[-5:]
    outs = refs[9:-5]
    ins = dict(enumerate(sources))
    pair_copy = pltpu.make_async_copy(pair_hbm, pair_ref, pair_sem)
    pair_copy.start()
    sign = sign_matrix()
    places = list(range(1, count_head)) + [0]
    jobs = [
        (fields_of(message)[0], outs[m * count_head : (m + 1) * count_head], s)
        for m, message in enumerate(messages)
        for s in places
    ]
    query_fields = [(0, 0, query_out.shape[-1], 0)]
    jobs += [(query_fields, by_distance([query_out], count_head, 1), s) for s in places]
    half = len(jobs) // 2
    for fields, pieces, s in jobs[:half]:
        rotate_here(fields, ins, pieces, [s], count_head, sign)
    pair_copy.wait()
    total_blocks, columns = pair_ref.shape
    pairs = pair_ref[...]
    lane = lax.broadcasted_iota(jnp.int32, named_ref.shape, 1)
    named = jnp.zeros(named_ref.shape, jnp.int32)
    for c in range(columns):
        named = jnp.where(pairs[:, c : c + 1] == lane, 1, named)
    named_ref[...] = named
    copy = pltpu.make_async_copy(named_ref, table_ref, table_sem)
    copy.start()
    for fields, pieces, s in jobs[half:]:
        rotate_here(fields, ins, pieces, [s], count_head, sign)
    copy.wait()
    shard = lax.axis_index("tm")
    place = lax.axis_index("head")
    mine = shard * blocks

    def two_picks(wanted):
        picks = [jnp.int32(0)] * NEAR_CAP
        count = jnp.int32(0)
        for j in range(blocks):
            for k in range(NEAR_CAP):
                picks[k] = jnp.where((wanted[j] > 0) & (count == k), j, picks[k])
            count = count + wanted[j]
        return picks, count

    def named_by(rows, column):
        found = table_ref[rows, column]
        for i in range(1, blocks):
            found = found | table_ref[rows + i, column]
        return found

    for d in range(count_tm):
        picks, _ = two_picks([named_by(d * blocks, mine + j) for j in range(blocks)])
        for k in range(NEAR_CAP):
            picks_ref[NEAR_CAP * d + k] = picks[k]

    kept = [[table_ref[mine + i, mine + j] * tokens_ref[mine + j] for j in range(blocks)] for i in range(blocks)]
    arrivals = {}
    for distance, k in remote_rows(count_tm):
        first = lax.rem(shard - distance + count_tm, count_tm) * blocks
        if k == 0:
            arrivals[distance] = two_picks([named_by(mine, first + j) for j in range(blocks)])
        picks, count = arrivals[distance]
        there = first + picks[k]
        live = jnp.where(count > k, tokens_ref[there], 0)
        for i in range(blocks):
            kept[i].append(table_ref[mine + i, there] * live)

    total = bias_ref.shape[1]
    piece_rows = BLK // count_head
    at = lax.broadcasted_iota(jnp.int32, (blocks, total), 1)
    query = lax.broadcasted_iota(jnp.int32, (blocks, total), 0)
    own = at < blocks * BLK
    group, token = split(at, piece_rows)
    own_piece, own_block = split(group, blocks)
    far_row, far_group = split(group, count_head)
    row = jnp.where(own, own_block, far_row)
    piece = jnp.where(own, own_piece, far_group)
    source = jnp.where(piece > place, place - piece + count_head, place - piece)
    position = source * piece_rows + token
    limit = jnp.zeros((blocks, total), jnp.int32)
    for r in range(len(kept[0])):
        value = jnp.zeros((blocks, total), jnp.int32)
        for i in range(blocks):
            value = jnp.where(query == i, kept[i][r], value)
        limit = jnp.where(row == r, value, limit)
    bias_ref[...] = jnp.where(position < limit, 0.0, NEG)


def plan(arrays, messages, pair_list, block_tokens, after, count_head, count_tm):
    blocks, tokens, _ = arrays[0].shape
    total_blocks, columns = pair_list.shape
    lanes = -(-total_blocks // 128) * 128
    total = (blocks + len(remote_rows(count_tm))) * BLK
    vmem = pl.BlockSpec(memory_space=pltpu.VMEM)
    smem = pl.BlockSpec(memory_space=pltpu.SMEM)
    stacked = (count_head, blocks, tokens, arrays[0].shape[2] // count_head)
    shapes = [jax.ShapeDtypeStruct(stacked, jnp.bfloat16)] + [
        jax.ShapeDtypeStruct((blocks, tokens, fields_of(message)[1]), jnp.bfloat16)
        for message in messages
        for _ in range(count_head)
    ]
    picks, bias, query, *pieces = pl.pallas_call(
        functools.partial(plan_kernel, messages, count_head, count_tm, blocks),
        in_specs=[vmem] * 3
        + [pl.BlockSpec(memory_space=pl.ANY), smem, pl.BlockSpec(memory_space=pl.ANY)],
        out_specs=[smem, vmem] + [vmem] * len(shapes),
        out_shape=[
            jax.ShapeDtypeStruct((NEAR_CAP * count_tm,), jnp.int32),
            jax.ShapeDtypeStruct((blocks, total), jnp.float32),
        ]
        + shapes,
        scratch_shapes=[
            pltpu.VMEM((total_blocks, columns), jnp.int32),
            pltpu.VMEM((total_blocks, lanes), jnp.int32),
            pltpu.SMEM((total_blocks, lanes), jnp.int32),
            pltpu.SemaphoreType.DMA,
            pltpu.SemaphoreType.DMA,
        ],
        cost_estimate=NO_COST,
        compiler_params=pltpu.CompilerParams(vmem_limit_bytes=VMEM),
    )(*arrays, pair_list, block_tokens, after)
    return picks, bias, query, [pieces[at : at + count_head] for at in range(0, len(pieces), count_head)]


def attend_kernel(counts, heads_of, distances, tokens_ref, bias_ref, query_ref, *refs):
    count_head, count_tm = counts
    queries = by_distance([query_ref], count_head, -1)
    per_part = count_head + count_tm - 1
    parts = [refs[p * per_part : (p + 1) * per_part] for p in range(len(heads_of))]
    outs = refs[len(heads_of) * per_part :][-len(distances) :]
    blocks, tokens, _ = outs[0].shape
    rows = len(distances) * tokens
    shard = lax.axis_index("tm")
    me = lax.axis_index("head")
    bias = bias_ref[...][:, None, :]
    place_of = [(p, h) for p, (_, size) in enumerate(heads_of) for h in range(size // HD)]

    def gathered(kind, head):
        p, h = place_of[head]
        first = kind * heads_of[p][1] + h * HD
        lanes = slice(first, first + HD)
        pieces = [rows_of(own[:, :, lanes]) for own in parts[p][:count_head]]
        pieces += [
            rows_of(parts[p][count_head + distance - 1][k, :, :, lanes])
            for distance, k in remote_rows(count_tm)
        ]
        return jnp.concatenate(pieces, axis=0)

    def products(head):
        first = heads_of[0][0] + head * HD
        lanes = slice(first, first + HD)
        query = jnp.concatenate(
            [rows_of(queries[s][i, :, lanes]) for i in range(blocks) for s in distances], axis=0
        )
        return lax.dot_general(
            query, gathered(0, head), (((1,), (1,)), ((), ())), preferred_element_type=jnp.float32
        )

    heads = len(place_of)
    dots = jnp.concatenate([products(h) for h in range(heads)], axis=0)
    dots = dots.reshape(heads, blocks, rows, -1) + bias
    peak = jnp.max(dots, axis=-1, keepdims=True)
    weights = jnp.exp2((dots - peak) * (SCORE_SCALE * LOG2E))
    inverse = 1.0 / jnp.sum(weights, axis=-1, keepdims=True)
    weights_half = weights.astype(jnp.bfloat16).reshape(heads, blocks * rows, -1)
    mixed = [
        jnp.dot(weights_half[h], gathered(1, h), preferred_element_type=jnp.float32)
        for h in range(heads)
    ]
    mixed = jnp.concatenate(mixed, axis=0) * inverse.reshape(heads * blocks * rows, 1)
    sign = sign_matrix()
    high = mixed.astype(jnp.bfloat16)
    low = (mixed - high.astype(jnp.float32)).astype(jnp.bfloat16)
    turned = jnp.dot(high, sign, preferred_element_type=jnp.float32)
    turned = turned + jnp.dot(low, sign, preferred_element_type=jnp.float32)
    turned = (turned * ROTATE_SCALE).reshape(heads, blocks, len(distances), tokens, HD)
    token = lax.broadcasted_iota(jnp.int32, (tokens, HD), 0)
    for at, s in enumerate(distances):
        position = lax.rem(me - s + count_head, count_head) * tokens + token
        for i in range(blocks):
            live = position < tokens_ref[shard * blocks + i]
            for h in range(heads):
                outs[at][i, :, h * HD : (h + 1) * HD] = jnp.where(
                    live, turned[h, i, at], 0.0
                ).astype(jnp.bfloat16)


def attend(block_tokens, bias, query, parts, heads_of, distances, after=(), cost=NO_COST):
    count_head, count_tm = query.shape[0], len(parts[0][1]) + 1
    operands = [ref for owns, slots in parts for ref in owns + slots]
    shape = query.shape[1:3] + (sum(size for _, size in heads_of),)
    vmem = pl.BlockSpec(memory_space=pltpu.VMEM)
    return pl.pallas_call(
        functools.partial(attend_kernel, (count_head, count_tm), heads_of, distances),
        in_specs=[pl.BlockSpec(memory_space=pltpu.SMEM)]
        + [vmem] * (2 + len(operands))
        + [pl.BlockSpec(memory_space=pl.ANY)] * len(after),
        out_specs=[vmem] * len(distances),
        out_shape=[jax.ShapeDtypeStruct(shape, jnp.bfloat16)] * len(distances),
        cost_estimate=cost,
        compiler_params=pltpu.CompilerParams(vmem_limit_bytes=VMEM),
    )(block_tokens, bias, query, *operands, *after)


def place_kernel(places, width_here, *refs):
    pieces, out_ref, sems = refs[:-2], refs[-2], refs[-1]
    me, count = lax.axis_index("head"), lax.axis_size("head")
    copies = []
    for at, (piece, (s, start)) in enumerate(zip(pieces, places)):
        column = pl.multiple_of(lax.rem(me + s, count) * width_here + start, HD)
        copies.append(
            pltpu.make_async_copy(
                piece, out_ref.at[:, :, pl.ds(column, piece.shape[-1])], sems.at[at]
            )
        )
        copies[-1].start()
    for copy in copies:
        copy.wait()


def place_pieces(pieces, places, width_here):
    blocks, tokens, _ = pieces[0].shape
    width = width_here * lax.axis_size("head")
    return pl.pallas_call(
        functools.partial(place_kernel, places, width_here),
        in_specs=[pl.BlockSpec(memory_space=pl.ANY)] * len(pieces),
        out_specs=pl.BlockSpec(memory_space=pltpu.HBM),
        out_shape=jax.ShapeDtypeStruct((blocks, tokens, width), jnp.bfloat16),
        scratch_shapes=[pltpu.SemaphoreType.DMA((len(pieces),))],
        compiler_params=pltpu.CompilerParams(vmem_limit_bytes=VMEM),
    )(*pieces)


def shifted(array, axis, distance):
    count = lax.axis_size(axis)
    return lax.ppermute(array, axis, [(i, (i + distance) % count) for i in range(count)])


def exchange(pieces, direction):
    return [shifted(piece, "head", direction * s) for s, piece in enumerate(pieces, 1)]


def forward(sent):
    return [shifted(block, "tm", distance) for distance, block in enumerate(sent, 1)]


def shards(query_rows, key_rows, value_rows, pair_list, block_tokens):
    count_head = lax.axis_size("head")
    count_tm = lax.axis_size("tm")
    blocks, tokens, width = query_rows.shape
    width_here = width // count_head
    heads = width_here // HD
    cut = (heads + 1) // 2 * HD
    parts = [(0, cut), (cut, width_here - cut)] if heads > 1 else [(0, width_here)]
    arrays = [query_rows, key_rows, value_rows]
    messages = [[(1,) + part, (2,) + part] for part in parts]
    pieces, token = rotate_pieces(arrays, messages[0], count_head)
    picks, bias, query, later = plan(
        arrays, messages[1:], pair_list, block_tokens, token, count_head, count_tm
    )
    received = [piece[:1] + exchange(piece[1:], 1) for piece in [pieces] + later]
    sent = []
    for owns, (_, size) in zip(received, parts):
        held = sent[-1][0] if sent else query
        picked = pick_blocks(picks, owns, (0, 2 * size), count_tm, held, not sent)
        if not sent:
            *picked, query = picked
        sent.append(list(picked))
    inputs = [(owns, forward(picked)) for owns, picked in zip(received, sent)]
    query = lax.all_to_all(query, "head", split_axis=0, concat_axis=0, tiled=True)
    distances, after = list(range(1, count_head)), ()
    pieces, places = [], []
    for at, part in enumerate(parts):
        cost = NO_COST if at == len(parts) - 1 else HIGH_COST
        leaving = attend(
            block_tokens, bias, query, [inputs[at]], [part], distances, after, cost
        )
        after = (leaving[0],)
        pieces += exchange(leaving, -1)
        places += [(s, part[0]) for s in distances]
    pieces += attend(block_tokens, bias, query, inputs, parts, [0], after)
    return place_pieces(pieces, places + [(0, 0)], width_here)


def solution(mesh):
    placed = (
        P(("grp", "tm"), "head", None),
        P(("grp", "tm"), "head", None),
        P(("grp", "tm"), "head", None),
        P("grp", None),
        P("grp"),
    )
    return jax.shard_map(
        shards,
        mesh=mesh,
        in_specs=placed,
        out_specs=P(("grp", "tm"), "head", None),
        check_vma=False,
    )
```

```python
import functools
import math

import jax
import jax.numpy as jnp
from jax import lax
from jax.experimental import pallas as pl
from jax.experimental.pallas import tpu as pltpu
from jax.sharding import PartitionSpec as P

HD = 128
BLK = 64
NEAR_CAP = 2
FAR_CAP = 1
NEG = -1e30
ROTATE_SCALE = 1.0 / math.sqrt(HD)
SCORE_SCALE = 1.0 / math.sqrt(HD)
VMEM = 24 * 1024 * 1024
WIDE_VMEM = 60 * 1024 * 1024
TOKEN = jax.ShapeDtypeStruct((8, 128), jnp.float32)
NO_COST = pl.CostEstimate(flops=0, bytes_accessed=0, transcendentals=0)
HIGH_COST = pl.CostEstimate(flops=10**11, bytes_accessed=0, transcendentals=0)
LOG2E = math.log2(math.e)


def sign_matrix():
    common = lax.broadcasted_iota(jnp.int32, (HD, HD), 0) & lax.broadcasted_iota(
        jnp.int32, (HD, HD), 1
    )
    bits = HD.bit_length() - 1
    parity = common
    for bit in range(1, bits):
        parity = parity ^ (common >> bit)
    return jnp.where((parity & 1) == 0, 1.0, -1.0).astype(jnp.bfloat16)


def rows_of(block):
    rows, width = math.prod(block.shape[:-1]), block.shape[-1]
    if block.shape[-2] % 16 == 0:
        return block.reshape(rows, width)
    return block.astype(jnp.float32).reshape(rows, width).astype(block.dtype)


def fields_of(message):
    at, fields = 0, []
    for source, start, size in message:
        fields.append((source, start, size, at))
        at += size
    return fields, at


def by_distance(refs, count, direction):
    if len(refs[0].shape) == 3:
        return list(refs)
    me = lax.axis_index("head")
    return [refs[0].at[lax.rem(me + direction * s + count, count)] for s in range(count)]


def rotated(block, sign):
    blocks, tokens, size = block.shape
    flat = rows_of(block)
    heads = [flat[:, at : at + HD] for at in range(0, size, HD)]
    turned = jnp.dot(jnp.concatenate(heads, axis=0), sign, preferred_element_type=jnp.float32)
    return (turned * ROTATE_SCALE).reshape(size // HD, blocks, tokens, HD).astype(jnp.bfloat16)


def store_heads(out, start, turned):
    for h in range(turned.shape[0]):
        at = start + h * HD
        out[:, :, at : at + HD] = turned[h]


def rotate_kernel(message, sources, count_head, *refs):
    fields, total = fields_of(message)
    ins = dict(zip(sources, refs))
    outs, (token, buffer, sems) = refs[len(sources) : -3], refs[-3:]
    token[...] = jnp.zeros_like(token)
    width_here = refs[0].shape[2] // count_head
    me = lax.axis_index("head")
    order = list(range(1, count_head)) + [0]
    copies = {}
    for s in order:
        goal = lax.rem(me + s, count_head)
        for f, (source, start, size, at) in enumerate(fields):
            column = pl.multiple_of(goal * width_here + start, HD)
            copies[s, f] = pltpu.make_async_copy(
                ins[source].at[:, :, pl.ds(column, size)],
                buffer.at[s, :, :, pl.ds(at, size)],
                sems.at[s, f],
            )
            copies[s, f].start()
    sign = sign_matrix()
    for s in order:
        for f, (_, _, size, start) in enumerate(fields):
            copies[s, f].wait()
            store_heads(outs[s], start, rotated(buffer[s, :, :, start : start + size], sign))


def rotate_here(fields, ins, outs, distances, count_head, sign):
    width_here = next(iter(ins.values())).shape[2] // count_head
    me = lax.axis_index("head")
    for s in distances:
        goal = lax.rem(me + s, count_head)
        for source, start, size, at in fields:
            column = pl.multiple_of(goal * width_here + start, HD)
            store_heads(outs[s], at, rotated(ins[source][:, :, pl.ds(column, size)], sign))


def rotate_pieces(arrays, message, count_head):
    blocks, tokens, _ = arrays[0].shape
    fields, total = fields_of(message)
    sources = sorted({source for source, _, _ in message})
    one = (blocks, tokens, total)
    *pieces, token = pl.pallas_call(
        functools.partial(rotate_kernel, message, sources, count_head),
        in_specs=[pl.BlockSpec(memory_space=pltpu.HBM)] * len(sources),
        out_specs=[pl.BlockSpec(memory_space=pltpu.VMEM)] * (count_head + 1),
        out_shape=[jax.ShapeDtypeStruct(one, jnp.bfloat16)] * count_head + [TOKEN],
        scratch_shapes=[
            pltpu.VMEM((count_head,) + one, jnp.bfloat16),
            pltpu.SemaphoreType.DMA((count_head, len(fields))),
        ],
        cost_estimate=NO_COST,
        compiler_params=pltpu.CompilerParams(vmem_limit_bytes=WIDE_VMEM),
    )(*[arrays[source] for source in sources])
    return pieces, token


def slots_at(distance, count_tm):
    return NEAR_CAP if distance in (1, count_tm - 1) else FAR_CAP


def pick_kernel(count_head, count_tm, lanes, picks_ref, *refs):
    pieces, outs = refs[:count_head], refs[count_head + 1 : count_head + count_tm]
    shard = lax.axis_index("tm")
    for distance, out in enumerate(outs, 1):
        goal = lax.rem(shard + distance, count_tm)
        for k in range(slots_at(distance, count_tm)):
            pick = picks_ref[NEAR_CAP * goal + k]
            for s in range(count_head):
                out[k, s] = pieces[s][pick, :, lanes[0] : lanes[1]]


def pick_blocks(picks, pieces, lanes, count_tm, held, passes):
    count_head = len(pieces)
    one = (count_head, pieces[0].shape[1], lanes[1] - lanes[0])
    vmem, anywhere = pl.BlockSpec(memory_space=pltpu.VMEM), pl.BlockSpec(memory_space=pl.ANY)
    shapes = [
        jax.ShapeDtypeStruct((slots_at(distance, count_tm),) + one, jnp.bfloat16)
        for distance in range(1, count_tm)
    ]
    passed = [jax.ShapeDtypeStruct(held.shape, held.dtype)] if passes else []
    return pl.pallas_call(
        functools.partial(pick_kernel, count_head, count_tm, lanes),
        in_specs=[pl.BlockSpec(memory_space=pltpu.SMEM)] + [vmem] * count_head + [anywhere],
        out_specs=[vmem] * len(shapes) + [anywhere] * len(passed),
        out_shape=shapes + passed,
        input_output_aliases={1 + count_head: len(shapes)} if passes else {},
        cost_estimate=HIGH_COST,
        compiler_params=pltpu.CompilerParams(vmem_limit_bytes=VMEM),
    )(picks, *pieces, held)


def remote_rows(count_tm):
    return [
        (distance, k)
        for distance in range(1, count_tm)
        for k in range(slots_at(distance, count_tm))
    ]


def split(value, by):
    if by & (by - 1) == 0:
        return value >> (by.bit_length() - 1), value & (by - 1)
    return lax.div(value, by), lax.rem(value, by)


def plan_kernel(messages, count_head, count_tm, blocks, *refs):
    *sources, pair_hbm, tokens_ref, _ = refs[:6]
    picks_ref, bias_ref, query_out = refs[6:9]
    pair_ref, named_ref, table_ref, pair_sem, table_sem = refs[-5:]
    outs = refs[9:-5]
    ins = dict(enumerate(sources))
    pair_copy = pltpu.make_async_copy(pair_hbm, pair_ref, pair_sem)
    pair_copy.start()
    sign = sign_matrix()
    places = list(range(1, count_head)) + [0]
    jobs = [
        (fields_of(message)[0], outs[m * count_head : (m + 1) * count_head], s)
        for m, message in enumerate(messages)
        for s in places
    ]
    query_fields = [(0, 0, query_out.shape[-1], 0)]
    jobs += [(query_fields, by_distance([query_out], count_head, 1), s) for s in places]
    half = len(jobs) // 2
    for fields, pieces, s in jobs[:half]:
        rotate_here(fields, ins, pieces, [s], count_head, sign)
    pair_copy.wait()
    total_blocks, columns = pair_ref.shape
    pairs = pair_ref[...]
    lane = lax.broadcasted_iota(jnp.int32, named_ref.shape, 1)
    named = jnp.zeros(named_ref.shape, jnp.int32)
    for c in range(columns):
        named = jnp.where(pairs[:, c : c + 1] == lane, 1, named)
    named_ref[...] = named
    copy = pltpu.make_async_copy(named_ref, table_ref, table_sem)
    copy.start()
    for fields, pieces, s in jobs[half:]:
        rotate_here(fields, ins, pieces, [s], count_head, sign)
    copy.wait()
    shard = lax.axis_index("tm")
    place = lax.axis_index("head")
    mine = shard * blocks

    def two_picks(wanted):
        picks = [jnp.int32(0)] * NEAR_CAP
        count = jnp.int32(0)
        for j in range(blocks):
            for k in range(NEAR_CAP):
                picks[k] = jnp.where((wanted[j] > 0) & (count == k), j, picks[k])
            count = count + wanted[j]
        return picks, count

    def named_by(rows, column):
        found = table_ref[rows, column]
        for i in range(1, blocks):
            found = found | table_ref[rows + i, column]
        return found

    for d in range(count_tm):
        picks, _ = two_picks([named_by(d * blocks, mine + j) for j in range(blocks)])
        for k in range(NEAR_CAP):
            picks_ref[NEAR_CAP * d + k] = picks[k]

    kept = [[table_ref[mine + i, mine + j] * tokens_ref[mine + j] for j in range(blocks)] for i in range(blocks)]
    arrivals = {}
    for distance, k in remote_rows(count_tm):
        first = lax.rem(shard - distance + count_tm, count_tm) * blocks
        if k == 0:
            arrivals[distance] = two_picks([named_by(mine, first + j) for j in range(blocks)])
        picks, count = arrivals[distance]
        there = first + picks[k]
        live = jnp.where(count > k, tokens_ref[there], 0)
        for i in range(blocks):
            kept[i].append(table_ref[mine + i, there] * live)

    total = bias_ref.shape[1]
    piece_rows = BLK // count_head
    at = lax.broadcasted_iota(jnp.int32, (blocks, total), 1)
    query = lax.broadcasted_iota(jnp.int32, (blocks, total), 0)
    own = at < blocks * BLK
    group, token = split(at, piece_rows)
    own_piece, own_block = split(group, blocks)
    far_row, far_group = split(group, count_head)
    row = jnp.where(own, own_block, far_row)
    piece = jnp.where(own, own_piece, far_group)
    source = jnp.where(piece > place, place - piece + count_head, place - piece)
    position = source * piece_rows + token
    limit = jnp.zeros((blocks, total), jnp.int32)
    for r in range(len(kept[0])):
        value = jnp.zeros((blocks, total), jnp.int32)
        for i in range(blocks):
            value = jnp.where(query == i, kept[i][r], value)
        limit = jnp.where(row == r, value, limit)
    bias_ref[...] = jnp.where(position < limit, 0.0, NEG)


def plan(arrays, messages, pair_list, block_tokens, after, count_head, count_tm):
    blocks, tokens, _ = arrays[0].shape
    total_blocks, columns = pair_list.shape
    lanes = -(-total_blocks // 128) * 128
    total = (blocks + len(remote_rows(count_tm))) * BLK
    vmem = pl.BlockSpec(memory_space=pltpu.VMEM)
    smem = pl.BlockSpec(memory_space=pltpu.SMEM)
    stacked = (count_head, blocks, tokens, arrays[0].shape[2] // count_head)
    shapes = [jax.ShapeDtypeStruct(stacked, jnp.bfloat16)] + [
        jax.ShapeDtypeStruct((blocks, tokens, fields_of(message)[1]), jnp.bfloat16)
        for message in messages
        for _ in range(count_head)
    ]
    picks, bias, query, *pieces = pl.pallas_call(
        functools.partial(plan_kernel, messages, count_head, count_tm, blocks),
        in_specs=[vmem] * 3
        + [pl.BlockSpec(memory_space=pl.ANY), smem, pl.BlockSpec(memory_space=pl.ANY)],
        out_specs=[smem, vmem] + [vmem] * len(shapes),
        out_shape=[
            jax.ShapeDtypeStruct((NEAR_CAP * count_tm,), jnp.int32),
            jax.ShapeDtypeStruct((blocks, total), jnp.float32),
        ]
        + shapes,
        scratch_shapes=[
            pltpu.VMEM((total_blocks, columns), jnp.int32),
            pltpu.VMEM((total_blocks, lanes), jnp.int32),
            pltpu.SMEM((total_blocks, lanes), jnp.int32),
            pltpu.SemaphoreType.DMA,
            pltpu.SemaphoreType.DMA,
        ],
        cost_estimate=NO_COST,
        compiler_params=pltpu.CompilerParams(vmem_limit_bytes=VMEM),
    )(*arrays, pair_list, block_tokens, after)
    return picks, bias, query, [pieces[at : at + count_head] for at in range(0, len(pieces), count_head)]


def attend_kernel(counts, heads_of, distances, tokens_ref, bias_ref, query_ref, *refs):
    count_head, count_tm = counts
    queries = by_distance([query_ref], count_head, -1)
    per_part = count_head + count_tm - 1
    parts = [refs[p * per_part : (p + 1) * per_part] for p in range(len(heads_of))]
    outs = refs[len(heads_of) * per_part :][-len(distances) :]
    blocks, tokens, _ = outs[0].shape
    rows = len(distances) * tokens
    shard = lax.axis_index("tm")
    me = lax.axis_index("head")
    bias = bias_ref[...][:, None, :]
    place_of = [(p, h) for p, (_, size) in enumerate(heads_of) for h in range(size // HD)]

    def gathered(kind, head):
        p, h = place_of[head]
        first = kind * heads_of[p][1] + h * HD
        lanes = slice(first, first + HD)
        pieces = [rows_of(own[:, :, lanes]) for own in parts[p][:count_head]]
        pieces += [
            rows_of(parts[p][count_head + distance - 1][k, :, :, lanes])
            for distance, k in remote_rows(count_tm)
        ]
        return jnp.concatenate(pieces, axis=0)

    def products(head):
        first = heads_of[0][0] + head * HD
        lanes = slice(first, first + HD)
        query = jnp.concatenate(
            [rows_of(queries[s][i, :, lanes]) for i in range(blocks) for s in distances], axis=0
        )
        return lax.dot_general(
            query, gathered(0, head), (((1,), (1,)), ((), ())), preferred_element_type=jnp.float32
        )

    heads = len(place_of)
    dots = jnp.concatenate([products(h) for h in range(heads)], axis=0)
    dots = dots.reshape(heads, blocks, rows, -1) + bias
    peak = jnp.max(dots, axis=-1, keepdims=True)
    weights = jnp.exp2((dots - peak) * (SCORE_SCALE * LOG2E))
    inverse = 1.0 / jnp.sum(weights, axis=-1, keepdims=True)
    weights_half = weights.astype(jnp.bfloat16).reshape(heads, blocks * rows, -1)
    mixed = [
        jnp.dot(weights_half[h], gathered(1, h), preferred_element_type=jnp.float32)
        for h in range(heads)
    ]
    mixed = jnp.concatenate(mixed, axis=0) * inverse.reshape(heads * blocks * rows, 1)
    sign = sign_matrix()
    high = mixed.astype(jnp.bfloat16)
    low = (mixed - high.astype(jnp.float32)).astype(jnp.bfloat16)
    turned = jnp.dot(high, sign, preferred_element_type=jnp.float32)
    turned = turned + jnp.dot(low, sign, preferred_element_type=jnp.float32)
    turned = (turned * ROTATE_SCALE).reshape(heads, blocks, len(distances), tokens, HD)
    token = lax.broadcasted_iota(jnp.int32, (tokens, HD), 0)
    for at, s in enumerate(distances):
        position = lax.rem(me - s + count_head, count_head) * tokens + token
        for i in range(blocks):
            live = position < tokens_ref[shard * blocks + i]
            for h in range(heads):
                outs[at][i, :, h * HD : (h + 1) * HD] = jnp.where(
                    live, turned[h, i, at], 0.0
                ).astype(jnp.bfloat16)


def attend(block_tokens, bias, query, parts, heads_of, distances, after=(), cost=NO_COST):
    count_head, count_tm = query.shape[0], len(parts[0][1]) + 1
    operands = [ref for owns, slots in parts for ref in owns + slots]
    shape = query.shape[1:3] + (sum(size for _, size in heads_of),)
    vmem = pl.BlockSpec(memory_space=pltpu.VMEM)
    return pl.pallas_call(
        functools.partial(attend_kernel, (count_head, count_tm), heads_of, distances),
        in_specs=[pl.BlockSpec(memory_space=pltpu.SMEM)]
        + [vmem] * (2 + len(operands))
        + [pl.BlockSpec(memory_space=pl.ANY)] * len(after),
        out_specs=[vmem] * len(distances),
        out_shape=[jax.ShapeDtypeStruct(shape, jnp.bfloat16)] * len(distances),
        cost_estimate=cost,
        compiler_params=pltpu.CompilerParams(vmem_limit_bytes=VMEM),
    )(block_tokens, bias, query, *operands, *after)


def place_kernel(places, width_here, *refs):
    pieces, out_ref, sems = refs[:-2], refs[-2], refs[-1]
    me, count = lax.axis_index("head"), lax.axis_size("head")
    copies = []
    for at, (piece, (s, start)) in enumerate(zip(pieces, places)):
        column = pl.multiple_of(lax.rem(me + s, count) * width_here + start, HD)
        copies.append(
            pltpu.make_async_copy(
                piece, out_ref.at[:, :, pl.ds(column, piece.shape[-1])], sems.at[at]
            )
        )
        copies[-1].start()
    for copy in copies:
        copy.wait()


def place_pieces(pieces, places, width_here):
    blocks, tokens, _ = pieces[0].shape
    width = width_here * lax.axis_size("head")
    return pl.pallas_call(
        functools.partial(place_kernel, places, width_here),
        in_specs=[pl.BlockSpec(memory_space=pl.ANY)] * len(pieces),
        out_specs=pl.BlockSpec(memory_space=pltpu.HBM),
        out_shape=jax.ShapeDtypeStruct((blocks, tokens, width), jnp.bfloat16),
        scratch_shapes=[pltpu.SemaphoreType.DMA((len(pieces),))],
        compiler_params=pltpu.CompilerParams(vmem_limit_bytes=VMEM),
    )(*pieces)


def shifted(array, axis, distance):
    count = lax.axis_size(axis)
    return lax.ppermute(array, axis, [(i, (i + distance) % count) for i in range(count)])


def exchange(pieces, direction):
    return [shifted(piece, "head", direction * s) for s, piece in enumerate(pieces, 1)]


def forward(sent):
    return [shifted(block, "tm", distance) for distance, block in enumerate(sent, 1)]


def shards(query_rows, key_rows, value_rows, pair_list, block_tokens):
    count_head = lax.axis_size("head")
    count_tm = lax.axis_size("tm")
    blocks, tokens, width = query_rows.shape
    width_here = width // count_head
    heads = width_here // HD
    cut = (heads + 1) // 2 * HD
    parts = [(0, cut), (cut, width_here - cut)] if heads > 1 else [(0, width_here)]
    arrays = [query_rows, key_rows, value_rows]
    messages = [[(1,) + part, (2,) + part] for part in parts]
    pieces, token = rotate_pieces(arrays, messages[0], count_head)
    picks, bias, query, later = plan(
        arrays, messages[1:], pair_list, block_tokens, token, count_head, count_tm
    )
    received = [piece[:1] + exchange(piece[1:], 1) for piece in [pieces] + later]
    inputs, held = [], query
    for owns, (_, size) in zip(received, parts):
        picked = pick_blocks(picks, owns, (0, 2 * size), count_tm, held, not inputs)
        if not inputs:
            *picked, query = picked
        inputs.append((owns, forward(picked)))
        held = inputs[-1][1][len(picked) // 2]
    query = lax.all_to_all(query, "head", split_axis=0, concat_axis=0, tiled=True)
    distances, after = list(range(1, count_head)), ()
    pieces, places = [], []
    for at, part in enumerate(parts):
        cost = NO_COST if at == len(parts) - 1 else HIGH_COST
        leaving = attend(
            block_tokens, bias, query, [inputs[at]], [part], distances, after, cost
        )
        after = (leaving[0],)
        pieces += exchange(leaving, -1)
        places += [(s, part[0]) for s in distances]
    pieces += attend(block_tokens, bias, query, inputs, parts, [0], after)
    return place_pieces(pieces, places + [(0, 0)], width_here)


def solution(mesh):
    placed = (
        P(("grp", "tm"), "head", None),
        P(("grp", "tm"), "head", None),
        P(("grp", "tm"), "head", None),
        P("grp", None),
        P("grp"),
    )
    return jax.shard_map(
        shards,
        mesh=mesh,
        in_specs=placed,
        out_specs=P(("grp", "tm"), "head", None),
        check_vma=False,
    )
```

```python
import functools
import math

import jax
import jax.numpy as jnp
from jax import lax
from jax.experimental import pallas as pl
from jax.experimental.pallas import tpu as pltpu
from jax.sharding import PartitionSpec as P

HD = 128
BLK = 64
NEAR_CAP = 2
FAR_CAP = 1
NEG = -1e30
ROTATE_SCALE = 1.0 / math.sqrt(HD)
SCORE_SCALE = 1.0 / math.sqrt(HD)
VMEM = 24 * 1024 * 1024
WIDE_VMEM = 60 * 1024 * 1024
TOKEN = jax.ShapeDtypeStruct((8, 128), jnp.float32)
NO_COST = pl.CostEstimate(flops=0, bytes_accessed=0, transcendentals=0)
HIGH_COST = pl.CostEstimate(flops=10**11, bytes_accessed=0, transcendentals=0)
LOG2E = math.log2(math.e)


def sign_matrix():
    common = lax.broadcasted_iota(jnp.int32, (HD, HD), 0) & lax.broadcasted_iota(
        jnp.int32, (HD, HD), 1
    )
    bits = HD.bit_length() - 1
    parity = common
    for bit in range(1, bits):
        parity = parity ^ (common >> bit)
    return jnp.where((parity & 1) == 0, 1.0, -1.0).astype(jnp.bfloat16)


def rows_of(block):
    rows, width = math.prod(block.shape[:-1]), block.shape[-1]
    if block.shape[-2] % 16 == 0:
        return block.reshape(rows, width)
    return block.astype(jnp.float32).reshape(rows, width).astype(block.dtype)


def fields_of(message):
    at, fields = 0, []
    for source, start, size in message:
        fields.append((source, start, size, at))
        at += size
    return fields, at


def by_distance(refs, count, direction):
    if len(refs[0].shape) == 3:
        return list(refs)
    me = lax.axis_index("head")
    return [refs[0].at[lax.rem(me + direction * s + count, count)] for s in range(count)]


def rotated(block, sign):
    blocks, tokens, size = block.shape
    flat = rows_of(block)
    heads = [flat[:, at : at + HD] for at in range(0, size, HD)]
    turned = jnp.dot(jnp.concatenate(heads, axis=0), sign, preferred_element_type=jnp.float32)
    return (turned * ROTATE_SCALE).reshape(size // HD, blocks, tokens, HD).astype(jnp.bfloat16)


def store_heads(out, start, turned):
    for h in range(turned.shape[0]):
        at = start + h * HD
        out[:, :, at : at + HD] = turned[h]


def rotate_kernel(message, sources, count_head, *refs):
    fields, total = fields_of(message)
    ins = dict(zip(sources, refs))
    outs, (token, buffer, sems) = refs[len(sources) : -3], refs[-3:]
    token[...] = jnp.zeros_like(token)
    width_here = refs[0].shape[2] // count_head
    me = lax.axis_index("head")
    order = list(range(1, count_head)) + [0]
    copies = {}
    for s in order:
        goal = lax.rem(me + s, count_head)
        for f, (source, start, size, at) in enumerate(fields):
            column = pl.multiple_of(goal * width_here + start, HD)
            copies[s, f] = pltpu.make_async_copy(
                ins[source].at[:, :, pl.ds(column, size)],
                buffer.at[s, :, :, pl.ds(at, size)],
                sems.at[s, f],
            )
            copies[s, f].start()
    sign = sign_matrix()
    for s in order:
        for f, (_, _, size, start) in enumerate(fields):
            copies[s, f].wait()
            store_heads(outs[s], start, rotated(buffer[s, :, :, start : start + size], sign))


def rotate_here(fields, ins, outs, distances, count_head, sign):
    width_here = next(iter(ins.values())).shape[2] // count_head
    me = lax.axis_index("head")
    for s in distances:
        goal = lax.rem(me + s, count_head)
        for source, start, size, at in fields:
            column = pl.multiple_of(goal * width_here + start, HD)
            store_heads(outs[s], at, rotated(ins[source][:, :, pl.ds(column, size)], sign))


def rotate_pieces(arrays, message, count_head):
    blocks, tokens, _ = arrays[0].shape
    fields, total = fields_of(message)
    sources = sorted({source for source, _, _ in message})
    one = (blocks, tokens, total)
    *pieces, token = pl.pallas_call(
        functools.partial(rotate_kernel, message, sources, count_head),
        in_specs=[pl.BlockSpec(memory_space=pltpu.HBM)] * len(sources),
        out_specs=[pl.BlockSpec(memory_space=pltpu.VMEM)] * (count_head + 1),
        out_shape=[jax.ShapeDtypeStruct(one, jnp.bfloat16)] * count_head + [TOKEN],
        scratch_shapes=[
            pltpu.VMEM((count_head,) + one, jnp.bfloat16),
            pltpu.SemaphoreType.DMA((count_head, len(fields))),
        ],
        cost_estimate=NO_COST,
        compiler_params=pltpu.CompilerParams(vmem_limit_bytes=WIDE_VMEM),
    )(*[arrays[source] for source in sources])
    return pieces, token


def slots_at(distance, count_tm):
    return NEAR_CAP if distance in (1, count_tm - 1) else FAR_CAP


def pick_kernel(count_head, count_tm, lanes, picks_ref, *refs):
    pieces, outs = refs[:count_head], refs[count_head + 1 : count_head + count_tm]
    shard = lax.axis_index("tm")
    for distance, out in enumerate(outs, 1):
        goal = lax.rem(shard + distance, count_tm)
        for k in range(slots_at(distance, count_tm)):
            pick = picks_ref[NEAR_CAP * goal + k]
            for s in range(count_head):
                out[k, s] = pieces[s][pick, :, lanes[0] : lanes[1]]


def pick_blocks(picks, pieces, lanes, count_tm, held, passes):
    count_head = len(pieces)
    one = (count_head, pieces[0].shape[1], lanes[1] - lanes[0])
    vmem, anywhere = pl.BlockSpec(memory_space=pltpu.VMEM), pl.BlockSpec(memory_space=pl.ANY)
    shapes = [
        jax.ShapeDtypeStruct((slots_at(distance, count_tm),) + one, jnp.bfloat16)
        for distance in range(1, count_tm)
    ]
    passed = [jax.ShapeDtypeStruct(held.shape, held.dtype)] if passes else []
    return pl.pallas_call(
        functools.partial(pick_kernel, count_head, count_tm, lanes),
        in_specs=[pl.BlockSpec(memory_space=pltpu.SMEM)] + [vmem] * count_head + [anywhere],
        out_specs=[vmem] * len(shapes) + [anywhere] * len(passed),
        out_shape=shapes + passed,
        input_output_aliases={1 + count_head: len(shapes)} if passes else {},
        cost_estimate=HIGH_COST,
        compiler_params=pltpu.CompilerParams(vmem_limit_bytes=VMEM),
    )(picks, *pieces, held)


def remote_rows(count_tm):
    return [
        (distance, k)
        for distance in range(1, count_tm)
        for k in range(slots_at(distance, count_tm))
    ]


def split(value, by):
    if by & (by - 1) == 0:
        return value >> (by.bit_length() - 1), value & (by - 1)
    return lax.div(value, by), lax.rem(value, by)


def plan_kernel(messages, count_head, count_tm, blocks, *refs):
    *sources, pair_hbm, tokens_ref, _ = refs[:6]
    picks_ref, bias_ref, query_out = refs[6:9]
    pair_ref, named_ref, table_ref, pair_sem, table_sem = refs[-5:]
    outs = refs[9:-5]
    ins = dict(enumerate(sources))
    pair_copy = pltpu.make_async_copy(pair_hbm, pair_ref, pair_sem)
    pair_copy.start()
    sign = sign_matrix()
    places = list(range(1, count_head)) + [0]
    jobs = [
        (fields_of(message)[0], outs[m * count_head : (m + 1) * count_head], s)
        for m, message in enumerate(messages)
        for s in places
    ]
    query_fields = [(0, 0, query_out.shape[-1], 0)]
    jobs += [(query_fields, by_distance([query_out], count_head, 1), s) for s in places]
    half = len(jobs) // 2
    for fields, pieces, s in jobs[:half]:
        rotate_here(fields, ins, pieces, [s], count_head, sign)
    pair_copy.wait()
    total_blocks, columns = pair_ref.shape
    pairs = pair_ref[...]
    lane = lax.broadcasted_iota(jnp.int32, named_ref.shape, 1)
    named = jnp.zeros(named_ref.shape, jnp.int32)
    for c in range(columns):
        named = jnp.where(pairs[:, c : c + 1] == lane, 1, named)
    named_ref[...] = named
    copy = pltpu.make_async_copy(named_ref, table_ref, table_sem)
    copy.start()
    for fields, pieces, s in jobs[half:]:
        rotate_here(fields, ins, pieces, [s], count_head, sign)
    copy.wait()
    shard = lax.axis_index("tm")
    place = lax.axis_index("head")
    mine = shard * blocks

    def two_picks(wanted):
        picks = [jnp.int32(0)] * NEAR_CAP
        count = jnp.int32(0)
        for j in range(blocks):
            for k in range(NEAR_CAP):
                picks[k] = jnp.where((wanted[j] > 0) & (count == k), j, picks[k])
            count = count + wanted[j]
        return picks, count

    def named_by(rows, column):
        found = table_ref[rows, column]
        for i in range(1, blocks):
            found = found | table_ref[rows + i, column]
        return found

    for d in range(count_tm):
        picks, _ = two_picks([named_by(d * blocks, mine + j) for j in range(blocks)])
        for k in range(NEAR_CAP):
            picks_ref[NEAR_CAP * d + k] = picks[k]

    kept = [[table_ref[mine + i, mine + j] * tokens_ref[mine + j] for j in range(blocks)] for i in range(blocks)]
    arrivals = {}
    for distance, k in remote_rows(count_tm):
        first = lax.rem(shard - distance + count_tm, count_tm) * blocks
        if k == 0:
            arrivals[distance] = two_picks([named_by(mine, first + j) for j in range(blocks)])
        picks, count = arrivals[distance]
        there = first + picks[k]
        live = jnp.where(count > k, tokens_ref[there], 0)
        for i in range(blocks):
            kept[i].append(table_ref[mine + i, there] * live)

    total = bias_ref.shape[1]
    piece_rows = BLK // count_head
    at = lax.broadcasted_iota(jnp.int32, (blocks, total), 1)
    query = lax.broadcasted_iota(jnp.int32, (blocks, total), 0)
    own = at < blocks * BLK
    group, token = split(at, piece_rows)
    own_piece, own_block = split(group, blocks)
    far_row, far_group = split(group, count_head)
    row = jnp.where(own, own_block, far_row)
    piece = jnp.where(own, own_piece, far_group)
    source = jnp.where(piece > place, place - piece + count_head, place - piece)
    position = source * piece_rows + token
    limit = jnp.zeros((blocks, total), jnp.int32)
    for r in range(len(kept[0])):
        value = jnp.zeros((blocks, total), jnp.int32)
        for i in range(blocks):
            value = jnp.where(query == i, kept[i][r], value)
        limit = jnp.where(row == r, value, limit)
    bias_ref[...] = jnp.where(position < limit, 0.0, NEG)


def plan(arrays, messages, pair_list, block_tokens, after, count_head, count_tm):
    blocks, tokens, _ = arrays[0].shape
    total_blocks, columns = pair_list.shape
    lanes = -(-total_blocks // 128) * 128
    total = (blocks + len(remote_rows(count_tm))) * BLK
    vmem = pl.BlockSpec(memory_space=pltpu.VMEM)
    smem = pl.BlockSpec(memory_space=pltpu.SMEM)
    stacked = (count_head, blocks, tokens, arrays[0].shape[2] // count_head)
    shapes = [jax.ShapeDtypeStruct(stacked, jnp.bfloat16)] + [
        jax.ShapeDtypeStruct((blocks, tokens, fields_of(message)[1]), jnp.bfloat16)
        for message in messages
        for _ in range(count_head)
    ]
    picks, bias, query, *pieces = pl.pallas_call(
        functools.partial(plan_kernel, messages, count_head, count_tm, blocks),
        in_specs=[vmem] * 3
        + [pl.BlockSpec(memory_space=pl.ANY), smem, pl.BlockSpec(memory_space=pl.ANY)],
        out_specs=[smem, vmem] + [vmem] * len(shapes),
        out_shape=[
            jax.ShapeDtypeStruct((NEAR_CAP * count_tm,), jnp.int32),
            jax.ShapeDtypeStruct((blocks, total), jnp.float32),
        ]
        + shapes,
        scratch_shapes=[
            pltpu.VMEM((total_blocks, columns), jnp.int32),
            pltpu.VMEM((total_blocks, lanes), jnp.int32),
            pltpu.SMEM((total_blocks, lanes), jnp.int32),
            pltpu.SemaphoreType.DMA,
            pltpu.SemaphoreType.DMA,
        ],
        cost_estimate=NO_COST,
        compiler_params=pltpu.CompilerParams(vmem_limit_bytes=VMEM),
    )(*arrays, pair_list, block_tokens, after)
    return picks, bias, query, [pieces[at : at + count_head] for at in range(0, len(pieces), count_head)]


def attend_kernel(counts, heads_of, distances, tokens_ref, bias_ref, query_ref, *refs):
    count_head, count_tm = counts
    queries = by_distance([query_ref], count_head, -1)
    per_part = count_head + count_tm - 1
    parts = [refs[p * per_part : (p + 1) * per_part] for p in range(len(heads_of))]
    outs = refs[len(heads_of) * per_part :][-len(distances) :]
    blocks, tokens, _ = outs[0].shape
    rows = len(distances) * tokens
    shard = lax.axis_index("tm")
    me = lax.axis_index("head")
    bias = bias_ref[...][:, None, :]
    place_of = [(p, h) for p, (_, size) in enumerate(heads_of) for h in range(size // HD)]

    def gathered(kind, head):
        p, h = place_of[head]
        first = kind * heads_of[p][1] + h * HD
        lanes = slice(first, first + HD)
        pieces = [rows_of(own[:, :, lanes]) for own in parts[p][:count_head]]
        pieces += [
            rows_of(parts[p][count_head + distance - 1][k, :, :, lanes])
            for distance, k in remote_rows(count_tm)
        ]
        return jnp.concatenate(pieces, axis=0)

    def products(head):
        first = heads_of[0][0] + head * HD
        lanes = slice(first, first + HD)
        query = jnp.concatenate(
            [rows_of(queries[s][i, :, lanes]) for i in range(blocks) for s in distances], axis=0
        )
        return lax.dot_general(
            query, gathered(0, head), (((1,), (1,)), ((), ())), preferred_element_type=jnp.float32
        )

    heads = len(place_of)
    dots = jnp.concatenate([products(h) for h in range(heads)], axis=0)
    dots = dots.reshape(heads, blocks, rows, -1) + bias
    peak = jnp.max(dots, axis=-1, keepdims=True)
    weights = jnp.exp2((dots - peak) * (SCORE_SCALE * LOG2E))
    inverse = 1.0 / jnp.sum(weights, axis=-1, keepdims=True)
    weights_half = weights.astype(jnp.bfloat16).reshape(heads, blocks * rows, -1)
    mixed = [
        jnp.dot(weights_half[h], gathered(1, h), preferred_element_type=jnp.float32)
        for h in range(heads)
    ]
    mixed = jnp.concatenate(mixed, axis=0) * inverse.reshape(heads * blocks * rows, 1)
    sign = sign_matrix()
    high = mixed.astype(jnp.bfloat16)
    low = (mixed - high.astype(jnp.float32)).astype(jnp.bfloat16)
    turned = jnp.dot(high, sign, preferred_element_type=jnp.float32)
    turned = turned + jnp.dot(low, sign, preferred_element_type=jnp.float32)
    turned = (turned * ROTATE_SCALE).reshape(heads, blocks, len(distances), tokens, HD)
    token = lax.broadcasted_iota(jnp.int32, (tokens, HD), 0)
    for at, s in enumerate(distances):
        position = lax.rem(me - s + count_head, count_head) * tokens + token
        for i in range(blocks):
            live = position < tokens_ref[shard * blocks + i]
            for h in range(heads):
                outs[at][i, :, h * HD : (h + 1) * HD] = jnp.where(
                    live, turned[h, i, at], 0.0
                ).astype(jnp.bfloat16)


def attend(block_tokens, bias, query, parts, heads_of, distances, after=(), cost=NO_COST):
    count_head, count_tm = query.shape[0], len(parts[0][1]) + 1
    operands = [ref for owns, slots in parts for ref in owns + slots]
    shape = query.shape[1:3] + (sum(size for _, size in heads_of),)
    vmem = pl.BlockSpec(memory_space=pltpu.VMEM)
    return pl.pallas_call(
        functools.partial(attend_kernel, (count_head, count_tm), heads_of, distances),
        in_specs=[pl.BlockSpec(memory_space=pltpu.SMEM)]
        + [vmem] * (2 + len(operands))
        + [pl.BlockSpec(memory_space=pl.ANY)] * len(after),
        out_specs=[vmem] * len(distances),
        out_shape=[jax.ShapeDtypeStruct(shape, jnp.bfloat16)] * len(distances),
        cost_estimate=cost,
        compiler_params=pltpu.CompilerParams(vmem_limit_bytes=VMEM),
    )(block_tokens, bias, query, *operands, *after)


def place_kernel(places, width_here, *refs):
    pieces, out_ref, sems = refs[:-2], refs[-2], refs[-1]
    me, count = lax.axis_index("head"), lax.axis_size("head")
    copies = []
    for at, (piece, (s, start)) in enumerate(zip(pieces, places)):
        column = pl.multiple_of(lax.rem(me + s, count) * width_here + start, HD)
        copies.append(
            pltpu.make_async_copy(
                piece, out_ref.at[:, :, pl.ds(column, piece.shape[-1])], sems.at[at]
            )
        )
        copies[-1].start()
    for copy in copies:
        copy.wait()


def place_pieces(pieces, places, width_here):
    blocks, tokens, _ = pieces[0].shape
    width = width_here * lax.axis_size("head")
    return pl.pallas_call(
        functools.partial(place_kernel, places, width_here),
        in_specs=[pl.BlockSpec(memory_space=pl.ANY)] * len(pieces),
        out_specs=pl.BlockSpec(memory_space=pltpu.HBM),
        out_shape=jax.ShapeDtypeStruct((blocks, tokens, width), jnp.bfloat16),
        scratch_shapes=[pltpu.SemaphoreType.DMA((len(pieces),))],
        compiler_params=pltpu.CompilerParams(vmem_limit_bytes=VMEM),
    )(*pieces)


def shifted(array, axis, distance):
    count = lax.axis_size(axis)
    return lax.ppermute(array, axis, [(i, (i + distance) % count) for i in range(count)])


def exchange(pieces, direction):
    return [shifted(piece, "head", direction * s) for s, piece in enumerate(pieces, 1)]


def forward(sent):
    return [shifted(block, "tm", distance) for distance, block in enumerate(sent, 1)]


def shards(query_rows, key_rows, value_rows, pair_list, block_tokens):
    count_head = lax.axis_size("head")
    count_tm = lax.axis_size("tm")
    blocks, tokens, width = query_rows.shape
    width_here = width // count_head
    heads = width_here // HD
    cut = (heads + 1) // 2 * HD
    parts = [(0, cut), (cut, width_here - cut)] if heads > 1 else [(0, width_here)]
    arrays = [query_rows, key_rows, value_rows]
    messages = [[(1,) + part, (2,) + part] for part in parts]
    pieces, token = rotate_pieces(arrays, messages[0], count_head)
    picks, bias, query, later = plan(
        arrays, messages[1:], pair_list, block_tokens, token, count_head, count_tm
    )
    received = [piece[:1] + exchange(piece[1:], 1) for piece in [pieces] + later]
    inputs, held = [], query
    for owns, (_, size) in zip(received, parts):
        picked = pick_blocks(picks, owns, (0, 2 * size), count_tm, held, not inputs)
        if not inputs:
            *picked, query = picked
        inputs.append((owns, forward(picked)))
        held = inputs[-1][1][0]
    query = lax.all_to_all(query, "head", split_axis=0, concat_axis=0, tiled=True)
    distances, after = list(range(1, count_head)), ()
    pieces, places = [], []
    for at, part in enumerate(parts):
        cost = NO_COST if at == len(parts) - 1 else HIGH_COST
        leaving = attend(
            block_tokens, bias, query, [inputs[at]], [part], distances, after, cost
        )
        after = (leaving[0],)
        pieces += exchange(leaving, -1)
        places += [(s, part[0]) for s in distances]
    pieces += attend(block_tokens, bias, query, inputs, parts, [0], after)
    return place_pieces(pieces, places + [(0, 0)], width_here)


def solution(mesh):
    placed = (
        P(("grp", "tm"), "head", None),
        P(("grp", "tm"), "head", None),
        P(("grp", "tm"), "head", None),
        P("grp", None),
        P("grp"),
    )
    return jax.shard_map(
        shards,
        mesh=mesh,
        in_specs=placed,
        out_specs=P(("grp", "tm"), "head", None),
        check_vma=False,
    )
```
